32 devices in a mesh: segment: 4 (over y, x), dom: 8 (over z, core).
Axes of the slice: x: 2, y: 2, z: 4, core: 2. Of those that a mesh axis runs over, the one named last changes fastest.
Arguments:
- grid_state: bfloat16 [4, 1024, 227], P(None, 'dom'), may hold values from -6 to 6
- w_embed: bfloat16 [227, 512], replicated, may hold values from -0.375 to 0.375
- w_project: bfloat16 [4, 512, 1024], P('segment'), may hold values from -0.25 to 0.25
- w_message: bfloat16 [4, 512, 512], P('segment'), may hold values from -0.25 to 0.25
- w_update: bfloat16 [4, 1024, 512], P('segment'), may hold values from -0.1875 to 0.1875
- w_decode: bfloat16 [1024, 512], replicated, may hold values from -0.1875 to 0.1875
- w_output: bfloat16 [512, 227], replicated, may hold values from -0.25 to 0.25
- grid_mesh: int32 [1024], P('dom'), may hold values from 0 to 63
- mesh_grid: int32 [1024], P('dom'), may hold values from 0 to 63
- neighbors: int32 [512, 8], P('dom'), may hold values from 0 to 319
- send_rows: int32 [4, 512], P(None, 'dom'), may hold values from 0 to 63
- halo_count: int32 [4, 8], P(None, 'dom'), may hold values from 16 to 64, as said below
Outputs:
- prediction: bfloat16 [4, 1024, 227], P('segment', 'dom')
The draws below stay inside these ranges and needn't reach their ends.
Inputs may be any that keep to these rules, and one draw needn't show every extreme that they name: `halo_count`: at least 16; some list of some partition is full in every draw. `neighbors`: rows 0 to 63 are the node's own partition, then four blocks of 64 rows from the partitions -1, +1, -2, +2 away.
All inputs are finite; a program needn't handle non-finite values.
Results may differ from the reference program's by a relative error of at most 0.018.
Values may be sent and summed in bfloat16 or wider, within the bound.
No kernel may reach another device: no remote copies, remote signals or barrier semaphores. Data moves between devices by JAX's collectives and lax.ppermute only.
A program may use at most 64 MiB of HBM per device.

```python
import jax
import jax.numpy as jnp
from jax import lax

WIDTH = 512
CHANNELS = 227
GRID_DEV = 128
MESH_DEV = 64
FANOUT = 8
MICRO = 4
HALO = 64
PARTS_SIZE = 8
NGRID = 1024
NMESH = 512
NHALO = 512


def draw_halo_count(key, part):
    key = jax.random.fold_in(key, 11)
    first, second = jax.random.split(key)
    counts = jax.random.randint(first, (4 * PARTS_SIZE,), HALO // 4, HALO + 1).astype(jnp.int32)
    chosen = jax.random.randint(second, (), 0, 4 * PARTS_SIZE).astype(jnp.int32)
    filled = jnp.where(jnp.arange(4 * PARTS_SIZE, dtype=jnp.int32) == chosen, HALO, counts)
    return filled.reshape(4, PARTS_SIZE).astype(jnp.int32)


def with_ends(result, stream_key, least, high):
    longest = result.shape.index(max(result.shape))
    spots = []
    for shift in (0, 1):
        where = [jax.random.randint(jax.random.fold_in(stream_key, axis), (), 0, length) for axis, length in enumerate(result.shape)]
        where[longest] = (where[longest] + shift) % result.shape[longest]
        spots.append(tuple(where))
    return result.at[spots[0]].set(least).at[spots[1]].set(high)


def shard_levels(stream_key, shape, cuts, low, top_value):
    factor_of, own = 1.0, jax.random.fold_in(stream_key, 6)
    for position, parts in cuts:
        draws = jnp.exp(jax.random.uniform(jax.random.fold_in(own, position), (parts,), jnp.float32, low / len(cuts), top_value / len(cuts)))
        factor_of = factor_of * jnp.repeat(draws, shape[position] // parts).reshape([-1 if axis == position else 1 for axis in range(len(shape))])
    return factor_of


def bell_draw(stream_key, shape, spread, reach, cuts=(), kind=jnp.bfloat16):
    factor_of = shard_levels(stream_key, shape, cuts, -0.22, 0.18) if cuts else 1.0
    drawn = jax.random.normal(stream_key, shape, jnp.float32) * spread * factor_of
    return jnp.minimum(jnp.maximum(drawn, -reach), reach).astype(kind)


def setup_inputs(seed: int = 0) -> dict:
    key_list = jax.random.split(jax.random.key(seed), 13)
    grid_state = bell_draw(key_list[0], (MICRO, NGRID, CHANNELS), 1.0, 6.0, ((1, 8),))
    w_embed = bell_draw(key_list[1], (CHANNELS, WIDTH), CHANNELS ** -0.5, 0.375)
    w_project = bell_draw(key_list[2], (4, WIDTH, 2 * WIDTH), WIDTH ** -0.5, 0.25, ((0, 4),))
    w_message = bell_draw(key_list[3], (4, WIDTH, WIDTH), WIDTH ** -0.5, 0.25, ((0, 4),))
    w_update = bell_draw(key_list[4], (4, 2 * WIDTH, WIDTH), (2 * WIDTH) ** -0.5, 0.1875, ((0, 4),))
    w_decode = bell_draw(key_list[5], (2 * WIDTH, WIDTH), (2 * WIDTH) ** -0.5, 0.1875)
    w_output = bell_draw(key_list[6], (WIDTH, CHANNELS), WIDTH ** -0.5, 0.25)
    grid_mesh = with_ends(jax.random.randint(key_list[7], (NGRID,), 0, MESH_DEV), jax.random.fold_in(key_list[7], 1), 0, MESH_DEV - 1).astype(jnp.int32)
    mesh_grid = with_ends(jax.random.randint(key_list[8], (NGRID,), 0, MESH_DEV), jax.random.fold_in(key_list[8], 1), 0, MESH_DEV - 1).astype(jnp.int32)
    neighbors = with_ends(jax.random.randint(key_list[9], (NMESH, FANOUT), 0, MESH_DEV + 4 * HALO), jax.random.fold_in(key_list[9], 1), 0, (MESH_DEV + 4 * HALO) - 1).astype(jnp.int32)
    send_rows = with_ends(jax.random.randint(key_list[10], (4, NHALO), 0, MESH_DEV), jax.random.fold_in(key_list[10], 1), 0, MESH_DEV - 1).astype(jnp.int32)
    halo_count = draw_halo_count(jax.random.fold_in(key_list[12], 71), 0)
    return dict(grid_state=grid_state, w_embed=w_embed, w_project=w_project, w_message=w_message, w_update=w_update, w_decode=w_decode, w_output=w_output, grid_mesh=grid_mesh, mesh_grid=mesh_grid, neighbors=neighbors, send_rows=send_rows, halo_count=halo_count)


epsilon = 1e-05

def rms_scale(values):
    return values * lax.rsqrt(lax.optimization_barrier(jnp.mean(values * values, axis=-1, keepdims=True)) + epsilon)

def encode(snapshot, w_embed, grid_mesh):
    latent = jax.nn.silu(jnp.dot(snapshot, w_embed, preferred_element_type=jnp.float32)).astype(jnp.bfloat16)
    grouped = latent.reshape(PARTS_SIZE, GRID_DEV, WIDTH).astype(jnp.float32)
    owners = grid_mesh.reshape(PARTS_SIZE, GRID_DEV)
    table = (owners[:, None, :] == jnp.arange(MESH_DEV, dtype=jnp.int32)[None, :, None]).astype(jnp.float32)
    pooled = jnp.einsum('pvg,pgw->pvw', table, grouped)
    return (latent, rms_scale(pooled).astype(jnp.bfloat16).reshape(NMESH, WIDTH))

def process(state, w_project, w_message, w_update, neighbors, send_rows, halo_count):
    projected = jnp.dot(state, w_project, preferred_element_type=jnp.float32)
    receiver = projected[:, :WIDTH]
    sender = projected[:, WIDTH:].astype(jnp.bfloat16).reshape(PARTS_SIZE, MESH_DEV, WIDTH)
    lists = jnp.transpose(send_rows.reshape(4, PARTS_SIZE, HALO), (1, 0, 2))
    picked = jax.vmap(lambda table, rows: table[rows])(sender, lists)
    valid = jnp.arange(HALO, dtype=jnp.int32)[None, None, :] < jnp.transpose(halo_count)[:, :, None]
    picked = jnp.where(valid[..., None], picked, jnp.zeros_like(picked))
    extended = jnp.concatenate([sender, jnp.roll(picked[:, 0], 1, axis=0), jnp.roll(picked[:, 1], -1, axis=0), jnp.roll(picked[:, 2], 2, axis=0), jnp.roll(picked[:, 3], -2, axis=0)], axis=1)
    sources = neighbors.reshape(PARTS_SIZE, MESH_DEV * FANOUT)
    fetched = jax.vmap(lambda table, rows: table[rows])(extended, sources).reshape(NMESH, FANOUT, WIDTH)
    edges = jax.nn.silu(receiver[:, None, :] + fetched.astype(jnp.float32)).astype(jnp.bfloat16)
    messages = jnp.dot(edges.reshape(NMESH * FANOUT, WIDTH), w_message, preferred_element_type=jnp.float32)
    aggregate = (lax.optimization_barrier(jnp.sum(messages.reshape(NMESH, FANOUT, WIDTH), axis=1)) / FANOUT).astype(jnp.bfloat16)
    update = jax.nn.silu(jnp.dot(state, w_update[:WIDTH], preferred_element_type=jnp.float32) + jnp.dot(aggregate, w_update[WIDTH:], preferred_element_type=jnp.float32))
    return (state.astype(jnp.float32) + rms_scale(update)).astype(jnp.bfloat16)

def decode(state, latent, mesh_grid, w_decode, w_output):
    tables = state.reshape(PARTS_SIZE, MESH_DEV, WIDTH)
    rows = mesh_grid.reshape(PARTS_SIZE, GRID_DEV)
    readout = jax.vmap(lambda table, picks: table[picks])(tables, rows).reshape(NGRID, WIDTH)
    hidden = jax.nn.silu(jnp.dot(latent, w_decode[:WIDTH], preferred_element_type=jnp.float32) + jnp.dot(readout, w_decode[WIDTH:], preferred_element_type=jnp.float32)).astype(jnp.bfloat16)
    return jnp.dot(hidden, w_output, preferred_element_type=jnp.float32).astype(jnp.bfloat16)

def reference(grid_state, w_embed, w_project, w_message, w_update, w_decode, w_output, grid_mesh, mesh_grid, neighbors, send_rows, halo_count):
    outputs = []
    for sample in range(MICRO):
        latent, state = encode(grid_state[sample], w_embed, grid_mesh)
        for layer in range(4):
            state = process(state, w_project[layer], w_message[layer], w_update[layer], neighbors, send_rows, halo_count)
        outputs.append(decode(state, latent, mesh_grid, w_decode, w_output))
    return jnp.stack(outputs)
```

```python
import functools

import jax
import jax.numpy as jnp
from jax import lax
from jax.experimental import pallas as pl
from jax.experimental.pallas import tpu as pltpu
from jax.sharding import PartitionSpec as P

epsilon = 1e-05
VMEM = pl.BlockSpec(memory_space=pltpu.VMEM)
SMEM = pl.BlockSpec(memory_space=pltpu.SMEM)


def from_behind(value, axis, steps):
    count = lax.axis_size(axis)
    pairs = [(source, (source + steps) % count) for source in range(count)]
    return lax.ppermute(value, axis, pairs)


def from_behind_2(block, axis, distance):
    devices = range(lax.axis_size(axis))
    route = [(i - distance, i) for i in devices if i - distance in devices]
    return lax.ppermute(block, axis, route)


def from_root(value, axis, source):
    kept = jnp.where(lax.axis_index(axis) == source, value, 0).astype(value.dtype)
    return lax.psum(kept, axis)


def rms_scale(values):
    return values * lax.rsqrt(jnp.mean(values * values, axis=-1, keepdims=True) + epsilon)


def streamed(
    grid_state,
    w_embed,
    w_project,
    w_message,
    w_update,
    w_decode,
    w_output,
    grid_mesh,
    mesh_grid,
    neighbors,
    send_rows,
    halo_count,
):
    segment_index = lax.axis_index("segment")
    segment_count = lax.axis_size("segment")
    final_segment = segment_count - 1
    samples, grid_rows, channels = grid_state.shape
    width = w_embed.shape[1]
    mesh_rows = neighbors.shape[0]
    fanout = neighbors.shape[1]
    halo_rows = send_rows.shape[1]
    share = samples // segment_count
    pool_table = (grid_mesh[None, :] == jnp.arange(mesh_rows, dtype=jnp.int32)[:, None]).astype(
        jnp.bfloat16
    )
    read_table = (mesh_grid[:, None] == jnp.arange(mesh_rows, dtype=jnp.int32)[None, :]).astype(
        jnp.bfloat16
    )
    valid_rows = jnp.arange(halo_rows, dtype=jnp.int32)[None, :] < halo_count[:, 0][:, None]
    source_rows = neighbors.reshape(mesh_rows * fanout)

    def embed_grid(snapshot):
        return jax.nn.silu(jnp.dot(snapshot, w_embed, preferred_element_type=jnp.float32)).astype(
            jnp.bfloat16
        )

    def encode(snapshot):
        latent = embed_grid(snapshot)
        pooled = jnp.dot(pool_table, latent, preferred_element_type=jnp.float32)
        return (rms_scale(pooled).astype(jnp.bfloat16), latent)

    def project(state, weights):
        projected = jnp.dot(state, weights[0], preferred_element_type=jnp.float32)
        return (projected[:, :width], projected[:, width:].astype(jnp.bfloat16))

    def renew(state, receiver, extended, weights):
        fetched = extended[source_rows].reshape(mesh_rows, fanout, width)
        edges = jax.nn.silu(receiver[:, None, :] + fetched.astype(jnp.float32)).astype(jnp.bfloat16)
        messages = jnp.dot(
            edges.reshape(mesh_rows * fanout, width), weights[1], preferred_element_type=jnp.float32
        )
        aggregate = (jnp.sum(messages.reshape(mesh_rows, fanout, width), axis=1) / fanout).astype(
            jnp.bfloat16
        )
        update = jax.nn.silu(
            jnp.dot(state, weights[2][:width], preferred_element_type=jnp.float32)
            + jnp.dot(aggregate, weights[2][width:], preferred_element_type=jnp.float32)
        )
        return (state.astype(jnp.float32) + rms_scale(update)).astype(jnp.bfloat16)

    def decode(state, latent):
        readout = jnp.dot(read_table, state, preferred_element_type=jnp.float32).astype(
            jnp.bfloat16
        )
        hidden = jax.nn.silu(
            jnp.dot(latent, w_decode[:width], preferred_element_type=jnp.float32)
            + jnp.dot(readout, w_decode[width:], preferred_element_type=jnp.float32)
        ).astype(jnp.bfloat16)
        return jnp.dot(hidden, w_output, preferred_element_type=jnp.float32).astype(jnp.bfloat16)

    own_weights = (w_project[0], w_message[0], w_update[0])
    empty_mesh = jnp.zeros((mesh_rows, width), jnp.bfloat16)
    empty_receiver = jnp.zeros((mesh_rows, width), jnp.float32)
    empty_grid = jnp.zeros((grid_rows, width), jnp.bfloat16)
    empty_output = jnp.zeros((grid_rows, channels), jnp.bfloat16)
    received = empty_mesh
    carried = {}
    results = [empty_output for sample in range(samples)]
    for moment in range(samples + final_segment):
        current = received
        if moment < samples:
            snapshot = grid_state[moment]
            started, latent = lax.cond(
                segment_index == 0, lambda: encode(snapshot), lambda: (empty_mesh, empty_grid)
            )
            current = jnp.where(segment_index == 0, started, received)
            carried[moment] = from_behind_2(latent, "segment", final_segment)
        active = (moment - segment_index >= 0) & (moment - segment_index < samples)
        receiver, outgoing = lax.cond(
            active, lambda: project(current, own_weights), lambda: (empty_receiver, empty_mesh)
        )
        picked = jnp.where(valid_rows[:, :, None], outgoing[send_rows], jnp.zeros((), jnp.bfloat16))
        arrived = [outgoing]
        for list_index, offset in enumerate((1, -1, 2, -2)):
            arrived.append(from_behind(picked[list_index], "dom", offset))
        extended = jnp.concatenate(arrived, axis=0)
        renewed = lax.cond(
            active, lambda: renew(current, receiver, extended, own_weights), lambda: empty_mesh
        )
        if moment >= final_segment:
            finished = moment - final_segment
            skipped = carried[finished]
            results[finished] = lax.cond(
                segment_index == final_segment,
                lambda: decode(renewed, skipped),
                lambda: empty_output,
            )
        if moment < samples + final_segment - 1:
            received = from_behind_2(renewed, "segment", 1)
    everything = from_root(jnp.stack(results), "segment", final_segment)
    return lax.dynamic_slice_in_dim(everything, segment_index * share, share, 0)


def silu_by_tanh(values):
    half = 0.5 * values
    return half + half * jnp.tanh(half)


def matmul(left, right):
    return jnp.dot(left, right, preferred_element_type=jnp.float32)


def matmul_nt(left, right):
    return lax.dot_general(left, right, (((1,), (1,)), ((), ())), preferred_element_type=jnp.float32)


def matmul_tn(left, right):
    return lax.dot_general(left, right, (((0,), (0,)), ((), ())), preferred_element_type=jnp.float32)


def encode_kernel(counts, snapshot, w_embed, grid_mesh, neighbors, send_rows, payload, latent_out):
    mesh_rows = neighbors.shape[1]
    fanout = neighbors.shape[0]
    grid_rows = snapshot.shape[1]
    lists, halo_rows = send_rows.shape
    width = w_embed.shape[1]
    latent = silu_by_tanh(matmul_tn(snapshot[...], w_embed[...])).astype(jnp.bfloat16)
    latent_out[...] = latent
    table = lax.broadcasted_iota(jnp.int32, (mesh_rows, grid_rows), 0) == grid_mesh[...]
    pooled = matmul(jnp.where(table, 1.0, 0.0).astype(jnp.bfloat16), latent)
    payload[:mesh_rows, :] = rms_scale(pooled).astype(jnp.bfloat16)
    near = neighbors[...]
    block = near // mesh_rows
    row = near - block * mesh_rows
    position = lax.broadcasted_iota(jnp.int32, (1, halo_rows), 1)
    rows = []
    for list_index in range(lists):
        kept = position < counts[list_index]
        rows.append(jnp.where(kept, send_rows[list_index : list_index + 1, :], mesh_rows))
    rows.append(jnp.zeros((fanout - lists, halo_rows), jnp.int32))
    filler = jnp.zeros((fanout, 128 - mesh_rows), jnp.int32)
    pieces = [block, filler, row, filler, jnp.concatenate(rows, axis=0), filler]
    coded = jnp.concatenate(pieces + [jnp.zeros((fanout, width - 384), jnp.int32)], axis=1)
    coded = jnp.concatenate([coded, jnp.zeros_like(coded)], axis=0)
    payload[mesh_rows:, :] = coded.astype(jnp.float32).astype(jnp.bfloat16)


def index_kernel(parts, mesh_rows, active, *refs):
    payloads, (index_out, state_out) = refs[:parts], refs[parts:]
    fanout = index_out.shape[0]

    @pl.when(active[0] == 1)
    def _():
        tables = []
        for part in range(parts):
            state_out[part * mesh_rows : (part + 1) * mesh_rows, :] = payloads[part][:mesh_rows, :]
            coded = payloads[part][mesh_rows:, :384].astype(jnp.float32).astype(jnp.int32)
            tables.append(coded[:fanout])
        for part in range(parts):
            block = tables[part][:, :128]
            row = tables[part][:, 128:256]
            found = part * mesh_rows + row
            for list_index, offset in enumerate((-1, 1, -2, 2)):
                source = (part + offset) % parts
                lists = tables[source][list_index : list_index + 1, 256:384]
                lists = jnp.broadcast_to(lists, (fanout, 128))
                picked = jnp.take_along_axis(lists, row, axis=1)
                picked = jnp.where(picked == mesh_rows, parts * mesh_rows, source * mesh_rows + picked)
                found = jnp.where(block == list_index + 1, picked, found)
            index_out[:, part * mesh_rows : (part + 1) * mesh_rows] = found[:, :mesh_rows]


def layer_kernel(active, index, state_in, w_project, w_message, w_update, state_out):
    nodes, width = state_in.shape
    fanout = index.shape[0]
    chunk = min(256, nodes)

    @pl.when(active[0] == 1)
    def _():
        state = state_in[...]
        sender = matmul(state, w_project[0, :, width:]).astype(jnp.bfloat16)
        columns = jnp.concatenate([index[...], jnp.zeros((128 - fanout, nodes), jnp.int32)], axis=0)
        columns = jnp.transpose(columns.astype(jnp.float32))
        names = lax.broadcasted_iota(jnp.int32, (chunk, nodes), 1).astype(jnp.float32)
        for start in range(0, nodes, chunk):
            own = state_in[start : start + chunk, :]
            receiver = matmul(own, w_project[0, :, :width])
            total = jnp.zeros((chunk, width), jnp.float32)
            for k in range(fanout):
                hit = columns[start : start + chunk, k : k + 1] == names
                fetched = matmul(jnp.where(hit, 1.0, 0.0).astype(jnp.bfloat16), sender)
                edge = silu_by_tanh(receiver + fetched).astype(jnp.bfloat16)
                total = total + edge.astype(jnp.float32)
            gathered = (total * (1.0 / fanout)).astype(jnp.bfloat16)
            aggregate = matmul(gathered, w_message[0]).astype(jnp.bfloat16)
            update = silu_by_tanh(
                matmul(own, w_update[0, :width, :]) + matmul(aggregate, w_update[0, width:, :])
            )
            renewed = own.astype(jnp.float32) + rms_scale(update)
            state_out[start : start + chunk, :] = renewed.astype(jnp.bfloat16)


def prepare_kernel(latent, w_decode, ready):
    ready[...] = matmul(latent[...], w_decode[: latent.shape[1], :])


def decode_kernel(parts, ready, mesh_grid, w_decode, w_output, *refs):
    blocks, out = refs[:parts], refs[parts]
    width = ready.shape[1]
    state = blocks[0][...]
    for other in blocks[1:]:
        state = state + other[...]
    mesh_rows = state.shape[0]
    grid_rows = ready.shape[0]
    table = lax.broadcasted_iota(jnp.int32, (mesh_rows, grid_rows), 0) == mesh_grid[...]
    readout = matmul_tn(jnp.where(table, 1.0, 0.0).astype(jnp.bfloat16), state).astype(jnp.bfloat16)
    hidden = silu_by_tanh(ready[...] + matmul(readout, w_decode[width:, :])).astype(jnp.bfloat16)
    out[...] = matmul_nt(w_output[...], hidden).astype(jnp.bfloat16)


def call(kernel, name, shapes, inputs, scalars=1, flops=0, moved=0):
    return pl.pallas_call(
        kernel,
        out_shape=shapes,
        in_specs=[SMEM] * scalars + [VMEM] * (len(inputs) - scalars),
        out_specs=[VMEM] * len(shapes),
        name=name,
        compiler_params=pltpu.CompilerParams(vmem_limit_bytes=40 * 1024 * 1024),
        cost_estimate=pl.CostEstimate(flops=flops, bytes_accessed=moved, transcendentals=0),
    )(*inputs)


def resident(
    grid_state,
    w_embed,
    w_project,
    w_message,
    w_update,
    w_decode,
    w_output,
    grid_mesh,
    mesh_grid,
    neighbors,
    send_rows,
    halo_count,
):
    segment = lax.axis_index("segment")
    place = lax.axis_index("dom")
    segments = lax.axis_size("segment")
    parts = lax.axis_size("dom")
    samples, grid_rows, channels = grid_state.shape
    width = w_embed.shape[1]
    mesh_rows, fanout = neighbors.shape
    nodes = parts * mesh_rows
    group = parts // samples
    bf16 = jnp.bfloat16

    def device(at_segment, at_dom):
        return at_segment * parts + at_dom

    snapshot = lax.dynamic_index_in_dim(jnp.transpose(grid_state, (2, 0, 1)), segment, 1, keepdims=False)
    payload, latent = call(
        encode_kernel,
        "encode",
        [
            jax.ShapeDtypeStruct((mesh_rows + 2 * fanout, width), bf16),
            jax.ShapeDtypeStruct((grid_rows, width), bf16),
        ],
        [
            halo_count.reshape(-1),
            snapshot,
            w_embed,
            grid_mesh.reshape(1, grid_rows),
            neighbors.T,
            send_rows,
        ],
    )
    payloads = []
    for turn in range(parts):
        pairs = [
            (device(m, (m * group + turn) % parts), device(0, m * group)) for m in range(samples)
        ]
        payloads.append(lax.ppermute(payload, ("segment", "dom"), pairs))
    is_owner = place % group == 0

    def active(at_segment):
        return ((segment == at_segment) & is_owner).astype(jnp.int32).reshape(1)

    index, state = call(
        functools.partial(index_kernel, parts, mesh_rows),
        "index",
        [jax.ShapeDtypeStruct((fanout, nodes), jnp.int32), jax.ShapeDtypeStruct((nodes, width), bf16)],
        [active(0)] + payloads,
    )
    indices = [index]
    for at_segment in range(1, segments):
        pairs = [(device(0, m * group), device(at_segment, m * group)) for m in range(samples)]
        indices.append(lax.ppermute(index, ("segment", "dom"), pairs))
    for at_segment in range(segments):
        (state,) = call(
            layer_kernel,
            "layer",
            [jax.ShapeDtypeStruct((nodes, width), bf16)],
            [active(at_segment), indices[at_segment], state, w_project, w_message, w_update],
        )
        if at_segment + 1 < segments:
            pairs = [
                (device(at_segment, m * group), device(at_segment + 1, m * group)) for m in range(samples)
            ]
            state = lax.ppermute(state, ("segment", "dom"), pairs)
        if at_segment == 0:
            (ready,) = call(
                prepare_kernel,
                "prepare",
                [jax.ShapeDtypeStruct((grid_rows, width), jnp.float32)],
                [latent, w_decode],
                scalars=0,
            )
    blocks = []
    for turn in range(parts):
        pairs = [
            (device(segments - 1, m * group), device(m, (m * group + turn) % parts))
            for m in range(samples)
        ]
        block = state[turn * mesh_rows : (turn + 1) * mesh_rows]
        blocks.append(lax.ppermute(block, ("segment", "dom"), pairs))
    (prediction,) = call(
        functools.partial(decode_kernel, parts),
        "decode",
        [jax.ShapeDtypeStruct((channels, grid_rows), bf16)],
        [ready, mesh_grid.reshape(1, grid_rows), w_decode, w_output.T] + blocks,
        scalars=0,
    )
    return prediction.T.reshape(1, grid_rows, channels)


def fits(mesh):
    segments, parts = mesh.shape["segment"], mesh.shape["dom"]
    return parts % segments == 0 and parts <= 16


def solution(mesh):
    return jax.shard_map(
        resident if fits(mesh) else streamed,
        mesh=mesh,
        in_specs=(
            P(None, "dom", None),
            P(),
            P("segment", None, None),
            P("segment", None, None),
            P("segment", None, None),
            P(),
            P(),
            P("dom"),
            P("dom"),
            P("dom", None),
            P(None, "dom"),
            P(None, "dom"),
        ),
        out_specs=P("segment", "dom", None),
        check_vma=False,
    )
```

```python
import functools

import jax
import jax.numpy as jnp
from jax import lax
from jax.experimental import pallas as pl
from jax.experimental.pallas import tpu as pltpu
from jax.sharding import PartitionSpec as P

epsilon = 1e-05
VMEM = pl.BlockSpec(memory_space=pltpu.VMEM)
SMEM = pl.BlockSpec(memory_space=pltpu.SMEM)
ANY = pl.BlockSpec(memory_space=pl.ANY)


def from_behind(value, axis, steps):
    count = lax.axis_size(axis)
    pairs = [(source, (source + steps) % count) for source in range(count)]
    return lax.ppermute(value, axis, pairs)


def from_behind_2(block, axis, distance):
    devices = range(lax.axis_size(axis))
    route = [(i - distance, i) for i in devices if i - distance in devices]
    return lax.ppermute(block, axis, route)


def from_root(value, axis, source):
    kept = jnp.where(lax.axis_index(axis) == source, value, 0).astype(value.dtype)
    return lax.psum(kept, axis)


def rms_scale(values):
    return values * lax.rsqrt(jnp.mean(values * values, axis=-1, keepdims=True) + epsilon)


def streamed(
    grid_state,
    w_embed,
    w_project,
    w_message,
    w_update,
    w_decode,
    w_output,
    grid_mesh,
    mesh_grid,
    neighbors,
    send_rows,
    halo_count,
):
    segment_index = lax.axis_index("segment")
    segment_count = lax.axis_size("segment")
    final_segment = segment_count - 1
    samples, grid_rows, channels = grid_state.shape
    width = w_embed.shape[1]
    mesh_rows = neighbors.shape[0]
    fanout = neighbors.shape[1]
    halo_rows = send_rows.shape[1]
    share = samples // segment_count
    pool_table = (grid_mesh[None, :] == jnp.arange(mesh_rows, dtype=jnp.int32)[:, None]).astype(
        jnp.bfloat16
    )
    read_table = (mesh_grid[:, None] == jnp.arange(mesh_rows, dtype=jnp.int32)[None, :]).astype(
        jnp.bfloat16
    )
    valid_rows = jnp.arange(halo_rows, dtype=jnp.int32)[None, :] < halo_count[:, 0][:, None]
    source_rows = neighbors.reshape(mesh_rows * fanout)

    def embed_grid(snapshot):
        return jax.nn.silu(jnp.dot(snapshot, w_embed, preferred_element_type=jnp.float32)).astype(
            jnp.bfloat16
        )

    def encode(snapshot):
        latent = embed_grid(snapshot)
        pooled = jnp.dot(pool_table, latent, preferred_element_type=jnp.float32)
        return (rms_scale(pooled).astype(jnp.bfloat16), latent)

    def project(state, weights):
        projected = jnp.dot(state, weights[0], preferred_element_type=jnp.float32)
        return (projected[:, :width], projected[:, width:].astype(jnp.bfloat16))

    def renew(state, receiver, extended, weights):
        fetched = extended[source_rows].reshape(mesh_rows, fanout, width)
        edges = jax.nn.silu(receiver[:, None, :] + fetched.astype(jnp.float32)).astype(jnp.bfloat16)
        messages = jnp.dot(
            edges.reshape(mesh_rows * fanout, width), weights[1], preferred_element_type=jnp.float32
        )
        aggregate = (jnp.sum(messages.reshape(mesh_rows, fanout, width), axis=1) / fanout).astype(
            jnp.bfloat16
        )
        update = jax.nn.silu(
            jnp.dot(state, weights[2][:width], preferred_element_type=jnp.float32)
            + jnp.dot(aggregate, weights[2][width:], preferred_element_type=jnp.float32)
        )
        return (state.astype(jnp.float32) + rms_scale(update)).astype(jnp.bfloat16)

    def decode(state, latent):
        readout = jnp.dot(read_table, state, preferred_element_type=jnp.float32).astype(
            jnp.bfloat16
        )
        hidden = jax.nn.silu(
            jnp.dot(latent, w_decode[:width], preferred_element_type=jnp.float32)
            + jnp.dot(readout, w_decode[width:], preferred_element_type=jnp.float32)
        ).astype(jnp.bfloat16)
        return jnp.dot(hidden, w_output, preferred_element_type=jnp.float32).astype(jnp.bfloat16)

    own_weights = (w_project[0], w_message[0], w_update[0])
    empty_mesh = jnp.zeros((mesh_rows, width), jnp.bfloat16)
    empty_receiver = jnp.zeros((mesh_rows, width), jnp.float32)
    empty_grid = jnp.zeros((grid_rows, width), jnp.bfloat16)
    empty_output = jnp.zeros((grid_rows, channels), jnp.bfloat16)
    received = empty_mesh
    carried = {}
    results = [empty_output for sample in range(samples)]
    for moment in range(samples + final_segment):
        current = received
        if moment < samples:
            snapshot = grid_state[moment]
            started, latent = lax.cond(
                segment_index == 0, lambda: encode(snapshot), lambda: (empty_mesh, empty_grid)
            )
            current = jnp.where(segment_index == 0, started, received)
            carried[moment] = from_behind_2(latent, "segment", final_segment)
        active = (moment - segment_index >= 0) & (moment - segment_index < samples)
        receiver, outgoing = lax.cond(
            active, lambda: project(current, own_weights), lambda: (empty_receiver, empty_mesh)
        )
        picked = jnp.where(valid_rows[:, :, None], outgoing[send_rows], jnp.zeros((), jnp.bfloat16))
        arrived = [outgoing]
        for list_index, offset in enumerate((1, -1, 2, -2)):
            arrived.append(from_behind(picked[list_index], "dom", offset))
        extended = jnp.concatenate(arrived, axis=0)
        renewed = lax.cond(
            active, lambda: renew(current, receiver, extended, own_weights), lambda: empty_mesh
        )
        if moment >= final_segment:
            finished = moment - final_segment
            skipped = carried[finished]
            results[finished] = lax.cond(
                segment_index == final_segment,
                lambda: decode(renewed, skipped),
                lambda: empty_output,
            )
        if moment < samples + final_segment - 1:
            received = from_behind_2(renewed, "segment", 1)
    everything = from_root(jnp.stack(results), "segment", final_segment)
    return lax.dynamic_slice_in_dim(everything, segment_index * share, share, 0)


def silu_by_tanh(values):
    half = 0.5 * values
    return half + half * jnp.tanh(half)


def matmul(left, right):
    return jnp.dot(left, right, preferred_element_type=jnp.float32)


def matmul_nt(left, right):
    return lax.dot_general(left, right, (((1,), (1,)), ((), ())), preferred_element_type=jnp.float32)


def matmul_tn(left, right):
    return lax.dot_general(left, right, (((0,), (0,)), ((), ())), preferred_element_type=jnp.float32)


def fetch(sources, targets, semaphores):
    copies = [
        pltpu.make_async_copy(source, target, semaphores.at[place])
        for place, (source, target) in enumerate(zip(sources, targets))
    ]
    for copy in copies:
        copy.start()
    return copies


def encode_kernel(*refs):
    inputs, (payload, latent_out), held, semaphores = refs[:6], refs[6:8], refs[8:14], refs[14]
    copies = fetch(inputs, held, semaphores)
    for copy in copies:
        copy.wait()
    snapshot, w_embed, grid_mesh, neighbors, send_rows, counts = held
    mesh_rows = neighbors.shape[1]
    fanout = neighbors.shape[0]
    grid_rows = snapshot.shape[1]
    lists, halo_rows = send_rows.shape
    width = w_embed.shape[1]
    latent = silu_by_tanh(matmul_tn(snapshot[...], w_embed[...])).astype(jnp.bfloat16)
    latent_out[...] = latent
    table = lax.broadcasted_iota(jnp.int32, (mesh_rows, grid_rows), 0) == grid_mesh[...]
    pooled = matmul(jnp.where(table, 1.0, 0.0).astype(jnp.bfloat16), latent)
    payload[:mesh_rows, :] = rms_scale(pooled).astype(jnp.bfloat16)
    near = neighbors[...]
    block = near // mesh_rows
    row = near - block * mesh_rows
    position = lax.broadcasted_iota(jnp.int32, (1, halo_rows), 1)
    rows = []
    for list_index in range(lists):
        kept = position < counts[list_index]
        rows.append(jnp.where(kept, send_rows[list_index : list_index + 1, :], mesh_rows))
    rows.append(jnp.zeros((fanout - lists, halo_rows), jnp.int32))
    filler = jnp.zeros((fanout, 128 - mesh_rows), jnp.int32)
    pieces = [block, filler, row, filler, jnp.concatenate(rows, axis=0), filler]
    coded = jnp.concatenate(pieces + [jnp.zeros((fanout, width - 384), jnp.int32)], axis=1)
    coded = jnp.concatenate([coded, jnp.zeros_like(coded)], axis=0)
    payload[mesh_rows:, :] = coded.astype(jnp.float32).astype(jnp.bfloat16)


def index_kernel(parts, mesh_rows, active, *refs):
    payloads, (index_out, state_out) = refs[:parts], refs[parts:]
    fanout = index_out.shape[0]

    @pl.when(active[0] == 1)
    def _():
        tables = []
        for part in range(parts):
            state_out[part * mesh_rows : (part + 1) * mesh_rows, :] = payloads[part][:mesh_rows, :]
            coded = payloads[part][mesh_rows:, :384].astype(jnp.float32).astype(jnp.int32)
            tables.append(coded[:fanout])
        for part in range(parts):
            block = tables[part][:, :128]
            row = tables[part][:, 128:256]
            found = part * mesh_rows + row
            for list_index, offset in enumerate((-1, 1, -2, 2)):
                source = (part + offset) % parts
                lists = tables[source][list_index : list_index + 1, 256:384]
                lists = jnp.broadcast_to(lists, (fanout, 128))
                picked = jnp.take_along_axis(lists, row, axis=1)
                picked = jnp.where(picked == mesh_rows, parts * mesh_rows, source * mesh_rows + picked)
                found = jnp.where(block == list_index + 1, picked, found)
            index_out[:, part * mesh_rows : (part + 1) * mesh_rows] = found[:, :mesh_rows]


def layer_kernel(active, index, state_in, *refs):
    inputs, state_out, held, semaphores = refs[:3], refs[3], refs[4:7], refs[7]
    nodes, width = state_in.shape
    fanout = index.shape[0]
    chunk = min(256, nodes)

    @pl.when(active[0] == 1)
    def _():
        copies = fetch([ref.at[0] for ref in inputs], held, semaphores)
        w_project, w_message, w_update = held
        columns = jnp.concatenate([index[...], jnp.zeros((128 - fanout, nodes), jnp.int32)], axis=0)
        columns = jnp.transpose(columns.astype(jnp.float32))
        names = lax.broadcasted_iota(jnp.int32, (chunk, nodes), 1).astype(jnp.float32)
        copies[0].wait()
        sender = matmul(state_in[...], w_project[:, width:]).astype(jnp.bfloat16)
        for start in range(0, nodes, chunk):
            own = state_in[start : start + chunk, :]
            receiver = matmul(own, w_project[:, :width])
            total = jnp.zeros((chunk, width), jnp.float32)
            for k in range(fanout):
                hit = columns[start : start + chunk, k : k + 1] == names
                fetched = matmul(jnp.where(hit, 1.0, 0.0).astype(jnp.bfloat16), sender)
                edge = silu_by_tanh(receiver + fetched).astype(jnp.bfloat16)
                total = total + edge.astype(jnp.float32)
            gathered = (total * (1.0 / fanout)).astype(jnp.bfloat16)
            if start == 0:
                copies[1].wait()
                copies[2].wait()
            aggregate = matmul(gathered, w_message[...]).astype(jnp.bfloat16)
            update = silu_by_tanh(
                matmul(own, w_update[:width, :]) + matmul(aggregate, w_update[width:, :])
            )
            renewed = own.astype(jnp.float32) + rms_scale(update)
            state_out[start : start + chunk, :] = renewed.astype(jnp.bfloat16)


def prepare_kernel(latent, w_decode, ready):
    ready[...] = matmul(latent[...], w_decode[: latent.shape[1], :])


def decode_kernel(parts, turn, ready, mesh_grid, w_decode, w_output, *refs):
    blocks, out, state = refs[:parts], refs[parts], refs[parts + 1]
    width = ready.shape[1]
    for number, block in enumerate(blocks):

        @pl.when(turn[0] == number)
        def _():
            state[...] = block[...]

    mesh_rows = state.shape[0]
    grid_rows = ready.shape[0]
    table = lax.broadcasted_iota(jnp.int32, (mesh_rows, grid_rows), 0) == mesh_grid[...]
    table = jnp.where(table, 1.0, 0.0).astype(jnp.bfloat16)
    readout = matmul_tn(table, state[...]).astype(jnp.bfloat16)
    hidden = silu_by_tanh(ready[...] + matmul(readout, w_decode[width:, :])).astype(jnp.bfloat16)
    out[...] = matmul_nt(w_output[...], hidden).astype(jnp.bfloat16)


def call(kernel, name, shapes, inputs, places, scratch=(), flops=0, moved=0):
    kinds = {"s": SMEM, "v": VMEM, "a": ANY}
    return pl.pallas_call(
        kernel,
        out_shape=shapes,
        in_specs=[kinds[place] for place in places],
        out_specs=[VMEM] * len(shapes),
        scratch_shapes=list(scratch),
        name=name,
        compiler_params=pltpu.CompilerParams(vmem_limit_bytes=32 * 1024 * 1024),
        cost_estimate=pl.CostEstimate(flops=flops, bytes_accessed=moved, transcendentals=0),
    )(*inputs)


def every_device(pairs, count):
    onward = dict(pairs)
    reached = set(onward.values())
    for first in range(count):
        if first in reached or first not in onward:
            continue
        last = first
        while last in onward:
            last = onward[last]
        onward[last] = first
    for other in range(count):
        onward.setdefault(other, other)
    return sorted(onward.items())


def resident(
    grid_state,
    w_embed,
    w_project,
    w_message,
    w_update,
    w_decode,
    w_output,
    grid_mesh,
    mesh_grid,
    neighbors,
    send_rows,
    halo_count,
):
    segment = lax.axis_index("segment")
    place = lax.axis_index("dom")
    segments = lax.axis_size("segment")
    parts = lax.axis_size("dom")
    samples, grid_rows, channels = grid_state.shape
    width = w_embed.shape[1]
    mesh_rows, fanout = neighbors.shape
    nodes = parts * mesh_rows
    group = parts // samples
    bf16 = jnp.bfloat16

    def device(at_segment, at_dom):
        return at_segment * parts + at_dom % parts

    def send(value, pairs):
        return lax.ppermute(value, ("segment", "dom"), every_device(pairs, segments * parts))

    def active(at_segment):
        return ((segment == at_segment) & (place % group == 0)).astype(jnp.int32).reshape(1)

    snapshot = lax.dynamic_index_in_dim(jnp.transpose(grid_state, (2, 0, 1)), segment, 1, keepdims=False)
    inputs = [
        snapshot,
        w_embed,
        grid_mesh.reshape(1, grid_rows),
        neighbors.T,
        send_rows,
        halo_count.reshape(-1),
    ]
    payload, latent = call(
        encode_kernel,
        "encode",
        [
            jax.ShapeDtypeStruct((mesh_rows + 2 * fanout, width), bf16),
            jax.ShapeDtypeStruct((grid_rows, width), bf16),
        ],
        inputs,
        "aaaaaa",
        [pltpu.VMEM(value.shape, value.dtype) for value in inputs[:-1]]
        + [pltpu.SMEM(inputs[-1].shape, jnp.int32), pltpu.SemaphoreType.DMA((6,))],
    )
    payloads = []
    for turn in range(parts):
        pairs = [(device(m, m * group + turn), device(0, m * group)) for m in range(samples)]
        payloads.append(send(payload, pairs))
    index, state = call(
        functools.partial(index_kernel, parts, mesh_rows),
        "index",
        [jax.ShapeDtypeStruct((fanout, nodes), jnp.int32), jax.ShapeDtypeStruct((nodes, width), bf16)],
        [active(0)] + payloads,
        "s" + "v" * parts,
    )
    indices = [index]
    for at_segment in range(1, segments):
        pairs = [(device(0, m * group), device(at_segment, m * group)) for m in range(samples)]
        indices.append(send(index, pairs))
    weights = [w_project, w_message, w_update]
    for at_segment in range(segments):
        (state,) = call(
            layer_kernel,
            "layer",
            [jax.ShapeDtypeStruct((nodes, width), bf16)],
            [active(at_segment), indices[at_segment], state] + weights,
            "svvaaa",
            [pltpu.VMEM(weight.shape[1:], bf16) for weight in weights] + [pltpu.SemaphoreType.DMA((3,))],
        )
        if at_segment + 1 < segments:
            pairs = [
                (device(at_segment, m * group), device(at_segment + 1, m * group)) for m in range(samples)
            ]
            state = send(state, pairs)
        if at_segment == 0:
            (ready,) = call(
                prepare_kernel,
                "prepare",
                [jax.ShapeDtypeStruct((grid_rows, width), jnp.float32)],
                [latent, w_decode],
                "vv",
            )
    blocks = []
    for turn in range(parts):
        pairs = [
            (device(segments - 1, m * group), device(m, m * group + turn)) for m in range(samples)
        ]
        blocks.append(send(state[turn * mesh_rows : (turn + 1) * mesh_rows], pairs))
    (prediction,) = call(
        functools.partial(decode_kernel, parts),
        "decode",
        [jax.ShapeDtypeStruct((channels, grid_rows), bf16)],
        [
            ((place - segment * group) % parts).reshape(1),
            ready,
            mesh_grid.reshape(1, grid_rows),
            w_decode,
            w_output.T,
        ]
        + blocks,
        "s" + "v" * (4 + parts),
        [pltpu.VMEM((mesh_rows, width), bf16)],
    )
    return prediction.T.reshape(1, grid_rows, channels)


def fits(mesh):
    segments, parts = mesh.shape["segment"], mesh.shape["dom"]
    return parts % segments == 0 and parts <= 16


def solution(mesh):
    return jax.shard_map(
        resident if fits(mesh) else streamed,
        mesh=mesh,
        in_specs=(
            P(None, "dom", None),
            P(),
            P("segment", None, None),
            P("segment", None, None),
            P("segment", None, None),
            P(),
            P(),
            P("dom"),
            P("dom"),
            P("dom", None),
            P(None, "dom"),
            P(None, "dom"),
        ),
        out_specs=P("segment", "dom", None),
        check_vma=False,
    )
```

```python
import functools

import jax
import jax.numpy as jnp
from jax import lax
from jax.experimental import pallas as pl
from jax.experimental.pallas import tpu as pltpu
from jax.sharding import PartitionSpec as P

epsilon = 1e-05
VMEM = pl.BlockSpec(memory_space=pltpu.VMEM)
SMEM = pl.BlockSpec(memory_space=pltpu.SMEM)
HBM = pl.BlockSpec(memory_space=pltpu.HBM)


def from_behind(value, axis, steps):
    count = lax.axis_size(axis)
    pairs = [(source, (source + steps) % count) for source in range(count)]
    return lax.ppermute(value, axis, pairs)


def from_behind_2(block, axis, distance):
    devices = range(lax.axis_size(axis))
    route = [(i - distance, i) for i in devices if i - distance in devices]
    return lax.ppermute(block, axis, route)


def from_root(value, axis, source):
    kept = jnp.where(lax.axis_index(axis) == source, value, 0).astype(value.dtype)
    return lax.psum(kept, axis)


def rms_scale(values):
    return values * lax.rsqrt(jnp.mean(values * values, axis=-1, keepdims=True) + epsilon)


def streamed(
    grid_state,
    w_embed,
    w_project,
    w_message,
    w_update,
    w_decode,
    w_output,
    grid_mesh,
    mesh_grid,
    neighbors,
    send_rows,
    halo_count,
):
    segment_index = lax.axis_index("segment")
    segment_count = lax.axis_size("segment")
    final_segment = segment_count - 1
    samples, grid_rows, channels = grid_state.shape
    width = w_embed.shape[1]
    mesh_rows = neighbors.shape[0]
    fanout = neighbors.shape[1]
    halo_rows = send_rows.shape[1]
    share = samples // segment_count
    pool_table = (grid_mesh[None, :] == jnp.arange(mesh_rows, dtype=jnp.int32)[:, None]).astype(
        jnp.bfloat16
    )
    read_table = (mesh_grid[:, None] == jnp.arange(mesh_rows, dtype=jnp.int32)[None, :]).astype(
        jnp.bfloat16
    )
    valid_rows = jnp.arange(halo_rows, dtype=jnp.int32)[None, :] < halo_count[:, 0][:, None]
    source_rows = neighbors.reshape(mesh_rows * fanout)

    def embed_grid(snapshot):
        return jax.nn.silu(jnp.dot(snapshot, w_embed, preferred_element_type=jnp.float32)).astype(
            jnp.bfloat16
        )

    def encode(snapshot):
        latent = embed_grid(snapshot)
        pooled = jnp.dot(pool_table, latent, preferred_element_type=jnp.float32)
        return (rms_scale(pooled).astype(jnp.bfloat16), latent)

    def project(state, weights):
        projected = jnp.dot(state, weights[0], preferred_element_type=jnp.float32)
        return (projected[:, :width], projected[:, width:].astype(jnp.bfloat16))

    def renew(state, receiver, extended, weights):
        fetched = extended[source_rows].reshape(mesh_rows, fanout, width)
        edges = jax.nn.silu(receiver[:, None, :] + fetched.astype(jnp.float32)).astype(jnp.bfloat16)
        messages = jnp.dot(
            edges.reshape(mesh_rows * fanout, width), weights[1], preferred_element_type=jnp.float32
        )
        aggregate = (jnp.sum(messages.reshape(mesh_rows, fanout, width), axis=1) / fanout).astype(
            jnp.bfloat16
        )
        update = jax.nn.silu(
            jnp.dot(state, weights[2][:width], preferred_element_type=jnp.float32)
            + jnp.dot(aggregate, weights[2][width:], preferred_element_type=jnp.float32)
        )
        return (state.astype(jnp.float32) + rms_scale(update)).astype(jnp.bfloat16)

    def decode(state, latent):
        readout = jnp.dot(read_table, state, preferred_element_type=jnp.float32).astype(
            jnp.bfloat16
        )
        hidden = jax.nn.silu(
            jnp.dot(latent, w_decode[:width], preferred_element_type=jnp.float32)
            + jnp.dot(readout, w_decode[width:], preferred_element_type=jnp.float32)
        ).astype(jnp.bfloat16)
        return jnp.dot(hidden, w_output, preferred_element_type=jnp.float32).astype(jnp.bfloat16)

    own_weights = (w_project[0], w_message[0], w_update[0])
    empty_mesh = jnp.zeros((mesh_rows, width), jnp.bfloat16)
    empty_receiver = jnp.zeros((mesh_rows, width), jnp.float32)
    empty_grid = jnp.zeros((grid_rows, width), jnp.bfloat16)
    empty_output = jnp.zeros((grid_rows, channels), jnp.bfloat16)
    received = empty_mesh
    carried = {}
    results = [empty_output for sample in range(samples)]
    for moment in range(samples + final_segment):
        current = received
        if moment < samples:
            snapshot = grid_state[moment]
            started, latent = lax.cond(
                segment_index == 0, lambda: encode(snapshot), lambda: (empty_mesh, empty_grid)
            )
            current = jnp.where(segment_index == 0, started, received)
            carried[moment] = from_behind_2(latent, "segment", final_segment)
        active = (moment - segment_index >= 0) & (moment - segment_index < samples)
        receiver, outgoing = lax.cond(
            active, lambda: project(current, own_weights), lambda: (empty_receiver, empty_mesh)
        )
        picked = jnp.where(valid_rows[:, :, None], outgoing[send_rows], jnp.zeros((), jnp.bfloat16))
        arrived = [outgoing]
        for list_index, offset in enumerate((1, -1, 2, -2)):
            arrived.append(from_behind(picked[list_index], "dom", offset))
        extended = jnp.concatenate(arrived, axis=0)
        renewed = lax.cond(
            active, lambda: renew(current, receiver, extended, own_weights), lambda: empty_mesh
        )
        if moment >= final_segment:
            finished = moment - final_segment
            skipped = carried[finished]
            results[finished] = lax.cond(
                segment_index == final_segment,
                lambda: decode(renewed, skipped),
                lambda: empty_output,
            )
        if moment < samples + final_segment - 1:
            received = from_behind_2(renewed, "segment", 1)
    everything = from_root(jnp.stack(results), "segment", final_segment)
    return lax.dynamic_slice_in_dim(everything, segment_index * share, share, 0)


def silu_by_tanh(values):
    half = 0.5 * values
    return half + half * jnp.tanh(half)


def matmul(left, right):
    return jnp.dot(left, right, preferred_element_type=jnp.float32)


def matmul_nt(left, right):
    return lax.dot_general(left, right, (((1,), (1,)), ((), ())), preferred_element_type=jnp.float32)


def matmul_tn(left, right):
    return lax.dot_general(left, right, (((0,), (0,)), ((), ())), preferred_element_type=jnp.float32)


def fetch(sources, targets, semaphores):
    copies = [
        pltpu.make_async_copy(source, target, semaphores.at[place])
        for place, (source, target) in enumerate(zip(sources, targets))
    ]
    for copy in copies:
        copy.start()
    return copies


def encode_kernel(*refs):
    inputs, (payload, latent_out), held, semaphores = refs[:6], refs[6:8], refs[8:14], refs[14]
    copies = fetch(inputs, held, semaphores)
    for copy in copies:
        copy.wait()
    snapshot, w_embed, grid_mesh, neighbors, send_rows, counts = held
    mesh_rows = neighbors.shape[1]
    fanout = neighbors.shape[0]
    grid_rows = snapshot.shape[1]
    lists, halo_rows = send_rows.shape
    width = w_embed.shape[1]
    latent = silu_by_tanh(matmul_tn(snapshot[...], w_embed[...])).astype(jnp.bfloat16)
    latent_out[...] = latent
    table = lax.broadcasted_iota(jnp.int32, (mesh_rows, grid_rows), 0) == grid_mesh[...]
    pooled = matmul(jnp.where(table, 1.0, 0.0).astype(jnp.bfloat16), latent)
    payload[:mesh_rows, :] = rms_scale(pooled).astype(jnp.bfloat16)
    near = neighbors[...]
    block = near // mesh_rows
    row = near - block * mesh_rows
    position = lax.broadcasted_iota(jnp.int32, (1, halo_rows), 1)
    rows = []
    for list_index in range(lists):
        kept = position < counts[list_index]
        rows.append(jnp.where(kept, send_rows[list_index : list_index + 1, :], mesh_rows))
    rows.append(jnp.zeros((fanout - lists, halo_rows), jnp.int32))
    filler = jnp.zeros((fanout, 128 - mesh_rows), jnp.int32)
    pieces = [block, filler, row, filler, jnp.concatenate(rows, axis=0), filler]
    coded = jnp.concatenate(pieces + [jnp.zeros((fanout, width - 384), jnp.int32)], axis=1)
    coded = jnp.concatenate([coded, jnp.zeros_like(coded)], axis=0)
    payload[mesh_rows:, :] = coded.astype(jnp.float32).astype(jnp.bfloat16)


def index_kernel(parts, mesh_rows, active, *refs):
    payloads, (index_out, state_out) = refs[:parts], refs[parts:]
    fanout = index_out.shape[0]

    @pl.when(active[0] == 1)
    def _():
        tables = []
        for part in range(parts):
            state_out[part * mesh_rows : (part + 1) * mesh_rows, :] = payloads[part][:mesh_rows, :]
            coded = payloads[part][mesh_rows:, :384].astype(jnp.float32).astype(jnp.int32)
            tables.append(coded[:fanout])
        for part in range(parts):
            block = tables[part][:, :128]
            row = tables[part][:, 128:256]
            found = part * mesh_rows + row
            for list_index, offset in enumerate((-1, 1, -2, 2)):
                source = (part + offset) % parts
                lists = tables[source][list_index : list_index + 1, 256:384]
                lists = jnp.broadcast_to(lists, (fanout, 128))
                picked = jnp.take_along_axis(lists, row, axis=1)
                picked = jnp.where(picked == mesh_rows, parts * mesh_rows, source * mesh_rows + picked)
                found = jnp.where(block == list_index + 1, picked, found)
            index_out[:, part * mesh_rows : (part + 1) * mesh_rows] = found[:, :mesh_rows]


def layer_kernel(active, index, state_in, w_project, w_message, w_update, state_out):
    nodes, width = state_in.shape
    fanout = index.shape[0]
    chunk = min(256, nodes)

    @pl.when(active[0] == 1)
    def _():
        columns = jnp.concatenate([index[...], jnp.zeros((128 - fanout, nodes), jnp.int32)], axis=0)
        columns = jnp.transpose(columns.astype(jnp.float32))
        names = lax.broadcasted_iota(jnp.int32, (chunk, nodes), 1).astype(jnp.float32)
        sender = matmul(state_in[...], w_project[0, :, width:]).astype(jnp.bfloat16)
        for start in range(0, nodes, chunk):
            own = state_in[start : start + chunk, :]
            receiver = matmul(own, w_project[0, :, :width])
            total = jnp.zeros((chunk, width), jnp.float32)
            for k in range(fanout):
                hit = columns[start : start + chunk, k : k + 1] == names
                fetched = matmul(jnp.where(hit, 1.0, 0.0).astype(jnp.bfloat16), sender)
                edge = silu_by_tanh(receiver + fetched).astype(jnp.bfloat16)
                total = total + edge.astype(jnp.float32)
            gathered = (total * (1.0 / fanout)).astype(jnp.bfloat16)
            aggregate = matmul(gathered, w_message[0]).astype(jnp.bfloat16)
            update = silu_by_tanh(
                matmul(own, w_update[0, :width, :]) + matmul(aggregate, w_update[0, width:, :])
            )
            renewed = own.astype(jnp.float32) + rms_scale(update)
            state_out[start : start + chunk, :] = renewed.astype(jnp.bfloat16)


def prepare_kernel(latent, w_decode, ready):
    ready[...] = matmul(latent[...], w_decode[: latent.shape[1], :])


def decode_kernel(parts, turn, ready, mesh_grid, w_decode, w_output, *refs):
    blocks, out, state = refs[:parts], refs[parts], refs[parts + 1]
    width = ready.shape[1]
    for number, block in enumerate(blocks):

        @pl.when(turn[0] == number)
        def _():
            state[...] = block[...]

    mesh_rows = state.shape[0]
    grid_rows = ready.shape[0]
    table = lax.broadcasted_iota(jnp.int32, (mesh_rows, grid_rows), 0) == mesh_grid[...]
    table = jnp.where(table, 1.0, 0.0).astype(jnp.bfloat16)
    readout = matmul_tn(table, state[...]).astype(jnp.bfloat16)
    hidden = silu_by_tanh(ready[...] + matmul(readout, w_decode[width:, :])).astype(jnp.bfloat16)
    out[...] = matmul_nt(w_output[...], hidden).astype(jnp.bfloat16)


def call(kernel, name, shapes, inputs, places, scratch=(), room=16):
    kinds = {"s": SMEM, "v": VMEM, "h": HBM}
    return pl.pallas_call(
        kernel,
        out_shape=shapes,
        in_specs=[kinds[place] for place in places],
        out_specs=[VMEM] * len(shapes),
        scratch_shapes=list(scratch),
        name=name,
        compiler_params=pltpu.CompilerParams(vmem_limit_bytes=room * 1024 * 1024),
    )(*inputs)


def every_device(pairs, count):
    onward = dict(pairs)
    reached = set(onward.values())
    for first in range(count):
        if first in reached or first not in onward:
            continue
        last = first
        while last in onward:
            last = onward[last]
        onward[last] = first
    rest = [other for other in range(count) if other not in onward]
    for place, other in enumerate(rest):
        onward[other] = rest[place ^ 1] if place | 1 < len(rest) else other
    return sorted(onward.items())


def resident(
    grid_state,
    w_embed,
    w_project,
    w_message,
    w_update,
    w_decode,
    w_output,
    grid_mesh,
    mesh_grid,
    neighbors,
    send_rows,
    halo_count,
):
    segment = lax.axis_index("segment")
    place = lax.axis_index("dom")
    segments = lax.axis_size("segment")
    parts = lax.axis_size("dom")
    samples, grid_rows, channels = grid_state.shape
    width = w_embed.shape[1]
    mesh_rows, fanout = neighbors.shape
    nodes = parts * mesh_rows
    group = parts // samples
    bf16 = jnp.bfloat16

    def device(at_segment, at_dom):
        return at_segment * parts + at_dom % parts

    def send(value, pairs):
        return lax.ppermute(value, ("segment", "dom"), every_device(pairs, segments * parts))

    def active(at_segment):
        return ((segment == at_segment) & (place % group == 0)).astype(jnp.int32).reshape(1)

    snapshot = lax.dynamic_index_in_dim(jnp.transpose(grid_state, (2, 0, 1)), segment, 1, keepdims=False)
    inputs = [
        snapshot,
        w_embed,
        grid_mesh.reshape(1, grid_rows),
        neighbors.T,
        send_rows,
        halo_count.reshape(-1),
    ]
    payload, latent = call(
        encode_kernel,
        "encode",
        [
            jax.ShapeDtypeStruct((mesh_rows + 2 * fanout, width), bf16),
            jax.ShapeDtypeStruct((grid_rows, width), bf16),
        ],
        inputs,
        "hhhhhh",
        [pltpu.VMEM(value.shape, value.dtype) for value in inputs[:-1]]
        + [pltpu.SMEM(inputs[-1].shape, jnp.int32), pltpu.SemaphoreType.DMA((6,))],
        room=60,
    )
    payloads = []
    for turn in range(parts):
        pairs = [(device(m, m * group + turn), device(0, m * group)) for m in range(samples)]
        payloads.append(send(payload, pairs))
    index, state = call(
        functools.partial(index_kernel, parts, mesh_rows),
        "index",
        [jax.ShapeDtypeStruct((fanout, nodes), jnp.int32), jax.ShapeDtypeStruct((nodes, width), bf16)],
        [active(0)] + payloads,
        "s" + "v" * parts,
    )
    indices = [index]
    for at_segment in range(1, segments):
        pairs = [(device(0, m * group), device(at_segment, m * group)) for m in range(samples)]
        indices.append(send(index, pairs))
    weights = [w_project, w_message, w_update]
    for at_segment in range(segments):
        (state,) = call(
            layer_kernel,
            "layer",
            [jax.ShapeDtypeStruct((nodes, width), bf16)],
            [active(at_segment), indices[at_segment], state] + weights,
            "svvvvv",
        )
        if at_segment + 1 < segments:
            pairs = [
                (device(at_segment, m * group), device(at_segment + 1, m * group)) for m in range(samples)
            ]
            state = send(state, pairs)
        if at_segment == 0:
            (ready,) = call(
                prepare_kernel,
                "prepare",
                [jax.ShapeDtypeStruct((grid_rows, width), jnp.float32)],
                [latent, w_decode],
                "vv",
            )
    blocks = []
    for turn in range(parts):
        pairs = [
            (device(segments - 1, m * group), device(m, m * group + turn)) for m in range(samples)
        ]
        blocks.append(send(state[turn * mesh_rows : (turn + 1) * mesh_rows], pairs))
    (prediction,) = call(
        functools.partial(decode_kernel, parts),
        "decode",
        [jax.ShapeDtypeStruct((channels, grid_rows), bf16)],
        [
            ((place - segment * group) % parts).reshape(1),
            ready,
            mesh_grid.reshape(1, grid_rows),
            w_decode,
            w_output.T,
        ]
        + blocks,
        "s" + "v" * (4 + parts),
        [pltpu.VMEM((mesh_rows, width), bf16)],
    )
    return prediction.T.reshape(1, grid_rows, channels)


def fits(mesh):
    segments, parts = mesh.shape["segment"], mesh.shape["dom"]
    return parts % segments == 0 and parts <= 16


def solution(mesh):
    return jax.shard_map(
        resident if fits(mesh) else streamed,
        mesh=mesh,
        in_specs=(
            P(None, "dom", None),
            P(),
            P("segment", None, None),
            P("segment", None, None),
            P("segment", None, None),
            P(),
            P(),
            P("dom"),
            P("dom"),
            P("dom", None),
            P(None, "dom"),
            P(None, "dom"),
        ),
        out_specs=P("segment", "dom", None),
        check_vma=False,
    )
```

```python
import functools

import jax
import jax.numpy as jnp
from jax import lax
from jax.experimental import pallas as pl
from jax.experimental.pallas import tpu as pltpu
from jax.sharding import PartitionSpec as P

epsilon = 1e-05
VMEM = pl.BlockSpec(memory_space=pltpu.VMEM)
SMEM = pl.BlockSpec(memory_space=pltpu.SMEM)
HBM = pl.BlockSpec(memory_space=pltpu.HBM)


def from_behind(value, axis, steps):
    count = lax.axis_size(axis)
    pairs = [(source, (source + steps) % count) for source in range(count)]
    return lax.ppermute(value, axis, pairs)


def from_behind_2(block, axis, distance):
    devices = range(lax.axis_size(axis))
    route = [(i - distance, i) for i in devices if i - distance in devices]
    return lax.ppermute(block, axis, route)


def from_root(value, axis, source):
    kept = jnp.where(lax.axis_index(axis) == source, value, 0).astype(value.dtype)
    return lax.psum(kept, axis)


def rms_scale(values):
    return values * lax.rsqrt(jnp.mean(values * values, axis=-1, keepdims=True) + epsilon)


def streamed(
    grid_state,
    w_embed,
    w_project,
    w_message,
    w_update,
    w_decode,
    w_output,
    grid_mesh,
    mesh_grid,
    neighbors,
    send_rows,
    halo_count,
):
    segment_index = lax.axis_index("segment")
    segment_count = lax.axis_size("segment")
    final_segment = segment_count - 1
    samples, grid_rows, channels = grid_state.shape
    width = w_embed.shape[1]
    mesh_rows = neighbors.shape[0]
    fanout = neighbors.shape[1]
    halo_rows = send_rows.shape[1]
    share = samples // segment_count
    pool_table = (grid_mesh[None, :] == jnp.arange(mesh_rows, dtype=jnp.int32)[:, None]).astype(
        jnp.bfloat16
    )
    read_table = (mesh_grid[:, None] == jnp.arange(mesh_rows, dtype=jnp.int32)[None, :]).astype(
        jnp.bfloat16
    )
    valid_rows = jnp.arange(halo_rows, dtype=jnp.int32)[None, :] < halo_count[:, 0][:, None]
    source_rows = neighbors.reshape(mesh_rows * fanout)

    def embed_grid(snapshot):
        return jax.nn.silu(jnp.dot(snapshot, w_embed, preferred_element_type=jnp.float32)).astype(
            jnp.bfloat16
        )

    def encode(snapshot):
        latent = embed_grid(snapshot)
        pooled = jnp.dot(pool_table, latent, preferred_element_type=jnp.float32)
        return (rms_scale(pooled).astype(jnp.bfloat16), latent)

    def project(state, weights):
        projected = jnp.dot(state, weights[0], preferred_element_type=jnp.float32)
        return (projected[:, :width], projected[:, width:].astype(jnp.bfloat16))

    def renew(state, receiver, extended, weights):
        fetched = extended[source_rows].reshape(mesh_rows, fanout, width)
        edges = jax.nn.silu(receiver[:, None, :] + fetched.astype(jnp.float32)).astype(jnp.bfloat16)
        messages = jnp.dot(
            edges.reshape(mesh_rows * fanout, width), weights[1], preferred_element_type=jnp.float32
        )
        aggregate = (jnp.sum(messages.reshape(mesh_rows, fanout, width), axis=1) / fanout).astype(
            jnp.bfloat16
        )
        update = jax.nn.silu(
            jnp.dot(state, weights[2][:width], preferred_element_type=jnp.float32)
            + jnp.dot(aggregate, weights[2][width:], preferred_element_type=jnp.float32)
        )
        return (state.astype(jnp.float32) + rms_scale(update)).astype(jnp.bfloat16)

    def decode(state, latent):
        readout = jnp.dot(read_table, state, preferred_element_type=jnp.float32).astype(
            jnp.bfloat16
        )
        hidden = jax.nn.silu(
            jnp.dot(latent, w_decode[:width], preferred_element_type=jnp.float32)
            + jnp.dot(readout, w_decode[width:], preferred_element_type=jnp.float32)
        ).astype(jnp.bfloat16)
        return jnp.dot(hidden, w_output, preferred_element_type=jnp.float32).astype(jnp.bfloat16)

    own_weights = (w_project[0], w_message[0], w_update[0])
    empty_mesh = jnp.zeros((mesh_rows, width), jnp.bfloat16)
    empty_receiver = jnp.zeros((mesh_rows, width), jnp.float32)
    empty_grid = jnp.zeros((grid_rows, width), jnp.bfloat16)
    empty_output = jnp.zeros((grid_rows, channels), jnp.bfloat16)
    received = empty_mesh
    carried = {}
    results = [empty_output for sample in range(samples)]
    for moment in range(samples + final_segment):
        current = received
        if moment < samples:
            snapshot = grid_state[moment]
            started, latent = lax.cond(
                segment_index == 0, lambda: encode(snapshot), lambda: (empty_mesh, empty_grid)
            )
            current = jnp.where(segment_index == 0, started, received)
            carried[moment] = from_behind_2(latent, "segment", final_segment)
        active = (moment - segment_index >= 0) & (moment - segment_index < samples)
        receiver, outgoing = lax.cond(
            active, lambda: project(current, own_weights), lambda: (empty_receiver, empty_mesh)
        )
        picked = jnp.where(valid_rows[:, :, None], outgoing[send_rows], jnp.zeros((), jnp.bfloat16))
        arrived = [outgoing]
        for list_index, offset in enumerate((1, -1, 2, -2)):
            arrived.append(from_behind(picked[list_index], "dom", offset))
        extended = jnp.concatenate(arrived, axis=0)
        renewed = lax.cond(
            active, lambda: renew(current, receiver, extended, own_weights), lambda: empty_mesh
        )
        if moment >= final_segment:
            finished = moment - final_segment
            skipped = carried[finished]
            results[finished] = lax.cond(
                segment_index == final_segment,
                lambda: decode(renewed, skipped),
                lambda: empty_output,
            )
        if moment < samples + final_segment - 1:
            received = from_behind_2(renewed, "segment", 1)
    everything = from_root(jnp.stack(results), "segment", final_segment)
    return lax.dynamic_slice_in_dim(everything, segment_index * share, share, 0)


def silu_by_tanh(values):
    half = 0.5 * values
    return half + half * jnp.tanh(half)


def matmul(left, right):
    return jnp.dot(left, right, preferred_element_type=jnp.float32)


def matmul_nt(left, right):
    return lax.dot_general(left, right, (((1,), (1,)), ((), ())), preferred_element_type=jnp.float32)


def matmul_tn(left, right):
    return lax.dot_general(left, right, (((0,), (0,)), ((), ())), preferred_element_type=jnp.float32)


def fetch(sources, targets, semaphores):
    copies = [
        pltpu.make_async_copy(source, target, semaphores.at[place])
        for place, (source, target) in enumerate(zip(sources, targets))
    ]
    for copy in copies:
        copy.start()
    return copies


def encode_kernel(samples, first, *refs):
    inputs, payloads = refs[:6], refs[6 : 6 + samples]
    held, latent, semaphores = refs[6 + samples : 12 + samples], refs[12 + samples], refs[13 + samples]
    copies = fetch(inputs, held, semaphores)
    for copy in copies:
        copy.wait()
    snapshots, w_embed, grid_mesh, neighbors, send_rows, counts = held
    mesh_rows = neighbors.shape[1]
    fanout = neighbors.shape[0]
    grid_rows = snapshots.shape[1] // samples
    lists, halo_rows = send_rows.shape
    width = w_embed.shape[1]
    latent[...] = silu_by_tanh(matmul_tn(snapshots[...], w_embed[...])).astype(jnp.bfloat16)
    table = lax.broadcasted_iota(jnp.int32, (mesh_rows, grid_rows), 0) == grid_mesh[...]
    table = jnp.where(table, 1.0, 0.0).astype(jnp.bfloat16)
    near = neighbors[...]
    block = near // mesh_rows
    row = near - block * mesh_rows
    position = lax.broadcasted_iota(jnp.int32, (1, halo_rows), 1)
    rows = []
    for list_index in range(lists):
        kept = position < counts[list_index]
        rows.append(jnp.where(kept, send_rows[list_index : list_index + 1, :], mesh_rows))
    rows.append(jnp.zeros((fanout - lists, halo_rows), jnp.int32))
    filler = jnp.zeros((fanout, 128 - mesh_rows), jnp.int32)
    pieces = [block, filler, row, filler, jnp.concatenate(rows, axis=0), filler]
    coded = jnp.concatenate(pieces + [jnp.zeros((fanout, width - 384), jnp.int32)], axis=1)
    coded = jnp.concatenate([coded, jnp.zeros_like(coded)], axis=0)
    coded = coded.astype(jnp.float32).astype(jnp.bfloat16)
    for turn, payload in enumerate(payloads):
        sample = lax.rem(first[0] + turn, samples)
        start = pl.multiple_of(sample * grid_rows, grid_rows)
        pooled = matmul(table, latent[pl.ds(start, grid_rows), :])
        payload[:mesh_rows, :] = rms_scale(pooled).astype(jnp.bfloat16)
        payload[mesh_rows:, :] = coded


def join_kernel(*refs):
    payloads, joined = refs[:-1], refs[-1]
    rows = payloads[0].shape[0]
    for place, payload in enumerate(payloads):
        joined[place * rows : (place + 1) * rows, :] = payload[...]


def index_kernel(parts, mesh_rows, active, *refs):
    lanes, (index_out, state_out) = refs[:-2], refs[-2:]
    fanout = index_out.shape[0]
    group = len(lanes)
    owners = parts // group
    rows = lanes[0].shape[0] // owners

    @pl.when(active[0] == 1)
    def _():
        tables = []
        for part in range(parts):
            lane, turn = lanes[part % group], (-(part // group)) % owners
            base = turn * rows
            state_out[part * mesh_rows : (part + 1) * mesh_rows, :] = lane[base : base + mesh_rows, :]
            coded = lane[base + mesh_rows : base + rows, :384].astype(jnp.float32).astype(jnp.int32)
            tables.append(coded[:fanout])
        for part in range(parts):
            block = tables[part][:, :128]
            row = tables[part][:, 128:256]
            found = part * mesh_rows + row
            for list_index, offset in enumerate((-1, 1, -2, 2)):
                source = (part + offset) % parts
                lists = tables[source][list_index : list_index + 1, 256:384]
                lists = jnp.broadcast_to(lists, (fanout, 128))
                picked = jnp.take_along_axis(lists, row, axis=1)
                picked = jnp.where(picked == mesh_rows, parts * mesh_rows, source * mesh_rows + picked)
                found = jnp.where(block == list_index + 1, picked, found)
            index_out[:, part * mesh_rows : (part + 1) * mesh_rows] = found[:, :mesh_rows]


def layer_kernel(active, index, state_in, w_project, w_message, w_update, state_out):
    nodes, width = state_in.shape
    fanout = index.shape[0]
    chunk = min(256, nodes)

    @pl.when(active[0] == 1)
    def _():
        columns = jnp.concatenate([index[...], jnp.zeros((128 - fanout, nodes), jnp.int32)], axis=0)
        columns = jnp.transpose(columns.astype(jnp.float32))
        names = lax.broadcasted_iota(jnp.int32, (chunk, nodes), 1).astype(jnp.float32)
        sender = matmul(state_in[...], w_project[0, :, width:]).astype(jnp.bfloat16)
        for start in range(0, nodes, chunk):
            own = state_in[start : start + chunk, :]
            receiver = matmul(own, w_project[0, :, :width])
            total = jnp.zeros((chunk, width), jnp.float32)
            for k in range(fanout):
                hit = columns[start : start + chunk, k : k + 1] == names
                fetched = matmul(jnp.where(hit, 1.0, 0.0).astype(jnp.bfloat16), sender)
                edge = silu_by_tanh(receiver + fetched).astype(jnp.bfloat16)
                total = total + edge.astype(jnp.float32)
            gathered = (total * (1.0 / fanout)).astype(jnp.bfloat16)
            aggregate = matmul(gathered, w_message[0]).astype(jnp.bfloat16)
            update = silu_by_tanh(
                matmul(own, w_update[0, :width, :]) + matmul(aggregate, w_update[0, width:, :])
            )
            renewed = own.astype(jnp.float32) + rms_scale(update)
            state_out[start : start + chunk, :] = renewed.astype(jnp.bfloat16)


def prepare_kernel(snapshot, w_embed, w_decode, mesh_grid, ready, table_out):
    latent = silu_by_tanh(matmul_tn(snapshot[...], w_embed[...])).astype(jnp.bfloat16)
    ready[...] = matmul(latent, w_decode[: latent.shape[1], :])
    mesh_rows, grid_rows = table_out.shape
    table = lax.broadcasted_iota(jnp.int32, (mesh_rows, grid_rows), 0) == mesh_grid[...]
    table_out[...] = jnp.where(table, 1.0, 0.0).astype(jnp.bfloat16)


def decode_kernel(turn, ready, table, w_decode, w_output, *refs):
    blocks, out, state = refs[:-2], refs[-2], refs[-1]
    width = ready.shape[1]
    for number, block in enumerate(blocks):

        @pl.when(turn[0] == number)
        def _():
            state[...] = block[: state.shape[0], :]

    readout = matmul_tn(table[...], state[...]).astype(jnp.bfloat16)
    hidden = silu_by_tanh(ready[...] + matmul(readout, w_decode[width:, :])).astype(jnp.bfloat16)
    out[...] = matmul_nt(w_output[...], hidden).astype(jnp.bfloat16)


def call(kernel, name, shapes, inputs, places, scratch=(), room=16, flops=0):
    kinds = {"s": SMEM, "v": VMEM, "h": HBM}
    return pl.pallas_call(
        kernel,
        out_shape=shapes,
        in_specs=[kinds[place] for place in places],
        out_specs=[VMEM] * len(shapes),
        scratch_shapes=list(scratch),
        name=name,
        compiler_params=pltpu.CompilerParams(vmem_limit_bytes=room * 1024 * 1024),
        cost_estimate=pl.CostEstimate(flops=flops, bytes_accessed=0, transcendentals=0),
    )(*inputs)


def every_device(pairs, count, kind):
    onward = dict(pairs)
    reached = set(onward.values())
    for first in range(count):
        if first in reached or first not in onward:
            continue
        last = first
        while last in onward:
            last = onward[last]
        onward[last] = first
    rest = sorted((other for other in range(count) if other not in onward), key=lambda at: (kind(at), at))
    if len(rest) % 2:
        alone = rest.pop()
        if rest:
            one, two = rest.pop(), rest.pop()
            onward.update({one: two, two: alone, alone: one})
        else:
            onward[alone] = alone
    for one, two in zip(rest[::2], rest[1::2]):
        onward.update({one: two, two: one})
    return sorted(onward.items())


def resident(
    grid_state,
    w_embed,
    w_project,
    w_message,
    w_update,
    w_decode,
    w_output,
    grid_mesh,
    mesh_grid,
    neighbors,
    send_rows,
    halo_count,
):
    segment = lax.axis_index("segment")
    place = lax.axis_index("dom")
    segments = lax.axis_size("segment")
    parts = lax.axis_size("dom")
    samples, grid_rows, channels = grid_state.shape
    width = w_embed.shape[1]
    mesh_rows, fanout = neighbors.shape
    nodes = parts * mesh_rows
    group = parts // samples
    bf16 = jnp.bfloat16

    def device(at_segment, at_dom):
        return at_segment * parts + at_dom % parts

    def send(value, pairs, kind=lambda at: 0):
        return lax.ppermute(value, ("segment", "dom"), every_device(pairs, segments * parts, kind))

    def rotate(value, steps):
        return lax.ppermute(value, "dom", [(at, (at + steps) % parts) for at in range(parts)])

    def change_lane(value, steps):
        pairs = [(at, at - at % group + (at + steps) % group) for at in range(parts)]
        return lax.ppermute(value, "dom", pairs)

    is_owner = (place % group == 0).astype(jnp.int32).reshape(1)

    def active(at_segment):
        return ((segment == at_segment) & (place % group == 0)).astype(jnp.int32).reshape(1)

    by_channel = jnp.transpose(grid_state, (2, 0, 1))
    inputs = [
        by_channel.reshape(channels, samples * grid_rows),
        w_embed,
        grid_mesh.reshape(1, grid_rows),
        neighbors.T,
        send_rows,
        halo_count.reshape(-1),
    ]
    payloads = call(
        functools.partial(encode_kernel, samples),
        "encode",
        [jax.ShapeDtypeStruct((mesh_rows + 2 * fanout, width), bf16)] * samples,
        [(place // group).reshape(1)] + inputs,
        "shhhhhh",
        [pltpu.VMEM(value.shape, value.dtype) for value in inputs[:-1]]
        + [
            pltpu.SMEM(inputs[-1].shape, jnp.int32),
            pltpu.VMEM((samples * grid_rows, width), bf16),
            pltpu.SemaphoreType.DMA((6,)),
        ],
        room=60,
    )
    arrived = [payloads[0]] + [rotate(payloads[turn], turn * group) for turn in range(1, samples)]
    (joined,) = call(
        join_kernel,
        "join",
        [jax.ShapeDtypeStruct((samples * (mesh_rows + 2 * fanout), width), bf16)],
        arrived,
        "v" * samples,
    )
    lanes = [joined] + [change_lane(joined, -steps) for steps in range(1, group)]
    index, state = call(
        functools.partial(index_kernel, parts, mesh_rows),
        "index",
        [jax.ShapeDtypeStruct((fanout, nodes), jnp.int32), jax.ShapeDtypeStruct((nodes, width), bf16)],
        [is_owner] + lanes,
        "s" + "v" * group,
    )
    weights = [w_project, w_message, w_update]
    for at_segment in range(segments):
        (state,) = call(
            layer_kernel,
            "layer",
            [jax.ShapeDtypeStruct((nodes, width), bf16)],
            [active(at_segment), index, state] + weights,
            "svvvvv",
            flops=10**10,
        )
        if at_segment + 1 < segments:
            pairs = [
                (device(at_segment, m * group), device(at_segment + 1, m * group)) for m in range(samples)
            ]
            state = send(state, pairs, lambda at: at % group > 0)
        if at_segment == 0:
            snapshot = lax.dynamic_index_in_dim(by_channel, segment, 1, keepdims=False)
            ready, table = call(
                prepare_kernel,
                "prepare",
                [
                    jax.ShapeDtypeStruct((grid_rows, width), jnp.float32),
                    jax.ShapeDtypeStruct((mesh_rows, grid_rows), bf16),
                ],
                [snapshot, w_embed, w_decode, mesh_grid.reshape(1, grid_rows)],
                "vvvv",
                flops=10**9,
            )
    own_turn = (place // group - segment) % samples
    share = group * mesh_rows
    blocks = []
    for turn in range(samples):
        pairs = [
            (device(segments - 1, m * group), device(m, (m + turn) * group)) for m in range(samples)
        ]

        def kind(at, turn=turn):
            at_segment, at_dom = divmod(at, parts)
            if at_dom % group:
                return samples
            own = (at_dom // group - at_segment) % samples
            return 0 if own > turn else 1

        pairs = [(source, target) for source, target in pairs if source != target]
        block = state[turn * share : (turn + 1) * share]
        blocks.append(send(block, pairs, kind))
    last_owner = (segment == segments - 1) & (place == (samples - 1) * group)
    blocks[0] = jnp.where(last_owner, state[:share], blocks[0])
    block = blocks[0]
    for turn in range(1, samples):
        block = jnp.where(own_turn == turn, blocks[turn], block)
    handed = [block]
    for steps in range(1, group):
        handed.append(change_lane(block[steps * mesh_rows : (steps + 1) * mesh_rows], steps))
    (prediction,) = call(
        decode_kernel,
        "decode",
        [jax.ShapeDtypeStruct((channels, grid_rows), bf16)],
        [(place % group).reshape(1), ready, table, w_decode, w_output.T] + handed,
        "svvvv" + "v" * group,
        [pltpu.VMEM((mesh_rows, width), bf16)],
    )
    return prediction.T.reshape(1, grid_rows, channels)


def fits(mesh):
    segments, parts = mesh.shape["segment"], mesh.shape["dom"]
    return parts % segments == 0 and parts <= 16


def solution(mesh):
    return jax.shard_map(
        resident if fits(mesh) else streamed,
        mesh=mesh,
        in_specs=(
            P(None, "dom", None),
            P(),
            P("segment", None, None),
            P("segment", None, None),
            P("segment", None, None),
            P(),
            P(),
            P("dom"),
            P("dom"),
            P("dom", None),
            P(None, "dom"),
            P(None, "dom"),
        ),
        out_specs=P("segment", "dom", None),
        check_vma=False,
    )
```

```python
import functools

import jax
import jax.numpy as jnp
from jax import lax
from jax.experimental import pallas as pl
from jax.experimental.pallas import tpu as pltpu
from jax.sharding import PartitionSpec as P

epsilon = 1e-05
VMEM = pl.BlockSpec(memory_space=pltpu.VMEM)
SMEM = pl.BlockSpec(memory_space=pltpu.SMEM)
HBM = pl.BlockSpec(memory_space=pltpu.HBM)


def from_behind(value, axis, steps):
    count = lax.axis_size(axis)
    pairs = [(source, (source + steps) % count) for source in range(count)]
    return lax.ppermute(value, axis, pairs)


def from_behind_2(block, axis, distance):
    devices = range(lax.axis_size(axis))
    route = [(i - distance, i) for i in devices if i - distance in devices]
    return lax.ppermute(block, axis, route)


def from_root(value, axis, source):
    kept = jnp.where(lax.axis_index(axis) == source, value, 0).astype(value.dtype)
    return lax.psum(kept, axis)


def rms_scale(values):
    return values * lax.rsqrt(jnp.mean(values * values, axis=-1, keepdims=True) + epsilon)


def streamed(
    grid_state,
    w_embed,
    w_project,
    w_message,
    w_update,
    w_decode,
    w_output,
    grid_mesh,
    mesh_grid,
    neighbors,
    send_rows,
    halo_count,
):
    segment_index = lax.axis_index("segment")
    segment_count = lax.axis_size("segment")
    final_segment = segment_count - 1
    samples, grid_rows, channels = grid_state.shape
    width = w_embed.shape[1]
    mesh_rows = neighbors.shape[0]
    fanout = neighbors.shape[1]
    halo_rows = send_rows.shape[1]
    share = samples // segment_count
    pool_table = (grid_mesh[None, :] == jnp.arange(mesh_rows, dtype=jnp.int32)[:, None]).astype(
        jnp.bfloat16
    )
    read_table = (mesh_grid[:, None] == jnp.arange(mesh_rows, dtype=jnp.int32)[None, :]).astype(
        jnp.bfloat16
    )
    valid_rows = jnp.arange(halo_rows, dtype=jnp.int32)[None, :] < halo_count[:, 0][:, None]
    source_rows = neighbors.reshape(mesh_rows * fanout)

    def embed_grid(snapshot):
        return jax.nn.silu(jnp.dot(snapshot, w_embed, preferred_element_type=jnp.float32)).astype(
            jnp.bfloat16
        )

    def encode(snapshot):
        latent = embed_grid(snapshot)
        pooled = jnp.dot(pool_table, latent, preferred_element_type=jnp.float32)
        return (rms_scale(pooled).astype(jnp.bfloat16), latent)

    def project(state, weights):
        projected = jnp.dot(state, weights[0], preferred_element_type=jnp.float32)
        return (projected[:, :width], projected[:, width:].astype(jnp.bfloat16))

    def renew(state, receiver, extended, weights):
        fetched = extended[source_rows].reshape(mesh_rows, fanout, width)
        edges = jax.nn.silu(receiver[:, None, :] + fetched.astype(jnp.float32)).astype(jnp.bfloat16)
        messages = jnp.dot(
            edges.reshape(mesh_rows * fanout, width), weights[1], preferred_element_type=jnp.float32
        )
        aggregate = (jnp.sum(messages.reshape(mesh_rows, fanout, width), axis=1) / fanout).astype(
            jnp.bfloat16
        )
        update = jax.nn.silu(
            jnp.dot(state, weights[2][:width], preferred_element_type=jnp.float32)
            + jnp.dot(aggregate, weights[2][width:], preferred_element_type=jnp.float32)
        )
        return (state.astype(jnp.float32) + rms_scale(update)).astype(jnp.bfloat16)

    def decode(state, latent):
        readout = jnp.dot(read_table, state, preferred_element_type=jnp.float32).astype(
            jnp.bfloat16
        )
        hidden = jax.nn.silu(
            jnp.dot(latent, w_decode[:width], preferred_element_type=jnp.float32)
            + jnp.dot(readout, w_decode[width:], preferred_element_type=jnp.float32)
        ).astype(jnp.bfloat16)
        return jnp.dot(hidden, w_output, preferred_element_type=jnp.float32).astype(jnp.bfloat16)

    own_weights = (w_project[0], w_message[0], w_update[0])
    empty_mesh = jnp.zeros((mesh_rows, width), jnp.bfloat16)
    empty_receiver = jnp.zeros((mesh_rows, width), jnp.float32)
    empty_grid = jnp.zeros((grid_rows, width), jnp.bfloat16)
    empty_output = jnp.zeros((grid_rows, channels), jnp.bfloat16)
    received = empty_mesh
    carried = {}
    results = [empty_output for sample in range(samples)]
    for moment in range(samples + final_segment):
        current = received
        if moment < samples:
            snapshot = grid_state[moment]
            started, latent = lax.cond(
                segment_index == 0, lambda: encode(snapshot), lambda: (empty_mesh, empty_grid)
            )
            current = jnp.where(segment_index == 0, started, received)
            carried[moment] = from_behind_2(latent, "segment", final_segment)
        active = (moment - segment_index >= 0) & (moment - segment_index < samples)
        receiver, outgoing = lax.cond(
            active, lambda: project(current, own_weights), lambda: (empty_receiver, empty_mesh)
        )
        picked = jnp.where(valid_rows[:, :, None], outgoing[send_rows], jnp.zeros((), jnp.bfloat16))
        arrived = [outgoing]
        for list_index, offset in enumerate((1, -1, 2, -2)):
            arrived.append(from_behind(picked[list_index], "dom", offset))
        extended = jnp.concatenate(arrived, axis=0)
        renewed = lax.cond(
            active, lambda: renew(current, receiver, extended, own_weights), lambda: empty_mesh
        )
        if moment >= final_segment:
            finished = moment - final_segment
            skipped = carried[finished]
            results[finished] = lax.cond(
                segment_index == final_segment,
                lambda: decode(renewed, skipped),
                lambda: empty_output,
            )
        if moment < samples + final_segment - 1:
            received = from_behind_2(renewed, "segment", 1)
    everything = from_root(jnp.stack(results), "segment", final_segment)
    return lax.dynamic_slice_in_dim(everything, segment_index * share, share, 0)


def silu_by_tanh(values):
    half = 0.5 * values
    return half + half * jnp.tanh(half)


def matmul(left, right):
    return jnp.dot(left, right, preferred_element_type=jnp.float32)


def matmul_nt(left, right):
    return lax.dot_general(left, right, (((1,), (1,)), ((), ())), preferred_element_type=jnp.float32)


def matmul_tn(left, right):
    return lax.dot_general(left, right, (((0,), (0,)), ((), ())), preferred_element_type=jnp.float32)


def fetch(sources, targets, semaphores):
    copies = [
        pltpu.make_async_copy(source, target, semaphores.at[place])
        for place, (source, target) in enumerate(zip(sources, targets))
    ]
    for copy in copies:
        copy.start()
    return copies


def encode_kernel(turns, held_states, chosen, *refs):
    inputs, payloads = refs[:6], refs[6 : 6 + turns]
    held, latent, semaphores = refs[6 + turns : 12 + turns], refs[12 + turns], refs[13 + turns]
    copies = fetch(inputs, held, semaphores)
    for copy in copies:
        copy.wait()
    snapshots, w_embed, grid_mesh, neighbors, send_rows, counts = held
    mesh_rows = neighbors.shape[1]
    fanout = neighbors.shape[0]
    grid_rows = snapshots.shape[1] // held_states
    lists, halo_rows = send_rows.shape
    width = w_embed.shape[1]
    latent[...] = silu_by_tanh(matmul_tn(snapshots[...], w_embed[...])).astype(jnp.bfloat16)
    table = lax.broadcasted_iota(jnp.int32, (mesh_rows, grid_rows), 0) == grid_mesh[...]
    table = jnp.where(table, 1.0, 0.0).astype(jnp.bfloat16)
    near = neighbors[...]
    block = near // mesh_rows
    row = near - block * mesh_rows
    position = lax.broadcasted_iota(jnp.int32, (1, halo_rows), 1)
    rows = []
    for list_index in range(lists):
        kept = position < counts[list_index]
        rows.append(jnp.where(kept, send_rows[list_index : list_index + 1, :], mesh_rows))
    rows.append(jnp.zeros((fanout - lists, halo_rows), jnp.int32))
    filler = jnp.zeros((fanout, 128 - mesh_rows), jnp.int32)
    pieces = [block, filler, row, filler, jnp.concatenate(rows, axis=0), filler]
    coded = jnp.concatenate(pieces + [jnp.zeros((fanout, width - 384), jnp.int32)], axis=1)
    coded = jnp.concatenate([coded, jnp.zeros_like(coded)], axis=0)
    coded = coded.astype(jnp.float32).astype(jnp.bfloat16)
    for turn, payload in enumerate(payloads):
        start = pl.multiple_of(chosen[turn] * grid_rows, grid_rows)
        pooled = matmul(table, latent[pl.ds(start, grid_rows), :])
        payload[:mesh_rows, :] = rms_scale(pooled).astype(jnp.bfloat16)
        payload[mesh_rows:, :] = coded


def join_kernel(*refs):
    payloads, joined = refs[:-1], refs[-1]
    rows = payloads[0].shape[0]
    for place, payload in enumerate(payloads):
        joined[place * rows : (place + 1) * rows, :] = payload[...]


def index_kernel(parts, mesh_rows, chip, *refs):
    lanes, (index_out, state_out) = refs[:-2], refs[-2:]
    fanout = index_out.shape[0]
    group = len(lanes)
    rows = lanes[0].shape[0] // (parts // group)

    @pl.when(chip[1] == 1)
    def _():
        tables = []
        for part in range(parts):
            lane, turn = lanes[part % group], jnp.bitwise_xor(chip[0], part // group)
            base = pl.multiple_of(turn * rows, 16)
            state_out[part * mesh_rows : (part + 1) * mesh_rows, :] = lane[pl.ds(base, mesh_rows), :]
            base = pl.multiple_of(turn * rows + mesh_rows, 16)
            coded = lane[pl.ds(base, rows - mesh_rows), :384].astype(jnp.float32).astype(jnp.int32)
            tables.append(coded[:fanout])
        for part in range(parts):
            block = tables[part][:, :128]
            row = tables[part][:, 128:256]
            found = part * mesh_rows + row
            for list_index, offset in enumerate((-1, 1, -2, 2)):
                source = (part + offset) % parts
                lists = tables[source][list_index : list_index + 1, 256:384]
                lists = jnp.broadcast_to(lists, (fanout, 128))
                picked = jnp.take_along_axis(lists, row, axis=1)
                picked = jnp.where(picked == mesh_rows, parts * mesh_rows, source * mesh_rows + picked)
                found = jnp.where(block == list_index + 1, picked, found)
            index_out[:, part * mesh_rows : (part + 1) * mesh_rows] = found[:, :mesh_rows]


def run_layer(fanout, columns, state_in, weights, copies, state_out):
    w_project, w_message, w_update = weights
    nodes, width = state_in.shape
    chunk = min(256, nodes)
    names = lax.broadcasted_iota(jnp.int32, (chunk, nodes), 1).astype(jnp.float32)
    copies[0].wait()
    sender = matmul(state_in[...], w_project[:, width:]).astype(jnp.bfloat16)
    for start in range(0, nodes, chunk):
        own = state_in[start : start + chunk, :]
        receiver = matmul(own, w_project[:, :width])
        total = jnp.zeros((chunk, width), jnp.float32)
        for k in range(fanout):
            hit = columns[start : start + chunk, k : k + 1] == names
            fetched = matmul(jnp.where(hit, 1.0, 0.0).astype(jnp.bfloat16), sender)
            edge = silu_by_tanh(receiver + fetched).astype(jnp.bfloat16)
            total = total + edge.astype(jnp.float32)
        gathered = (total * (1.0 / fanout)).astype(jnp.bfloat16)
        if start == 0:
            copies[1].wait()
            copies[2].wait()
        aggregate = matmul(gathered, w_message[...]).astype(jnp.bfloat16)
        update = silu_by_tanh(
            matmul(own, w_update[:width, :]) + matmul(aggregate, w_update[width:, :])
        )
        renewed = own.astype(jnp.float32) + rms_scale(update)
        state_out[start : start + chunk, :] = renewed.astype(jnp.bfloat16)


def stage_kernel(where, index, state_in, *refs):
    own, other, state_out = refs[:3], refs[3:6], refs[6]
    first, second, between, columns, semaphores = refs[7:10], refs[10:13], refs[13], refs[14], refs[15]
    nodes = state_in.shape[0]
    fanout = index.shape[0]

    @pl.when(where[0] == 1)
    def _():
        @pl.when(where[1] == 0)
        def _():
            fetch([ref.at[0] for ref in own + other], first + second, semaphores)

        @pl.when(where[1] == 1)
        def _():
            fetch([ref.at[0] for ref in other + own], first + second, semaphores)

        copies = [
            pltpu.make_async_copy(source.at[0], target, semaphores.at[place])
            for place, (source, target) in enumerate(zip(own + other, first + second))
        ]
        rows = jnp.concatenate([index[...], jnp.zeros((128 - fanout, nodes), jnp.int32)], axis=0)
        columns[...] = jnp.transpose(rows.astype(jnp.float32))
        run_layer(fanout, columns, state_in, first, copies[:3], between)
        run_layer(fanout, columns, between, second, copies[3:], state_out)


def prepare_kernel(snapshot, w_embed, w_decode, mesh_grid, ready, table_out):
    latent = silu_by_tanh(matmul_tn(snapshot[...], w_embed[...])).astype(jnp.bfloat16)
    ready[...] = matmul(latent, w_decode[: latent.shape[1], :])
    mesh_rows, grid_rows = table_out.shape
    table = lax.broadcasted_iota(jnp.int32, (mesh_rows, grid_rows), 0) == mesh_grid[...]
    table_out[...] = jnp.where(table, 1.0, 0.0).astype(jnp.bfloat16)


def decode_kernel(turn, ready, table, w_decode, w_output, *refs):
    blocks, out, state = refs[:-2], refs[-2], refs[-1]
    width = ready.shape[1]
    for number, block in enumerate(blocks):

        @pl.when(turn[0] == number)
        def _():
            state[...] = block[: state.shape[0], :]

    readout = matmul_tn(table[...], state[...]).astype(jnp.bfloat16)
    hidden = silu_by_tanh(ready[...] + matmul(readout, w_decode[width:, :])).astype(jnp.bfloat16)
    out[...] = matmul_nt(w_output[...], hidden).astype(jnp.bfloat16)


def call(kernel, name, shapes, inputs, places, scratch=(), room=16, flops=0):
    kinds = {"s": SMEM, "v": VMEM, "h": HBM}
    return pl.pallas_call(
        kernel,
        out_shape=shapes,
        in_specs=[kinds[place] for place in places],
        out_specs=[VMEM] * len(shapes),
        scratch_shapes=list(scratch),
        name=name,
        compiler_params=pltpu.CompilerParams(vmem_limit_bytes=room * 1024 * 1024),
        cost_estimate=pl.CostEstimate(flops=flops, bytes_accessed=0, transcendentals=0),
    )(*inputs)


def every_device(pairs, count, kind):
    onward = dict(pairs)
    reached = set(onward.values())
    for first in range(count):
        if first in reached or first not in onward:
            continue
        last = first
        while last in onward:
            last = onward[last]
        onward[last] = first
    rest = sorted((other for other in range(count) if other not in onward), key=lambda at: (kind(at), at))
    if len(rest) % 2:
        alone = rest.pop()
        if rest:
            one, two = rest.pop(), rest.pop()
            onward.update({one: two, two: alone, alone: one})
        else:
            onward[alone] = alone
    for one, two in zip(rest[::2], rest[1::2]):
        onward.update({one: two, two: one})
    return sorted(onward.items())


def resident(
    grid_state,
    w_embed,
    w_project,
    w_message,
    w_update,
    w_decode,
    w_output,
    grid_mesh,
    mesh_grid,
    neighbors,
    send_rows,
    halo_count,
):
    segment = lax.axis_index("segment")
    place = lax.axis_index("dom")
    segments = lax.axis_size("segment")
    parts = lax.axis_size("dom")
    samples, grid_rows, channels = grid_state.shape
    width = w_embed.shape[1]
    mesh_rows, fanout = neighbors.shape
    nodes = parts * mesh_rows
    group = parts // samples
    bf16 = jnp.bfloat16

    def device(at_segment, at_dom):
        return at_segment * parts + at_dom % parts

    def send(value, pairs, kind=lambda at: 0):
        return lax.ppermute(value, ("segment", "dom"), every_device(pairs, segments * parts, kind))

    def to_chip(value, steps):
        pairs = [(at, (at // group ^ steps) * group + at % group) for at in range(parts)]
        return lax.ppermute(value, "dom", pairs)

    def change_lane(value, steps):
        pairs = [(at, at - at % group + (at + steps) % group) for at in range(parts)]
        return lax.ppermute(value, "dom", pairs)

    def chip_of(m):
        return samples // 2 - 1 + m // 2

    def owner(m, stage):
        return device(2 * stage + m % 2, chip_of(m) * group)

    by_channel = jnp.transpose(grid_state, (2, 0, 1))
    weights = [w_project, w_message, w_update]
    chip, lane, parity = place // group, place % group, segment % 2
    held_states = samples // 2

    def beside(skip):
        across = segments // 2
        return [
            (device(at, dom), device((at + across) % segments, dom))
            for at in range(segments)
            for dom in range(parts)
            if dom % group and dom // group not in skip
        ]

    chips = [chip_of(m) for m in range(0, samples, 2)]
    ends = [0, samples - 1]
    direct = [
        (device(at, one * group), device(at ^ 1, one * group)) for at in range(segments) for one in chips
    ] + beside(ends)
    around = []
    for at in range(segments):
        for one, end in zip(chips, ends):
            around.append((device(at ^ 1, end * group), device(at, one * group)))
            around.append((device(at, one * group), device(at, end * group)))
    around += beside([])
    swapped = [send(w_project, direct), send(w_message, direct), send(w_update, around)]
    inputs = [
        jnp.concatenate(
            [
                lax.dynamic_index_in_dim(by_channel, parity + 2 * one, 1, keepdims=False)
                for one in range(held_states)
            ],
            axis=1,
        ),
        w_embed,
        grid_mesh.reshape(1, grid_rows),
        neighbors.T,
        send_rows,
        halo_count.reshape(-1),
    ]
    chosen = jnp.clip((chip ^ jnp.arange(samples, dtype=jnp.int32)) - chips[0], 0, held_states - 1)
    payloads = call(
        functools.partial(encode_kernel, samples, held_states),
        "encode",
        [jax.ShapeDtypeStruct((mesh_rows + 2 * fanout, width), bf16)] * samples,
        [chosen] + inputs,
        "shhhhhh",
        [pltpu.VMEM(value.shape, value.dtype) for value in inputs[:-1]]
        + [
            pltpu.SMEM(inputs[-1].shape, jnp.int32),
            pltpu.VMEM((held_states * grid_rows, width), bf16),
            pltpu.SemaphoreType.DMA((6,)),
        ],
        room=60,
    )
    arrived = [payloads[0]] + [to_chip(payloads[turn], turn) for turn in range(1, samples)]
    (joined,) = call(
        join_kernel,
        "join",
        [jax.ShapeDtypeStruct((samples * (mesh_rows + 2 * fanout), width), bf16)],
        arrived,
        "v" * samples,
    )
    lanes = [joined] + [change_lane(joined, -steps) for steps in range(1, group)]
    is_owner = (lane == 0) & (chip >= chips[0]) & (chip <= chips[-1])
    index, state = call(
        functools.partial(index_kernel, parts, mesh_rows),
        "index",
        [jax.ShapeDtypeStruct((fanout, nodes), jnp.int32), jax.ShapeDtypeStruct((nodes, width), bf16)],
        [jnp.stack([chip, is_owner.astype(jnp.int32)])] + lanes,
        "s" + "v" * group,
    )
    for stage in range(segments // 2):
        active = is_owner & (segment // 2 == stage)
        (state,) = call(
            stage_kernel,
            "stage",
            [jax.ShapeDtypeStruct((nodes, width), bf16)],
            [jnp.stack([active.astype(jnp.int32), parity]), index, state] + weights + swapped,
            "svv" + "h" * 6,
            [pltpu.VMEM(weight.shape[1:], bf16) for weight in weights * 2]
            + [
                pltpu.VMEM((nodes, width), bf16),
                pltpu.VMEM((nodes, 128), jnp.float32),
                pltpu.SemaphoreType.DMA((6,)),
            ],
            room=24,
            flops=10**10,
        )
        if 2 * stage + 2 < segments:
            pairs = [(owner(m, stage), owner(m, stage + 1)) for m in range(samples)]
            state = send(state, pairs)
        if stage == 0:
            snapshot = lax.dynamic_index_in_dim(by_channel, segment, 1, keepdims=False)
            ready, table = call(
                prepare_kernel,
                "prepare",
                [
                    jax.ShapeDtypeStruct((grid_rows, width), jnp.float32),
                    jax.ShapeDtypeStruct((mesh_rows, grid_rows), bf16),
                ],
                [snapshot, w_embed, w_decode, mesh_grid.reshape(1, grid_rows)],
                "vvvv",
                flops=10**9,
            )
    share = group * mesh_rows
    last = segments // 2 - 1
    blocks = []
    for turn in range(samples):

        def kind(at, turn=turn):
            dom = at % parts
            return 2 if dom % group else int(dom // group <= turn)

        pairs = [(owner(m, last), device(m, turn * group)) for m in range(samples)]
        kept = [source for source, target in pairs if source == target]
        pairs = [(source, target) for source, target in pairs if source != target]
        block = state[turn * share : (turn + 1) * share]
        came = send(block, pairs, kind)
        for at in kept:
            came = jnp.where(segment * parts + place == at, block, came)
        blocks.append(came)
    block = blocks[0]
    for turn in range(1, samples):
        block = jnp.where(chip == turn, blocks[turn], block)
    handed = [block]
    for steps in range(1, group):
        handed.append(change_lane(block[steps * mesh_rows : (steps + 1) * mesh_rows], steps))
    (prediction,) = call(
        decode_kernel,
        "decode",
        [jax.ShapeDtypeStruct((channels, grid_rows), bf16)],
        [lane.reshape(1), ready, table, w_decode, w_output.T] + handed,
        "svvvv" + "v" * group,
        [pltpu.VMEM((mesh_rows, width), bf16)],
    )
    return prediction.T.reshape(1, grid_rows, channels)


def fits(mesh):
    segments, parts = mesh.shape["segment"], mesh.shape["dom"]
    return segments == 4 and parts % segments == 0 and parts <= 16


def solution(mesh):
    return jax.shard_map(
        resident if fits(mesh) else streamed,
        mesh=mesh,
        in_specs=(
            P(None, "dom", None),
            P(),
            P("segment", None, None),
            P("segment", None, None),
            P("segment", None, None),
            P(),
            P(),
            P("dom"),
            P("dom"),
            P("dom", None),
            P(None, "dom"),
            P(None, "dom"),
        ),
        out_specs=P("segment", "dom", None),
        check_vma=False,
    )
```

```python
import functools

import jax
import jax.numpy as jnp
from jax import lax
from jax.experimental import pallas as pl
from jax.experimental.pallas import tpu as pltpu
from jax.sharding import PartitionSpec as P

epsilon = 1e-05
VMEM = pl.BlockSpec(memory_space=pltpu.VMEM)
SMEM = pl.BlockSpec(memory_space=pltpu.SMEM)
HBM = pl.BlockSpec(memory_space=pltpu.HBM)


def from_behind(value, axis, steps):
    count = lax.axis_size(axis)
    pairs = [(source, (source + steps) % count) for source in range(count)]
    return lax.ppermute(value, axis, pairs)


def from_behind_2(block, axis, distance):
    devices = range(lax.axis_size(axis))
    route = [(i - distance, i) for i in devices if i - distance in devices]
    return lax.ppermute(block, axis, route)


def from_root(value, axis, source):
    kept = jnp.where(lax.axis_index(axis) == source, value, 0).astype(value.dtype)
    return lax.psum(kept, axis)


def rms_scale(values):
    return values * lax.rsqrt(jnp.mean(values * values, axis=-1, keepdims=True) + epsilon)


def streamed(
    grid_state,
    w_embed,
    w_project,
    w_message,
    w_update,
    w_decode,
    w_output,
    grid_mesh,
    mesh_grid,
    neighbors,
    send_rows,
    halo_count,
):
    segment_index = lax.axis_index("segment")
    segment_count = lax.axis_size("segment")
    final_segment = segment_count - 1
    samples, grid_rows, channels = grid_state.shape
    width = w_embed.shape[1]
    mesh_rows = neighbors.shape[0]
    fanout = neighbors.shape[1]
    halo_rows = send_rows.shape[1]
    share = samples // segment_count
    pool_table = (grid_mesh[None, :] == jnp.arange(mesh_rows, dtype=jnp.int32)[:, None]).astype(
        jnp.bfloat16
    )
    read_table = (mesh_grid[:, None] == jnp.arange(mesh_rows, dtype=jnp.int32)[None, :]).astype(
        jnp.bfloat16
    )
    valid_rows = jnp.arange(halo_rows, dtype=jnp.int32)[None, :] < halo_count[:, 0][:, None]
    source_rows = neighbors.reshape(mesh_rows * fanout)

    def embed_grid(snapshot):
        return jax.nn.silu(jnp.dot(snapshot, w_embed, preferred_element_type=jnp.float32)).astype(
            jnp.bfloat16
        )

    def encode(snapshot):
        latent = embed_grid(snapshot)
        pooled = jnp.dot(pool_table, latent, preferred_element_type=jnp.float32)
        return (rms_scale(pooled).astype(jnp.bfloat16), latent)

    def project(state, weights):
        projected = jnp.dot(state, weights[0], preferred_element_type=jnp.float32)
        return (projected[:, :width], projected[:, width:].astype(jnp.bfloat16))

    def renew(state, receiver, extended, weights):
        fetched = extended[source_rows].reshape(mesh_rows, fanout, width)
        edges = jax.nn.silu(receiver[:, None, :] + fetched.astype(jnp.float32)).astype(jnp.bfloat16)
        messages = jnp.dot(
            edges.reshape(mesh_rows * fanout, width), weights[1], preferred_element_type=jnp.float32
        )
        aggregate = (jnp.sum(messages.reshape(mesh_rows, fanout, width), axis=1) / fanout).astype(
            jnp.bfloat16
        )
        update = jax.nn.silu(
            jnp.dot(state, weights[2][:width], preferred_element_type=jnp.float32)
            + jnp.dot(aggregate, weights[2][width:], preferred_element_type=jnp.float32)
        )
        return (state.astype(jnp.float32) + rms_scale(update)).astype(jnp.bfloat16)

    def decode(state, latent):
        readout = jnp.dot(read_table, state, preferred_element_type=jnp.float32).astype(
            jnp.bfloat16
        )
        hidden = jax.nn.silu(
            jnp.dot(latent, w_decode[:width], preferred_element_type=jnp.float32)
            + jnp.dot(readout, w_decode[width:], preferred_element_type=jnp.float32)
        ).astype(jnp.bfloat16)
        return jnp.dot(hidden, w_output, preferred_element_type=jnp.float32).astype(jnp.bfloat16)

    own_weights = (w_project[0], w_message[0], w_update[0])
    empty_mesh = jnp.zeros((mesh_rows, width), jnp.bfloat16)
    empty_receiver = jnp.zeros((mesh_rows, width), jnp.float32)
    empty_grid = jnp.zeros((grid_rows, width), jnp.bfloat16)
    empty_output = jnp.zeros((grid_rows, channels), jnp.bfloat16)
    received = empty_mesh
    carried = {}
    results = [empty_output for sample in range(samples)]
    for moment in range(samples + final_segment):
        current = received
        if moment < samples:
            snapshot = grid_state[moment]
            started, latent = lax.cond(
                segment_index == 0, lambda: encode(snapshot), lambda: (empty_mesh, empty_grid)
            )
            current = jnp.where(segment_index == 0, started, received)
            carried[moment] = from_behind_2(latent, "segment", final_segment)
        active = (moment - segment_index >= 0) & (moment - segment_index < samples)
        receiver, outgoing = lax.cond(
            active, lambda: project(current, own_weights), lambda: (empty_receiver, empty_mesh)
        )
        picked = jnp.where(valid_rows[:, :, None], outgoing[send_rows], jnp.zeros((), jnp.bfloat16))
        arrived = [outgoing]
        for list_index, offset in enumerate((1, -1, 2, -2)):
            arrived.append(from_behind(picked[list_index], "dom", offset))
        extended = jnp.concatenate(arrived, axis=0)
        renewed = lax.cond(
            active, lambda: renew(current, receiver, extended, own_weights), lambda: empty_mesh
        )
        if moment >= final_segment:
            finished = moment - final_segment
            skipped = carried[finished]
            results[finished] = lax.cond(
                segment_index == final_segment,
                lambda: decode(renewed, skipped),
                lambda: empty_output,
            )
        if moment < samples + final_segment - 1:
            received = from_behind_2(renewed, "segment", 1)
    everything = from_root(jnp.stack(results), "segment", final_segment)
    return lax.dynamic_slice_in_dim(everything, segment_index * share, share, 0)


def silu_by_tanh(values):
    half = 0.5 * values
    return half + half * jnp.tanh(half)


def matmul(left, right):
    return jnp.dot(left, right, preferred_element_type=jnp.float32)


def matmul_nt(left, right):
    return lax.dot_general(left, right, (((1,), (1,)), ((), ())), preferred_element_type=jnp.float32)


def matmul_tn(left, right):
    return lax.dot_general(left, right, (((0,), (0,)), ((), ())), preferred_element_type=jnp.float32)


def fetch(sources, targets, semaphores):
    copies = [
        pltpu.make_async_copy(source, target, semaphores.at[place])
        for place, (source, target) in enumerate(zip(sources, targets))
    ]
    for copy in copies:
        copy.start()
    return copies


def encode_kernel(mesh_rows, fanout, lists, chip, snapshots, w_embed, packed, *refs):
    payloads, latent = refs[:-1], refs[-1]
    neighbors = packed[:fanout, :mesh_rows]
    grid_rows = snapshots.shape[2]
    grid_mesh = packed[fanout + lists : fanout + lists + 1, :grid_rows]
    counts = packed[fanout + lists + 1 : fanout + lists + 2, :lists]
    width = w_embed.shape[1]
    for place in range(snapshots.shape[0]):
        found = silu_by_tanh(matmul_tn(snapshots[place], w_embed[...])).astype(jnp.bfloat16)
        latent[place * grid_rows : (place + 1) * grid_rows, :] = found
    table = lax.broadcasted_iota(jnp.int32, (mesh_rows, grid_rows), 0) == grid_mesh
    table = jnp.where(table, 1.0, 0.0).astype(jnp.bfloat16)
    block = neighbors // mesh_rows
    row = neighbors - block * mesh_rows
    halo_rows = mesh_rows
    position = lax.broadcasted_iota(jnp.int32, (1, halo_rows), 1)
    rows = []
    for list_index in range(lists):
        kept = position < counts[:, list_index : list_index + 1]
        listed = packed[fanout + list_index : fanout + list_index + 1, :halo_rows]
        rows.append(jnp.where(kept, listed, mesh_rows))
    rows.append(jnp.zeros((fanout - lists, halo_rows), jnp.int32))
    filler = jnp.zeros((fanout, 128 - mesh_rows), jnp.int32)
    pieces = [block, filler, row, filler, jnp.concatenate(rows, axis=0), filler]
    coded = jnp.concatenate(pieces + [jnp.zeros((fanout, width - 384), jnp.int32)], axis=1)
    coded = jnp.concatenate([coded, jnp.zeros_like(coded)], axis=0)
    coded = coded.astype(jnp.float32).astype(jnp.bfloat16)
    for turn, payload in enumerate(payloads):
        start = pl.multiple_of(jnp.bitwise_xor(chip[0], turn) * grid_rows, grid_rows)
        pooled = matmul(table, latent[pl.ds(start, grid_rows), :])
        payload[:mesh_rows, :] = rms_scale(pooled).astype(jnp.bfloat16)
        payload[mesh_rows:, :] = coded


def join_kernel(*refs):
    payloads, joined = refs[:-1], refs[-1]
    rows = payloads[0].shape[0]
    for place, payload in enumerate(payloads):
        joined[place * rows : (place + 1) * rows, :] = payload[...]


def index_kernel(parts, mesh_rows, chip, active, *refs):
    lanes, (columns_out, low, high), index_out = refs[:-4], refs[-4:-1], refs[-1]
    nodes = columns_out.shape[0]
    group = len(lanes)
    rows = lanes[0].shape[0] // (parts // group)

    @pl.when(active[0] == 1)
    def _():
        tables = []
        for part in range(parts):
            lane, turn = lanes[part % group], jnp.bitwise_xor(chip[0], part // group)
            base = pl.multiple_of(turn * rows, 16)
            half, spot = (low, part) if part < parts // 2 else (high, part - parts // 2)
            half[spot * mesh_rows : (spot + 1) * mesh_rows, :] = lane[pl.ds(base, mesh_rows), :]
            base = pl.multiple_of(turn * rows + mesh_rows, 16)
            coded = lane[pl.ds(base, rows - mesh_rows), :384].astype(jnp.float32).astype(jnp.int32)
            tables.append(coded[: coded.shape[0] // 2])
        fanout = tables[0].shape[0]
        index_out[fanout:, :] = jnp.zeros((index_out.shape[0] - fanout, nodes), jnp.int32)
        for part in range(parts):
            block = tables[part][:, :128]
            row = tables[part][:, 128:256]
            found = part * mesh_rows + row
            for list_index, offset in enumerate((-1, 1, -2, 2)):
                source = (part + offset) % parts
                lists = tables[source][list_index : list_index + 1, 256:384]
                lists = jnp.broadcast_to(lists, (fanout, 128))
                picked = jnp.take_along_axis(lists, row, axis=1)
                picked = jnp.where(picked == mesh_rows, parts * mesh_rows, source * mesh_rows + picked)
                found = jnp.where(block == list_index + 1, picked, found)
            index_out[:fanout, part * mesh_rows : (part + 1) * mesh_rows] = found[:, :mesh_rows]
        columns_out[...] = jnp.transpose(index_out[...].astype(jnp.float32))


def hold_kernel(*refs):
    half = len(refs) // 2
    for copy in fetch(refs[:half], refs[half:-1], refs[-1]):
        copy.wait()


def renew(fanout, columns, sender, own, w_project, w_message, w_update):
    chunk, width = own.shape
    nodes = sender.shape[0]
    names = lax.broadcasted_iota(jnp.int32, (chunk, nodes), 1).astype(jnp.float32)
    receiver = matmul(own, w_project[0, :, :width])
    total = jnp.zeros((chunk, width), jnp.float32)
    for k in range(fanout):
        hit = columns[:, k : k + 1] == names
        fetched = matmul(jnp.where(hit, 1.0, 0.0).astype(jnp.bfloat16), sender)
        edge = silu_by_tanh(receiver + fetched).astype(jnp.bfloat16)
        total = total + edge.astype(jnp.float32)
    gathered = (total * (1.0 / fanout)).astype(jnp.bfloat16)
    aggregate = matmul(gathered, w_message[0]).astype(jnp.bfloat16)
    update = silu_by_tanh(
        matmul(own, w_update[0, :width, :]) + matmul(aggregate, w_update[0, width:, :])
    )
    return (own.astype(jnp.float32) + rms_scale(update)).astype(jnp.bfloat16)


def sender_kernel(active, low, w_project, sender_low):
    width = low.shape[1]

    @pl.when(active[0] == 1)
    def _():
        sender_low[...] = matmul(low[...], w_project[0, :, width:]).astype(jnp.bfloat16)


def low_kernel(fanout, active, columns, sender_low, low, high, w_project, w_message, w_update, *outs):
    sender, new_low = outs
    half, width = low.shape

    @pl.when(active[0] == 1)
    def _():
        sender[:half, :] = sender_low[...]
        sender[half:, :] = matmul(high[...], w_project[0, :, width:]).astype(jnp.bfloat16)
        new_low[...] = renew(
            fanout, columns[:half, :], sender[...], low[...], w_project, w_message, w_update
        )


def high_kernel(fanout, active, columns, sender, high, w_project, w_message, w_update, new_high):
    half = high.shape[0]

    @pl.when(active[0] == 1)
    def _():
        new_high[...] = renew(
            fanout, columns[half:, :], sender[...], high[...], w_project, w_message, w_update
        )


def prepare_kernel(snapshot, w_embed, w_decode, mesh_grid, ready, table_out):
    latent = silu_by_tanh(matmul_tn(snapshot[...], w_embed[...])).astype(jnp.bfloat16)
    ready[...] = matmul(latent, w_decode[: latent.shape[1], :])
    mesh_rows, grid_rows = table_out.shape
    table = lax.broadcasted_iota(jnp.int32, (mesh_rows, grid_rows), 0) == mesh_grid[...]
    table_out[...] = jnp.where(table, 1.0, 0.0).astype(jnp.bfloat16)


def decode_kernel(turn, ready, table, w_decode, w_output, *refs):
    blocks, out, state = refs[:-2], refs[-2], refs[-1]
    width = ready.shape[1]
    for number, block in enumerate(blocks):

        @pl.when(turn[0] == number)
        def _():
            state[...] = block[: state.shape[0], :]

    readout = matmul_tn(table[...], state[...]).astype(jnp.bfloat16)
    hidden = silu_by_tanh(ready[...] + matmul(readout, w_decode[width:, :])).astype(jnp.bfloat16)
    out[...] = matmul_nt(w_output[...], hidden).astype(jnp.bfloat16)


def call(kernel, name, shapes, inputs, places, scratch=(), room=16, flops=0):
    kinds = {"s": SMEM, "v": VMEM, "h": HBM}
    return pl.pallas_call(
        kernel,
        out_shape=shapes,
        in_specs=[kinds[place] for place in places],
        out_specs=[VMEM] * len(shapes),
        scratch_shapes=list(scratch),
        name=name,
        compiler_params=pltpu.CompilerParams(vmem_limit_bytes=room * 1024 * 1024),
        cost_estimate=pl.CostEstimate(flops=flops, bytes_accessed=0, transcendentals=0),
    )(*inputs)


def every_device(pairs, count, group):
    onward = dict(pairs)
    reached = set(onward.values())
    for first in [source for source in onward if source not in reached]:
        last = first
        while last in onward:
            last = onward[last]
        onward.update({last: last + group - 1, last + group - 1: first + group - 1, first + group - 1: first})
    reached = set(onward.values())
    for at in range(0, count, group):
        givers = [lane for lane in range(at, at + group) if lane not in onward]
        takers = [lane for lane in range(at, at + group) if lane not in reached]
        onward.update(zip(givers, takers[1:] + takers[:1]))
    return sorted(onward.items())


def resident(
    grid_state,
    w_embed,
    w_project,
    w_message,
    w_update,
    w_decode,
    w_output,
    grid_mesh,
    mesh_grid,
    neighbors,
    send_rows,
    halo_count,
):
    segment = lax.axis_index("segment")
    place = lax.axis_index("dom")
    segments = lax.axis_size("segment")
    parts = lax.axis_size("dom")
    samples, grid_rows, channels = grid_state.shape
    width = w_embed.shape[1]
    mesh_rows, fanout = neighbors.shape
    nodes = parts * mesh_rows
    group = parts // samples
    bf16 = jnp.bfloat16

    def device(at_segment, at_dom):
        return at_segment * parts + at_dom % parts

    def send(value, pairs):
        return lax.ppermute(value, ("segment", "dom"), every_device(pairs, segments * parts, group))

    def to_chip(value, steps):
        pairs = [(at, (at // group ^ steps) * group + at % group) for at in range(parts)]
        return lax.ppermute(value, "dom", pairs)

    def change_lane(value, steps):
        pairs = [(at, at - at % group + (at + steps) % group) for at in range(parts)]
        return lax.ppermute(value, "dom", pairs)

    def owner(m, at_segment):
        return device(at_segment, m * group)

    chip, lane = place // group, place % group
    weights = [w_project, w_message, w_update]
    last = segments - 2
    pairs = [(owner(m, last + 1), owner(m, last)) for m in range(samples)]
    came_weights = [send(weight, pairs) for weight in weights]
    snapshots = jnp.transpose(grid_state, (0, 2, 1))
    lists = send_rows.shape[0]

    def rows_of(value):
        return jnp.pad(value, ((0, 0), (0, 128 - value.shape[1])))

    packed = jnp.concatenate(
        [
            rows_of(neighbors.T),
            rows_of(send_rows),
            rows_of(grid_mesh.reshape(1, grid_rows)),
            rows_of(halo_count.reshape(1, lists)),
        ],
        axis=0,
    )
    payloads = call(
        functools.partial(encode_kernel, mesh_rows, fanout, lists),
        "encode",
        [jax.ShapeDtypeStruct((mesh_rows + 2 * fanout, width), bf16)] * samples,
        [chip.reshape(1), snapshots, w_embed, packed],
        "svvv",
        [pltpu.VMEM((samples * grid_rows, width), bf16)],
    )
    held = call(
        hold_kernel,
        "hold",
        [jax.ShapeDtypeStruct(weight.shape, bf16) for weight in weights],
        weights,
        "hhh",
        [pltpu.SemaphoreType.DMA((3,))],
    )
    arrived = [payloads[0]] + [to_chip(payloads[turn], turn) for turn in range(1, samples)]
    (joined,) = call(
        join_kernel,
        "join",
        [jax.ShapeDtypeStruct((samples * (mesh_rows + 2 * fanout), width), bf16)],
        arrived,
        "v" * samples,
    )
    lanes = [joined] + [change_lane(joined, -steps) for steps in range(1, group)]
    half = nodes // 2
    columns, low, high = call(
        functools.partial(index_kernel, parts, mesh_rows),
        "index",
        [
            jax.ShapeDtypeStruct((nodes, 128), jnp.float32),
            jax.ShapeDtypeStruct((half, width), bf16),
            jax.ShapeDtypeStruct((half, width), bf16),
        ],
        [chip.reshape(1), (lane == 0).astype(jnp.int32).reshape(1)] + lanes,
        "ss" + "v" * group,
        [pltpu.VMEM((128, nodes), jnp.int32)],
    )
    state_shape = jax.ShapeDtypeStruct((half, width), bf16)
    for layer in range(segments):
        at_segment = min(layer, last)
        active = ((segment == at_segment) & (lane == 0)).astype(jnp.int32).reshape(1)
        used = list(held) if layer <= last else came_weights
        (sender_low,) = call(sender_kernel, "sender", [state_shape], [active, low, used[0]], "svv")
        sender, new_low = call(
            functools.partial(low_kernel, fanout),
            "low",
            [jax.ShapeDtypeStruct((nodes, width), bf16), state_shape],
            [active, columns, sender_low, low, high] + used,
            "svvvvvvv",
        )
        pairs = [(owner(m, layer), owner(m, layer + 1)) for m in range(samples)]
        if layer < last:
            low = send(new_low, pairs)
        else:
            low = new_low
        (new_high,) = call(
            functools.partial(high_kernel, fanout),
            "high",
            [state_shape],
            [active, columns, sender, high] + used,
            "svvvvvv",
        )
        if layer < last:
            high = send(new_high, pairs)
        else:
            high = new_high
        if layer == 0:
            snapshot = lax.dynamic_index_in_dim(snapshots, segment, 0, keepdims=False)
            ready, table = call(
                prepare_kernel,
                "prepare",
                [
                    jax.ShapeDtypeStruct((grid_rows, width), jnp.float32),
                    jax.ShapeDtypeStruct((mesh_rows, grid_rows), bf16),
                ],
                [snapshot, w_embed, w_decode, mesh_grid.reshape(1, grid_rows)],
                "vvvv",
                    )
            low, ready, table = lax.optimization_barrier((low, ready, table))
    share = group * mesh_rows
    blocks = []
    for turn in range(samples):
        pairs = [(owner(m, last), device(m, turn * group)) for m in range(samples)]
        kept = [source for source, target in pairs if source == target]
        pairs = [(source, target) for source, target in pairs if source != target]
        part = low if turn < samples // 2 else high
        start = turn % (samples // 2) * share
        block = part[start : start + share]
        came = send(block, pairs)
        for at in kept:
            came = jnp.where(segment * parts + place == at, block, came)
        blocks.append(came)
    block = blocks[0]
    for turn in range(1, samples):
        block = jnp.where(chip == turn, blocks[turn], block)
    handed = [block]
    for steps in range(1, group):
        handed.append(change_lane(block[steps * mesh_rows : (steps + 1) * mesh_rows], steps))
    (prediction,) = call(
        decode_kernel,
        "decode",
        [jax.ShapeDtypeStruct((channels, grid_rows), bf16)],
        [lane.reshape(1), ready, table, w_decode, w_output.T] + handed,
        "svvvv" + "v" * group,
        [pltpu.VMEM((mesh_rows, width), bf16)],
    )
    return prediction.T.reshape(1, grid_rows, channels)


def fits(mesh):
    segments, parts = mesh.shape["segment"], mesh.shape["dom"]
    return segments == 4 and parts % segments == 0 and parts <= 16


def solution(mesh):
    return jax.shard_map(
        resident if fits(mesh) else streamed,
        mesh=mesh,
        in_specs=(
            P(None, "dom", None),
            P(),
            P("segment", None, None),
            P("segment", None, None),
            P("segment", None, None),
            P(),
            P(),
            P("dom"),
            P("dom"),
            P("dom", None),
            P(None, "dom"),
            P(None, "dom"),
        ),
        out_specs=P("segment", "dom", None),
        check_vma=False,
    )
```

```python
import functools

import jax
import jax.numpy as jnp
from jax import lax
from jax.experimental import pallas as pl
from jax.experimental.pallas import tpu as pltpu
from jax.sharding import PartitionSpec as P

epsilon = 1e-05
VMEM = pl.BlockSpec(memory_space=pltpu.VMEM)
SMEM = pl.BlockSpec(memory_space=pltpu.SMEM)
HBM = pl.BlockSpec(memory_space=pltpu.HBM)


def from_behind(value, axis, steps):
    count = lax.axis_size(axis)
    pairs = [(source, (source + steps) % count) for source in range(count)]
    return lax.ppermute(value, axis, pairs)


def from_behind_2(block, axis, distance):
    devices = range(lax.axis_size(axis))
    route = [(i - distance, i) for i in devices if i - distance in devices]
    return lax.ppermute(block, axis, route)


def from_root(value, axis, source):
    kept = jnp.where(lax.axis_index(axis) == source, value, 0).astype(value.dtype)
    return lax.psum(kept, axis)


def rms_scale(values):
    return values * lax.rsqrt(jnp.mean(values * values, axis=-1, keepdims=True) + epsilon)


def streamed(
    grid_state,
    w_embed,
    w_project,
    w_message,
    w_update,
    w_decode,
    w_output,
    grid_mesh,
    mesh_grid,
    neighbors,
    send_rows,
    halo_count,
):
    segment_index = lax.axis_index("segment")
    segment_count = lax.axis_size("segment")
    final_segment = segment_count - 1
    samples, grid_rows, channels = grid_state.shape
    width = w_embed.shape[1]
    mesh_rows = neighbors.shape[0]
    fanout = neighbors.shape[1]
    halo_rows = send_rows.shape[1]
    share = samples // segment_count
    pool_table = (grid_mesh[None, :] == jnp.arange(mesh_rows, dtype=jnp.int32)[:, None]).astype(
        jnp.bfloat16
    )
    read_table = (mesh_grid[:, None] == jnp.arange(mesh_rows, dtype=jnp.int32)[None, :]).astype(
        jnp.bfloat16
    )
    valid_rows = jnp.arange(halo_rows, dtype=jnp.int32)[None, :] < halo_count[:, 0][:, None]
    source_rows = neighbors.reshape(mesh_rows * fanout)

    def embed_grid(snapshot):
        return jax.nn.silu(jnp.dot(snapshot, w_embed, preferred_element_type=jnp.float32)).astype(
            jnp.bfloat16
        )

    def encode(snapshot):
        latent = embed_grid(snapshot)
        pooled = jnp.dot(pool_table, latent, preferred_element_type=jnp.float32)
        return (rms_scale(pooled).astype(jnp.bfloat16), latent)

    def project(state, weights):
        projected = jnp.dot(state, weights[0], preferred_element_type=jnp.float32)
        return (projected[:, :width], projected[:, width:].astype(jnp.bfloat16))

    def renew(state, receiver, extended, weights):
        fetched = extended[source_rows].reshape(mesh_rows, fanout, width)
        edges = jax.nn.silu(receiver[:, None, :] + fetched.astype(jnp.float32)).astype(jnp.bfloat16)
        messages = jnp.dot(
            edges.reshape(mesh_rows * fanout, width), weights[1], preferred_element_type=jnp.float32
        )
        aggregate = (jnp.sum(messages.reshape(mesh_rows, fanout, width), axis=1) / fanout).astype(
            jnp.bfloat16
        )
        update = jax.nn.silu(
            jnp.dot(state, weights[2][:width], preferred_element_type=jnp.float32)
            + jnp.dot(aggregate, weights[2][width:], preferred_element_type=jnp.float32)
        )
        return (state.astype(jnp.float32) + rms_scale(update)).astype(jnp.bfloat16)

    def decode(state, latent):
        readout = jnp.dot(read_table, state, preferred_element_type=jnp.float32).astype(
            jnp.bfloat16
        )
        hidden = jax.nn.silu(
            jnp.dot(latent, w_decode[:width], preferred_element_type=jnp.float32)
            + jnp.dot(readout, w_decode[width:], preferred_element_type=jnp.float32)
        ).astype(jnp.bfloat16)
        return jnp.dot(hidden, w_output, preferred_element_type=jnp.float32).astype(jnp.bfloat16)

    own_weights = (w_project[0], w_message[0], w_update[0])
    empty_mesh = jnp.zeros((mesh_rows, width), jnp.bfloat16)
    empty_receiver = jnp.zeros((mesh_rows, width), jnp.float32)
    empty_grid = jnp.zeros((grid_rows, width), jnp.bfloat16)
    empty_output = jnp.zeros((grid_rows, channels), jnp.bfloat16)
    received = empty_mesh
    carried = {}
    results = [empty_output for sample in range(samples)]
    for moment in range(samples + final_segment):
        current = received
        if moment < samples:
            snapshot = grid_state[moment]
            started, latent = lax.cond(
                segment_index == 0, lambda: encode(snapshot), lambda: (empty_mesh, empty_grid)
            )
            current = jnp.where(segment_index == 0, started, received)
            carried[moment] = from_behind_2(latent, "segment", final_segment)
        active = (moment - segment_index >= 0) & (moment - segment_index < samples)
        receiver, outgoing = lax.cond(
            active, lambda: project(current, own_weights), lambda: (empty_receiver, empty_mesh)
        )
        picked = jnp.where(valid_rows[:, :, None], outgoing[send_rows], jnp.zeros((), jnp.bfloat16))
        arrived = [outgoing]
        for list_index, offset in enumerate((1, -1, 2, -2)):
            arrived.append(from_behind(picked[list_index], "dom", offset))
        extended = jnp.concatenate(arrived, axis=0)
        renewed = lax.cond(
            active, lambda: renew(current, receiver, extended, own_weights), lambda: empty_mesh
        )
        if moment >= final_segment:
            finished = moment - final_segment
            skipped = carried[finished]
            results[finished] = lax.cond(
                segment_index == final_segment,
                lambda: decode(renewed, skipped),
                lambda: empty_output,
            )
        if moment < samples + final_segment - 1:
            received = from_behind_2(renewed, "segment", 1)
    everything = from_root(jnp.stack(results), "segment", final_segment)
    return lax.dynamic_slice_in_dim(everything, segment_index * share, share, 0)


def silu_by_tanh(values):
    half = 0.5 * values
    return half + half * jnp.tanh(half)


def matmul(left, right):
    return jnp.dot(left, right, preferred_element_type=jnp.float32)


def matmul_nt(left, right):
    return lax.dot_general(left, right, (((1,), (1,)), ((), ())), preferred_element_type=jnp.float32)


def matmul_tn(left, right):
    return lax.dot_general(left, right, (((0,), (0,)), ((), ())), preferred_element_type=jnp.float32)


def fetch(sources, targets, semaphores):
    copies = [
        pltpu.make_async_copy(source, target, semaphores.at[place])
        for place, (source, target) in enumerate(zip(sources, targets))
    ]
    for copy in copies:
        copy.start()
    return copies


def encode_kernel(mesh_rows, fanout, lists, chip, snapshots, w_embed, packed, *refs):
    payloads, latent = refs[:-1], refs[-1]
    neighbors = packed[:fanout, :mesh_rows]
    grid_rows = snapshots.shape[2]
    grid_mesh = packed[fanout + lists : fanout + lists + 1, :grid_rows]
    counts = packed[fanout + lists + 1 : fanout + lists + 2, :lists]
    width = w_embed.shape[1]
    for place in range(snapshots.shape[0]):
        found = silu_by_tanh(matmul_tn(snapshots[place], w_embed[...])).astype(jnp.bfloat16)
        latent[place * grid_rows : (place + 1) * grid_rows, :] = found
    table = lax.broadcasted_iota(jnp.int32, (mesh_rows, grid_rows), 0) == grid_mesh
    table = jnp.where(table, 1.0, 0.0).astype(jnp.bfloat16)
    block = neighbors // mesh_rows
    row = neighbors - block * mesh_rows
    halo_rows = mesh_rows
    position = lax.broadcasted_iota(jnp.int32, (1, halo_rows), 1)
    rows = []
    for list_index in range(lists):
        kept = position < counts[:, list_index : list_index + 1]
        listed = packed[fanout + list_index : fanout + list_index + 1, :halo_rows]
        rows.append(jnp.where(kept, listed, mesh_rows))
    rows.append(jnp.zeros((fanout - lists, halo_rows), jnp.int32))
    filler = jnp.zeros((fanout, 128 - mesh_rows), jnp.int32)
    pieces = [block, filler, row, filler, jnp.concatenate(rows, axis=0), filler]
    coded = jnp.concatenate(pieces + [jnp.zeros((fanout, width - 384), jnp.int32)], axis=1)
    coded = jnp.concatenate([coded, jnp.zeros_like(coded)], axis=0)
    coded = coded.astype(jnp.float32).astype(jnp.bfloat16)
    for turn, payload in enumerate(payloads):
        start = pl.multiple_of(jnp.bitwise_xor(chip[0], turn) * grid_rows, grid_rows)
        pooled = matmul(table, latent[pl.ds(start, grid_rows), :])
        payload[:mesh_rows, :] = rms_scale(pooled).astype(jnp.bfloat16)
        payload[mesh_rows:, :] = coded


def join_kernel(*refs):
    payloads, joined = refs[:-1], refs[-1]
    rows = payloads[0].shape[0]
    for place, payload in enumerate(payloads):
        joined[place * rows : (place + 1) * rows, :] = payload[...]


def index_kernel(parts, mesh_rows, chip, active, *refs):
    lanes, (columns_out, low, high), index_out = refs[:-4], refs[-4:-1], refs[-1]
    nodes = columns_out.shape[0]
    group = len(lanes)
    rows = lanes[0].shape[0] // (parts // group)

    @pl.when(active[0] == 1)
    def _():
        tables = []
        for part in range(parts):
            lane, turn = lanes[part % group], jnp.bitwise_xor(chip[0], part // group)
            base = pl.multiple_of(turn * rows, 16)
            half, spot = (low, part) if part < parts // 2 else (high, part - parts // 2)
            half[spot * mesh_rows : (spot + 1) * mesh_rows, :] = lane[pl.ds(base, mesh_rows), :]
            base = pl.multiple_of(turn * rows + mesh_rows, 16)
            coded = lane[pl.ds(base, rows - mesh_rows), :384].astype(jnp.float32).astype(jnp.int32)
            tables.append(coded[: coded.shape[0] // 2])
        fanout = tables[0].shape[0]
        index_out[fanout:, :] = jnp.zeros((index_out.shape[0] - fanout, nodes), jnp.int32)
        for part in range(parts):
            block = tables[part][:, :128]
            row = tables[part][:, 128:256]
            found = part * mesh_rows + row
            for list_index, offset in enumerate((-1, 1, -2, 2)):
                source = (part + offset) % parts
                lists = tables[source][list_index : list_index + 1, 256:384]
                lists = jnp.broadcast_to(lists, (fanout, 128))
                picked = jnp.take_along_axis(lists, row, axis=1)
                picked = jnp.where(picked == mesh_rows, parts * mesh_rows, source * mesh_rows + picked)
                found = jnp.where(block == list_index + 1, picked, found)
            index_out[:fanout, part * mesh_rows : (part + 1) * mesh_rows] = found[:, :mesh_rows]
        columns_out[...] = jnp.transpose(index_out[...].astype(jnp.float32))


def hold_kernel(*refs):
    half = len(refs) // 2
    for copy in fetch(refs[:half], refs[half:-1], refs[-1]):
        copy.wait()


def renew(fanout, columns, sender, own, w_project, w_message, w_update):
    chunk, width = own.shape
    nodes = sender.shape[0]
    names = lax.broadcasted_iota(jnp.int32, (chunk, nodes), 1).astype(jnp.float32)
    receiver = matmul(own, w_project[0, :, :width])
    total = jnp.zeros((chunk, width), jnp.float32)
    for k in range(fanout):
        hit = columns[:, k : k + 1] == names
        fetched = matmul(jnp.where(hit, 1.0, 0.0).astype(jnp.bfloat16), sender)
        edge = silu_by_tanh(receiver + fetched).astype(jnp.bfloat16)
        total = total + edge.astype(jnp.float32)
    gathered = (total * (1.0 / fanout)).astype(jnp.bfloat16)
    aggregate = matmul(gathered, w_message[0]).astype(jnp.bfloat16)
    update = silu_by_tanh(
        matmul(own, w_update[0, :width, :]) + matmul(aggregate, w_update[0, width:, :])
    )
    return (own.astype(jnp.float32) + rms_scale(update)).astype(jnp.bfloat16)


def write_pieces(pieces, value):
    rows = pieces[0].shape[0]
    for place, piece in enumerate(pieces):
        piece[...] = value[place * rows : (place + 1) * rows]


def sender_kernel(active, low, w_project, sender_low):
    width = low.shape[1]

    @pl.when(active[0] == 1)
    def _():
        sender_low[...] = matmul(low[...], w_project[0, :, width:]).astype(jnp.bfloat16)


def low_kernel(fanout, active, columns, sender_low, low, high, w_project, w_message, w_update, *outs):
    sender, new_low = outs[0], outs[1:]
    half, width = low.shape

    @pl.when(active[0] == 1)
    def _():
        sender[:half, :] = sender_low[...]
        sender[half:, :] = matmul(high[...], w_project[0, :, width:]).astype(jnp.bfloat16)
        write_pieces(
            new_low,
            renew(fanout, columns[:half, :], sender[...], low[...], w_project, w_message, w_update),
        )


def high_kernel(fanout, active, columns, sender, high, w_project, w_message, w_update, *new_high):
    half = high.shape[0]

    @pl.when(active[0] == 1)
    def _():
        write_pieces(
            new_high,
            renew(fanout, columns[half:, :], sender[...], high[...], w_project, w_message, w_update),
        )


def prepare_kernel(segment, snapshots, w_embed, w_decode, mesh_grid, ready, table_out):
    snapshot = snapshots[segment[0]]
    latent = silu_by_tanh(matmul_tn(snapshot, w_embed[...])).astype(jnp.bfloat16)
    ready[...] = matmul(latent, w_decode[: latent.shape[1], :])
    mesh_rows, grid_rows = table_out.shape
    table = lax.broadcasted_iota(jnp.int32, (mesh_rows, grid_rows), 0) == mesh_grid[...]
    table_out[...] = jnp.where(table, 1.0, 0.0).astype(jnp.bfloat16)


def decode_kernel(turn, ready, table, w_decode, w_output, *refs):
    blocks, out, state = refs[:-2], refs[-2], refs[-1]
    width = ready.shape[1]
    for number, block in enumerate(blocks):

        @pl.when(turn[0] == number)
        def _():
            state[...] = block[: state.shape[0], :]

    readout = matmul_tn(table[...], state[...]).astype(jnp.bfloat16)
    hidden = silu_by_tanh(ready[...] + matmul(readout, w_decode[width:, :])).astype(jnp.bfloat16)
    out[...] = matmul_nt(w_output[...], hidden).astype(jnp.bfloat16)


def call(kernel, name, shapes, inputs, places, scratch=(), room=16, flops=0):
    kinds = {"s": SMEM, "v": VMEM, "h": HBM}
    moved = sum(value.size * value.dtype.itemsize for value in list(inputs) + list(shapes))
    return pl.pallas_call(
        kernel,
        out_shape=shapes,
        in_specs=[kinds[place] for place in places],
        out_specs=[VMEM] * len(shapes),
        scratch_shapes=list(scratch),
        name=name,
        compiler_params=pltpu.CompilerParams(vmem_limit_bytes=room * 1024 * 1024),
        cost_estimate=pl.CostEstimate(flops=flops, bytes_accessed=moved, transcendentals=0),
    )(*inputs)


def every_device(pairs, count, group):
    onward = dict(pairs)
    reached = set(onward.values())
    for first in [source for source in onward if source not in reached]:
        last = first
        while last in onward:
            last = onward[last]
        onward.update({last: last + group - 1, last + group - 1: first + group - 1, first + group - 1: first})
    alone = []
    for at in range(0, count, group):
        rest = [lane for lane in range(at, at + group) if lane not in onward]
        if len(rest) > 1:
            onward.update(zip(rest, rest[1:] + rest[:1]))
        else:
            alone += rest
    if len(alone) == 1:
        before = next(at for at in onward if at % group and onward[at] % group == 0)
        onward.update({before: alone[0], alone[0]: onward[before]})
    else:
        onward.update(zip(alone, alone[1:] + alone[:1]))
    return sorted(onward.items())


def resident(
    grid_state,
    w_embed,
    w_project,
    w_message,
    w_update,
    w_decode,
    w_output,
    grid_mesh,
    mesh_grid,
    neighbors,
    send_rows,
    halo_count,
):
    segment = lax.axis_index("segment")
    place = lax.axis_index("dom")
    segments = lax.axis_size("segment")
    parts = lax.axis_size("dom")
    samples, grid_rows, channels = grid_state.shape
    width = w_embed.shape[1]
    mesh_rows, fanout = neighbors.shape
    nodes = parts * mesh_rows
    group = parts // samples
    bf16 = jnp.bfloat16

    def device(at_segment, at_dom):
        return at_segment * parts + at_dom % parts

    def send(value, pairs):
        return lax.ppermute(value, ("segment", "dom"), every_device(pairs, segments * parts, group))

    def to_chip(value, steps):
        pairs = [(at, (at // group ^ steps) * group + at % group) for at in range(parts)]
        return lax.ppermute(value, "dom", pairs)

    def change_lane(value, steps):
        pairs = [(at, at - at % group + (at + steps) % group) for at in range(parts)]
        return lax.ppermute(value, "dom", pairs)

    def owner(m, at_segment):
        return device(at_segment, m * group)

    chip, lane = place // group, place % group
    weights = [w_project, w_message, w_update]
    last = segments - 2
    pairs = [(owner(m, last + 1), owner(m, last)) for m in range(samples)]
    came_weights = [send(weight, pairs) for weight in weights]
    snapshots = jnp.transpose(grid_state, (0, 2, 1))
    lists = send_rows.shape[0]

    def rows_of(value):
        return jnp.pad(value, ((0, 0), (0, 128 - value.shape[1])))

    packed = jnp.concatenate(
        [
            rows_of(neighbors.T),
            rows_of(send_rows),
            rows_of(grid_mesh.reshape(1, grid_rows)),
            rows_of(halo_count.reshape(1, lists)),
        ],
        axis=0,
    )
    payloads = call(
        functools.partial(encode_kernel, mesh_rows, fanout, lists),
        "encode",
        [jax.ShapeDtypeStruct((mesh_rows + 2 * fanout, width), bf16)] * samples,
        [chip.reshape(1), snapshots, w_embed, packed],
        "svvv",
        [pltpu.VMEM((samples * grid_rows, width), bf16)],
    )
    held = call(
        hold_kernel,
        "hold",
        [jax.ShapeDtypeStruct(weight.shape, bf16) for weight in weights],
        weights,
        "hhh",
        [pltpu.SemaphoreType.DMA((3,))],
    )
    own_payload, *held = lax.optimization_barrier((payloads[0], *held))
    arrived = [own_payload] + [to_chip(payloads[turn], turn) for turn in range(1, samples)]
    (joined,) = call(
        join_kernel,
        "join",
        [jax.ShapeDtypeStruct((samples * (mesh_rows + 2 * fanout), width), bf16)],
        arrived,
        "v" * samples,
    )
    lanes = [joined] + [change_lane(joined, -steps) for steps in range(1, group)]
    half = nodes // 2
    share = group * mesh_rows
    columns, low, high = call(
        functools.partial(index_kernel, parts, mesh_rows),
        "index",
        [
            jax.ShapeDtypeStruct((nodes, 128), jnp.float32),
            jax.ShapeDtypeStruct((half, width), bf16),
            jax.ShapeDtypeStruct((half, width), bf16),
        ],
        [chip.reshape(1), (lane == 0).astype(jnp.int32).reshape(1)] + lanes,
        "ss" + "v" * group,
        [pltpu.VMEM((128, nodes), jnp.int32)],
    )
    state_shape = jax.ShapeDtypeStruct((half, width), bf16)
    for layer in range(segments):
        at_segment = min(layer, last)
        active = ((segment == at_segment) & (lane == 0)).astype(jnp.int32).reshape(1)
        used = list(held) if layer <= last else came_weights
        (sender_low,) = call(sender_kernel, "sender", [state_shape], [active, low, used[0]], "svv")
        pieces = [state_shape]
        if layer > last:
            pieces = [jax.ShapeDtypeStruct((share, width), bf16)] * (half // share)
        sender, *new_low = call(
            functools.partial(low_kernel, fanout),
            "low",
            [jax.ShapeDtypeStruct((nodes, width), bf16)] + pieces,
            [active, columns, sender_low, low, high] + used,
            "svvvvvvv",
        )
        pairs = [(owner(m, layer), owner(m, layer + 1)) for m in range(samples)]
        if layer < last:
            low = send(new_low[0], pairs)
        else:
            low = new_low[0]
        new_high = call(
            functools.partial(high_kernel, fanout),
            "high",
            pieces,
            [active, columns, sender, high] + used,
            "svvvvvv",
        )
        if layer < last:
            high = send(new_high[0], pairs)
        else:
            high = new_high[0]
        if layer == 0:
            ready, table = call(
                prepare_kernel,
                "prepare",
                [
                    jax.ShapeDtypeStruct((grid_rows, width), jnp.float32),
                    jax.ShapeDtypeStruct((mesh_rows, grid_rows), bf16),
                ],
                [segment.reshape(1), snapshots, w_embed, w_decode, mesh_grid.reshape(1, grid_rows)],
                "svvvv",
                    )
            low, ready, table = lax.optimization_barrier((low, ready, table))
    blocks = []
    for turn in range(samples):
        pairs = [(owner(m, last), device(m, turn * group)) for m in range(samples)]
        kept = [source for source, target in pairs if source == target]
        pairs = [(source, target) for source, target in pairs if source != target]
        block = (list(new_low) + list(new_high))[turn]
        came = send(block, pairs)
        for at in kept:
            came = jnp.where(segment * parts + place == at, block, came)
        blocks.append(came)
    block = blocks[0]
    for turn in range(1, samples):
        block = jnp.where(chip == turn, blocks[turn], block)
    handed = [block]
    for steps in range(1, group):
        handed.append(change_lane(block[steps * mesh_rows : (steps + 1) * mesh_rows], steps))
    (prediction,) = call(
        decode_kernel,
        "decode",
        [jax.ShapeDtypeStruct((channels, grid_rows), bf16)],
        [lane.reshape(1), ready, table, w_decode, w_output.T] + handed,
        "svvvv" + "v" * group,
        [pltpu.VMEM((mesh_rows, width), bf16)],
    )
    return prediction.T.reshape(1, grid_rows, channels)


def fits(mesh):
    segments, parts = mesh.shape["segment"], mesh.shape["dom"]
    return segments == 4 and parts % segments == 0 and parts <= 16


def solution(mesh):
    return jax.shard_map(
        resident if fits(mesh) else streamed,
        mesh=mesh,
        in_specs=(
            P(None, "dom", None),
            P(),
            P("segment", None, None),
            P("segment", None, None),
            P("segment", None, None),
            P(),
            P(),
            P("dom"),
            P("dom"),
            P("dom", None),
            P(None, "dom"),
            P(None, "dom"),
        ),
        out_specs=P("segment", "dom", None),
        check_vma=False,
    )
```

```python
import functools

import jax
import jax.numpy as jnp
from jax import lax
from jax.experimental import pallas as pl
from jax.experimental.pallas import tpu as pltpu
from jax.sharding import PartitionSpec as P

epsilon = 1e-05
VMEM = pl.BlockSpec(memory_space=pltpu.VMEM)
SMEM = pl.BlockSpec(memory_space=pltpu.SMEM)
HBM = pl.BlockSpec(memory_space=pltpu.HBM)


def from_behind(value, axis, steps):
    count = lax.axis_size(axis)
    pairs = [(source, (source + steps) % count) for source in range(count)]
    return lax.ppermute(value, axis, pairs)


def from_behind_2(block, axis, distance):
    devices = range(lax.axis_size(axis))
    route = [(i - distance, i) for i in devices if i - distance in devices]
    return lax.ppermute(block, axis, route)


def from_root(value, axis, source):
    kept = jnp.where(lax.axis_index(axis) == source, value, 0).astype(value.dtype)
    return lax.psum(kept, axis)


def rms_scale(values):
    return values * lax.rsqrt(jnp.mean(values * values, axis=-1, keepdims=True) + epsilon)


def streamed(
    grid_state,
    w_embed,
    w_project,
    w_message,
    w_update,
    w_decode,
    w_output,
    grid_mesh,
    mesh_grid,
    neighbors,
    send_rows,
    halo_count,
):
    segment_index = lax.axis_index("segment")
    segment_count = lax.axis_size("segment")
    final_segment = segment_count - 1
    samples, grid_rows, channels = grid_state.shape
    width = w_embed.shape[1]
    mesh_rows = neighbors.shape[0]
    fanout = neighbors.shape[1]
    halo_rows = send_rows.shape[1]
    share = samples // segment_count
    pool_table = (grid_mesh[None, :] == jnp.arange(mesh_rows, dtype=jnp.int32)[:, None]).astype(
        jnp.bfloat16
    )
    read_table = (mesh_grid[:, None] == jnp.arange(mesh_rows, dtype=jnp.int32)[None, :]).astype(
        jnp.bfloat16
    )
    valid_rows = jnp.arange(halo_rows, dtype=jnp.int32)[None, :] < halo_count[:, 0][:, None]
    source_rows = neighbors.reshape(mesh_rows * fanout)

    def embed_grid(snapshot):
        return jax.nn.silu(jnp.dot(snapshot, w_embed, preferred_element_type=jnp.float32)).astype(
            jnp.bfloat16
        )

    def encode(snapshot):
        latent = embed_grid(snapshot)
        pooled = jnp.dot(pool_table, latent, preferred_element_type=jnp.float32)
        return (rms_scale(pooled).astype(jnp.bfloat16), latent)

    def project(state, weights):
        projected = jnp.dot(state, weights[0], preferred_element_type=jnp.float32)
        return (projected[:, :width], projected[:, width:].astype(jnp.bfloat16))

    def renew(state, receiver, extended, weights):
        fetched = extended[source_rows].reshape(mesh_rows, fanout, width)
        edges = jax.nn.silu(receiver[:, None, :] + fetched.astype(jnp.float32)).astype(jnp.bfloat16)
        messages = jnp.dot(
            edges.reshape(mesh_rows * fanout, width), weights[1], preferred_element_type=jnp.float32
        )
        aggregate = (jnp.sum(messages.reshape(mesh_rows, fanout, width), axis=1) / fanout).astype(
            jnp.bfloat16
        )
        update = jax.nn.silu(
            jnp.dot(state, weights[2][:width], preferred_element_type=jnp.float32)
            + jnp.dot(aggregate, weights[2][width:], preferred_element_type=jnp.float32)
        )
        return (state.astype(jnp.float32) + rms_scale(update)).astype(jnp.bfloat16)

    def decode(state, latent):
        readout = jnp.dot(read_table, state, preferred_element_type=jnp.float32).astype(
            jnp.bfloat16
        )
        hidden = jax.nn.silu(
            jnp.dot(latent, w_decode[:width], preferred_element_type=jnp.float32)
            + jnp.dot(readout, w_decode[width:], preferred_element_type=jnp.float32)
        ).astype(jnp.bfloat16)
        return jnp.dot(hidden, w_output, preferred_element_type=jnp.float32).astype(jnp.bfloat16)

    own_weights = (w_project[0], w_message[0], w_update[0])
    empty_mesh = jnp.zeros((mesh_rows, width), jnp.bfloat16)
    empty_receiver = jnp.zeros((mesh_rows, width), jnp.float32)
    empty_grid = jnp.zeros((grid_rows, width), jnp.bfloat16)
    empty_output = jnp.zeros((grid_rows, channels), jnp.bfloat16)
    received = empty_mesh
    carried = {}
    results = [empty_output for sample in range(samples)]
    for moment in range(samples + final_segment):
        current = received
        if moment < samples:
            snapshot = grid_state[moment]
            started, latent = lax.cond(
                segment_index == 0, lambda: encode(snapshot), lambda: (empty_mesh, empty_grid)
            )
            current = jnp.where(segment_index == 0, started, received)
            carried[moment] = from_behind_2(latent, "segment", final_segment)
        active = (moment - segment_index >= 0) & (moment - segment_index < samples)
        receiver, outgoing = lax.cond(
            active, lambda: project(current, own_weights), lambda: (empty_receiver, empty_mesh)
        )
        picked = jnp.where(valid_rows[:, :, None], outgoing[send_rows], jnp.zeros((), jnp.bfloat16))
        arrived = [outgoing]
        for list_index, offset in enumerate((1, -1, 2, -2)):
            arrived.append(from_behind(picked[list_index], "dom", offset))
        extended = jnp.concatenate(arrived, axis=0)
        renewed = lax.cond(
            active, lambda: renew(current, receiver, extended, own_weights), lambda: empty_mesh
        )
        if moment >= final_segment:
            finished = moment - final_segment
            skipped = carried[finished]
            results[finished] = lax.cond(
                segment_index == final_segment,
                lambda: decode(renewed, skipped),
                lambda: empty_output,
            )
        if moment < samples + final_segment - 1:
            received = from_behind_2(renewed, "segment", 1)
    everything = from_root(jnp.stack(results), "segment", final_segment)
    return lax.dynamic_slice_in_dim(everything, segment_index * share, share, 0)


def silu_by_tanh(values):
    half = 0.5 * values
    return half + half * jnp.tanh(half)


def matmul(left, right):
    return jnp.dot(left, right, preferred_element_type=jnp.float32)


def matmul_nt(left, right):
    return lax.dot_general(left, right, (((1,), (1,)), ((), ())), preferred_element_type=jnp.float32)


def matmul_tn(left, right):
    return lax.dot_general(left, right, (((0,), (0,)), ((), ())), preferred_element_type=jnp.float32)


def place_of(where, group):
    return lax.div(where[1], group), lax.rem(where[1], group)


def owns(where, group, at_segment):
    return jnp.logical_and(where[0] == at_segment, lax.rem(where[1], group) == 0)


def fetch(sources, targets, semaphores):
    copies = [
        pltpu.make_async_copy(source, target, semaphores.at[place])
        for place, (source, target) in enumerate(zip(sources, targets))
    ]
    for copy in copies:
        copy.start()
    return copies


def encode_kernel(group, mesh_rows, fanout, lists, where, snapshots, w_embed, packed, *refs):
    payloads, latent = refs[:-1], refs[-1]
    chip, _ = place_of(where, group)
    neighbors = packed[:fanout, :mesh_rows]
    grid_rows = snapshots.shape[2]
    grid_mesh = packed[fanout + lists : fanout + lists + 1, :grid_rows]
    counts = packed[fanout + lists + 1 : fanout + lists + 2, :lists]
    width = w_embed.shape[1]
    for place in range(snapshots.shape[0]):
        found = silu_by_tanh(matmul_tn(snapshots[place], w_embed[...])).astype(jnp.bfloat16)
        latent[place * grid_rows : (place + 1) * grid_rows, :] = found
    table = lax.broadcasted_iota(jnp.int32, (mesh_rows, grid_rows), 0) == grid_mesh
    table = jnp.where(table, 1.0, 0.0).astype(jnp.bfloat16)
    block = neighbors // mesh_rows
    row = neighbors - block * mesh_rows
    halo_rows = mesh_rows
    position = lax.broadcasted_iota(jnp.int32, (1, halo_rows), 1)
    rows = []
    for list_index in range(lists):
        kept = position < counts[:, list_index : list_index + 1]
        listed = packed[fanout + list_index : fanout + list_index + 1, :halo_rows]
        rows.append(jnp.where(kept, listed, mesh_rows))
    rows.append(jnp.zeros((fanout - lists, halo_rows), jnp.int32))
    filler = jnp.zeros((fanout, 128 - mesh_rows), jnp.int32)
    pieces = [block, filler, row, filler, jnp.concatenate(rows, axis=0), filler]
    coded = jnp.concatenate(pieces + [jnp.zeros((fanout, width - 384), jnp.int32)], axis=1)
    coded = jnp.concatenate([coded, jnp.zeros_like(coded)], axis=0)
    coded = coded.astype(jnp.float32).astype(jnp.bfloat16)
    for turn, payload in enumerate(payloads):
        start = pl.multiple_of(jnp.bitwise_xor(chip, turn) * grid_rows, grid_rows)
        pooled = matmul(table, latent[pl.ds(start, grid_rows), :])
        payload[:mesh_rows, :] = rms_scale(pooled).astype(jnp.bfloat16)
        payload[mesh_rows:, :] = coded


def join_kernel(*refs):
    payloads, joined = refs[:-1], refs[-1]
    rows = payloads[0].shape[0]
    for place, payload in enumerate(payloads):
        joined[place * rows : (place + 1) * rows, :] = payload[...]


def index_kernel(parts, mesh_rows, where, *refs):
    lanes, (columns_out, low, high), index_out = refs[:-4], refs[-4:-1], refs[-1]
    nodes = columns_out.shape[0]
    group = len(lanes)
    rows = lanes[0].shape[0] // (parts // group)
    chip, lane_place = place_of(where, group)

    @pl.when(lane_place == 0)
    def _():
        tables = []
        for part in range(parts):
            lane, turn = lanes[part % group], jnp.bitwise_xor(chip, part // group)
            base = pl.multiple_of(turn * rows, 16)
            half, spot = (low, part) if part < parts // 2 else (high, part - parts // 2)
            half[spot * mesh_rows : (spot + 1) * mesh_rows, :] = lane[pl.ds(base, mesh_rows), :]
            base = pl.multiple_of(turn * rows + mesh_rows, 16)
            coded = lane[pl.ds(base, rows - mesh_rows), :384].astype(jnp.float32).astype(jnp.int32)
            tables.append(coded[: coded.shape[0] // 2])
        fanout = tables[0].shape[0]
        index_out[fanout:, :] = jnp.zeros((index_out.shape[0] - fanout, nodes), jnp.int32)
        for part in range(parts):
            block = tables[part][:, :128]
            row = tables[part][:, 128:256]
            found = part * mesh_rows + row
            for list_index, offset in enumerate((-1, 1, -2, 2)):
                source = (part + offset) % parts
                lists = tables[source][list_index : list_index + 1, 256:384]
                lists = jnp.broadcast_to(lists, (fanout, 128))
                picked = jnp.take_along_axis(lists, row, axis=1)
                picked = jnp.where(picked == mesh_rows, parts * mesh_rows, source * mesh_rows + picked)
                found = jnp.where(block == list_index + 1, picked, found)
            index_out[:fanout, part * mesh_rows : (part + 1) * mesh_rows] = found[:, :mesh_rows]
        columns_out[...] = jnp.transpose(index_out[...].astype(jnp.float32))


def hold_kernel(*refs):
    half = len(refs) // 2
    for copy in fetch(refs[:half], refs[half:-1], refs[-1]):
        copy.wait()


def renew(fanout, columns, sender, own, w_project, w_message, w_update):
    chunk, width = own.shape
    nodes = sender.shape[0]
    names = lax.broadcasted_iota(jnp.int32, (chunk, nodes), 1).astype(jnp.float32)
    receiver = matmul(own, w_project[0, :, :width])
    total = jnp.zeros((chunk, width), jnp.float32)
    for k in range(fanout):
        hit = columns[:, k : k + 1] == names
        fetched = matmul(jnp.where(hit, 1.0, 0.0).astype(jnp.bfloat16), sender)
        edge = silu_by_tanh(receiver + fetched).astype(jnp.bfloat16)
        total = total + edge.astype(jnp.float32)
    gathered = (total * (1.0 / fanout)).astype(jnp.bfloat16)
    aggregate = matmul(gathered, w_message[0]).astype(jnp.bfloat16)
    update = silu_by_tanh(
        matmul(own, w_update[0, :width, :]) + matmul(aggregate, w_update[0, width:, :])
    )
    return (own.astype(jnp.float32) + rms_scale(update)).astype(jnp.bfloat16)


def write_pieces(pieces, value):
    rows = pieces[0].shape[0]
    for place, piece in enumerate(pieces):
        piece[...] = value[place * rows : (place + 1) * rows]


def sender_kernel(group, at_segment, where, low, w_project, sender_low):
    width = low.shape[1]

    @pl.when(owns(where, group, at_segment))
    def _():
        sender_low[...] = matmul(low[...], w_project[0, :, width:]).astype(jnp.bfloat16)


def half_of(where, group, chips, far, low, high, own):
    half = low.shape[0]
    chip, _ = place_of(where, group)
    upper = (chip < chips // 2) if far else (chip >= chips // 2)

    @pl.when(upper)
    def _():
        own[...] = high[...]

    @pl.when(jnp.logical_not(upper))
    def _():
        own[...] = low[...]

    return pl.multiple_of(jnp.where(upper, half, 0), half)


def first_kernel(
    group, at_segment, chips, fanout, where, columns, sender_low, low, high, w_project, w_message, w_update, *outs
):
    sender, pieces, own = outs[0], outs[1:-1], outs[-1]
    half, width = low.shape

    @pl.when(owns(where, group, at_segment))
    def _():
        sender[:half, :] = sender_low[...]
        sender[half:, :] = matmul(high[...], w_project[0, :, width:]).astype(jnp.bfloat16)
        start, state = 0, low
        if chips:
            start, state = half_of(where, group, chips, True, low, high, own), own
        rows = columns[pl.ds(start, half), :]
        write_pieces(pieces, renew(fanout, rows, sender[...], state[...], w_project, w_message, w_update))


def second_kernel(
    group, at_segment, chips, fanout, where, columns, sender, low, high, w_project, w_message, w_update, *outs
):
    pieces, own = outs[:-1], outs[-1]
    half = low.shape[0]

    @pl.when(owns(where, group, at_segment))
    def _():
        start, state = half, high
        if chips:
            start, state = half_of(where, group, chips, False, low, high, own), own
        rows = columns[pl.ds(start, half), :]
        write_pieces(pieces, renew(fanout, rows, sender[...], state[...], w_project, w_message, w_update))


def arrival(where, group, chips, last):
    each = chips // 2
    segment = where[0]
    chip, _ = place_of(where, group)
    crosses = lax.div(chip, each) != lax.div(segment, each)
    return crosses, jnp.logical_and(segment == last, chip == last), lax.rem(chip, each)


def far_kernel(group, chips, last, where, *refs):
    far, out = refs[:-1], refs[-1]
    crosses, _, spot = arrival(where, group, chips, last)
    for number, block in enumerate(far):

        @pl.when(jnp.logical_and(crosses, spot == number))
        def _(block=block):
            out[...] = block[...]


def near_kernel(group, chips, last, where, crossed, *refs):
    each = chips // 2
    near, kept, outs = refs[:each], refs[each : 2 * each], refs[2 * each :]
    rows = outs[0].shape[0]
    crosses, stays, spot = arrival(where, group, chips, last)
    arrives = jnp.logical_not(jnp.logical_or(crosses, stays))

    def give(block):
        for place, out in enumerate(outs):
            out[...] = block[place * rows : (place + 1) * rows, :]

    @pl.when(crosses)
    def _():
        give(crossed)

    for number in range(each):
        for blocks, chosen in ((near, arrives), (kept, stays)):

            @pl.when(jnp.logical_and(chosen, spot == number))
            def _(block=blocks[number]):
                give(block)


def prepare_kernel(where, snapshots, w_embed, w_decode, mesh_grid, ready, table_out):
    snapshot = snapshots[where[0]]
    latent = silu_by_tanh(matmul_tn(snapshot, w_embed[...])).astype(jnp.bfloat16)
    ready[...] = matmul(latent, w_decode[: latent.shape[1], :])
    mesh_rows, grid_rows = table_out.shape
    table = lax.broadcasted_iota(jnp.int32, (mesh_rows, grid_rows), 0) == mesh_grid[...]
    table_out[...] = jnp.where(table, 1.0, 0.0).astype(jnp.bfloat16)


def decode_kernel(where, ready, table, w_decode, w_output, *refs):
    blocks, out, state = refs[:-2], refs[-2], refs[-1]
    width = ready.shape[1]
    _, lane = place_of(where, len(blocks))
    for number, block in enumerate(blocks):

        @pl.when(lane == number)
        def _(block=block):
            state[...] = block[...]

    readout = matmul_tn(table[...], state[...]).astype(jnp.bfloat16)
    hidden = silu_by_tanh(ready[...] + matmul(readout, w_decode[width:, :])).astype(jnp.bfloat16)
    out[...] = matmul_nt(w_output[...], hidden).astype(jnp.bfloat16)


def call(kernel, name, shapes, inputs, places, scratch=(), room=16, flops=0):
    kinds = {"s": SMEM, "v": VMEM, "h": HBM}
    moved = sum(value.size * value.dtype.itemsize for value in list(inputs) + list(shapes))
    return pl.pallas_call(
        kernel,
        out_shape=shapes,
        in_specs=[kinds[place] for place in places],
        out_specs=[VMEM] * len(shapes),
        scratch_shapes=list(scratch),
        name=name,
        compiler_params=pltpu.CompilerParams(vmem_limit_bytes=room * 1024 * 1024),
        cost_estimate=pl.CostEstimate(flops=flops, bytes_accessed=moved, transcendentals=0),
    )(*inputs)


def every_device(pairs, count, group):
    onward = dict(pairs)
    reached = set(onward.values())
    for first in [source for source in onward if source not in reached]:
        last = first
        while last in onward:
            last = onward[last]
        onward.update({last: last + group - 1, last + group - 1: first + group - 1, first + group - 1: first})
    alone = []
    for at in range(0, count, group):
        rest = [lane for lane in range(at, at + group) if lane not in onward]
        if len(rest) > 1:
            onward.update(zip(rest, rest[1:] + rest[:1]))
        else:
            alone += rest
    if len(alone) == 1:
        before = next(at for at in onward if at % group and onward[at] % group == 0)
        onward.update({before: alone[0], alone[0]: onward[before]})
    else:
        onward.update(zip(alone, alone[1:] + alone[:1]))
    return sorted(onward.items())


def resident(
    grid_state,
    w_embed,
    w_project,
    w_message,
    w_update,
    w_decode,
    w_output,
    grid_mesh,
    mesh_grid,
    neighbors,
    send_rows,
    halo_count,
):
    segment = lax.axis_index("segment")
    place = lax.axis_index("dom")
    segments = lax.axis_size("segment")
    parts = lax.axis_size("dom")
    samples, grid_rows, channels = grid_state.shape
    width = w_embed.shape[1]
    mesh_rows, fanout = neighbors.shape
    nodes = parts * mesh_rows
    group = parts // samples
    bf16 = jnp.bfloat16

    def device(at_segment, at_dom):
        return at_segment * parts + at_dom % parts

    def send(value, pairs):
        return lax.ppermute(value, ("segment", "dom"), every_device(pairs, segments * parts, group))

    def to_chip(value, steps):
        pairs = [(at, (at // group ^ steps) * group + at % group) for at in range(parts)]
        return lax.ppermute(value, "dom", pairs)

    def change_lane(value, steps):
        pairs = [(at, at - at % group + (at + steps) % group) for at in range(parts)]
        return lax.ppermute(value, "dom", pairs)

    def owner(m, at_segment):
        return device(at_segment, m * group)

    where, *weights = lax.optimization_barrier(
        (jnp.stack([segment, place]).astype(jnp.int32), w_project, w_message, w_update)
    )
    last = segments - 2
    pairs = [(owner(m, last + 1), owner(m, last)) for m in range(samples)]
    came_weights = [send(weight, pairs) for weight in weights]
    snapshots = jnp.transpose(grid_state, (0, 2, 1))
    lists = send_rows.shape[0]

    def rows_of(value):
        return jnp.pad(value, ((0, 0), (0, 128 - value.shape[1])))

    packed = jnp.concatenate(
        [
            rows_of(neighbors.T),
            rows_of(send_rows),
            rows_of(grid_mesh.reshape(1, grid_rows)),
            rows_of(halo_count.reshape(1, lists)),
        ],
        axis=0,
    )
    payloads = call(
        functools.partial(encode_kernel, group, mesh_rows, fanout, lists),
        "encode",
        [jax.ShapeDtypeStruct((mesh_rows + 2 * fanout, width), bf16)] * samples,
        [where, snapshots, w_embed, packed],
        "svvv",
        [pltpu.VMEM((samples * grid_rows, width), bf16)],
    )
    held = call(
        hold_kernel,
        "hold",
        [jax.ShapeDtypeStruct(weight.shape, bf16) for weight in weights],
        weights,
        "hhh",
        [pltpu.SemaphoreType.DMA((3,))],
    )
    own_payload, *held = lax.optimization_barrier((payloads[0], *held))
    arrived = [own_payload] + [to_chip(payloads[turn], turn) for turn in range(1, samples)]
    (joined,) = call(
        join_kernel,
        "join",
        [jax.ShapeDtypeStruct((samples * (mesh_rows + 2 * fanout), width), bf16)],
        arrived,
        "v" * samples,
    )
    lanes = [joined] + [change_lane(joined, -steps) for steps in range(1, group)]
    half = nodes // 2
    share = group * mesh_rows
    columns, low, high = call(
        functools.partial(index_kernel, parts, mesh_rows),
        "index",
        [
            jax.ShapeDtypeStruct((nodes, 128), jnp.float32),
            jax.ShapeDtypeStruct((half, width), bf16),
            jax.ShapeDtypeStruct((half, width), bf16),
        ],
        [where] + lanes,
        "s" + "v" * group,
        [pltpu.VMEM((128, nodes), jnp.int32)],
    )
    state_shape = jax.ShapeDtypeStruct((half, width), bf16)
    for layer in range(segments):
        at_segment, ends = min(layer, last), layer > last
        used = list(held) if layer <= last else came_weights
        role = (group, at_segment, samples if ends else 0, fanout)
        pieces = [jax.ShapeDtypeStruct((share, width), bf16)] * (half // share) if ends else [state_shape]
        scratch = [pltpu.VMEM((half, width), bf16)]
        (sender_low,) = call(
            functools.partial(sender_kernel, group, at_segment),
            "sender",
            [state_shape],
            [where, low, used[0]],
            "svv",
        )
        sender, *first = call(
            functools.partial(first_kernel, *role),
            "first",
            [jax.ShapeDtypeStruct((nodes, width), bf16)] + pieces,
            [where, columns, sender_low, low, high] + used,
            "svvvvvvv",
            scratch,
        )
        pairs = [(owner(m, layer), owner(m, layer + 1)) for m in range(samples)]
        new_low = send(first[0], pairs) if layer < last else first[0]
        second = call(
            functools.partial(second_kernel, *role),
            "second",
            pieces,
            [where, columns, sender, low, high] + used,
            "svvvvvvv",
            scratch,
        )
        low, high = new_low, send(second[0], pairs) if layer < last else second[0]
        if layer == 0:
            ready, table = call(
                prepare_kernel,
                "prepare",
                [
                    jax.ShapeDtypeStruct((grid_rows, width), jnp.float32),
                    jax.ShapeDtypeStruct((mesh_rows, grid_rows), bf16),
                ],
                [where, snapshots, w_embed, w_decode, mesh_grid.reshape(1, grid_rows)],
                "svvvv",
                    )
            low, ready, table = lax.optimization_barrier((low, ready, table))
    each = samples // 2
    arrived = []
    for far, blocks in ((1, first), (0, second)):
        for turn, block in enumerate(blocks):
            pairs = [
                (owner(m, last), device(m, ((m // each ^ far) * each + turn) * group)) for m in range(samples)
            ]
            arrived.append(send(block, [pair for pair in pairs if pair[0] != pair[1]]))
    (crossed,) = call(
        functools.partial(far_kernel, group, samples, last),
        "far",
        [jax.ShapeDtypeStruct((share, width), bf16)],
        [where] + arrived[:each],
        "s" + "v" * each,
    )
    parts_of_block = call(
        functools.partial(near_kernel, group, samples, last),
        "near",
        [jax.ShapeDtypeStruct((mesh_rows, width), bf16)] * group,
        [where, crossed] + arrived[each:] + list(second),
        "s" + "v" * (1 + 2 * each),
    )
    handed = [parts_of_block[0]]
    for steps in range(1, group):
        handed.append(change_lane(parts_of_block[steps], steps))
    (prediction,) = call(
        decode_kernel,
        "decode",
        [jax.ShapeDtypeStruct((channels, grid_rows), bf16)],
        [where, ready, table, w_decode, w_output.T] + handed,
        "svvvv" + "v" * group,
        [pltpu.VMEM((mesh_rows, width), bf16)],
    )
    return prediction.T.reshape(1, grid_rows, channels)


def fits(mesh):
    segments, parts = mesh.shape["segment"], mesh.shape["dom"]
    return segments == 4 and parts % segments == 0 and parts <= 16


def solution(mesh):
    return jax.shard_map(
        resident if fits(mesh) else streamed,
        mesh=mesh,
        in_specs=(
            P(None, "dom", None),
            P(),
            P("segment", None, None),
            P("segment", None, None),
            P("segment", None, None),
            P(),
            P(),
            P("dom"),
            P("dom"),
            P("dom", None),
            P(None, "dom"),
            P(None, "dom"),
        ),
        out_specs=P("segment", "dom", None),
        check_vma=False,
    )
```

```python
import functools

import jax
import jax.numpy as jnp
from jax import lax
from jax.experimental import pallas as pl
from jax.experimental.pallas import tpu as pltpu
from jax.sharding import PartitionSpec as P

epsilon = 1e-05
VMEM = pl.BlockSpec(memory_space=pltpu.VMEM)
SMEM = pl.BlockSpec(memory_space=pltpu.SMEM)
HBM = pl.BlockSpec(memory_space=pltpu.HBM)


def from_behind(value, axis, steps):
    count = lax.axis_size(axis)
    pairs = [(source, (source + steps) % count) for source in range(count)]
    return lax.ppermute(value, axis, pairs)


def from_behind_2(block, axis, distance):
    devices = range(lax.axis_size(axis))
    route = [(i - distance, i) for i in devices if i - distance in devices]
    return lax.ppermute(block, axis, route)


def from_root(value, axis, source):
    kept = jnp.where(lax.axis_index(axis) == source, value, 0).astype(value.dtype)
    return lax.psum(kept, axis)


def rms_scale(values):
    return values * lax.rsqrt(jnp.mean(values * values, axis=-1, keepdims=True) + epsilon)


def streamed(
    grid_state,
    w_embed,
    w_project,
    w_message,
    w_update,
    w_decode,
    w_output,
    grid_mesh,
    mesh_grid,
    neighbors,
    send_rows,
    halo_count,
):
    segment_index = lax.axis_index("segment")
    segment_count = lax.axis_size("segment")
    final_segment = segment_count - 1
    samples, grid_rows, channels = grid_state.shape
    width = w_embed.shape[1]
    mesh_rows = neighbors.shape[0]
    fanout = neighbors.shape[1]
    halo_rows = send_rows.shape[1]
    share = samples // segment_count
    pool_table = (grid_mesh[None, :] == jnp.arange(mesh_rows, dtype=jnp.int32)[:, None]).astype(
        jnp.bfloat16
    )
    read_table = (mesh_grid[:, None] == jnp.arange(mesh_rows, dtype=jnp.int32)[None, :]).astype(
        jnp.bfloat16
    )
    valid_rows = jnp.arange(halo_rows, dtype=jnp.int32)[None, :] < halo_count[:, 0][:, None]
    source_rows = neighbors.reshape(mesh_rows * fanout)

    def embed_grid(snapshot):
        return jax.nn.silu(jnp.dot(snapshot, w_embed, preferred_element_type=jnp.float32)).astype(
            jnp.bfloat16
        )

    def encode(snapshot):
        latent = embed_grid(snapshot)
        pooled = jnp.dot(pool_table, latent, preferred_element_type=jnp.float32)
        return (rms_scale(pooled).astype(jnp.bfloat16), latent)

    def project(state, weights):
        projected = jnp.dot(state, weights[0], preferred_element_type=jnp.float32)
        return (projected[:, :width], projected[:, width:].astype(jnp.bfloat16))

    def renew(state, receiver, extended, weights):
        fetched = extended[source_rows].reshape(mesh_rows, fanout, width)
        edges = jax.nn.silu(receiver[:, None, :] + fetched.astype(jnp.float32)).astype(jnp.bfloat16)
        messages = jnp.dot(
            edges.reshape(mesh_rows * fanout, width), weights[1], preferred_element_type=jnp.float32
        )
        aggregate = (jnp.sum(messages.reshape(mesh_rows, fanout, width), axis=1) / fanout).astype(
            jnp.bfloat16
        )
        update = jax.nn.silu(
            jnp.dot(state, weights[2][:width], preferred_element_type=jnp.float32)
            + jnp.dot(aggregate, weights[2][width:], preferred_element_type=jnp.float32)
        )
        return (state.astype(jnp.float32) + rms_scale(update)).astype(jnp.bfloat16)

    def decode(state, latent):
        readout = jnp.dot(read_table, state, preferred_element_type=jnp.float32).astype(
            jnp.bfloat16
        )
        hidden = jax.nn.silu(
            jnp.dot(latent, w_decode[:width], preferred_element_type=jnp.float32)
            + jnp.dot(readout, w_decode[width:], preferred_element_type=jnp.float32)
        ).astype(jnp.bfloat16)
        return jnp.dot(hidden, w_output, preferred_element_type=jnp.float32).astype(jnp.bfloat16)

    own_weights = (w_project[0], w_message[0], w_update[0])
    empty_mesh = jnp.zeros((mesh_rows, width), jnp.bfloat16)
    empty_receiver = jnp.zeros((mesh_rows, width), jnp.float32)
    empty_grid = jnp.zeros((grid_rows, width), jnp.bfloat16)
    empty_output = jnp.zeros((grid_rows, channels), jnp.bfloat16)
    received = empty_mesh
    carried = {}
    results = [empty_output for sample in range(samples)]
    for moment in range(samples + final_segment):
        current = received
        if moment < samples:
            snapshot = grid_state[moment]
            started, latent = lax.cond(
                segment_index == 0, lambda: encode(snapshot), lambda: (empty_mesh, empty_grid)
            )
            current = jnp.where(segment_index == 0, started, received)
            carried[moment] = from_behind_2(latent, "segment", final_segment)
        active = (moment - segment_index >= 0) & (moment - segment_index < samples)
        receiver, outgoing = lax.cond(
            active, lambda: project(current, own_weights), lambda: (empty_receiver, empty_mesh)
        )
        picked = jnp.where(valid_rows[:, :, None], outgoing[send_rows], jnp.zeros((), jnp.bfloat16))
        arrived = [outgoing]
        for list_index, offset in enumerate((1, -1, 2, -2)):
            arrived.append(from_behind(picked[list_index], "dom", offset))
        extended = jnp.concatenate(arrived, axis=0)
        renewed = lax.cond(
            active, lambda: renew(current, receiver, extended, own_weights), lambda: empty_mesh
        )
        if moment >= final_segment:
            finished = moment - final_segment
            skipped = carried[finished]
            results[finished] = lax.cond(
                segment_index == final_segment,
                lambda: decode(renewed, skipped),
                lambda: empty_output,
            )
        if moment < samples + final_segment - 1:
            received = from_behind_2(renewed, "segment", 1)
    everything = from_root(jnp.stack(results), "segment", final_segment)
    return lax.dynamic_slice_in_dim(everything, segment_index * share, share, 0)


def silu_by_tanh(values):
    half = 0.5 * values
    return half + half * jnp.tanh(half)


def matmul(left, right):
    return jnp.dot(left, right, preferred_element_type=jnp.float32)


def matmul_nt(left, right):
    return lax.dot_general(left, right, (((1,), (1,)), ((), ())), preferred_element_type=jnp.float32)


def matmul_tn(left, right):
    return lax.dot_general(left, right, (((0,), (0,)), ((), ())), preferred_element_type=jnp.float32)


def place_of(where, group):
    return lax.div(where[1], group), lax.rem(where[1], group)


def owns(where, group, at_segment):
    return jnp.logical_and(where[0] == at_segment, lax.rem(where[1], group) == 0)


def fetch(sources, targets, semaphores):
    copies = [
        pltpu.make_async_copy(source, target, semaphores.at[place])
        for place, (source, target) in enumerate(zip(sources, targets))
    ]
    for copy in copies:
        copy.start()
    return copies


def encode_kernel(group, mesh_rows, fanout, lists, where, snapshots, w_embed, packed, *refs):
    payloads, latent = refs[:-1], refs[-1]
    chip, _ = place_of(where, group)
    neighbors = packed[:fanout, :mesh_rows]
    grid_rows = snapshots.shape[2]
    grid_mesh = packed[fanout + lists : fanout + lists + 1, :grid_rows]
    counts = packed[fanout + lists + 1 : fanout + lists + 2, :lists]
    width = w_embed.shape[1]
    for place in range(snapshots.shape[0]):
        found = silu_by_tanh(matmul_tn(snapshots[place], w_embed[...])).astype(jnp.bfloat16)
        latent[place * grid_rows : (place + 1) * grid_rows, :] = found
    table = lax.broadcasted_iota(jnp.int32, (mesh_rows, grid_rows), 0) == grid_mesh
    table = jnp.where(table, 1.0, 0.0).astype(jnp.bfloat16)
    block = neighbors // mesh_rows
    row = neighbors - block * mesh_rows
    halo_rows = mesh_rows
    position = lax.broadcasted_iota(jnp.int32, (1, halo_rows), 1)
    rows = []
    for list_index in range(lists):
        kept = position < counts[:, list_index : list_index + 1]
        listed = packed[fanout + list_index : fanout + list_index + 1, :halo_rows]
        rows.append(jnp.where(kept, listed, mesh_rows))
    rows.append(jnp.zeros((fanout - lists, halo_rows), jnp.int32))
    filler = jnp.zeros((fanout, 128 - mesh_rows), jnp.int32)
    pieces = [block, filler, row, filler, jnp.concatenate(rows, axis=0), filler]
    coded = jnp.concatenate(pieces + [jnp.zeros((fanout, width - 384), jnp.int32)], axis=1)
    coded = jnp.concatenate([coded, jnp.zeros_like(coded)], axis=0)
    coded = coded.astype(jnp.float32).astype(jnp.bfloat16)
    for turn, payload in enumerate(payloads):
        start = pl.multiple_of(jnp.bitwise_xor(chip, turn) * grid_rows, grid_rows)
        pooled = matmul(table, latent[pl.ds(start, grid_rows), :])
        payload[:mesh_rows, :] = rms_scale(pooled).astype(jnp.bfloat16)
        payload[mesh_rows:, :] = coded


def join_kernel(*refs):
    payloads, joined = refs[:-1], refs[-1]
    rows = payloads[0].shape[0]
    for place, payload in enumerate(payloads):
        joined[place * rows : (place + 1) * rows, :] = payload[...]


def index_kernel(parts, mesh_rows, where, *refs):
    lanes, (columns_out, low, high), index_out = refs[:-4], refs[-4:-1], refs[-1]
    nodes = columns_out.shape[0]
    group = len(lanes)
    rows = lanes[0].shape[0] // (parts // group)
    chip, lane_place = place_of(where, group)

    @pl.when(lane_place == 0)
    def _():
        tables = []
        for part in range(parts):
            lane, turn = lanes[part % group], jnp.bitwise_xor(chip, part // group)
            base = pl.multiple_of(turn * rows, 16)
            half, spot = (low, part) if part < parts // 2 else (high, part - parts // 2)
            half[spot * mesh_rows : (spot + 1) * mesh_rows, :] = lane[pl.ds(base, mesh_rows), :]
            base = pl.multiple_of(turn * rows + mesh_rows, 16)
            coded = lane[pl.ds(base, rows - mesh_rows), :384].astype(jnp.float32).astype(jnp.int32)
            tables.append(coded[: coded.shape[0] // 2])
        fanout = tables[0].shape[0]
        index_out[fanout:, :] = jnp.zeros((index_out.shape[0] - fanout, nodes), jnp.int32)
        for part in range(parts):
            block = tables[part][:, :128]
            row = tables[part][:, 128:256]
            found = part * mesh_rows + row
            for list_index, offset in enumerate((-1, 1, -2, 2)):
                source = (part + offset) % parts
                lists = tables[source][list_index : list_index + 1, 256:384]
                lists = jnp.broadcast_to(lists, (fanout, 128))
                picked = jnp.take_along_axis(lists, row, axis=1)
                picked = jnp.where(picked == mesh_rows, parts * mesh_rows, source * mesh_rows + picked)
                found = jnp.where(block == list_index + 1, picked, found)
            index_out[:fanout, part * mesh_rows : (part + 1) * mesh_rows] = found[:, :mesh_rows]
        tile = min(nodes, 256)
        for number in range(1, nodes // tile):
            index_out[number * fanout : (number + 1) * fanout, :] = index_out[:fanout, :] - number * tile
        columns_out[...] = jnp.transpose(index_out[...].astype(jnp.float32)).astype(jnp.bfloat16)


def hold_kernel(*refs):
    half = len(refs) // 2
    for copy in fetch(refs[:half], refs[half:-1], refs[-1]):
        copy.wait()


def renew(fanout, columns, sender, own, w_project, w_message, w_update):
    chunk, width = own.shape
    nodes = sender.shape[0]
    tile = min(nodes, 256)
    names = lax.broadcasted_iota(jnp.int32, (chunk, tile), 1).astype(jnp.float32).astype(jnp.bfloat16)
    one_half = jnp.full((chunk, tile), 0.5, jnp.bfloat16)
    none = jnp.zeros((chunk, tile), jnp.bfloat16)
    receiver = 0.5 * matmul(own, w_project[0, :, :width])
    total = jnp.zeros((chunk, width), jnp.float32)
    for k in range(fanout):
        hits = []
        for number in range(nodes // tile):
            lane = number * fanout + k
            hits.append(jnp.where(columns[:, lane : lane + 1] == names, one_half, none))
        half = receiver + matmul(jnp.concatenate(hits, axis=1), sender)
        total = total + (half + half * jnp.tanh(half))
    gathered = (total * (1.0 / fanout)).astype(jnp.bfloat16)
    aggregate = matmul(gathered, w_message[0]).astype(jnp.bfloat16)
    update = silu_by_tanh(
        matmul(own, w_update[0, :width, :]) + matmul(aggregate, w_update[0, width:, :])
    )
    return (own.astype(jnp.float32) + rms_scale(update)).astype(jnp.bfloat16)


def write_pieces(pieces, value):
    rows = pieces[0].shape[0]
    for place, piece in enumerate(pieces):
        piece[...] = value[place * rows : (place + 1) * rows]


def sender_kernel(group, at_segment, where, low, w_project, sender_low):
    width = low.shape[1]

    @pl.when(owns(where, group, at_segment))
    def _():
        sender_low[...] = matmul(low[...], w_project[0, :, width:]).astype(jnp.bfloat16)


def half_of(where, group, chips, far, low, high, own):
    half = low.shape[0]
    chip, _ = place_of(where, group)
    upper = (chip < chips // 2) if far else (chip >= chips // 2)

    @pl.when(upper)
    def _():
        own[...] = high[...]

    @pl.when(jnp.logical_not(upper))
    def _():
        own[...] = low[...]

    return pl.multiple_of(jnp.where(upper, half, 0), half)


def first_kernel(
    group, at_segment, chips, fanout, where, columns, sender_low, low, high, w_project, w_message, w_update, *outs
):
    sender, pieces, own = outs[0], outs[1:-1], outs[-1]
    half, width = low.shape

    @pl.when(owns(where, group, at_segment))
    def _():
        sender[:half, :] = sender_low[...]
        sender[half:, :] = matmul(high[...], w_project[0, :, width:]).astype(jnp.bfloat16)
        start, state = 0, low
        if chips:
            start, state = half_of(where, group, chips, True, low, high, own), own
        rows = columns[pl.ds(start, half), :]
        write_pieces(pieces, renew(fanout, rows, sender[...], state[...], w_project, w_message, w_update))


def second_kernel(
    group, at_segment, chips, fanout, where, columns, sender, low, high, w_project, w_message, w_update, *outs
):
    pieces, own = outs[:-1], outs[-1]
    half = low.shape[0]

    @pl.when(owns(where, group, at_segment))
    def _():
        start, state = half, high
        if chips:
            start, state = half_of(where, group, chips, False, low, high, own), own
        rows = columns[pl.ds(start, half), :]
        write_pieces(pieces, renew(fanout, rows, sender[...], state[...], w_project, w_message, w_update))


def arrival(where, group, chips, last):
    each = chips // 2
    segment = where[0]
    chip, _ = place_of(where, group)
    crosses = lax.div(chip, each) != lax.div(segment, each)
    return crosses, jnp.logical_and(segment == last, chip == last), lax.rem(chip, each)


def far_kernel(group, chips, last, where, *refs):
    far, out = refs[:-1], refs[-1]
    crosses, _, spot = arrival(where, group, chips, last)
    for number, block in enumerate(far):

        @pl.when(jnp.logical_and(crosses, spot == number))
        def _(block=block):
            out[...] = block[...]


def near_kernel(group, chips, last, where, crossed, *refs):
    each = chips // 2
    near, kept, outs = refs[:each], refs[each : 2 * each], refs[2 * each :]
    rows = outs[0].shape[0]
    crosses, stays, spot = arrival(where, group, chips, last)
    arrives = jnp.logical_not(jnp.logical_or(crosses, stays))

    def give(block):
        for place, out in enumerate(outs):
            out[...] = block[place * rows : (place + 1) * rows, :]

    @pl.when(crosses)
    def _():
        give(crossed)

    for number in range(each):
        for blocks, chosen in ((near, arrives), (kept, stays)):

            @pl.when(jnp.logical_and(chosen, spot == number))
            def _(block=blocks[number]):
                give(block)


def prepare_kernel(where, snapshots, w_embed, w_decode, mesh_grid, ready, table_out):
    snapshot = snapshots[where[0]]
    latent = silu_by_tanh(matmul_tn(snapshot, w_embed[...])).astype(jnp.bfloat16)
    ready[...] = matmul(latent, w_decode[: latent.shape[1], :])
    mesh_rows, grid_rows = table_out.shape
    table = lax.broadcasted_iota(jnp.int32, (mesh_rows, grid_rows), 0) == mesh_grid[...]
    table_out[...] = jnp.where(table, 1.0, 0.0).astype(jnp.bfloat16)


def decode_kernel(where, ready, table, w_decode, w_output, *refs):
    blocks, out, state = refs[:-2], refs[-2], refs[-1]
    width = ready.shape[1]
    _, lane = place_of(where, len(blocks))
    for number, block in enumerate(blocks):

        @pl.when(lane == number)
        def _(block=block):
            state[...] = block[...]

    readout = matmul_tn(table[...], state[...]).astype(jnp.bfloat16)
    hidden = silu_by_tanh(ready[...] + matmul(readout, w_decode[width:, :])).astype(jnp.bfloat16)
    out[...] = matmul_nt(w_output[...], hidden).astype(jnp.bfloat16)


def call(kernel, name, shapes, inputs, places, scratch=(), room=16):
    specs, given = [], []
    for value, place in zip(inputs, places):
        specs += [SMEM] * 2 if place == "w" else [VMEM if place == "v" else HBM]
        given += list(value) if place == "w" else [value]
    moved = sum(value.size * value.dtype.itemsize for value in given + list(shapes))

    def located(segment, place, *refs):
        kernel((segment[0], place[0]), *refs)

    return pl.pallas_call(
        located if places[0] == "w" else kernel,
        out_shape=shapes,
        in_specs=specs,
        out_specs=[VMEM] * len(shapes),
        scratch_shapes=list(scratch),
        name=name,
        compiler_params=pltpu.CompilerParams(vmem_limit_bytes=room * 1024 * 1024),
        cost_estimate=pl.CostEstimate(flops=0, bytes_accessed=moved, transcendentals=0),
    )(*given)


def every_device(pairs, count, group):
    onward = dict(pairs)
    reached = set(onward.values())
    for first in [source for source in onward if source not in reached]:
        last = first
        while last in onward:
            last = onward[last]
        onward.update({last: last + group - 1, last + group - 1: first + group - 1, first + group - 1: first})
    alone = []
    for at in range(0, count, group):
        rest = [lane for lane in range(at, at + group) if lane not in onward]
        if len(rest) > 1:
            onward.update(zip(rest, rest[1:] + rest[:1]))
        else:
            alone += rest
    if len(alone) == 1:
        before = next(at for at in onward if at % group and onward[at] % group == 0)
        onward.update({before: alone[0], alone[0]: onward[before]})
    else:
        onward.update(zip(alone, alone[1:] + alone[:1]))
    return sorted(onward.items())


def resident(
    grid_state,
    w_embed,
    w_project,
    w_message,
    w_update,
    w_decode,
    w_output,
    grid_mesh,
    mesh_grid,
    neighbors,
    send_rows,
    halo_count,
):
    segment = lax.axis_index("segment")
    place = lax.axis_index("dom")
    segments = lax.axis_size("segment")
    parts = lax.axis_size("dom")
    samples, grid_rows, channels = grid_state.shape
    width = w_embed.shape[1]
    mesh_rows, fanout = neighbors.shape
    nodes = parts * mesh_rows
    group = parts // samples
    bf16 = jnp.bfloat16

    def device(at_segment, at_dom):
        return at_segment * parts + at_dom % parts

    def send(value, pairs):
        return lax.ppermute(value, ("segment", "dom"), every_device(pairs, segments * parts, group))

    def to_chip(value, steps):
        pairs = [(at, (at // group ^ steps) * group + at % group) for at in range(parts)]
        return lax.ppermute(value, "dom", pairs)

    def change_lane(value, steps):
        pairs = [(at, at - at % group + (at + steps) % group) for at in range(parts)]
        return lax.ppermute(value, "dom", pairs)

    def owner(m, at_segment):
        return device(at_segment, m * group)

    own_segment, own_place, *weights = lax.optimization_barrier(
        (segment.reshape(1), place.reshape(1), w_project, w_message, w_update)
    )
    where = (own_segment, own_place)
    last = segments - 2
    pairs = [(owner(m, last + 1), owner(m, last)) for m in range(samples)]
    came_weights = [send(weight, pairs) for weight in weights]
    snapshots = jnp.transpose(grid_state, (0, 2, 1))
    lists = send_rows.shape[0]

    def rows_of(value):
        return jnp.pad(value, ((0, 0), (0, 128 - value.shape[1])))

    packed = jnp.concatenate(
        [
            rows_of(neighbors.T),
            rows_of(send_rows),
            rows_of(grid_mesh.reshape(1, grid_rows)),
            rows_of(halo_count.reshape(1, lists)),
        ],
        axis=0,
    )
    payloads = call(
        functools.partial(encode_kernel, group, mesh_rows, fanout, lists),
        "encode",
        [jax.ShapeDtypeStruct((mesh_rows + 2 * fanout, width), bf16)] * samples,
        [where, snapshots, w_embed, packed],
        "wvvv",
        [pltpu.VMEM((samples * grid_rows, width), bf16)],
    )
    held = call(
        hold_kernel,
        "hold",
        [jax.ShapeDtypeStruct(weight.shape, bf16) for weight in weights],
        weights,
        "hhh",
        [pltpu.SemaphoreType.DMA((3,))],
    )
    own_payload, *held = lax.optimization_barrier((payloads[0], *held))
    arrived = [own_payload] + [to_chip(payloads[turn], turn) for turn in range(1, samples)]
    (joined,) = call(
        join_kernel,
        "join",
        [jax.ShapeDtypeStruct((samples * (mesh_rows + 2 * fanout), width), bf16)],
        arrived,
        "v" * samples,
    )
    lanes = [joined] + [change_lane(joined, -steps) for steps in range(1, group)]
    half = nodes // 2
    share = group * mesh_rows
    columns, low, high = call(
        functools.partial(index_kernel, parts, mesh_rows),
        "index",
        [
            jax.ShapeDtypeStruct((nodes, 128), bf16),
            jax.ShapeDtypeStruct((half, width), bf16),
            jax.ShapeDtypeStruct((half, width), bf16),
        ],
        [where] + lanes,
        "w" + "v" * group,
        [pltpu.VMEM((128, nodes), jnp.int32)],
    )
    state_shape = jax.ShapeDtypeStruct((half, width), bf16)
    for layer in range(segments):
        at_segment, ends = min(layer, last), layer > last
        used = list(held) if layer <= last else came_weights
        role = (group, at_segment, samples if ends else 0, fanout)
        pieces = [jax.ShapeDtypeStruct((share, width), bf16)] * (half // share) if ends else [state_shape]
        scratch = [pltpu.VMEM((half, width), bf16)]
        (sender_low,) = call(
            functools.partial(sender_kernel, group, at_segment),
            "sender",
            [state_shape],
            [where, low, used[0]],
            "wvv",
        )
        sender, *first = call(
            functools.partial(first_kernel, *role),
            "first",
            [jax.ShapeDtypeStruct((nodes, width), bf16)] + pieces,
            [where, columns, sender_low, low, high] + used,
            "wvvvvvvv",
            scratch,
        )
        pairs = [(owner(m, layer), owner(m, layer + 1)) for m in range(samples)]
        new_low = send(first[0], pairs) if layer < last else first[0]
        second = call(
            functools.partial(second_kernel, *role),
            "second",
            pieces,
            [where, columns, sender, low, high] + used,
            "wvvvvvvv",
            scratch,
        )
        low, high = new_low, send(second[0], pairs) if layer < last else second[0]
        if layer == 0:
            ready, table = call(
                prepare_kernel,
                "prepare",
                [
                    jax.ShapeDtypeStruct((grid_rows, width), jnp.float32),
                    jax.ShapeDtypeStruct((mesh_rows, grid_rows), bf16),
                ],
                [where, snapshots, w_embed, w_decode, mesh_grid.reshape(1, grid_rows)],
                "wvvvv",
                    )
            low, ready, table = lax.optimization_barrier((low, ready, table))
    each = samples // 2
    arrived = []
    for far, blocks in ((1, first), (0, second)):
        for turn, block in enumerate(blocks):
            pairs = [
                (owner(m, last), device(m, ((m // each ^ far) * each + turn) * group)) for m in range(samples)
            ]
            arrived.append(send(block, [pair for pair in pairs if pair[0] != pair[1]]))
    (crossed,) = call(
        functools.partial(far_kernel, group, samples, last),
        "far",
        [jax.ShapeDtypeStruct((share, width), bf16)],
        [where] + arrived[:each],
        "w" + "v" * each,
    )
    parts_of_block = call(
        functools.partial(near_kernel, group, samples, last),
        "near",
        [jax.ShapeDtypeStruct((mesh_rows, width), bf16)] * group,
        [where, crossed] + arrived[each:] + list(second),
        "w" + "v" * (1 + 2 * each),
    )
    handed = [parts_of_block[0]]
    for steps in range(1, group):
        handed.append(change_lane(parts_of_block[steps], steps))
    (prediction,) = call(
        decode_kernel,
        "decode",
        [jax.ShapeDtypeStruct((channels, grid_rows), bf16)],
        [where, ready, table, w_decode, w_output.T] + handed,
        "wvvvv" + "v" * group,
        [pltpu.VMEM((mesh_rows, width), bf16)],
    )
    return prediction.T.reshape(1, grid_rows, channels)


def fits(mesh):
    segments, parts = mesh.shape["segment"], mesh.shape["dom"]
    return segments == 4 and parts % segments == 0 and parts <= 16


def solution(mesh):
    return jax.shard_map(
        resident if fits(mesh) else streamed,
        mesh=mesh,
        in_specs=(
            P(None, "dom", None),
            P(),
            P("segment", None, None),
            P("segment", None, None),
            P("segment", None, None),
            P(),
            P(),
            P("dom"),
            P("dom"),
            P("dom", None),
            P(None, "dom"),
            P(None, "dom"),
        ),
        out_specs=P("segment", "dom", None),
        check_vma=False,
    )
```

```python
import functools

import jax
import jax.numpy as jnp
from jax import lax
from jax.experimental import pallas as pl
from jax.experimental.pallas import tpu as pltpu
from jax.sharding import PartitionSpec as P

epsilon = 1e-05
VMEM = pl.BlockSpec(memory_space=pltpu.VMEM)
SMEM = pl.BlockSpec(memory_space=pltpu.SMEM)
HBM = pl.BlockSpec(memory_space=pltpu.HBM)


def from_behind(value, axis, steps):
    count = lax.axis_size(axis)
    pairs = [(source, (source + steps) % count) for source in range(count)]
    return lax.ppermute(value, axis, pairs)


def from_behind_2(block, axis, distance):
    devices = range(lax.axis_size(axis))
    route = [(i - distance, i) for i in devices if i - distance in devices]
    return lax.ppermute(block, axis, route)


def from_root(value, axis, source):
    kept = jnp.where(lax.axis_index(axis) == source, value, 0).astype(value.dtype)
    return lax.psum(kept, axis)


def rms_scale(values):
    return values * lax.rsqrt(jnp.mean(values * values, axis=-1, keepdims=True) + epsilon)


def streamed(
    grid_state,
    w_embed,
    w_project,
    w_message,
    w_update,
    w_decode,
    w_output,
    grid_mesh,
    mesh_grid,
    neighbors,
    send_rows,
    halo_count,
):
    segment_index = lax.axis_index("segment")
    segment_count = lax.axis_size("segment")
    final_segment = segment_count - 1
    samples, grid_rows, channels = grid_state.shape
    width = w_embed.shape[1]
    mesh_rows = neighbors.shape[0]
    fanout = neighbors.shape[1]
    halo_rows = send_rows.shape[1]
    share = samples // segment_count
    pool_table = (grid_mesh[None, :] == jnp.arange(mesh_rows, dtype=jnp.int32)[:, None]).astype(
        jnp.bfloat16
    )
    read_table = (mesh_grid[:, None] == jnp.arange(mesh_rows, dtype=jnp.int32)[None, :]).astype(
        jnp.bfloat16
    )
    valid_rows = jnp.arange(halo_rows, dtype=jnp.int32)[None, :] < halo_count[:, 0][:, None]
    source_rows = neighbors.reshape(mesh_rows * fanout)

    def embed_grid(snapshot):
        return jax.nn.silu(jnp.dot(snapshot, w_embed, preferred_element_type=jnp.float32)).astype(
            jnp.bfloat16
        )

    def encode(snapshot):
        latent = embed_grid(snapshot)
        pooled = jnp.dot(pool_table, latent, preferred_element_type=jnp.float32)
        return (rms_scale(pooled).astype(jnp.bfloat16), latent)

    def project(state, weights):
        projected = jnp.dot(state, weights[0], preferred_element_type=jnp.float32)
        return (projected[:, :width], projected[:, width:].astype(jnp.bfloat16))

    def renew(state, receiver, extended, weights):
        fetched = extended[source_rows].reshape(mesh_rows, fanout, width)
        edges = jax.nn.silu(receiver[:, None, :] + fetched.astype(jnp.float32)).astype(jnp.bfloat16)
        messages = jnp.dot(
            edges.reshape(mesh_rows * fanout, width), weights[1], preferred_element_type=jnp.float32
        )
        aggregate = (jnp.sum(messages.reshape(mesh_rows, fanout, width), axis=1) / fanout).astype(
            jnp.bfloat16
        )
        update = jax.nn.silu(
            jnp.dot(state, weights[2][:width], preferred_element_type=jnp.float32)
            + jnp.dot(aggregate, weights[2][width:], preferred_element_type=jnp.float32)
        )
        return (state.astype(jnp.float32) + rms_scale(update)).astype(jnp.bfloat16)

    def decode(state, latent):
        readout = jnp.dot(read_table, state, preferred_element_type=jnp.float32).astype(
            jnp.bfloat16
        )
        hidden = jax.nn.silu(
            jnp.dot(latent, w_decode[:width], preferred_element_type=jnp.float32)
            + jnp.dot(readout, w_decode[width:], preferred_element_type=jnp.float32)
        ).astype(jnp.bfloat16)
        return jnp.dot(hidden, w_output, preferred_element_type=jnp.float32).astype(jnp.bfloat16)

    own_weights = (w_project[0], w_message[0], w_update[0])
    empty_mesh = jnp.zeros((mesh_rows, width), jnp.bfloat16)
    empty_receiver = jnp.zeros((mesh_rows, width), jnp.float32)
    empty_grid = jnp.zeros((grid_rows, width), jnp.bfloat16)
    empty_output = jnp.zeros((grid_rows, channels), jnp.bfloat16)
    received = empty_mesh
    carried = {}
    results = [empty_output for sample in range(samples)]
    for moment in range(samples + final_segment):
        current = received
        if moment < samples:
            snapshot = grid_state[moment]
            started, latent = lax.cond(
                segment_index == 0, lambda: encode(snapshot), lambda: (empty_mesh, empty_grid)
            )
            current = jnp.where(segment_index == 0, started, received)
            carried[moment] = from_behind_2(latent, "segment", final_segment)
        active = (moment - segment_index >= 0) & (moment - segment_index < samples)
        receiver, outgoing = lax.cond(
            active, lambda: project(current, own_weights), lambda: (empty_receiver, empty_mesh)
        )
        picked = jnp.where(valid_rows[:, :, None], outgoing[send_rows], jnp.zeros((), jnp.bfloat16))
        arrived = [outgoing]
        for list_index, offset in enumerate((1, -1, 2, -2)):
            arrived.append(from_behind(picked[list_index], "dom", offset))
        extended = jnp.concatenate(arrived, axis=0)
        renewed = lax.cond(
            active, lambda: renew(current, receiver, extended, own_weights), lambda: empty_mesh
        )
        if moment >= final_segment:
            finished = moment - final_segment
            skipped = carried[finished]
            results[finished] = lax.cond(
                segment_index == final_segment,
                lambda: decode(renewed, skipped),
                lambda: empty_output,
            )
        if moment < samples + final_segment - 1:
            received = from_behind_2(renewed, "segment", 1)
    everything = from_root(jnp.stack(results), "segment", final_segment)
    return lax.dynamic_slice_in_dim(everything, segment_index * share, share, 0)


def silu_by_tanh(values):
    half = 0.5 * values
    return half + half * jnp.tanh(half)


def matmul(left, right):
    return jnp.dot(left, right, preferred_element_type=jnp.float32)


def matmul_nt(left, right):
    return lax.dot_general(left, right, (((1,), (1,)), ((), ())), preferred_element_type=jnp.float32)


def matmul_tn(left, right):
    return lax.dot_general(left, right, (((0,), (0,)), ((), ())), preferred_element_type=jnp.float32)


def place_of(where, group):
    return lax.div(where[1], group), lax.rem(where[1], group)


def owns(where, group, at_segment):
    return jnp.logical_and(where[0] == at_segment, lax.rem(where[1], group) == 0)


def fetch(sources, targets, semaphores):
    copies = [
        pltpu.make_async_copy(source, target, semaphores.at[place])
        for place, (source, target) in enumerate(zip(sources, targets))
    ]
    for copy in copies:
        copy.start()
    return copies


def encode_kernel(group, mesh_rows, fanout, lists, where, snapshots, w_embed, packed, *refs):
    payloads, latent = refs[:-1], refs[-1]
    chip, _ = place_of(where, group)
    neighbors = packed[:fanout, :mesh_rows]
    grid_rows = snapshots.shape[2]
    grid_mesh = packed[fanout + lists : fanout + lists + 1, :grid_rows]
    counts = packed[fanout + lists + 1 : fanout + lists + 2, :lists]
    width = w_embed.shape[1]
    for place in range(snapshots.shape[0]):
        found = silu_by_tanh(matmul_tn(snapshots[place], w_embed[...])).astype(jnp.bfloat16)
        latent[place * grid_rows : (place + 1) * grid_rows, :] = found
    table = lax.broadcasted_iota(jnp.int32, (mesh_rows, grid_rows), 0) == grid_mesh
    table = jnp.where(table, 1.0, 0.0).astype(jnp.bfloat16)
    block = neighbors // mesh_rows
    row = neighbors - block * mesh_rows
    halo_rows = mesh_rows
    position = lax.broadcasted_iota(jnp.int32, (1, halo_rows), 1)
    rows = []
    for list_index in range(lists):
        kept = position < counts[:, list_index : list_index + 1]
        listed = packed[fanout + list_index : fanout + list_index + 1, :halo_rows]
        rows.append(jnp.where(kept, listed, mesh_rows))
    rows.append(jnp.zeros((fanout - lists, halo_rows), jnp.int32))
    filler = jnp.zeros((fanout, 128 - mesh_rows), jnp.int32)
    pieces = [block, filler, row, filler, jnp.concatenate(rows, axis=0), filler]
    coded = jnp.concatenate(pieces + [jnp.zeros((fanout, width - 384), jnp.int32)], axis=1)
    coded = jnp.concatenate([coded, jnp.zeros_like(coded)], axis=0)
    coded = coded.astype(jnp.float32).astype(jnp.bfloat16)
    for turn, payload in enumerate(payloads):
        start = pl.multiple_of(jnp.bitwise_xor(chip, turn) * grid_rows, grid_rows)
        pooled = matmul(table, latent[pl.ds(start, grid_rows), :])
        payload[:mesh_rows, :] = rms_scale(pooled).astype(jnp.bfloat16)
        payload[mesh_rows:, :] = coded


def join_kernel(*refs):
    payloads, joined = refs[:-1], refs[-1]
    rows = payloads[0].shape[0]
    for place, payload in enumerate(payloads):
        joined[place * rows : (place + 1) * rows, :] = payload[...]


def index_kernel(parts, quarters, mesh_rows, where, *refs):
    group = parts // quarters
    lanes, columns_out, state, index_out = refs[:group], refs[group], refs[group + 1 : -1], refs[-1]
    nodes = columns_out.shape[0]
    rows = lanes[0].shape[0] // (parts // group)
    chip, lane_place = place_of(where, group)

    @pl.when(lane_place == 0)
    def _():
        tables = []
        for part in range(parts):
            lane, turn = lanes[part % group], jnp.bitwise_xor(chip, part // group)
            base = pl.multiple_of(turn * rows, 16)
            spot = part % group * mesh_rows
            state[part // group][spot : spot + mesh_rows, :] = lane[pl.ds(base, mesh_rows), :]
            base = pl.multiple_of(turn * rows + mesh_rows, 16)
            coded = lane[pl.ds(base, rows - mesh_rows), :384].astype(jnp.float32).astype(jnp.int32)
            tables.append(coded[: coded.shape[0] // 2])
        fanout = tables[0].shape[0]
        index_out[fanout:, :] = jnp.zeros((index_out.shape[0] - fanout, nodes), jnp.int32)
        for part in range(parts):
            block = tables[part][:, :128]
            row = tables[part][:, 128:256]
            found = part * mesh_rows + row
            for list_index, offset in enumerate((-1, 1, -2, 2)):
                source = (part + offset) % parts
                lists = tables[source][list_index : list_index + 1, 256:384]
                lists = jnp.broadcast_to(lists, (fanout, 128))
                picked = jnp.take_along_axis(lists, row, axis=1)
                picked = jnp.where(picked == mesh_rows, parts * mesh_rows, source * mesh_rows + picked)
                found = jnp.where(block == list_index + 1, picked, found)
            index_out[:fanout, part * mesh_rows : (part + 1) * mesh_rows] = found[:, :mesh_rows]
        tile = min(nodes, 256)
        for number in range(1, nodes // tile):
            index_out[number * fanout : (number + 1) * fanout, :] = index_out[:fanout, :] - number * tile
        columns_out[...] = jnp.transpose(index_out[...].astype(jnp.float32)).astype(jnp.bfloat16)


def hold_kernel(w_project, w_message, w_update, held, semaphores):
    width = held.shape[1]
    sources = [
        w_project.at[0, :, :width],
        w_project.at[0, :, width:],
        w_message.at[0],
        w_update.at[0, :width],
        w_update.at[0, width:],
    ]
    for copy in fetch(sources, [held.at[place] for place in range(len(sources))], semaphores):
        copy.wait()


def renew(fanout, columns, sender, own, weights):
    chunk, width = own.shape
    nodes = sender.shape[0]
    tile = min(nodes, 256)
    together = max(1, min(fanout, 1024 // chunk))
    names = lax.broadcasted_iota(jnp.int32, (chunk, tile), 1).astype(jnp.float32).astype(jnp.bfloat16)
    one_half = jnp.full((chunk, tile), 0.5, jnp.bfloat16)
    none = jnp.zeros((chunk, tile), jnp.bfloat16)
    receiver = 0.5 * matmul(own, weights[0])
    total = jnp.zeros((chunk, width), jnp.float32)
    for first in range(0, fanout, together):
        tables = []
        for k in range(first, first + together):
            hits = []
            for number in range(nodes // tile):
                lane = number * fanout + k
                hits.append(jnp.where(columns[:, lane : lane + 1] == names, one_half, none))
            tables.append(jnp.concatenate(hits, axis=1))
        fetched = matmul(jnp.concatenate(tables, axis=0), sender)
        for place in range(together):
            half = receiver + fetched[place * chunk : (place + 1) * chunk]
            total = total + (half + half * jnp.tanh(half))
    gathered = (total * (1.0 / fanout)).astype(jnp.bfloat16)
    aggregate = matmul(gathered, weights[2]).astype(jnp.bfloat16)
    update = silu_by_tanh(matmul(own, weights[3]) + matmul(aggregate, weights[4]))
    return (own.astype(jnp.float32) + rms_scale(update)).astype(jnp.bfloat16)


def sender_kernel(group, at_segment, where, state, weights, sender):
    @pl.when(owns(where, group, at_segment))
    def _():
        sender[...] = matmul(state[...], weights[1]).astype(jnp.bfloat16)


def choose(where, group, chips, far, start, count, state, own):
    rows = state[0].shape[0]

    def take(start):
        for place in range(count):
            own[place * rows : (place + 1) * rows, :] = state[start + place][...]

    if not chips:
        take(start)
        return start * rows
    chip, _ = place_of(where, group)
    upper = (chip < chips // 2) if far else (chip >= chips // 2)

    @pl.when(upper)
    def _():
        take(count)

    @pl.when(jnp.logical_not(upper))
    def _():
        take(0)

    return pl.multiple_of(jnp.where(upper, count * rows, 0), count * rows)


def write_pieces(pieces, value):
    rows = pieces[0].shape[0]
    for place, piece in enumerate(pieces):
        piece[...] = value[place * rows : (place + 1) * rows]


def first_kernel(group, at_segment, chips, fanout, quarters, where, columns, *refs):
    senders, refs = refs[: quarters - 1], refs[quarters - 1 :]
    state, (weights, sender), refs = refs[:quarters], refs[quarters : quarters + 2], refs[quarters + 2 :]
    pieces, own = refs[:-1], refs[-1]
    rows = state[0].shape[0]

    @pl.when(owns(where, group, at_segment))
    def _():
        for place, part in enumerate(senders):
            sender[place * rows : (place + 1) * rows, :] = part[...]
        rest = matmul(state[-1][...], weights[1]).astype(jnp.bfloat16)
        sender[(quarters - 1) * rows :, :] = rest
        start = choose(where, group, chips, True, 0, len(pieces), state, own)
        lanes = columns[pl.ds(start, own.shape[0]), :]
        write_pieces(pieces, renew(fanout, lanes, sender[...], own[...], weights))


def next_kernel(group, at_segment, chips, fanout, quarters, done, where, columns, sender, *refs):
    state, weights, refs = refs[:quarters], refs[quarters], refs[quarters + 1 :]
    pieces, own = refs[:-1], refs[-1]

    @pl.when(owns(where, group, at_segment))
    def _():
        start = choose(where, group, chips, False, done, len(pieces), state, own)
        lanes = columns[pl.ds(start, own.shape[0]), :]
        write_pieces(pieces, renew(fanout, lanes, sender[...], own[...], weights))


def arrival(where, group, chips, last):
    each = chips // 2
    segment = where[0]
    chip, _ = place_of(where, group)
    crosses = lax.div(chip, each) != lax.div(segment, each)
    return crosses, jnp.logical_and(segment == last, chip == last), lax.rem(chip, each)


def far_kernel(group, chips, last, where, *refs):
    far, out = refs[:-1], refs[-1]
    crosses, _, spot = arrival(where, group, chips, last)
    for number, block in enumerate(far):

        @pl.when(jnp.logical_and(crosses, spot == number))
        def _(block=block):
            out[...] = block[...]


def near_kernel(group, chips, last, where, crossed, *refs):
    each = chips // 2
    near, kept, outs = refs[:each], refs[each : 2 * each], refs[2 * each :]
    rows = outs[0].shape[0]
    crosses, stays, spot = arrival(where, group, chips, last)
    arrives = jnp.logical_not(jnp.logical_or(crosses, stays))

    def give(block):
        for place, out in enumerate(outs):
            out[...] = block[place * rows : (place + 1) * rows, :]

    @pl.when(crosses)
    def _():
        give(crossed)

    for number in range(each):
        for blocks, chosen in ((near, arrives), (kept, stays)):

            @pl.when(jnp.logical_and(chosen, spot == number))
            def _(block=blocks[number]):
                give(block)


def prepare_kernel(where, snapshots, w_embed, w_decode, mesh_grid, ready, table_out):
    snapshot = snapshots[where[0]]
    latent = silu_by_tanh(matmul_tn(snapshot, w_embed[...])).astype(jnp.bfloat16)
    ready[...] = matmul(latent, w_decode[: latent.shape[1], :])
    mesh_rows, grid_rows = table_out.shape
    table = lax.broadcasted_iota(jnp.int32, (mesh_rows, grid_rows), 0) == mesh_grid[...]
    table_out[...] = jnp.where(table, 1.0, 0.0).astype(jnp.bfloat16)


def decode_kernel(where, ready, table, w_decode, w_output, *refs):
    blocks, out, state = refs[:-2], refs[-2], refs[-1]
    width = ready.shape[1]
    _, lane = place_of(where, len(blocks))
    for number, block in enumerate(blocks):

        @pl.when(lane == number)
        def _(block=block):
            state[...] = block[...]

    readout = matmul_tn(table[...], state[...]).astype(jnp.bfloat16)
    hidden = silu_by_tanh(ready[...] + matmul(readout, w_decode[width:, :])).astype(jnp.bfloat16)
    out[...] = matmul_nt(w_output[...], hidden).astype(jnp.bfloat16)


def call(kernel, name, shapes, inputs, places, scratch=(), room=16):
    specs, given = [], []
    for value, place in zip(inputs, places):
        specs += [SMEM] * 2 if place == "w" else [VMEM if place == "v" else HBM]
        given += list(value) if place == "w" else [value]
    moved = sum(value.size * value.dtype.itemsize for value in given + list(shapes))

    def located(segment, place, *refs):
        kernel((segment[0], place[0]), *refs)

    return pl.pallas_call(
        located if places[0] == "w" else kernel,
        out_shape=shapes,
        in_specs=specs,
        out_specs=[VMEM] * len(shapes),
        scratch_shapes=list(scratch),
        name=name,
        compiler_params=pltpu.CompilerParams(vmem_limit_bytes=room * 1024 * 1024),
        cost_estimate=pl.CostEstimate(flops=0, bytes_accessed=moved, transcendentals=0),
    )(*given)


def every_device(pairs, count, group):
    onward = dict(pairs)
    reached = set(onward.values())
    for first in [source for source in onward if source not in reached]:
        last = first
        while last in onward:
            last = onward[last]
        onward.update({last: last + group - 1, last + group - 1: first + group - 1, first + group - 1: first})
    alone = []
    for at in range(0, count, group):
        rest = [lane for lane in range(at, at + group) if lane not in onward]
        if len(rest) > 1:
            onward.update(zip(rest, rest[1:] + rest[:1]))
        else:
            alone += rest
    if len(alone) == 1:
        before = next(at for at in onward if at % group and onward[at] % group == 0)
        onward.update({before: alone[0], alone[0]: onward[before]})
    else:
        onward.update(zip(alone, alone[1:] + alone[:1]))
    return sorted(onward.items())


def resident(
    grid_state,
    w_embed,
    w_project,
    w_message,
    w_update,
    w_decode,
    w_output,
    grid_mesh,
    mesh_grid,
    neighbors,
    send_rows,
    halo_count,
):
    segment = lax.axis_index("segment")
    place = lax.axis_index("dom")
    segments = lax.axis_size("segment")
    parts = lax.axis_size("dom")
    samples, grid_rows, channels = grid_state.shape
    width = w_embed.shape[1]
    mesh_rows, fanout = neighbors.shape
    nodes = parts * mesh_rows
    group = parts // samples
    bf16 = jnp.bfloat16

    def device(at_segment, at_dom):
        return at_segment * parts + at_dom % parts

    def send(value, pairs):
        return lax.ppermute(value, ("segment", "dom"), every_device(pairs, segments * parts, group))

    def to_chip(value, steps):
        pairs = [(at, (at // group ^ steps) * group + at % group) for at in range(parts)]
        return lax.ppermute(value, "dom", pairs)

    def change_lane(value, steps):
        pairs = [(at, at - at % group + (at + steps) % group) for at in range(parts)]
        return lax.ppermute(value, "dom", pairs)

    def owner(m, at_segment):
        return device(at_segment, m * group)

    own_segment, own_place, *weights = lax.optimization_barrier(
        (segment.reshape(1), place.reshape(1), w_project, w_message, w_update)
    )
    where = (own_segment, own_place)
    last = segments - 2
    pairs = [(owner(m, last + 1), owner(m, last)) for m in range(samples)]
    (held,) = call(
        hold_kernel,
        "hold",
        [jax.ShapeDtypeStruct((5, width, width), bf16)],
        weights,
        "hhh",
        [pltpu.SemaphoreType.DMA((5,))],
        room=16,
    )
    came = send(held, pairs)
    snapshots = jnp.transpose(grid_state, (0, 2, 1))
    lists = send_rows.shape[0]

    def rows_of(value):
        return jnp.pad(value, ((0, 0), (0, 128 - value.shape[1])))

    packed = jnp.concatenate(
        [
            rows_of(neighbors.T),
            rows_of(send_rows),
            rows_of(grid_mesh.reshape(1, grid_rows)),
            rows_of(halo_count.reshape(1, lists)),
        ],
        axis=0,
    )
    payloads = call(
        functools.partial(encode_kernel, group, mesh_rows, fanout, lists),
        "encode",
        [jax.ShapeDtypeStruct((mesh_rows + 2 * fanout, width), bf16)] * samples,
        [where, snapshots, w_embed, packed],
        "wvvv",
        [pltpu.VMEM((samples * grid_rows, width), bf16)],
    )
    own_payload, held = lax.optimization_barrier((payloads[0], held))
    arrived = [own_payload] + [to_chip(payloads[turn], turn) for turn in range(1, samples)]
    (joined,) = call(
        join_kernel,
        "join",
        [jax.ShapeDtypeStruct((samples * (mesh_rows + 2 * fanout), width), bf16)],
        arrived,
        "v" * samples,
    )
    lanes = [joined] + [change_lane(joined, -steps) for steps in range(1, group)]
    share = group * mesh_rows
    quarter = jax.ShapeDtypeStruct((share, width), bf16)
    columns, *state = call(
        functools.partial(index_kernel, parts, samples, mesh_rows),
        "index",
        [jax.ShapeDtypeStruct((nodes, 128), bf16)] + [quarter] * samples,
        [where] + lanes,
        "w" + "v" * group,
        [pltpu.VMEM((128, nodes), jnp.int32)],
    )
    for layer in range(segments):
        at_segment, ends = min(layer, last), layer > last
        used = held if layer <= last else came
        role = (group, at_segment, samples if ends else 0, fanout, samples)
        count = 1 if layer < last else samples // 2
        scratch = [pltpu.VMEM((count * share, width), bf16)]
        pairs = [(owner(m, layer), owner(m, layer + 1)) for m in range(samples)]
        senders = []
        for part in state[:-1]:
            if senders:
                part, senders[-1] = lax.optimization_barrier((part, senders[-1]))
            senders += call(
                functools.partial(sender_kernel, group, at_segment),
                "sender",
                [quarter],
                [where, part, used],
                "wvv",
            )
        sender, *made = call(
            functools.partial(first_kernel, *role),
            "first",
            [jax.ShapeDtypeStruct((nodes, width), bf16)] + [quarter] * count,
            [where, columns] + senders + list(state) + [used],
            "w" + "v" * (2 * samples + 1),
            scratch,
        )
        renewed = [send(made[0], pairs)] if layer < last else list(made)
        for done in range(count, samples, count):
            made = call(
                functools.partial(next_kernel, *role, done),
                "next",
                [quarter] * count,
                [where, columns, sender] + list(state) + [used],
                "w" + "v" * (samples + 3),
                scratch,
            )
            renewed += [send(made[0], pairs)] if layer < last else list(made)
        state = renewed
        if layer == 0:
            ready, table = call(
                prepare_kernel,
                "prepare",
                [
                    jax.ShapeDtypeStruct((grid_rows, width), jnp.float32),
                    jax.ShapeDtypeStruct((mesh_rows, grid_rows), bf16),
                ],
                [where, snapshots, w_embed, w_decode, mesh_grid.reshape(1, grid_rows)],
                "wvvvv",
                    )
            state[0], ready, table = lax.optimization_barrier((state[0], ready, table))
    each = samples // 2
    arrived = []
    for far, blocks in ((1, state[: samples // 2]), (0, state[samples // 2 :])):
        for turn, block in enumerate(blocks):
            pairs = [
                (owner(m, last), device(m, ((m // each ^ far) * each + turn) * group)) for m in range(samples)
            ]
            arrived.append(send(block, [pair for pair in pairs if pair[0] != pair[1]]))
    (crossed,) = call(
        functools.partial(far_kernel, group, samples, last),
        "far",
        [jax.ShapeDtypeStruct((share, width), bf16)],
        [where] + arrived[:each],
        "w" + "v" * each,
    )
    parts_of_block = call(
        functools.partial(near_kernel, group, samples, last),
        "near",
        [jax.ShapeDtypeStruct((mesh_rows, width), bf16)] * group,
        [where, crossed] + arrived[each:] + state[each:],
        "w" + "v" * (1 + 2 * each),
    )
    handed = [parts_of_block[0]]
    for steps in range(1, group):
        handed.append(change_lane(parts_of_block[steps], steps))
    (prediction,) = call(
        decode_kernel,
        "decode",
        [jax.ShapeDtypeStruct((channels, grid_rows), bf16)],
        [where, ready, table, w_decode, w_output.T] + handed,
        "wvvvv" + "v" * group,
        [pltpu.VMEM((mesh_rows, width), bf16)],
    )
    return prediction.T.reshape(1, grid_rows, channels)


def fits(mesh):
    segments, parts = mesh.shape["segment"], mesh.shape["dom"]
    return segments == 4 and parts % segments == 0 and parts <= 16


def solution(mesh):
    return jax.shard_map(
        resident if fits(mesh) else streamed,
        mesh=mesh,
        in_specs=(
            P(None, "dom", None),
            P(),
            P("segment", None, None),
            P("segment", None, None),
            P("segment", None, None),
            P(),
            P(),
            P("dom"),
            P("dom"),
            P("dom", None),
            P(None, "dom"),
            P(None, "dom"),
        ),
        out_specs=P("segment", "dom", None),
        check_vma=False,
    )
```

```python
import functools

import jax
import jax.numpy as jnp
from jax import lax
from jax.experimental import pallas as pl
from jax.experimental.pallas import tpu as pltpu
from jax.sharding import PartitionSpec as P

epsilon = 1e-05
VMEM = pl.BlockSpec(memory_space=pltpu.VMEM)
SMEM = pl.BlockSpec(memory_space=pltpu.SMEM)
HBM = pl.BlockSpec(memory_space=pltpu.HBM)


def from_behind(value, axis, steps):
    count = lax.axis_size(axis)
    pairs = [(source, (source + steps) % count) for source in range(count)]
    return lax.ppermute(value, axis, pairs)


def from_behind_2(block, axis, distance):
    devices = range(lax.axis_size(axis))
    route = [(i - distance, i) for i in devices if i - distance in devices]
    return lax.ppermute(block, axis, route)


def from_root(value, axis, source):
    kept = jnp.where(lax.axis_index(axis) == source, value, 0).astype(value.dtype)
    return lax.psum(kept, axis)


def rms_scale(values):
    return values * lax.rsqrt(jnp.mean(values * values, axis=-1, keepdims=True) + epsilon)


def streamed(
    grid_state,
    w_embed,
    w_project,
    w_message,
    w_update,
    w_decode,
    w_output,
    grid_mesh,
    mesh_grid,
    neighbors,
    send_rows,
    halo_count,
):
    segment_index = lax.axis_index("segment")
    segment_count = lax.axis_size("segment")
    final_segment = segment_count - 1
    samples, grid_rows, channels = grid_state.shape
    width = w_embed.shape[1]
    mesh_rows = neighbors.shape[0]
    fanout = neighbors.shape[1]
    halo_rows = send_rows.shape[1]
    share = samples // segment_count
    pool_table = (grid_mesh[None, :] == jnp.arange(mesh_rows, dtype=jnp.int32)[:, None]).astype(
        jnp.bfloat16
    )
    read_table = (mesh_grid[:, None] == jnp.arange(mesh_rows, dtype=jnp.int32)[None, :]).astype(
        jnp.bfloat16
    )
    valid_rows = jnp.arange(halo_rows, dtype=jnp.int32)[None, :] < halo_count[:, 0][:, None]
    source_rows = neighbors.reshape(mesh_rows * fanout)

    def embed_grid(snapshot):
        return jax.nn.silu(jnp.dot(snapshot, w_embed, preferred_element_type=jnp.float32)).astype(
            jnp.bfloat16
        )

    def encode(snapshot):
        latent = embed_grid(snapshot)
        pooled = jnp.dot(pool_table, latent, preferred_element_type=jnp.float32)
        return (rms_scale(pooled).astype(jnp.bfloat16), latent)

    def project(state, weights):
        projected = jnp.dot(state, weights[0], preferred_element_type=jnp.float32)
        return (projected[:, :width], projected[:, width:].astype(jnp.bfloat16))

    def renew(state, receiver, extended, weights):
        fetched = extended[source_rows].reshape(mesh_rows, fanout, width)
        edges = jax.nn.silu(receiver[:, None, :] + fetched.astype(jnp.float32)).astype(jnp.bfloat16)
        messages = jnp.dot(
            edges.reshape(mesh_rows * fanout, width), weights[1], preferred_element_type=jnp.float32
        )
        aggregate = (jnp.sum(messages.reshape(mesh_rows, fanout, width), axis=1) / fanout).astype(
            jnp.bfloat16
        )
        update = jax.nn.silu(
            jnp.dot(state, weights[2][:width], preferred_element_type=jnp.float32)
            + jnp.dot(aggregate, weights[2][width:], preferred_element_type=jnp.float32)
        )
        return (state.astype(jnp.float32) + rms_scale(update)).astype(jnp.bfloat16)

    def decode(state, latent):
        readout = jnp.dot(read_table, state, preferred_element_type=jnp.float32).astype(
            jnp.bfloat16
        )
        hidden = jax.nn.silu(
            jnp.dot(latent, w_decode[:width], preferred_element_type=jnp.float32)
            + jnp.dot(readout, w_decode[width:], preferred_element_type=jnp.float32)
        ).astype(jnp.bfloat16)
        return jnp.dot(hidden, w_output, preferred_element_type=jnp.float32).astype(jnp.bfloat16)

    own_weights = (w_project[0], w_message[0], w_update[0])
    empty_mesh = jnp.zeros((mesh_rows, width), jnp.bfloat16)
    empty_receiver = jnp.zeros((mesh_rows, width), jnp.float32)
    empty_grid = jnp.zeros((grid_rows, width), jnp.bfloat16)
    empty_output = jnp.zeros((grid_rows, channels), jnp.bfloat16)
    received = empty_mesh
    carried = {}
    results = [empty_output for sample in range(samples)]
    for moment in range(samples + final_segment):
        current = received
        if moment < samples:
            snapshot = grid_state[moment]
            started, latent = lax.cond(
                segment_index == 0, lambda: encode(snapshot), lambda: (empty_mesh, empty_grid)
            )
            current = jnp.where(segment_index == 0, started, received)
            carried[moment] = from_behind_2(latent, "segment", final_segment)
        active = (moment - segment_index >= 0) & (moment - segment_index < samples)
        receiver, outgoing = lax.cond(
            active, lambda: project(current, own_weights), lambda: (empty_receiver, empty_mesh)
        )
        picked = jnp.where(valid_rows[:, :, None], outgoing[send_rows], jnp.zeros((), jnp.bfloat16))
        arrived = [outgoing]
        for list_index, offset in enumerate((1, -1, 2, -2)):
            arrived.append(from_behind(picked[list_index], "dom", offset))
        extended = jnp.concatenate(arrived, axis=0)
        renewed = lax.cond(
            active, lambda: renew(current, receiver, extended, own_weights), lambda: empty_mesh
        )
        if moment >= final_segment:
            finished = moment - final_segment
            skipped = carried[finished]
            results[finished] = lax.cond(
                segment_index == final_segment,
                lambda: decode(renewed, skipped),
                lambda: empty_output,
            )
        if moment < samples + final_segment - 1:
            received = from_behind_2(renewed, "segment", 1)
    everything = from_root(jnp.stack(results), "segment", final_segment)
    return lax.dynamic_slice_in_dim(everything, segment_index * share, share, 0)


def silu_by_tanh(values):
    half = 0.5 * values
    return half + half * jnp.tanh(half)


def matmul(left, right):
    return jnp.dot(left, right, preferred_element_type=jnp.float32)


def matmul_nt(left, right):
    return lax.dot_general(left, right, (((1,), (1,)), ((), ())), preferred_element_type=jnp.float32)


def matmul_tn(left, right):
    return lax.dot_general(left, right, (((0,), (0,)), ((), ())), preferred_element_type=jnp.float32)


def place_of(where, group):
    return lax.div(where[1], group), lax.rem(where[1], group)


def owns(where, group, at_segment):
    return jnp.logical_and(where[0] == at_segment, lax.rem(where[1], group) == 0)


def fetch(sources, targets, semaphores):
    copies = [
        pltpu.make_async_copy(source, target, semaphores.at[place])
        for place, (source, target) in enumerate(zip(sources, targets))
    ]
    for copy in copies:
        copy.start()
    return copies


def encode_kernel(group, mesh_rows, fanout, lists, where, snapshots, w_embed, packed, *refs):
    payloads, latent = refs[:-1], refs[-1]
    chip, _ = place_of(where, group)
    neighbors = packed[:fanout, :mesh_rows]
    grid_rows = snapshots.shape[2]
    grid_mesh = packed[fanout + lists : fanout + lists + 1, :grid_rows]
    counts = packed[fanout + lists + 1 : fanout + lists + 2, :lists]
    width = w_embed.shape[1]
    for place in range(snapshots.shape[0]):
        found = silu_by_tanh(matmul_tn(snapshots[place], w_embed[...])).astype(jnp.bfloat16)
        latent[place * grid_rows : (place + 1) * grid_rows, :] = found
    table = lax.broadcasted_iota(jnp.int32, (mesh_rows, grid_rows), 0) == grid_mesh
    table = jnp.where(table, 1.0, 0.0).astype(jnp.bfloat16)
    block = neighbors // mesh_rows
    row = neighbors - block * mesh_rows
    halo_rows = mesh_rows
    position = lax.broadcasted_iota(jnp.int32, (1, halo_rows), 1)
    rows = []
    for list_index in range(lists):
        kept = position < counts[:, list_index : list_index + 1]
        listed = packed[fanout + list_index : fanout + list_index + 1, :halo_rows]
        rows.append(jnp.where(kept, listed, mesh_rows))
    rows.append(jnp.zeros((fanout - lists, halo_rows), jnp.int32))
    filler = jnp.zeros((fanout, 128 - mesh_rows), jnp.int32)
    pieces = [block, filler, row, filler, jnp.concatenate(rows, axis=0), filler]
    coded = jnp.concatenate(pieces + [jnp.zeros((fanout, width - 384), jnp.int32)], axis=1)
    coded = jnp.concatenate([coded, jnp.zeros_like(coded)], axis=0)
    coded = coded.astype(jnp.float32).astype(jnp.bfloat16)
    for turn, payload in enumerate(payloads):
        start = pl.multiple_of(jnp.bitwise_xor(chip, turn) * grid_rows, grid_rows)
        pooled = matmul(table, latent[pl.ds(start, grid_rows), :])
        payload[:mesh_rows, :] = rms_scale(pooled).astype(jnp.bfloat16)
        payload[mesh_rows:, :] = coded


def join_kernel(*refs):
    payloads, joined = refs[:-1], refs[-1]
    rows = payloads[0].shape[0]
    for place, payload in enumerate(payloads):
        joined[place * rows : (place + 1) * rows, :] = payload[...]


def index_kernel(parts, mesh_rows, where, *refs):
    lanes, (columns_out, low, high), index_out = refs[:-4], refs[-4:-1], refs[-1]
    nodes = columns_out.shape[0]
    group = len(lanes)
    rows = lanes[0].shape[0] // (parts // group)
    chip, lane_place = place_of(where, group)

    @pl.when(lane_place == 0)
    def _():
        tables = []
        for part in range(parts):
            lane, turn = lanes[part % group], jnp.bitwise_xor(chip, part // group)
            base = pl.multiple_of(turn * rows, 16)
            half, spot = (low, part) if part < parts // 2 else (high, part - parts // 2)
            half[spot * mesh_rows : (spot + 1) * mesh_rows, :] = lane[pl.ds(base, mesh_rows), :]
            base = pl.multiple_of(turn * rows + mesh_rows, 16)
            coded = lane[pl.ds(base, rows - mesh_rows), :384].astype(jnp.float32).astype(jnp.int32)
            tables.append(coded[: coded.shape[0] // 2])
        fanout = tables[0].shape[0]
        index_out[fanout:, :] = jnp.zeros((index_out.shape[0] - fanout, nodes), jnp.int32)
        for part in range(parts):
            block = tables[part][:, :128]
            row = tables[part][:, 128:256]
            found = part * mesh_rows + row
            for list_index, offset in enumerate((-1, 1, -2, 2)):
                source = (part + offset) % parts
                lists = tables[source][list_index : list_index + 1, 256:384]
                lists = jnp.broadcast_to(lists, (fanout, 128))
                picked = jnp.take_along_axis(lists, row, axis=1)
                picked = jnp.where(picked == mesh_rows, parts * mesh_rows, source * mesh_rows + picked)
                found = jnp.where(block == list_index + 1, picked, found)
            index_out[:fanout, part * mesh_rows : (part + 1) * mesh_rows] = found[:, :mesh_rows]
        tile = min(nodes, 256)
        for number in range(1, nodes // tile):
            index_out[number * fanout : (number + 1) * fanout, :] = index_out[:fanout, :] - number * tile
        columns_out[...] = jnp.transpose(index_out[...].astype(jnp.float32)).astype(jnp.bfloat16)


def hold_kernel(w_project, w_message, w_update, held):
    width = held.shape[1]
    held[0] = w_project[0, :, :width]
    held[1] = w_project[0, :, width:]
    held[2] = w_update[0, :width, :]
    held[3] = matmul(w_message[0], w_update[0, width:, :]).astype(jnp.bfloat16)


def blocks_of(weights):
    if len(weights) == 1:
        (held,) = weights
        return held[0], held[1], held[2], lambda gathered: matmul(gathered, held[3])
    w_project, w_message, w_update = weights
    width = w_message.shape[1]

    def finish(gathered):
        aggregate = matmul(gathered, w_message[0]).astype(jnp.bfloat16)
        return matmul(aggregate, w_update[0, width:, :])

    return w_project[0, :, :width], w_project[0, :, width:], w_update[0, :width, :], finish


def renew(fanout, columns, sender, own, weights):
    chunk, width = own.shape
    nodes = sender.shape[0]
    tile = min(nodes, 256)
    names = lax.broadcasted_iota(jnp.int32, (chunk, tile), 1).astype(jnp.float32).astype(jnp.bfloat16)
    one_half = jnp.full((chunk, tile), 0.5, jnp.bfloat16)
    none = jnp.zeros((chunk, tile), jnp.bfloat16)
    w_receive, _, w_own, finish = blocks_of(weights)
    receiver = 0.5 * matmul(own, w_receive)
    update = matmul(own, w_own)
    total = jnp.zeros((chunk, width), jnp.float32)
    for k in range(fanout):
        hits = []
        for number in range(nodes // tile):
            lane = number * fanout + k
            hits.append(jnp.where(columns[:, lane : lane + 1] == names, one_half, none))
        half = receiver + matmul(jnp.concatenate(hits, axis=1), sender)
        total = total + (half + half * jnp.tanh(half))
    gathered = (total * (1.0 / fanout)).astype(jnp.bfloat16)
    update = silu_by_tanh(update + finish(gathered))
    return (own.astype(jnp.float32) + rms_scale(update)).astype(jnp.bfloat16)


def write_pieces(pieces, value):
    rows = pieces[0].shape[0]
    for place, piece in enumerate(pieces):
        piece[...] = value[place * rows : (place + 1) * rows]


def sender_kernel(group, at_segment, where, low, *refs):
    weights, sender_low = refs[:-1], refs[-1]

    @pl.when(owns(where, group, at_segment))
    def _():
        sender_low[...] = matmul(low[...], blocks_of(weights)[1]).astype(jnp.bfloat16)


def half_of(where, group, chips, far, low, high, own):
    half = low.shape[0]
    chip, _ = place_of(where, group)
    upper = (chip < chips // 2) if far else (chip >= chips // 2)

    @pl.when(upper)
    def _():
        own[...] = high[...]

    @pl.when(jnp.logical_not(upper))
    def _():
        own[...] = low[...]

    return pl.multiple_of(jnp.where(upper, half, 0), half)


def first_kernel(
    group, at_segment, chips, fanout, given, where, columns, sender_low, low, high, *refs
):
    weights, sender, pieces, own = refs[:given], refs[given], refs[given + 1 : -1], refs[-1]
    half = low.shape[0]

    @pl.when(owns(where, group, at_segment))
    def _():
        sender[:half, :] = sender_low[...]
        sender[half:, :] = matmul(high[...], blocks_of(weights)[1]).astype(jnp.bfloat16)
        start, state = 0, low
        if chips:
            start, state = half_of(where, group, chips, True, low, high, own), own
        rows = columns[pl.ds(start, half), :]
        write_pieces(pieces, renew(fanout, rows, sender[...], state[...], weights))


def second_kernel(
    group, at_segment, chips, fanout, given, where, columns, sender, low, high, *refs
):
    weights, pieces, own = refs[:given], refs[given:-1], refs[-1]
    half = low.shape[0]

    @pl.when(owns(where, group, at_segment))
    def _():
        start, state = half, high
        if chips:
            start, state = half_of(where, group, chips, False, low, high, own), own
        rows = columns[pl.ds(start, half), :]
        write_pieces(pieces, renew(fanout, rows, sender[...], state[...], weights))


def arrival(where, group, chips, last):
    each = chips // 2
    segment = where[0]
    chip, _ = place_of(where, group)
    crosses = lax.div(chip, each) != lax.div(segment, each)
    return crosses, jnp.logical_and(segment == last, chip == last), lax.rem(chip, each)


def far_kernel(group, chips, last, where, *refs):
    far, out = refs[:-1], refs[-1]
    crosses, _, spot = arrival(where, group, chips, last)
    for number, block in enumerate(far):

        @pl.when(jnp.logical_and(crosses, spot == number))
        def _(block=block):
            out[...] = block[...]


def near_kernel(group, chips, last, where, crossed, *refs):
    each = chips // 2
    near, kept, outs = refs[:each], refs[each : 2 * each], refs[2 * each :]
    rows = outs[0].shape[0]
    crosses, stays, spot = arrival(where, group, chips, last)
    arrives = jnp.logical_not(jnp.logical_or(crosses, stays))

    def give(block):
        for place, out in enumerate(outs):
            out[...] = block[place * rows : (place + 1) * rows, :]

    @pl.when(crosses)
    def _():
        give(crossed)

    for number in range(each):
        for blocks, chosen in ((near, arrives), (kept, stays)):

            @pl.when(jnp.logical_and(chosen, spot == number))
            def _(block=blocks[number]):
                give(block)


def prepare_kernel(where, snapshots, w_embed, w_decode, mesh_grid, ready, table_out):
    snapshot = snapshots[where[0]]
    latent = silu_by_tanh(matmul_tn(snapshot, w_embed[...])).astype(jnp.bfloat16)
    ready[...] = matmul(latent, w_decode[: latent.shape[1], :])
    mesh_rows, grid_rows = table_out.shape
    table = lax.broadcasted_iota(jnp.int32, (mesh_rows, grid_rows), 0) == mesh_grid[...]
    table_out[...] = jnp.where(table, 1.0, 0.0).astype(jnp.bfloat16)


def decode_kernel(where, ready, table, w_decode, w_output, *refs):
    blocks, out, state = refs[:-2], refs[-2], refs[-1]
    width = ready.shape[1]
    _, lane = place_of(where, len(blocks))
    for number, block in enumerate(blocks):

        @pl.when(lane == number)
        def _(block=block):
            state[...] = block[...]

    readout = matmul_tn(table[...], state[...]).astype(jnp.bfloat16)
    hidden = silu_by_tanh(ready[...] + matmul(readout, w_decode[width:, :])).astype(jnp.bfloat16)
    out[...] = matmul_nt(w_output[...], hidden).astype(jnp.bfloat16)


def call(kernel, name, shapes, inputs, places, scratch=(), room=16):
    specs, given = [], []
    for value, place in zip(inputs, places):
        specs += [SMEM] * 2 if place == "w" else [VMEM if place == "v" else HBM]
        given += list(value) if place == "w" else [value]
    moved = sum(value.size * value.dtype.itemsize for value in given + list(shapes))

    def located(segment, place, *refs):
        kernel((segment[0], place[0]), *refs)

    return pl.pallas_call(
        located if places[0] == "w" else kernel,
        out_shape=shapes,
        in_specs=specs,
        out_specs=[VMEM] * len(shapes),
        scratch_shapes=list(scratch),
        name=name,
        compiler_params=pltpu.CompilerParams(vmem_limit_bytes=room * 1024 * 1024),
        cost_estimate=pl.CostEstimate(flops=0, bytes_accessed=moved, transcendentals=0),
    )(*given)


def every_device(pairs, count, group):
    onward = dict(pairs)
    reached = set(onward.values())
    for first in [source for source in onward if source not in reached]:
        last = first
        while last in onward:
            last = onward[last]
        onward.update({last: last + group - 1, last + group - 1: first + group - 1, first + group - 1: first})
    alone = []
    for at in range(0, count, group):
        rest = [lane for lane in range(at, at + group) if lane not in onward]
        if len(rest) > 1:
            onward.update(zip(rest, rest[1:] + rest[:1]))
        else:
            alone += rest
    if len(alone) == 1:
        before = next(at for at in onward if at % group and onward[at] % group == 0)
        onward.update({before: alone[0], alone[0]: onward[before]})
    else:
        onward.update(zip(alone, alone[1:] + alone[:1]))
    return sorted(onward.items())


def resident(
    grid_state,
    w_embed,
    w_project,
    w_message,
    w_update,
    w_decode,
    w_output,
    grid_mesh,
    mesh_grid,
    neighbors,
    send_rows,
    halo_count,
):
    segment = lax.axis_index("segment")
    place = lax.axis_index("dom")
    segments = lax.axis_size("segment")
    parts = lax.axis_size("dom")
    samples, grid_rows, channels = grid_state.shape
    width = w_embed.shape[1]
    mesh_rows, fanout = neighbors.shape
    nodes = parts * mesh_rows
    group = parts // samples
    bf16 = jnp.bfloat16

    def device(at_segment, at_dom):
        return at_segment * parts + at_dom % parts

    def send(value, pairs):
        return lax.ppermute(value, ("segment", "dom"), every_device(pairs, segments * parts, group))

    def to_chip(value, steps):
        pairs = [(at, (at // group ^ steps) * group + at % group) for at in range(parts)]
        return lax.ppermute(value, "dom", pairs)

    def change_lane(value, steps):
        pairs = [(at, at - at % group + (at + steps) % group) for at in range(parts)]
        return lax.ppermute(value, "dom", pairs)

    def owner(m, at_segment):
        return device(at_segment, m * group)

    own_segment, own_place, *weights = lax.optimization_barrier(
        (segment.reshape(1), place.reshape(1), w_project, w_message, w_update)
    )
    where = (own_segment, own_place)
    last = segments - 2
    pairs = [(owner(m, last + 1), owner(m, last)) for m in range(samples)]
    came_weights = [send(weight, pairs) for weight in weights]
    snapshots = jnp.transpose(grid_state, (0, 2, 1))
    lists = send_rows.shape[0]

    def rows_of(value):
        return jnp.pad(value, ((0, 0), (0, 128 - value.shape[1])))

    packed = jnp.concatenate(
        [
            rows_of(neighbors.T),
            rows_of(send_rows),
            rows_of(grid_mesh.reshape(1, grid_rows)),
            rows_of(halo_count.reshape(1, lists)),
        ],
        axis=0,
    )
    payloads = call(
        functools.partial(encode_kernel, group, mesh_rows, fanout, lists),
        "encode",
        [jax.ShapeDtypeStruct((mesh_rows + 2 * fanout, width), bf16)] * samples,
        [where, snapshots, w_embed, packed],
        "wvvv",
        [pltpu.VMEM((samples * grid_rows, width), bf16)],
    )
    held = call(
        hold_kernel,
        "hold",
        [jax.ShapeDtypeStruct((4, width, width), bf16)],
        weights,
        "vvv",
    )
    own_payload, *held = lax.optimization_barrier((payloads[0], *held))
    arrived = [own_payload] + [to_chip(payloads[turn], turn) for turn in range(1, samples)]
    (joined,) = call(
        join_kernel,
        "join",
        [jax.ShapeDtypeStruct((samples * (mesh_rows + 2 * fanout), width), bf16)],
        arrived,
        "v" * samples,
    )
    lanes = [joined] + [change_lane(joined, -steps) for steps in range(1, group)]
    half = nodes // 2
    share = group * mesh_rows
    columns, low, high = call(
        functools.partial(index_kernel, parts, mesh_rows),
        "index",
        [
            jax.ShapeDtypeStruct((nodes, 128), bf16),
            jax.ShapeDtypeStruct((half, width), bf16),
            jax.ShapeDtypeStruct((half, width), bf16),
        ],
        [where] + lanes,
        "w" + "v" * group,
        [pltpu.VMEM((128, nodes), jnp.int32)],
    )
    state_shape = jax.ShapeDtypeStruct((half, width), bf16)
    for layer in range(segments):
        at_segment, ends = min(layer, last), layer > last
        used = list(held) if layer <= last else came_weights
        role = (group, at_segment, samples if ends else 0, fanout, len(used))
        pieces = [jax.ShapeDtypeStruct((share, width), bf16)] * (half // share) if ends else [state_shape]
        scratch = [pltpu.VMEM((half, width), bf16)]
        (sender_low,) = call(
            functools.partial(sender_kernel, group, at_segment),
            "sender",
            [state_shape],
            [where, low] + used,
            "wv" + "v" * len(used),
        )
        sender, *first = call(
            functools.partial(first_kernel, *role),
            "first",
            [jax.ShapeDtypeStruct((nodes, width), bf16)] + pieces,
            [where, columns, sender_low, low, high] + used,
            "wvvvv" + "v" * len(used),
            scratch,
        )
        pairs = [(owner(m, layer), owner(m, layer + 1)) for m in range(samples)]
        new_low = send(first[0], pairs) if layer < last else first[0]
        second = call(
            functools.partial(second_kernel, *role),
            "second",
            pieces,
            [where, columns, sender, low, high] + used,
            "wvvvv" + "v" * len(used),
            scratch,
        )
        low, high = new_low, send(second[0], pairs) if layer < last else second[0]
        if layer == 0:
            ready, table = call(
                prepare_kernel,
                "prepare",
                [
                    jax.ShapeDtypeStruct((grid_rows, width), jnp.float32),
                    jax.ShapeDtypeStruct((mesh_rows, grid_rows), bf16),
                ],
                [where, snapshots, w_embed, w_decode, mesh_grid.reshape(1, grid_rows)],
                "wvvvv",
                    )
            low, ready, table = lax.optimization_barrier((low, ready, table))
    each = samples // 2
    arrived = []
    for far, blocks in ((1, first), (0, second)):
        for turn, block in enumerate(blocks):
            pairs = [
                (owner(m, last), device(m, ((m // each ^ far) * each + turn) * group)) for m in range(samples)
            ]
            arrived.append(send(block, [pair for pair in pairs if pair[0] != pair[1]]))
    (crossed,) = call(
        functools.partial(far_kernel, group, samples, last),
        "far",
        [jax.ShapeDtypeStruct((share, width), bf16)],
        [where] + arrived[:each],
        "w" + "v" * each,
    )
    parts_of_block = call(
        functools.partial(near_kernel, group, samples, last),
        "near",
        [jax.ShapeDtypeStruct((mesh_rows, width), bf16)] * group,
        [where, crossed] + arrived[each:] + list(second),
        "w" + "v" * (1 + 2 * each),
    )
    handed = [parts_of_block[0]]
    for steps in range(1, group):
        handed.append(change_lane(parts_of_block[steps], steps))
    (prediction,) = call(
        decode_kernel,
        "decode",
        [jax.ShapeDtypeStruct((channels, grid_rows), bf16)],
        [where, ready, table, w_decode, w_output.T] + handed,
        "wvvvv" + "v" * group,
        [pltpu.VMEM((mesh_rows, width), bf16)],
    )
    return prediction.T.reshape(1, grid_rows, channels)


def fits(mesh):
    segments, parts = mesh.shape["segment"], mesh.shape["dom"]
    return segments == 4 and parts % segments == 0 and parts <= 16


def solution(mesh):
    return jax.shard_map(
        resident if fits(mesh) else streamed,
        mesh=mesh,
        in_specs=(
            P(None, "dom", None),
            P(),
            P("segment", None, None),
            P("segment", None, None),
            P("segment", None, None),
            P(),
            P(),
            P("dom"),
            P("dom"),
            P("dom", None),
            P(None, "dom"),
            P(None, "dom"),
        ),
        out_specs=P("segment", "dom", None),
        check_vma=False,
    )
```

```python
import functools

import jax
import jax.numpy as jnp
from jax import lax
from jax.experimental import pallas as pl
from jax.experimental.pallas import tpu as pltpu
from jax.sharding import PartitionSpec as P

epsilon = 1e-05
DIGIT = 256
VMEM = pl.BlockSpec(memory_space=pltpu.VMEM)
SMEM = pl.BlockSpec(memory_space=pltpu.SMEM)
HBM = pl.BlockSpec(memory_space=pltpu.HBM)


def from_behind(value, axis, steps):
    count = lax.axis_size(axis)
    pairs = [(source, (source + steps) % count) for source in range(count)]
    return lax.ppermute(value, axis, pairs)


def from_behind_2(block, axis, distance):
    devices = range(lax.axis_size(axis))
    route = [(i - distance, i) for i in devices if i - distance in devices]
    return lax.ppermute(block, axis, route)


def from_root(value, axis, source):
    kept = jnp.where(lax.axis_index(axis) == source, value, 0).astype(value.dtype)
    return lax.psum(kept, axis)


def rms_scale(values):
    return values * lax.rsqrt(jnp.mean(values * values, axis=-1, keepdims=True) + epsilon)


def streamed(
    grid_state,
    w_embed,
    w_project,
    w_message,
    w_update,
    w_decode,
    w_output,
    grid_mesh,
    mesh_grid,
    neighbors,
    send_rows,
    halo_count,
):
    segment_index = lax.axis_index("segment")
    segment_count = lax.axis_size("segment")
    final_segment = segment_count - 1
    samples, grid_rows, channels = grid_state.shape
    width = w_embed.shape[1]
    mesh_rows = neighbors.shape[0]
    fanout = neighbors.shape[1]
    halo_rows = send_rows.shape[1]
    share = samples // segment_count
    pool_table = (grid_mesh[None, :] == jnp.arange(mesh_rows, dtype=jnp.int32)[:, None]).astype(
        jnp.bfloat16
    )
    read_table = (mesh_grid[:, None] == jnp.arange(mesh_rows, dtype=jnp.int32)[None, :]).astype(
        jnp.bfloat16
    )
    valid_rows = jnp.arange(halo_rows, dtype=jnp.int32)[None, :] < halo_count[:, 0][:, None]
    source_rows = neighbors.reshape(mesh_rows * fanout)

    def embed_grid(snapshot):
        return jax.nn.silu(jnp.dot(snapshot, w_embed, preferred_element_type=jnp.float32)).astype(
            jnp.bfloat16
        )

    def encode(snapshot):
        latent = embed_grid(snapshot)
        pooled = jnp.dot(pool_table, latent, preferred_element_type=jnp.float32)
        return (rms_scale(pooled).astype(jnp.bfloat16), latent)

    def project(state, weights):
        projected = jnp.dot(state, weights[0], preferred_element_type=jnp.float32)
        return (projected[:, :width], projected[:, width:].astype(jnp.bfloat16))

    def renew(state, receiver, extended, weights):
        fetched = extended[source_rows].reshape(mesh_rows, fanout, width)
        edges = jax.nn.silu(receiver[:, None, :] + fetched.astype(jnp.float32)).astype(jnp.bfloat16)
        messages = jnp.dot(
            edges.reshape(mesh_rows * fanout, width), weights[1], preferred_element_type=jnp.float32
        )
        aggregate = (jnp.sum(messages.reshape(mesh_rows, fanout, width), axis=1) / fanout).astype(
            jnp.bfloat16
        )
        update = jax.nn.silu(
            jnp.dot(state, weights[2][:width], preferred_element_type=jnp.float32)
            + jnp.dot(aggregate, weights[2][width:], preferred_element_type=jnp.float32)
        )
        return (state.astype(jnp.float32) + rms_scale(update)).astype(jnp.bfloat16)

    def decode(state, latent):
        readout = jnp.dot(read_table, state, preferred_element_type=jnp.float32).astype(
            jnp.bfloat16
        )
        hidden = jax.nn.silu(
            jnp.dot(latent, w_decode[:width], preferred_element_type=jnp.float32)
            + jnp.dot(readout, w_decode[width:], preferred_element_type=jnp.float32)
        ).astype(jnp.bfloat16)
        return jnp.dot(hidden, w_output, preferred_element_type=jnp.float32).astype(jnp.bfloat16)

    own_weights = (w_project[0], w_message[0], w_update[0])
    empty_mesh = jnp.zeros((mesh_rows, width), jnp.bfloat16)
    empty_receiver = jnp.zeros((mesh_rows, width), jnp.float32)
    empty_grid = jnp.zeros((grid_rows, width), jnp.bfloat16)
    empty_output = jnp.zeros((grid_rows, channels), jnp.bfloat16)
    received = empty_mesh
    carried = {}
    results = [empty_output for sample in range(samples)]
    for moment in range(samples + final_segment):
        current = received
        if moment < samples:
            snapshot = grid_state[moment]
            started, latent = lax.cond(
                segment_index == 0, lambda: encode(snapshot), lambda: (empty_mesh, empty_grid)
            )
            current = jnp.where(segment_index == 0, started, received)
            carried[moment] = from_behind_2(latent, "segment", final_segment)
        active = (moment - segment_index >= 0) & (moment - segment_index < samples)
        receiver, outgoing = lax.cond(
            active, lambda: project(current, own_weights), lambda: (empty_receiver, empty_mesh)
        )
        picked = jnp.where(valid_rows[:, :, None], outgoing[send_rows], jnp.zeros((), jnp.bfloat16))
        arrived = [outgoing]
        for list_index, offset in enumerate((1, -1, 2, -2)):
            arrived.append(from_behind(picked[list_index], "dom", offset))
        extended = jnp.concatenate(arrived, axis=0)
        renewed = lax.cond(
            active, lambda: renew(current, receiver, extended, own_weights), lambda: empty_mesh
        )
        if moment >= final_segment:
            finished = moment - final_segment
            skipped = carried[finished]
            results[finished] = lax.cond(
                segment_index == final_segment,
                lambda: decode(renewed, skipped),
                lambda: empty_output,
            )
        if moment < samples + final_segment - 1:
            received = from_behind_2(renewed, "segment", 1)
    everything = from_root(jnp.stack(results), "segment", final_segment)
    return lax.dynamic_slice_in_dim(everything, segment_index * share, share, 0)


def silu_by_tanh(values):
    half = 0.5 * values
    return half + half * jnp.tanh(half)


def matmul(left, right):
    return jnp.dot(left, right, preferred_element_type=jnp.float32)


def matmul_nt(left, right):
    return lax.dot_general(left, right, (((1,), (1,)), ((), ())), preferred_element_type=jnp.float32)


def matmul_tn(left, right):
    return lax.dot_general(left, right, (((0,), (0,)), ((), ())), preferred_element_type=jnp.float32)


def place_of(where, group):
    return lax.div(where[1], group), lax.rem(where[1], group)


def owns(where, group, at_segment):
    return jnp.logical_and(where[0] == at_segment, lax.rem(where[1], group) == 0)


def fetch(sources, targets, semaphores):
    copies = [
        pltpu.make_async_copy(source, target, semaphores.at[place])
        for place, (source, target) in enumerate(zip(sources, targets))
    ]
    for copy in copies:
        copy.start()
    return copies


def encode_kernel(group, mesh_rows, fanout, lists, where, snapshots, w_embed, packed, *refs):
    payloads, latent = refs[:-1], refs[-1]
    chip, _ = place_of(where, group)
    neighbors = packed[:fanout, :mesh_rows]
    grid_rows = snapshots.shape[2]
    grid_mesh = packed[fanout + lists : fanout + lists + 1, :grid_rows]
    counts = packed[fanout + lists + 1 : fanout + lists + 2, :lists]
    width = w_embed.shape[1]
    for place in range(snapshots.shape[0]):
        found = silu_by_tanh(matmul_tn(snapshots[place], w_embed[...])).astype(jnp.bfloat16)
        latent[place * grid_rows : (place + 1) * grid_rows, :] = found
    table = lax.broadcasted_iota(jnp.int32, (mesh_rows, grid_rows), 0) == grid_mesh
    table = jnp.where(table, 1.0, 0.0).astype(jnp.bfloat16)
    block = neighbors // mesh_rows
    row = neighbors - block * mesh_rows
    halo_rows = mesh_rows
    position = lax.broadcasted_iota(jnp.int32, (1, halo_rows), 1)
    rows = []
    for list_index in range(lists):
        kept = position < counts[:, list_index : list_index + 1]
        listed = packed[fanout + list_index : fanout + list_index + 1, :halo_rows]
        rows.append(jnp.where(kept, listed, mesh_rows))
    rows.append(jnp.zeros((fanout - lists, halo_rows), jnp.int32))
    filler = jnp.zeros((fanout, 128 - mesh_rows), jnp.int32)
    pieces = [block, filler, row, filler, jnp.concatenate(rows, axis=0), filler]
    coded = jnp.concatenate(pieces + [jnp.zeros((fanout, width - 384), jnp.int32)], axis=1)
    coded = jnp.concatenate([coded, jnp.zeros_like(coded)], axis=0)
    coded = coded.astype(jnp.float32).astype(jnp.bfloat16)
    for turn, payload in enumerate(payloads):
        start = pl.multiple_of(jnp.bitwise_xor(chip, turn) * grid_rows, grid_rows)
        pooled = matmul(table, latent[pl.ds(start, grid_rows), :])
        payload[:mesh_rows, :] = rms_scale(pooled).astype(jnp.bfloat16)
        payload[mesh_rows:, :] = coded


def join_kernel(*refs):
    payloads, joined = refs[:-1], refs[-1]
    rows = payloads[0].shape[0]
    for place, payload in enumerate(payloads):
        joined[place * rows : (place + 1) * rows, :] = payload[...]


def columns_of(names):
    fanout, nodes = names.shape
    tile = min(nodes, DIGIT)
    rows = [names - number * tile for number in range(nodes // tile)]
    rows.append(jnp.zeros((128 - fanout * len(rows), nodes), jnp.float32))
    return jnp.transpose(jnp.concatenate(rows, axis=0)).astype(jnp.bfloat16)


def index_kernel(parts, mesh_rows, where, *refs):
    lanes, (columns_out, low, high), index_out = refs[:-4], refs[-4:-1], refs[-1]
    nodes = columns_out.shape[0]
    group = len(lanes)
    rows = lanes[0].shape[0] // (parts // group)
    chip, _ = place_of(where, group)

    @pl.when(owns(where, group, 0))
    def _():
        tables = []
        for part in range(parts):
            lane, turn = lanes[part % group], jnp.bitwise_xor(chip, part // group)
            base = pl.multiple_of(turn * rows, 16)
            half, spot = (low, part) if part < parts // 2 else (high, part - parts // 2)
            half[spot * mesh_rows : (spot + 1) * mesh_rows, :] = lane[pl.ds(base, mesh_rows), :]
            base = pl.multiple_of(turn * rows + mesh_rows, 16)
            coded = lane[pl.ds(base, rows - mesh_rows), :384].astype(jnp.float32).astype(jnp.int32)
            tables.append(coded[: coded.shape[0] // 2])
        fanout = tables[0].shape[0]
        for part in range(parts):
            block = tables[part][:, :128]
            row = tables[part][:, 128:256]
            found = part * mesh_rows + row
            for list_index, offset in enumerate((-1, 1, -2, 2)):
                source = (part + offset) % parts
                lists = tables[source][list_index : list_index + 1, 256:384]
                lists = jnp.broadcast_to(lists, (fanout, 128))
                picked = jnp.take_along_axis(lists, row, axis=1)
                picked = jnp.where(picked == mesh_rows, parts * mesh_rows, source * mesh_rows + picked)
                found = jnp.where(block == list_index + 1, picked, found)
            index_out[:, part * mesh_rows : (part + 1) * mesh_rows] = found[:, :mesh_rows]
        names = index_out[...]
        high_digit = names // DIGIT
        digits = jnp.concatenate([high_digit, names - high_digit * DIGIT], axis=0)
        low[parts // 2 * mesh_rows :, :] = digits.astype(jnp.float32).astype(jnp.bfloat16)
        columns_out[...] = columns_of(names.astype(jnp.float32))


def hold_kernel(w_project, w_message, w_update, receive, send, own, edges, message, update, semaphores):
    width = own.shape[0]
    sources = [
        w_message.at[0],
        w_update.at[0, width:],
        w_project.at[0, :, :width],
        w_project.at[0, :, width:],
        w_update.at[0, :width],
    ]
    copies = fetch(sources, [message, update, receive, send, own], semaphores)
    copies[0].wait()
    copies[1].wait()
    edges[...] = matmul(message[...], update[...]).astype(jnp.bfloat16)
    for copy in copies[2:]:
        copy.wait()


def blocks_of(weights):
    if len(weights) == 4:
        receive, send, own, edges = weights
        return receive[...], send[...], own[...], lambda gathered: matmul(gathered, edges[...])
    w_project, w_message, w_update = weights
    width = w_message.shape[1]

    def finish(gathered):
        aggregate = matmul(gathered, w_message[0]).astype(jnp.bfloat16)
        return matmul(aggregate, w_update[0, width:, :])

    return w_project[0, :, :width], w_project[0, :, width:], w_update[0, :width, :], finish


def renew(fanout, columns, sender, own, weights):
    chunk, width = own.shape
    nodes = sender.shape[0]
    tile = min(nodes, DIGIT)
    names = lax.broadcasted_iota(jnp.int32, (chunk, tile), 1).astype(jnp.float32).astype(jnp.bfloat16)
    one_half = jnp.full((chunk, tile), 0.5, jnp.bfloat16)
    none = jnp.zeros((chunk, tile), jnp.bfloat16)
    w_receive, _, w_own, finish = blocks_of(weights)
    receiver = 0.5 * matmul(own, w_receive)
    update = matmul(own, w_own)
    total = jnp.zeros((chunk, width), jnp.float32)
    for k in range(fanout):
        hits = []
        for number in range(nodes // tile):
            lane = number * fanout + k
            hits.append(jnp.where(columns[:, lane : lane + 1] == names, one_half, none))
        half = receiver + matmul(jnp.concatenate(hits, axis=1), sender)
        total = total + (half + half * jnp.tanh(half))
    gathered = (total * (1.0 / fanout)).astype(jnp.bfloat16)
    update = silu_by_tanh(update + finish(gathered))
    return (own.astype(jnp.float32) + rms_scale(update)).astype(jnp.bfloat16)


def write_pieces(pieces, value):
    rows = value.shape[0] // len(pieces)
    for place, piece in enumerate(pieces):
        piece[:rows, :] = value[place * rows : (place + 1) * rows]


def sender_kernel(group, at_segment, fanout, rows, where, low, *refs):
    weights, sender_low, columns = (refs[:-2], *refs[-2:]) if fanout else (refs[:-1], refs[-1], None)

    @pl.when(owns(where, group, at_segment))
    def _():
        sender_low[...] = matmul(low[:rows, :], blocks_of(weights)[1]).astype(jnp.bfloat16)
        if fanout:
            digits = low[rows:, :].astype(jnp.float32)
            columns[...] = columns_of(digits[:fanout] * DIGIT + digits[fanout:])


def half_of(where, group, chips, far, low, high, own):
    half = high.shape[0]
    chip, _ = place_of(where, group)
    upper = (chip < chips // 2) if far else (chip >= chips // 2)

    @pl.when(upper)
    def _():
        own[...] = high[...]

    @pl.when(jnp.logical_not(upper))
    def _():
        own[...] = low[...]

    return pl.multiple_of(jnp.where(upper, half, 0), half)


def first_kernel(
    group, at_segment, chips, fanout, given, where, columns, sender_low, low, high, *refs
):
    weights, sender, pieces, own = refs[:given], refs[given], refs[given + 1 : -1], refs[-1]
    half = high.shape[0]

    @pl.when(owns(where, group, at_segment))
    def _():
        sender[:half, :] = sender_low[...]
        sender[half:, :] = matmul(high[...], blocks_of(weights)[1]).astype(jnp.bfloat16)
        start, state = 0, low[:half, :]
        if chips:
            start = half_of(where, group, chips, True, low, high, own)
            state = own[...]
        rows = columns[pl.ds(start, half), :]
        write_pieces(pieces, renew(fanout, rows, sender[...], state, weights))
        if pieces[0].shape[0] > half:
            pieces[0][half:, :] = low[half:, :]


def second_kernel(
    group, at_segment, chips, fanout, given, where, columns, sender, low, high, *refs
):
    weights, pieces, own = refs[:given], refs[given:-1], refs[-1]
    half = high.shape[0]

    @pl.when(owns(where, group, at_segment))
    def _():
        start, state = half, high
        if chips:
            start, state = half_of(where, group, chips, False, low, high, own), own
        rows = columns[pl.ds(start, half), :]
        write_pieces(pieces, renew(fanout, rows, sender[...], state[...], weights))


def arrival(where, group, chips, last):
    each = chips // 2
    segment = where[0]
    chip, _ = place_of(where, group)
    crosses = lax.div(chip, each) != lax.div(segment, each)
    return crosses, jnp.logical_and(segment == last, chip == last), lax.rem(chip, each)


def far_kernel(group, chips, last, where, *refs):
    far, out = refs[:-1], refs[-1]
    crosses, _, spot = arrival(where, group, chips, last)
    for number, block in enumerate(far):

        @pl.when(jnp.logical_and(crosses, spot == number))
        def _(block=block):
            out[...] = block[...]


def near_kernel(group, chips, last, where, crossed, *refs):
    each = chips // 2
    near, kept, outs = refs[:each], refs[each : 2 * each], refs[2 * each :]
    rows = outs[0].shape[0]
    crosses, stays, spot = arrival(where, group, chips, last)
    arrives = jnp.logical_not(jnp.logical_or(crosses, stays))

    def give(block):
        for place, out in enumerate(outs):
            out[...] = block[place * rows : (place + 1) * rows, :]

    @pl.when(crosses)
    def _():
        give(crossed)

    for number in range(each):
        for blocks, chosen in ((near, arrives), (kept, stays)):

            @pl.when(jnp.logical_and(chosen, spot == number))
            def _(block=blocks[number]):
                give(block)


def prepare_kernel(where, snapshots, w_embed, w_decode, mesh_grid, ready, table_out):
    snapshot = snapshots[where[0]]
    latent = silu_by_tanh(matmul_tn(snapshot, w_embed[...])).astype(jnp.bfloat16)
    ready[...] = matmul(latent, w_decode[: latent.shape[1], :])
    mesh_rows, grid_rows = table_out.shape
    table = lax.broadcasted_iota(jnp.int32, (mesh_rows, grid_rows), 0) == mesh_grid[...]
    table_out[...] = jnp.where(table, 1.0, 0.0).astype(jnp.bfloat16)


def decode_kernel(where, ready, table, w_decode, w_output, *refs):
    blocks, out, state = refs[:-2], refs[-2], refs[-1]
    width = ready.shape[1]
    _, lane = place_of(where, len(blocks))
    for number, block in enumerate(blocks):

        @pl.when(lane == number)
        def _(block=block):
            state[...] = block[...]

    readout = matmul_tn(table[...], state[...]).astype(jnp.bfloat16)
    hidden = silu_by_tanh(ready[...] + matmul(readout, w_decode[width:, :])).astype(jnp.bfloat16)
    out[...] = matmul_nt(w_output[...], hidden).astype(jnp.bfloat16)


def call(kernel, name, shapes, inputs, places, scratch=(), room=16):
    specs, given = [], []
    for value, place in zip(inputs, places):
        specs += [SMEM] * 2 if place == "w" else [VMEM if place == "v" else HBM]
        given += list(value) if place == "w" else [value]
    moved = sum(value.size * value.dtype.itemsize for value in given + list(shapes))

    def located(segment, place, *refs):
        kernel((segment[0], place[0]), *refs)

    return pl.pallas_call(
        located if places[0] == "w" else kernel,
        out_shape=shapes,
        in_specs=specs,
        out_specs=[VMEM] * len(shapes),
        scratch_shapes=list(scratch),
        name=name,
        compiler_params=pltpu.CompilerParams(vmem_limit_bytes=room * 1024 * 1024),
        cost_estimate=pl.CostEstimate(flops=0, bytes_accessed=moved, transcendentals=0),
    )(*given)


def every_device(pairs, count, group):
    onward = dict(pairs)
    reached = set(onward.values())
    for first in [source for source in onward if source not in reached]:
        last = first
        while last in onward:
            last = onward[last]
        onward.update({last: last + group - 1, last + group - 1: first + group - 1, first + group - 1: first})
    alone = []
    for at in range(0, count, group):
        rest = [lane for lane in range(at, at + group) if lane not in onward]
        if len(rest) > 1:
            onward.update(zip(rest, rest[1:] + rest[:1]))
        else:
            alone += rest
    if len(alone) == 1:
        before = next(at for at in onward if at % group and onward[at] % group == 0)
        onward.update({before: alone[0], alone[0]: onward[before]})
    else:
        onward.update(zip(alone, alone[1:] + alone[:1]))
    return sorted(onward.items())


def resident(
    grid_state,
    w_embed,
    w_project,
    w_message,
    w_update,
    w_decode,
    w_output,
    grid_mesh,
    mesh_grid,
    neighbors,
    send_rows,
    halo_count,
):
    segment = lax.axis_index("segment")
    place = lax.axis_index("dom")
    segments = lax.axis_size("segment")
    parts = lax.axis_size("dom")
    samples, grid_rows, channels = grid_state.shape
    width = w_embed.shape[1]
    mesh_rows, fanout = neighbors.shape
    nodes = parts * mesh_rows
    group = parts // samples
    bf16 = jnp.bfloat16

    def device(at_segment, at_dom):
        return at_segment * parts + at_dom % parts

    def send(value, pairs):
        return lax.ppermute(value, ("segment", "dom"), every_device(pairs, segments * parts, group))

    def to_chip(value, steps):
        giver = steps - 1
        pairs = []
        for at in range(segments):
            for dom in range(parts):
                chip, lane = divmod(dom, group)
                across = (chip ^ steps) * group + lane
                if at == giver:
                    pairs.append((device(at, dom), device(0, across)))
                elif at == 0:
                    pairs.append((device(at, dom), device(giver, dom)))
                else:
                    pairs.append((device(at, dom), device(at, chip * group + (lane + 1) % group)))
        return lax.ppermute(value, ("segment", "dom"), pairs)

    def change_lane(value, steps):
        pairs = [(at, at - at % group + (at + steps) % group) for at in range(parts)]
        return lax.ppermute(value, "dom", pairs)

    def owner(m, at_segment):
        return device(at_segment, m * group)

    own_segment, own_place, *weights = lax.optimization_barrier(
        (segment.reshape(1), place.reshape(1), w_project, w_message, w_update)
    )
    where = (own_segment, own_place)
    last = segments - 2
    pairs = [(owner(m, last + 1), owner(m, last)) for m in range(samples)]
    came_weights = [send(weight, pairs) for weight in weights]
    snapshots = jnp.transpose(grid_state, (0, 2, 1))
    lists = send_rows.shape[0]

    def rows_of(value):
        return jnp.pad(value, ((0, 0), (0, 128 - value.shape[1])))

    packed = jnp.concatenate(
        [
            rows_of(neighbors.T),
            rows_of(send_rows),
            rows_of(grid_mesh.reshape(1, grid_rows)),
            rows_of(halo_count.reshape(1, lists)),
        ],
        axis=0,
    )
    payloads = call(
        functools.partial(encode_kernel, group, mesh_rows, fanout, lists),
        "encode",
        [jax.ShapeDtypeStruct((mesh_rows + 2 * fanout, width), bf16)] * samples,
        [where, snapshots, w_embed, packed],
        "wvvv",
        [pltpu.VMEM((samples * grid_rows, width), bf16)],
    )
    held = call(
        hold_kernel,
        "hold",
        [jax.ShapeDtypeStruct((width, width), bf16)] * 4,
        weights,
        "hhh",
        [pltpu.VMEM((width, width), bf16)] * 2 + [pltpu.SemaphoreType.DMA((5,))],
    )
    own_payload, *held = lax.optimization_barrier((payloads[0], *held))
    arrived = [own_payload] + [to_chip(payloads[turn], turn) for turn in range(1, samples)]
    (joined,) = call(
        join_kernel,
        "join",
        [jax.ShapeDtypeStruct((samples * (mesh_rows + 2 * fanout), width), bf16)],
        arrived,
        "v" * samples,
    )
    lanes = [joined] + [change_lane(joined, -steps) for steps in range(1, group)]
    half = nodes // 2
    share = group * mesh_rows
    columns, low, high = call(
        functools.partial(index_kernel, parts, mesh_rows),
        "index",
        [
            jax.ShapeDtypeStruct((nodes, 128), bf16),
            jax.ShapeDtypeStruct((half + 2 * fanout, width), bf16),
            jax.ShapeDtypeStruct((half, width), bf16),
        ],
        [where] + lanes,
        "w" + "v" * group,
        [pltpu.VMEM((fanout, nodes), jnp.int32)],
    )
    state_shape = jax.ShapeDtypeStruct((half, width), bf16)
    for layer in range(segments):
        at_segment, ends = min(layer, last), layer > last
        used = list(held) if layer <= last else came_weights
        role = (group, at_segment, samples if ends else 0, fanout, len(used))
        pieces = [jax.ShapeDtypeStruct((share, width), bf16)] * (half // share) if ends else [state_shape]
        scratch = [pltpu.VMEM((half, width), bf16)]
        arrives = 0 < layer <= last
        sender_low, *found = call(
            functools.partial(sender_kernel, group, at_segment, fanout if arrives else 0, half),
            "sender",
            [state_shape] + [jax.ShapeDtypeStruct((nodes, 128), bf16)] * arrives,
            [where, low] + used,
            "wv" + "v" * len(used),
        )
        columns = found[0] if arrives else columns
        tall = jax.ShapeDtypeStruct((half + 2 * fanout, width), bf16)
        sender, *first = call(
            functools.partial(first_kernel, *role),
            "first",
            [jax.ShapeDtypeStruct((nodes, width), bf16)] + ([tall] if layer < last else pieces),
            [where, columns, sender_low, low, high] + used,
            "wvvvv" + "v" * len(used),
            scratch,
        )
        pairs = [(owner(m, layer), owner(m, layer + 1)) for m in range(samples)]
        new_low = send(first[0], pairs) if layer < last else first[0]
        second = call(
            functools.partial(second_kernel, *role),
            "second",
            pieces,
            [where, columns, sender, low, high] + used,
            "wvvvv" + "v" * len(used),
            scratch,
        )
        low, high = new_low, send(second[0], pairs) if layer < last else second[0]
        if layer == 0:
            ready, table = call(
                prepare_kernel,
                "prepare",
                [
                    jax.ShapeDtypeStruct((grid_rows, width), jnp.float32),
                    jax.ShapeDtypeStruct((mesh_rows, grid_rows), bf16),
                ],
                [where, snapshots, w_embed, w_decode, mesh_grid.reshape(1, grid_rows)],
                "wvvvv",
                    )
            low, ready, table = lax.optimization_barrier((low, ready, table))
    each = samples // 2
    arrived = []
    for far, blocks in ((1, first), (0, second)):
        for turn, block in enumerate(blocks):
            pairs = [
                (owner(m, last), device(m, ((m // each ^ far) * each + turn) * group)) for m in range(samples)
            ]
            arrived.append(send(block, [pair for pair in pairs if pair[0] != pair[1]]))
    (crossed,) = call(
        functools.partial(far_kernel, group, samples, last),
        "far",
        [jax.ShapeDtypeStruct((share, width), bf16)],
        [where] + arrived[:each],
        "w" + "v" * each,
    )
    parts_of_block = call(
        functools.partial(near_kernel, group, samples, last),
        "near",
        [jax.ShapeDtypeStruct((mesh_rows, width), bf16)] * group,
        [where, crossed] + arrived[each:] + list(second),
        "w" + "v" * (1 + 2 * each),
    )
    handed = [parts_of_block[0]]
    for steps in range(1, group):
        handed.append(change_lane(parts_of_block[steps], steps))
    (prediction,) = call(
        decode_kernel,
        "decode",
        [jax.ShapeDtypeStruct((channels, grid_rows), bf16)],
        [where, ready, table, w_decode, w_output.T] + handed,
        "wvvvv" + "v" * group,
        [pltpu.VMEM((mesh_rows, width), bf16)],
    )
    return prediction.T.reshape(1, grid_rows, channels)


def chosen_plan(mesh, *arrays):
    segments, parts = mesh.shape["segment"], mesh.shape["dom"]
    samples, width = arrays[0].shape[0], arrays[1].shape[1]
    nodes = parts * arrays[9].shape[0]
    fits = samples == segments == 4 and parts % samples == 0 and parts > samples and nodes == width
    return (resident if fits else streamed)(*arrays)


def solution(mesh):
    return jax.shard_map(
        functools.partial(chosen_plan, mesh),
        mesh=mesh,
        in_specs=(
            P(None, "dom", None),
            P(),
            P("segment", None, None),
            P("segment", None, None),
            P("segment", None, None),
            P(),
            P(),
            P("dom"),
            P("dom"),
            P("dom", None),
            P(None, "dom"),
            P(None, "dom"),
        ),
        out_specs=P("segment", "dom", None),
        check_vma=False,
    )
```

```python
import functools

import jax
import jax.numpy as jnp
from jax import lax
from jax.experimental import pallas as pl
from jax.experimental.pallas import tpu as pltpu
from jax.sharding import PartitionSpec as P

epsilon = 1e-05
DIGIT = 256
VMEM = pl.BlockSpec(memory_space=pltpu.VMEM)
SMEM = pl.BlockSpec(memory_space=pltpu.SMEM)
HBM = pl.BlockSpec(memory_space=pltpu.HBM)


def from_behind(value, axis, steps):
    count = lax.axis_size(axis)
    pairs = [(source, (source + steps) % count) for source in range(count)]
    return lax.ppermute(value, axis, pairs)


def from_behind_2(block, axis, distance):
    devices = range(lax.axis_size(axis))
    route = [(i - distance, i) for i in devices if i - distance in devices]
    return lax.ppermute(block, axis, route)


def from_root(value, axis, source):
    kept = jnp.where(lax.axis_index(axis) == source, value, 0).astype(value.dtype)
    return lax.psum(kept, axis)


def rms_scale(values):
    return values * lax.rsqrt(jnp.mean(values * values, axis=-1, keepdims=True) + epsilon)


def streamed(
    grid_state,
    w_embed,
    w_project,
    w_message,
    w_update,
    w_decode,
    w_output,
    grid_mesh,
    mesh_grid,
    neighbors,
    send_rows,
    halo_count,
):
    segment_index = lax.axis_index("segment")
    segment_count = lax.axis_size("segment")
    final_segment = segment_count - 1
    samples, grid_rows, channels = grid_state.shape
    width = w_embed.shape[1]
    mesh_rows = neighbors.shape[0]
    fanout = neighbors.shape[1]
    halo_rows = send_rows.shape[1]
    share = samples // segment_count
    pool_table = (grid_mesh[None, :] == jnp.arange(mesh_rows, dtype=jnp.int32)[:, None]).astype(
        jnp.bfloat16
    )
    read_table = (mesh_grid[:, None] == jnp.arange(mesh_rows, dtype=jnp.int32)[None, :]).astype(
        jnp.bfloat16
    )
    valid_rows = jnp.arange(halo_rows, dtype=jnp.int32)[None, :] < halo_count[:, 0][:, None]
    source_rows = neighbors.reshape(mesh_rows * fanout)

    def embed_grid(snapshot):
        return jax.nn.silu(jnp.dot(snapshot, w_embed, preferred_element_type=jnp.float32)).astype(
            jnp.bfloat16
        )

    def encode(snapshot):
        latent = embed_grid(snapshot)
        pooled = jnp.dot(pool_table, latent, preferred_element_type=jnp.float32)
        return (rms_scale(pooled).astype(jnp.bfloat16), latent)

    def project(state, weights):
        projected = jnp.dot(state, weights[0], preferred_element_type=jnp.float32)
        return (projected[:, :width], projected[:, width:].astype(jnp.bfloat16))

    def renew(state, receiver, extended, weights):
        fetched = extended[source_rows].reshape(mesh_rows, fanout, width)
        edges = jax.nn.silu(receiver[:, None, :] + fetched.astype(jnp.float32)).astype(jnp.bfloat16)
        messages = jnp.dot(
            edges.reshape(mesh_rows * fanout, width), weights[1], preferred_element_type=jnp.float32
        )
        aggregate = (jnp.sum(messages.reshape(mesh_rows, fanout, width), axis=1) / fanout).astype(
            jnp.bfloat16
        )
        update = jax.nn.silu(
            jnp.dot(state, weights[2][:width], preferred_element_type=jnp.float32)
            + jnp.dot(aggregate, weights[2][width:], preferred_element_type=jnp.float32)
        )
        return (state.astype(jnp.float32) + rms_scale(update)).astype(jnp.bfloat16)

    def decode(state, latent):
        readout = jnp.dot(read_table, state, preferred_element_type=jnp.float32).astype(
            jnp.bfloat16
        )
        hidden = jax.nn.silu(
            jnp.dot(latent, w_decode[:width], preferred_element_type=jnp.float32)
            + jnp.dot(readout, w_decode[width:], preferred_element_type=jnp.float32)
        ).astype(jnp.bfloat16)
        return jnp.dot(hidden, w_output, preferred_element_type=jnp.float32).astype(jnp.bfloat16)

    own_weights = (w_project[0], w_message[0], w_update[0])
    empty_mesh = jnp.zeros((mesh_rows, width), jnp.bfloat16)
    empty_receiver = jnp.zeros((mesh_rows, width), jnp.float32)
    empty_grid = jnp.zeros((grid_rows, width), jnp.bfloat16)
    empty_output = jnp.zeros((grid_rows, channels), jnp.bfloat16)
    received = empty_mesh
    carried = {}
    results = [empty_output for sample in range(samples)]
    for moment in range(samples + final_segment):
        current = received
        if moment < samples:
            snapshot = grid_state[moment]
            started, latent = lax.cond(
                segment_index == 0, lambda: encode(snapshot), lambda: (empty_mesh, empty_grid)
            )
            current = jnp.where(segment_index == 0, started, received)
            carried[moment] = from_behind_2(latent, "segment", final_segment)
        active = (moment - segment_index >= 0) & (moment - segment_index < samples)
        receiver, outgoing = lax.cond(
            active, lambda: project(current, own_weights), lambda: (empty_receiver, empty_mesh)
        )
        picked = jnp.where(valid_rows[:, :, None], outgoing[send_rows], jnp.zeros((), jnp.bfloat16))
        arrived = [outgoing]
        for list_index, offset in enumerate((1, -1, 2, -2)):
            arrived.append(from_behind(picked[list_index], "dom", offset))
        extended = jnp.concatenate(arrived, axis=0)
        renewed = lax.cond(
            active, lambda: renew(current, receiver, extended, own_weights), lambda: empty_mesh
        )
        if moment >= final_segment:
            finished = moment - final_segment
            skipped = carried[finished]
            results[finished] = lax.cond(
                segment_index == final_segment,
                lambda: decode(renewed, skipped),
                lambda: empty_output,
            )
        if moment < samples + final_segment - 1:
            received = from_behind_2(renewed, "segment", 1)
    everything = from_root(jnp.stack(results), "segment", final_segment)
    return lax.dynamic_slice_in_dim(everything, segment_index * share, share, 0)


def silu_by_tanh(values):
    half = 0.5 * values
    return half + half * jnp.tanh(half)


def matmul(left, right):
    return jnp.dot(left, right, preferred_element_type=jnp.float32)


def matmul_nt(left, right):
    return lax.dot_general(left, right, (((1,), (1,)), ((), ())), preferred_element_type=jnp.float32)


def matmul_tn(left, right):
    return lax.dot_general(left, right, (((0,), (0,)), ((), ())), preferred_element_type=jnp.float32)


def place_of(where, group):
    return lax.div(where[1], group), lax.rem(where[1], group)


def owns(where, group, at_segment):
    return jnp.logical_and(where[0] == at_segment, lax.rem(where[1], group) == 0)


def fetch(sources, targets, semaphores):
    copies = [
        pltpu.make_async_copy(source, target, semaphores.at[place])
        for place, (source, target) in enumerate(zip(sources, targets))
    ]
    for copy in copies:
        copy.start()
    return copies


def encode_kernel(group, mesh_rows, fanout, lists, where, snapshots, w_embed, packed, *refs):
    payloads, latent = refs[:-1], refs[-1]
    chip, _ = place_of(where, group)
    neighbors = packed[:fanout, :mesh_rows]
    grid_rows = snapshots.shape[2]
    grid_mesh = packed[fanout + lists : fanout + lists + 1, :grid_rows]
    counts = packed[fanout + lists + 1 : fanout + lists + 2, :lists]
    width = w_embed.shape[1]
    for place in range(snapshots.shape[0]):
        found = silu_by_tanh(matmul_tn(snapshots[place], w_embed[...])).astype(jnp.bfloat16)
        latent[place * grid_rows : (place + 1) * grid_rows, :] = found
    table = lax.broadcasted_iota(jnp.int32, (mesh_rows, grid_rows), 0) == grid_mesh
    table = jnp.where(table, 1.0, 0.0).astype(jnp.bfloat16)
    block = neighbors // mesh_rows
    row = neighbors - block * mesh_rows
    halo_rows = mesh_rows
    position = lax.broadcasted_iota(jnp.int32, (1, halo_rows), 1)
    rows = []
    for list_index in range(lists):
        kept = position < counts[:, list_index : list_index + 1]
        listed = packed[fanout + list_index : fanout + list_index + 1, :halo_rows]
        rows.append(jnp.where(kept, listed, mesh_rows))
    rows.append(jnp.zeros((fanout - lists, halo_rows), jnp.int32))
    filler = jnp.zeros((fanout, 128 - mesh_rows), jnp.int32)
    pieces = [block, filler, row, filler, jnp.concatenate(rows, axis=0), filler]
    coded = jnp.concatenate(pieces + [jnp.zeros((fanout, width - 384), jnp.int32)], axis=1)
    coded = jnp.concatenate([coded, jnp.zeros_like(coded)], axis=0)
    coded = coded.astype(jnp.float32).astype(jnp.bfloat16)
    for turn, payload in enumerate(payloads):
        start = pl.multiple_of(jnp.bitwise_xor(chip, turn) * grid_rows, grid_rows)
        pooled = matmul(table, latent[pl.ds(start, grid_rows), :])
        payload[:mesh_rows, :] = rms_scale(pooled).astype(jnp.bfloat16)
        payload[mesh_rows:, :] = coded


def join_kernel(*refs):
    payloads, joined = refs[:-1], refs[-1]
    rows = payloads[0].shape[0]
    for place, payload in enumerate(payloads):
        joined[place * rows : (place + 1) * rows, :] = payload[...]


def columns_of(names):
    fanout, nodes = names.shape
    tile = min(nodes, DIGIT)
    rows = [names - number * tile for number in range(nodes // tile)]
    rows.append(jnp.zeros((128 - fanout * len(rows), nodes), jnp.float32))
    return jnp.transpose(jnp.concatenate(rows, axis=0)).astype(jnp.bfloat16)


def index_kernel(parts, mesh_rows, where, *refs):
    lanes, (columns_out, low, *high), index_out = refs[:-5], refs[-5:-1], refs[-1]
    nodes = columns_out.shape[0]
    group = len(lanes)
    rows = lanes[0].shape[0] // (parts // group)
    chip, _ = place_of(where, group)

    @pl.when(owns(where, group, 0))
    def _():
        tables = []
        for part in range(parts):
            lane, turn = lanes[part % group], jnp.bitwise_xor(chip, part // group)
            base = pl.multiple_of(turn * rows, 16)
            piece, spot = low, part * mesh_rows
            if part >= parts // 2:
                piece, spot = high[part * 4 // parts - 2], part % (parts // 4) * mesh_rows
            piece[spot : spot + mesh_rows, :] = lane[pl.ds(base, mesh_rows), :]
            base = pl.multiple_of(turn * rows + mesh_rows, 16)
            coded = lane[pl.ds(base, rows - mesh_rows), :384].astype(jnp.float32).astype(jnp.int32)
            tables.append(coded[: coded.shape[0] // 2])
        fanout = tables[0].shape[0]
        for part in range(parts):
            block = tables[part][:, :128]
            row = tables[part][:, 128:256]
            found = part * mesh_rows + row
            for list_index, offset in enumerate((-1, 1, -2, 2)):
                source = (part + offset) % parts
                lists = tables[source][list_index : list_index + 1, 256:384]
                lists = jnp.broadcast_to(lists, (fanout, 128))
                picked = jnp.take_along_axis(lists, row, axis=1)
                picked = jnp.where(picked == mesh_rows, parts * mesh_rows, source * mesh_rows + picked)
                found = jnp.where(block == list_index + 1, picked, found)
            index_out[:, part * mesh_rows : (part + 1) * mesh_rows] = found[:, :mesh_rows]
        names = index_out[...]
        high_digit = names // DIGIT
        digits = jnp.concatenate([high_digit, names - high_digit * DIGIT], axis=0)
        low[parts // 2 * mesh_rows :, :] = digits.astype(jnp.float32).astype(jnp.bfloat16)
        columns_out[...] = columns_of(names.astype(jnp.float32))


def hold_kernel(w_project, w_message, w_update, receive, send, own, edges, message, update, semaphores):
    width = own.shape[0]
    sources = [
        w_message.at[0],
        w_update.at[0, width:],
        w_project.at[0, :, :width],
        w_project.at[0, :, width:],
        w_update.at[0, :width],
    ]
    copies = fetch(sources, [message, update, receive, send, own], semaphores)
    copies[0].wait()
    copies[1].wait()
    edges[...] = matmul(message[...], update[...]).astype(jnp.bfloat16)
    for copy in copies[2:]:
        copy.wait()


def pack_kernel(group, at_segment, where, own, edges, pair):
    @pl.when(owns(where, group, at_segment))
    def _():
        pair[0] = own[...]
        pair[1] = edges[...]


def blocks_of(weights):
    if len(weights) == 4:
        return [block[...] for block in weights]
    w_project, pair = weights
    width = pair.shape[1]
    return w_project[0, :, :width], w_project[0, :, width:], pair[0], pair[1]


def renew(fanout, columns, sender, own, weights):
    chunk, width = own.shape
    nodes = sender.shape[0]
    tile = min(nodes, DIGIT)
    names = lax.broadcasted_iota(jnp.int32, (chunk, tile), 1).astype(jnp.float32).astype(jnp.bfloat16)
    one_half = jnp.full((chunk, tile), 0.5, jnp.bfloat16)
    none = jnp.zeros((chunk, tile), jnp.bfloat16)
    w_receive, _, w_own, w_edges = blocks_of(weights)
    receiver = 0.5 * matmul(own, w_receive)
    update = matmul(own, w_own)
    total = jnp.zeros((chunk, width), jnp.float32)
    for k in range(fanout):
        hits = []
        for number in range(nodes // tile):
            lane = number * fanout + k
            hits.append(jnp.where(columns[:, lane : lane + 1] == names, one_half, none))
        half = receiver + matmul(jnp.concatenate(hits, axis=1), sender)
        total = total + (half + half * jnp.tanh(half))
    gathered = (total * (1.0 / fanout)).astype(jnp.bfloat16)
    update = silu_by_tanh(update + matmul(gathered, w_edges))
    return (own.astype(jnp.float32) + rms_scale(update)).astype(jnp.bfloat16)


def write_pieces(pieces, value):
    rows = value.shape[0] // len(pieces)
    for place, piece in enumerate(pieces):
        piece[:rows, :] = value[place * rows : (place + 1) * rows]


def sender_kernel(group, at_segment, fanout, rows, where, state, *refs):
    weights, sender, columns = (refs[:-2], *refs[-2:]) if fanout else (refs[:-1], refs[-1], None)

    @pl.when(owns(where, group, at_segment))
    def _():
        sender[...] = matmul(state[:rows, :], blocks_of(weights)[1]).astype(jnp.bfloat16)
        if fanout:
            digits = state[rows:, :].astype(jnp.float32)
            columns[...] = columns_of(digits[:fanout] * DIGIT + digits[fanout:])


def take(parts, own):
    start = 0
    for part in parts:
        rows = min(part.shape[0], own.shape[0] - start)
        own[start : start + rows, :] = part[:rows, :]
        start += rows


def choose(where, group, chips, far, state, own):
    half = own.shape[0]
    chip, _ = place_of(where, group)
    upper = (chip < chips // 2) if far else (chip >= chips // 2)

    @pl.when(upper)
    def _():
        take(state[1:], own)

    @pl.when(jnp.logical_not(upper))
    def _():
        take(state[:1], own)

    return pl.multiple_of(jnp.where(upper, half, 0), half)


def first_kernel(group, at_segment, chips, fanout, counts, where, columns, *refs):
    parts, given = counts
    senders, refs = refs[: parts - 1], refs[parts - 1 :]
    state, weights, refs = refs[:parts], refs[parts : parts + given], refs[parts + given :]
    sender, pieces, own = refs[0], refs[1:-1], refs[-1]
    rows = own.shape[0]

    @pl.when(owns(where, group, at_segment))
    def _():
        start = 0
        for part in senders:
            sender[start : start + part.shape[0], :] = part[...]
            start += part.shape[0]
        sender[start:, :] = matmul(state[-1][...], blocks_of(weights)[1]).astype(jnp.bfloat16)
        if chips:
            start = choose(where, group, chips, True, state, own)
        else:
            start = 0
            take(state[:1], own)
        lanes = columns[pl.ds(start, rows), :]
        write_pieces(pieces, renew(fanout, lanes, sender[...], own[...], weights))
        if pieces[0].shape[0] > rows:
            pieces[0][rows:, :] = state[0][rows:, :]


def next_kernel(group, at_segment, chips, fanout, counts, start, where, columns, sender, *refs):
    parts, given = counts
    state, weights, refs = refs[:parts], refs[parts : parts + given], refs[parts + given :]
    pieces, own = refs[:-1], refs[-1]
    rows = own.shape[0]

    @pl.when(owns(where, group, at_segment))
    def _():
        if chips:
            first = choose(where, group, chips, False, state, own)
        else:
            first = start
            take(state, own)
        lanes = columns[pl.ds(first, rows), :]
        write_pieces(pieces, renew(fanout, lanes, sender[...], own[...], weights))


def arrival(where, group, chips, last):
    each = chips // 2
    segment = where[0]
    chip, _ = place_of(where, group)
    crosses = lax.div(chip, each) != lax.div(segment, each)
    return crosses, jnp.logical_and(segment == last, chip == last), lax.rem(chip, each)


def far_kernel(group, chips, last, where, *refs):
    far, out = refs[:-1], refs[-1]
    crosses, _, spot = arrival(where, group, chips, last)
    for number, block in enumerate(far):

        @pl.when(jnp.logical_and(crosses, spot == number))
        def _(block=block):
            out[...] = block[...]


def near_kernel(group, chips, last, where, crossed, *refs):
    each = chips // 2
    near, kept, outs = refs[:each], refs[each : 2 * each], refs[2 * each :]
    rows = outs[0].shape[0]
    crosses, stays, spot = arrival(where, group, chips, last)
    arrives = jnp.logical_not(jnp.logical_or(crosses, stays))

    def give(block):
        for place, out in enumerate(outs):
            out[...] = block[place * rows : (place + 1) * rows, :]

    @pl.when(crosses)
    def _():
        give(crossed)

    for number in range(each):
        for blocks, chosen in ((near, arrives), (kept, stays)):

            @pl.when(jnp.logical_and(chosen, spot == number))
            def _(block=blocks[number]):
                give(block)


def prepare_kernel(where, snapshots, w_embed, w_decode, mesh_grid, ready, table_out):
    snapshot = snapshots[where[0]]
    latent = silu_by_tanh(matmul_tn(snapshot, w_embed[...])).astype(jnp.bfloat16)
    ready[...] = matmul(latent, w_decode[: latent.shape[1], :])
    mesh_rows, grid_rows = table_out.shape
    table = lax.broadcasted_iota(jnp.int32, (mesh_rows, grid_rows), 0) == mesh_grid[...]
    table_out[...] = jnp.where(table, 1.0, 0.0).astype(jnp.bfloat16)


def decode_kernel(where, ready, table, w_decode, w_output, *refs):
    blocks, out, state = refs[:-2], refs[-2], refs[-1]
    width = ready.shape[1]
    _, lane = place_of(where, len(blocks))
    for number, block in enumerate(blocks):

        @pl.when(lane == number)
        def _(block=block):
            state[...] = block[...]

    readout = matmul_tn(table[...], state[...]).astype(jnp.bfloat16)
    hidden = silu_by_tanh(ready[...] + matmul(readout, w_decode[width:, :])).astype(jnp.bfloat16)
    out[...] = matmul_nt(w_output[...], hidden).astype(jnp.bfloat16)


def call(kernel, name, shapes, inputs, places, scratch=(), room=16):
    specs, given = [], []
    for value, place in zip(inputs, places):
        specs += [SMEM] * 2 if place == "w" else [VMEM if place == "v" else HBM]
        given += list(value) if place == "w" else [value]
    moved = sum(value.size * value.dtype.itemsize for value in given + list(shapes))

    def located(segment, place, *refs):
        kernel((segment[0], place[0]), *refs)

    return pl.pallas_call(
        located if places[0] == "w" else kernel,
        out_shape=shapes,
        in_specs=specs,
        out_specs=[VMEM] * len(shapes),
        scratch_shapes=list(scratch),
        name=name,
        compiler_params=pltpu.CompilerParams(vmem_limit_bytes=room * 1024 * 1024),
        cost_estimate=pl.CostEstimate(flops=0, bytes_accessed=moved, transcendentals=0),
    )(*given)


def every_device(pairs, count, group):
    onward = dict(pairs)
    reached = set(onward.values())
    for first in [source for source in onward if source not in reached]:
        last = first
        while last in onward:
            last = onward[last]
        onward.update({last: last + group - 1, last + group - 1: first + group - 1, first + group - 1: first})
    alone = []
    for at in range(0, count, group):
        rest = [lane for lane in range(at, at + group) if lane not in onward]
        if len(rest) > 1:
            onward.update(zip(rest, rest[1:] + rest[:1]))
        else:
            alone += rest
    if len(alone) == 1:
        before = next(at for at in onward if at % group and onward[at] % group == 0)
        onward.update({before: alone[0], alone[0]: onward[before]})
    else:
        onward.update(zip(alone, alone[1:] + alone[:1]))
    return sorted(onward.items())


def resident(
    grid_state,
    w_embed,
    w_project,
    w_message,
    w_update,
    w_decode,
    w_output,
    grid_mesh,
    mesh_grid,
    neighbors,
    send_rows,
    halo_count,
):
    segment = lax.axis_index("segment")
    place = lax.axis_index("dom")
    segments = lax.axis_size("segment")
    parts = lax.axis_size("dom")
    samples, grid_rows, channels = grid_state.shape
    width = w_embed.shape[1]
    mesh_rows, fanout = neighbors.shape
    nodes = parts * mesh_rows
    group = parts // samples
    bf16 = jnp.bfloat16

    def device(at_segment, at_dom):
        return at_segment * parts + at_dom % parts

    def send(value, pairs):
        return lax.ppermute(value, ("segment", "dom"), every_device(pairs, segments * parts, group))

    def to_chip(value, steps):
        giver = steps - 1
        pairs = []
        for at in range(segments):
            for dom in range(parts):
                chip, lane = divmod(dom, group)
                across = (chip ^ steps) * group + lane
                if at == giver:
                    pairs.append((device(at, dom), device(0, across)))
                elif at == 0:
                    pairs.append((device(at, dom), device(giver, dom)))
                else:
                    pairs.append((device(at, dom), device(at, chip * group + (lane + 1) % group)))
        return lax.ppermute(value, ("segment", "dom"), pairs)

    def change_lane(value, steps):
        pairs = [(at, at - at % group + (at + steps) % group) for at in range(parts)]
        return lax.ppermute(value, "dom", pairs)

    def owner(m, at_segment):
        return device(at_segment, m * group)

    own_segment, own_place, w_project = lax.optimization_barrier(
        (segment.reshape(1), place.reshape(1), w_project)
    )
    where = (own_segment, own_place)
    weights = [w_project, w_message, w_update]
    last = segments - 2
    pairs = [(owner(m, last + 1), owner(m, last)) for m in range(samples)]
    came = [send(w_project, pairs)]
    snapshots = jnp.transpose(grid_state, (0, 2, 1))
    lists = send_rows.shape[0]

    def rows_of(value):
        return jnp.pad(value, ((0, 0), (0, 128 - value.shape[1])))

    packed = jnp.concatenate(
        [
            rows_of(neighbors.T),
            rows_of(send_rows),
            rows_of(grid_mesh.reshape(1, grid_rows)),
            rows_of(halo_count.reshape(1, lists)),
        ],
        axis=0,
    )
    payloads = call(
        functools.partial(encode_kernel, group, mesh_rows, fanout, lists),
        "encode",
        [jax.ShapeDtypeStruct((mesh_rows + 2 * fanout, width), bf16)] * samples,
        [where, snapshots, w_embed, packed],
        "wvvv",
        [pltpu.VMEM((samples * grid_rows, width), bf16)],
    )
    held = call(
        hold_kernel,
        "hold",
        [jax.ShapeDtypeStruct((width, width), bf16)] * 4,
        weights,
        "hhh",
        [pltpu.VMEM((width, width), bf16)] * 2 + [pltpu.SemaphoreType.DMA((5,))],
    )
    own_payload, *held = lax.optimization_barrier((payloads[0], *held))
    arrived = [own_payload] + [to_chip(payloads[turn], turn) for turn in range(1, samples)]
    (joined,) = call(
        join_kernel,
        "join",
        [jax.ShapeDtypeStruct((samples * (mesh_rows + 2 * fanout), width), bf16)],
        arrived,
        "v" * samples,
    )
    lanes = [joined] + [change_lane(joined, -steps) for steps in range(1, group)]
    half, share = nodes // 2, group * mesh_rows
    tall, short = [jax.ShapeDtypeStruct((rows, width), bf16) for rows in (half + 2 * fanout, share)]
    columns, *state = call(
        functools.partial(index_kernel, parts, mesh_rows),
        "index",
        [jax.ShapeDtypeStruct((nodes, 128), bf16), tall, short, short],
        [where] + lanes,
        "w" + "v" * group,
        [pltpu.VMEM((fanout, nodes), jnp.int32)],
    )
    columns, *held[2:] = lax.optimization_barrier((columns, *held[2:]))
    (pair,) = call(
        functools.partial(pack_kernel, group, last + 1),
        "pack",
        [jax.ShapeDtypeStruct((2, width, width), bf16)],
        [where] + held[2:],
        "wvv",
    )
    came.append(send(pair, pairs))
    for layer in range(segments):
        at_segment, ends = min(layer, last), layer > last
        used = list(held) if layer <= last else came
        role = (group, at_segment, samples if ends else 0, fanout, (len(state), len(used)))
        arrives = 0 < layer <= last
        senders = []
        for place_in_state, part in enumerate(state[:-1]):
            if senders:
                part, senders[-1] = lax.optimization_barrier((part, senders[-1]))
            rows = min(part.shape[0], half)
            coded = part.shape[0] > rows and arrives
            found = call(
                functools.partial(sender_kernel, group, at_segment, fanout if coded else 0, rows),
                "sender",
                [jax.ShapeDtypeStruct((rows, width), bf16)]
                + [jax.ShapeDtypeStruct((nodes, 128), bf16)] * coded,
                [where, part] + used,
                "wv" + "v" * len(used),
            )
            senders.append(found[0])
            columns = found[1] if coded else columns
        if layer < last:
            steps = [[tall], [short], [short]]
        elif layer == last:
            steps = [[jax.ShapeDtypeStruct((half, width), bf16)], [short, short]]
        else:
            steps = [[short, short], [short, short]]
        pairs = [(owner(m, layer), owner(m, layer + 1)) for m in range(samples)]
        renewed, start = [], 0
        for step, pieces in enumerate(steps):
            rows = min(sum(piece.shape[0] for piece in pieces), half)
            scratch = [pltpu.VMEM((rows, width), bf16)]
            if step == 0:
                sender, *made = call(
                    functools.partial(first_kernel, *role),
                    "first",
                    [jax.ShapeDtypeStruct((nodes, width), bf16)] + pieces,
                    [where, columns] + senders + state + used,
                    "w" + "v" * (2 * len(state) + len(used)),
                    scratch,
                )
            else:
                parts_used = state if ends else state[1:] if layer == last else state[step : step + 1]
                made = call(
                    functools.partial(next_kernel, *role[:-1], (len(parts_used), len(used)), start),
                    "next",
                    pieces,
                    [where, columns, sender] + parts_used + used,
                    "w" + "v" * (2 + len(parts_used) + len(used)),
                    scratch,
                )
            renewed += [send(piece, pairs) for piece in made] if layer < last else list(made)
            start += rows
        state = renewed
        if layer == 0:
            ready, table = call(
                prepare_kernel,
                "prepare",
                [
                    jax.ShapeDtypeStruct((grid_rows, width), jnp.float32),
                    jax.ShapeDtypeStruct((mesh_rows, grid_rows), bf16),
                ],
                [where, snapshots, w_embed, w_decode, mesh_grid.reshape(1, grid_rows)],
                "wvvvv",
                    )
            state[0], ready, table = lax.optimization_barrier((state[0], ready, table))
    each = samples // 2
    arrived = []
    for far, blocks in ((1, state[:each]), (0, state[each:])):
        for turn, block in enumerate(blocks):
            pairs = [
                (owner(m, last), device(m, ((m // each ^ far) * each + turn) * group)) for m in range(samples)
            ]
            arrived.append(send(block, [pair for pair in pairs if pair[0] != pair[1]]))
    (crossed,) = call(
        functools.partial(far_kernel, group, samples, last),
        "far",
        [jax.ShapeDtypeStruct((share, width), bf16)],
        [where] + arrived[:each],
        "w" + "v" * each,
    )
    parts_of_block = call(
        functools.partial(near_kernel, group, samples, last),
        "near",
        [jax.ShapeDtypeStruct((mesh_rows, width), bf16)] * group,
        [where, crossed] + arrived[each:] + state[each:],
        "w" + "v" * (1 + 2 * each),
    )
    handed = [parts_of_block[0]]
    for steps in range(1, group):
        handed.append(change_lane(parts_of_block[steps], steps))
    (prediction,) = call(
        decode_kernel,
        "decode",
        [jax.ShapeDtypeStruct((channels, grid_rows), bf16)],
        [where, ready, table, w_decode, w_output.T] + handed,
        "wvvvv" + "v" * group,
        [pltpu.VMEM((mesh_rows, width), bf16)],
    )
    return prediction.T.reshape(1, grid_rows, channels)


def chosen_plan(mesh, *arrays):
    segments, parts = mesh.shape["segment"], mesh.shape["dom"]
    samples, width = arrays[0].shape[0], arrays[1].shape[1]
    nodes = parts * arrays[9].shape[0]
    fits = samples == segments == 4 and parts % samples == 0 and parts > samples and nodes == width
    return (resident if fits else streamed)(*arrays)


def solution(mesh):
    return jax.shard_map(
        functools.partial(chosen_plan, mesh),
        mesh=mesh,
        in_specs=(
            P(None, "dom", None),
            P(),
            P("segment", None, None),
            P("segment", None, None),
            P("segment", None, None),
            P(),
            P(),
            P("dom"),
            P("dom"),
            P("dom", None),
            P(None, "dom"),
            P(None, "dom"),
        ),
        out_specs=P("segment", "dom", None),
        check_vma=False,
    )
```

```python
import functools

import jax
import jax.numpy as jnp
from jax import lax
from jax.experimental import pallas as pl
from jax.experimental.pallas import tpu as pltpu
from jax.sharding import PartitionSpec as P

epsilon = 1e-05
DIGIT = 256
VMEM = pl.BlockSpec(memory_space=pltpu.VMEM)
SMEM = pl.BlockSpec(memory_space=pltpu.SMEM)
HBM = pl.BlockSpec(memory_space=pltpu.HBM)


def from_behind(value, axis, steps):
    count = lax.axis_size(axis)
    pairs = [(source, (source + steps) % count) for source in range(count)]
    return lax.ppermute(value, axis, pairs)


def from_behind_2(block, axis, distance):
    devices = range(lax.axis_size(axis))
    route = [(i - distance, i) for i in devices if i - distance in devices]
    return lax.ppermute(block, axis, route)


def from_root(value, axis, source):
    kept = jnp.where(lax.axis_index(axis) == source, value, 0).astype(value.dtype)
    return lax.psum(kept, axis)


def rms_scale(values):
    return values * lax.rsqrt(jnp.mean(values * values, axis=-1, keepdims=True) + epsilon)


def streamed(
    grid_state,
    w_embed,
    w_project,
    w_message,
    w_update,
    w_decode,
    w_output,
    grid_mesh,
    mesh_grid,
    neighbors,
    send_rows,
    halo_count,
):
    segment_index = lax.axis_index("segment")
    segment_count = lax.axis_size("segment")
    final_segment = segment_count - 1
    samples, grid_rows, channels = grid_state.shape
    width = w_embed.shape[1]
    mesh_rows = neighbors.shape[0]
    fanout = neighbors.shape[1]
    halo_rows = send_rows.shape[1]
    share = samples // segment_count
    pool_table = (grid_mesh[None, :] == jnp.arange(mesh_rows, dtype=jnp.int32)[:, None]).astype(
        jnp.bfloat16
    )
    read_table = (mesh_grid[:, None] == jnp.arange(mesh_rows, dtype=jnp.int32)[None, :]).astype(
        jnp.bfloat16
    )
    valid_rows = jnp.arange(halo_rows, dtype=jnp.int32)[None, :] < halo_count[:, 0][:, None]
    source_rows = neighbors.reshape(mesh_rows * fanout)

    def embed_grid(snapshot):
        return jax.nn.silu(jnp.dot(snapshot, w_embed, preferred_element_type=jnp.float32)).astype(
            jnp.bfloat16
        )

    def encode(snapshot):
        latent = embed_grid(snapshot)
        pooled = jnp.dot(pool_table, latent, preferred_element_type=jnp.float32)
        return (rms_scale(pooled).astype(jnp.bfloat16), latent)

    def project(state, weights):
        projected = jnp.dot(state, weights[0], preferred_element_type=jnp.float32)
        return (projected[:, :width], projected[:, width:].astype(jnp.bfloat16))

    def renew(state, receiver, extended, weights):
        fetched = extended[source_rows].reshape(mesh_rows, fanout, width)
        edges = jax.nn.silu(receiver[:, None, :] + fetched.astype(jnp.float32)).astype(jnp.bfloat16)
        messages = jnp.dot(
            edges.reshape(mesh_rows * fanout, width), weights[1], preferred_element_type=jnp.float32
        )
        aggregate = (jnp.sum(messages.reshape(mesh_rows, fanout, width), axis=1) / fanout).astype(
            jnp.bfloat16
        )
        update = jax.nn.silu(
            jnp.dot(state, weights[2][:width], preferred_element_type=jnp.float32)
            + jnp.dot(aggregate, weights[2][width:], preferred_element_type=jnp.float32)
        )
        return (state.astype(jnp.float32) + rms_scale(update)).astype(jnp.bfloat16)

    def decode(state, latent):
        readout = jnp.dot(read_table, state, preferred_element_type=jnp.float32).astype(
            jnp.bfloat16
        )
        hidden = jax.nn.silu(
            jnp.dot(latent, w_decode[:width], preferred_element_type=jnp.float32)
            + jnp.dot(readout, w_decode[width:], preferred_element_type=jnp.float32)
        ).astype(jnp.bfloat16)
        return jnp.dot(hidden, w_output, preferred_element_type=jnp.float32).astype(jnp.bfloat16)

    own_weights = (w_project[0], w_message[0], w_update[0])
    empty_mesh = jnp.zeros((mesh_rows, width), jnp.bfloat16)
    empty_receiver = jnp.zeros((mesh_rows, width), jnp.float32)
    empty_grid = jnp.zeros((grid_rows, width), jnp.bfloat16)
    empty_output = jnp.zeros((grid_rows, channels), jnp.bfloat16)
    received = empty_mesh
    carried = {}
    results = [empty_output for sample in range(samples)]
    for moment in range(samples + final_segment):
        current = received
        if moment < samples:
            snapshot = grid_state[moment]
            started, latent = lax.cond(
                segment_index == 0, lambda: encode(snapshot), lambda: (empty_mesh, empty_grid)
            )
            current = jnp.where(segment_index == 0, started, received)
            carried[moment] = from_behind_2(latent, "segment", final_segment)
        active = (moment - segment_index >= 0) & (moment - segment_index < samples)
        receiver, outgoing = lax.cond(
            active, lambda: project(current, own_weights), lambda: (empty_receiver, empty_mesh)
        )
        picked = jnp.where(valid_rows[:, :, None], outgoing[send_rows], jnp.zeros((), jnp.bfloat16))
        arrived = [outgoing]
        for list_index, offset in enumerate((1, -1, 2, -2)):
            arrived.append(from_behind(picked[list_index], "dom", offset))
        extended = jnp.concatenate(arrived, axis=0)
        renewed = lax.cond(
            active, lambda: renew(current, receiver, extended, own_weights), lambda: empty_mesh
        )
        if moment >= final_segment:
            finished = moment - final_segment
            skipped = carried[finished]
            results[finished] = lax.cond(
                segment_index == final_segment,
                lambda: decode(renewed, skipped),
                lambda: empty_output,
            )
        if moment < samples + final_segment - 1:
            received = from_behind_2(renewed, "segment", 1)
    everything = from_root(jnp.stack(results), "segment", final_segment)
    return lax.dynamic_slice_in_dim(everything, segment_index * share, share, 0)


def silu_by_tanh(values):
    half = 0.5 * values
    return half + half * jnp.tanh(half)


def matmul(left, right):
    return jnp.dot(left, right, preferred_element_type=jnp.float32)


def matmul_nt(left, right):
    return lax.dot_general(left, right, (((1,), (1,)), ((), ())), preferred_element_type=jnp.float32)


def matmul_tn(left, right):
    return lax.dot_general(left, right, (((0,), (0,)), ((), ())), preferred_element_type=jnp.float32)


def place_of(where, group):
    return lax.div(where[1], group), lax.rem(where[1], group)


def owns(where, group, at_segment):
    return jnp.logical_and(where[0] == at_segment, lax.rem(where[1], group) == 0)


def fetch(sources, targets, semaphores):
    copies = [
        pltpu.make_async_copy(source, target, semaphores.at[place])
        for place, (source, target) in enumerate(zip(sources, targets))
    ]
    for copy in copies:
        copy.start()
    return copies


def encode_kernel(group, mesh_rows, fanout, lists, where, snapshots, w_embed, packed, *refs):
    payloads, latent = refs[:-1], refs[-1]
    chip, _ = place_of(where, group)
    neighbors = packed[:fanout, :mesh_rows]
    grid_rows = snapshots.shape[2]
    grid_mesh = packed[fanout + lists : fanout + lists + 1, :grid_rows]
    counts = packed[fanout + lists + 1 : fanout + lists + 2, :lists]
    width = w_embed.shape[1]
    for place in range(snapshots.shape[0]):
        found = silu_by_tanh(matmul_tn(snapshots[place], w_embed[...])).astype(jnp.bfloat16)
        latent[place * grid_rows : (place + 1) * grid_rows, :] = found
    table = lax.broadcasted_iota(jnp.int32, (mesh_rows, grid_rows), 0) == grid_mesh
    table = jnp.where(table, 1.0, 0.0).astype(jnp.bfloat16)
    block = neighbors // mesh_rows
    row = neighbors - block * mesh_rows
    halo_rows = mesh_rows
    position = lax.broadcasted_iota(jnp.int32, (1, halo_rows), 1)
    rows = []
    for list_index in range(lists):
        kept = position < counts[:, list_index : list_index + 1]
        listed = packed[fanout + list_index : fanout + list_index + 1, :halo_rows]
        rows.append(jnp.where(kept, listed, mesh_rows))
    rows.append(jnp.zeros((fanout - lists, halo_rows), jnp.int32))
    filler = jnp.zeros((fanout, 128 - mesh_rows), jnp.int32)
    pieces = [block, filler, row, filler, jnp.concatenate(rows, axis=0), filler]
    coded = jnp.concatenate(pieces + [jnp.zeros((fanout, width - 384), jnp.int32)], axis=1)
    coded = jnp.concatenate([coded, jnp.zeros_like(coded)], axis=0)
    coded = coded.astype(jnp.float32).astype(jnp.bfloat16)
    for turn, payload in enumerate(payloads):
        start = pl.multiple_of(jnp.bitwise_xor(chip, turn) * grid_rows, grid_rows)
        pooled = matmul(table, latent[pl.ds(start, grid_rows), :])
        payload[:mesh_rows, :] = rms_scale(pooled).astype(jnp.bfloat16)
        payload[mesh_rows:, :] = coded


def join_kernel(*refs):
    payloads, joined = refs[:-1], refs[-1]
    rows = payloads[0].shape[0]
    for place, payload in enumerate(payloads):
        joined[place * rows : (place + 1) * rows, :] = payload[...]


def columns_of(names):
    fanout, nodes = names.shape
    tile = min(nodes, DIGIT)
    rows = [names - number * tile for number in range(nodes // tile)]
    rows.append(jnp.zeros((128 - fanout * len(rows), nodes), jnp.float32))
    return jnp.transpose(jnp.concatenate(rows, axis=0)).astype(jnp.bfloat16)


def index_kernel(parts, mesh_rows, where, *refs):
    lanes, (columns_out, codes, state), index_out = refs[:-4], refs[-4:-1], refs[-1]
    nodes = columns_out.shape[0]
    group = len(lanes)
    rows = lanes[0].shape[0] // (parts // group)
    chip, _ = place_of(where, group)

    @pl.when(owns(where, group, 0))
    def _():
        tables = []
        for part in range(parts):
            lane, turn = lanes[part % group], jnp.bitwise_xor(chip, part // group)
            base = pl.multiple_of(turn * rows, 16)
            state[part * mesh_rows : (part + 1) * mesh_rows, :] = lane[pl.ds(base, mesh_rows), :]
            base = pl.multiple_of(turn * rows + mesh_rows, 16)
            coded = lane[pl.ds(base, rows - mesh_rows), :384].astype(jnp.float32).astype(jnp.int32)
            tables.append(coded[: coded.shape[0] // 2])
        fanout = tables[0].shape[0]
        for part in range(parts):
            block = tables[part][:, :128]
            row = tables[part][:, 128:256]
            found = part * mesh_rows + row
            for list_index, offset in enumerate((-1, 1, -2, 2)):
                source = (part + offset) % parts
                lists = tables[source][list_index : list_index + 1, 256:384]
                lists = jnp.broadcast_to(lists, (fanout, 128))
                picked = jnp.take_along_axis(lists, row, axis=1)
                picked = jnp.where(picked == mesh_rows, parts * mesh_rows, source * mesh_rows + picked)
                found = jnp.where(block == list_index + 1, picked, found)
            index_out[:, part * mesh_rows : (part + 1) * mesh_rows] = found[:, :mesh_rows]
        names = index_out[...]
        high_digit = names // DIGIT
        digits = jnp.concatenate([high_digit, names - high_digit * DIGIT], axis=0)
        codes[...] = digits.astype(jnp.float32).astype(jnp.bfloat16)
        columns_out[...] = columns_of(names.astype(jnp.float32))


def pack_kernel(group, where, w_message, w_update, pair, message, update, semaphores):
    width = message.shape[0]

    @pl.when(jnp.logical_and(lax.rem(where[0], 2) == 1, lax.rem(where[1], group) == 0))
    def _():
        sources = [w_message.at[0], w_update.at[0, width:], w_update.at[0, :width]]
        copies = fetch(sources, [message, update, pair.at[0]], semaphores)
        copies[0].wait()
        copies[1].wait()
        pair[1] = matmul(message[...], update[...]).astype(jnp.bfloat16)
        copies[2].wait()


def hold_kernel(w_project, w_message, w_update, receive, send, pair, message, update, semaphores):
    width = receive.shape[0]
    sources = [
        w_message.at[0],
        w_update.at[0, width:],
        w_project.at[0, :, :width],
        w_project.at[0, :, width:],
        w_update.at[0, :width],
    ]
    copies = fetch(sources, [message, update, receive, send, pair.at[0]], semaphores)
    copies[0].wait()
    copies[1].wait()
    pair[1] = matmul(message[...], update[...]).astype(jnp.bfloat16)
    for copy in copies[2:]:
        copy.wait()


def sum_edges(fanout, columns, sender, own, w_receive):
    chunk, width = own.shape
    nodes = sender.shape[0]
    tile = min(nodes, DIGIT)
    names = lax.broadcasted_iota(jnp.int32, (chunk, tile), 1).astype(jnp.float32).astype(jnp.bfloat16)
    one_half = jnp.full((chunk, tile), 0.5, jnp.bfloat16)
    none = jnp.zeros((chunk, tile), jnp.bfloat16)
    receiver = 0.5 * matmul(own, w_receive)
    total = jnp.zeros((chunk, width), jnp.float32)
    for k in range(fanout):
        hits = []
        for number in range(nodes // tile):
            lane = number * fanout + k
            hits.append(jnp.where(columns[:, lane : lane + 1] == names, one_half, none))
        half = receiver + matmul(jnp.concatenate(hits, axis=1), sender)
        total = total + (half + half * jnp.tanh(half))
    return (total * (1.0 / fanout)).astype(jnp.bfloat16)


def update_nodes(own, gathered, w_own, w_edges):
    update = silu_by_tanh(matmul(own, w_own) + matmul(gathered, w_edges))
    return (own.astype(jnp.float32) + rms_scale(update)).astype(jnp.bfloat16)


def sender_kernel(group, at_segment, fanout, rows, where, state, w_send, sender, *columns):
    @pl.when(owns(where, group, at_segment))
    def _():
        sender[...] = matmul(state[:rows, :], w_send[...]).astype(jnp.bfloat16)
        if columns:
            digits = state[rows:, :].astype(jnp.float32)
            columns[0][...] = columns_of(digits[:fanout] * DIGIT + digits[fanout:])


def layer_kernel(group, at_segment, fanout, rows, where, columns, *refs):
    parts = len(rows)
    state, senders, refs = refs[:parts], refs[parts : 2 * parts - 1], refs[2 * parts - 1 :]
    (w_receive, w_send, pair), (renewed, whole, sender) = refs[:3], refs[3:]
    nodes = renewed.shape[0]
    chunk = min(nodes, 256)

    @pl.when(owns(where, group, at_segment))
    def _():
        start = 0
        for part, count in zip(state, rows):
            whole[start : start + count, :] = part[:count, :]
            start += count
        start = 0
        for part in senders:
            sender[start : start + part.shape[0], :] = part[...]
            start += part.shape[0]
        sender[start:, :] = matmul(whole[start:, :], w_send[...]).astype(jnp.bfloat16)
        for start in range(0, nodes, chunk):
            span = slice(start, start + chunk)
            gathered = sum_edges(fanout, columns[span, :], sender[...], whole[span, :], w_receive[...])
            renewed[span, :] = update_nodes(whole[span, :], gathered, pair[0], pair[1])


def edges_kernel(group, at_segment, fanout, where, columns, state, w_project, gathered, sender):
    nodes, width = state.shape
    chunk = min(nodes, 256)

    @pl.when(owns(where, group, at_segment))
    def _():
        sender[...] = matmul(state[...], w_project[0, :, width:]).astype(jnp.bfloat16)
        for start in range(0, nodes, chunk):
            span = slice(start, start + chunk)
            gathered[span, :] = sum_edges(
                fanout, columns[span, :], sender[...], state[span, :], w_project[0, :, :width]
            )


def update_kernel(group, at_segment, start, where, gathered, state, codes, pair, piece):
    rows = piece.shape[0] - (codes.shape[0] if start == 0 else 0)

    @pl.when(owns(where, group, at_segment))
    def _():
        span = slice(start, start + rows)
        piece[:rows, :] = update_nodes(state[span, :], gathered[span, :], pair[0], pair[1])
        if start == 0:
            piece[rows:, :] = codes[...]


def half_kernel(group, at_segment, chips, far, fanout, where, columns, state, *refs):
    senders, refs = (refs[:0], refs) if far else (refs[:1], refs[1:])
    (w_project, pair), outs = refs[:2], refs[2:]
    nodes, width = state.shape
    half = nodes // 2
    chip, _ = place_of(where, group)

    @pl.when(owns(where, group, at_segment))
    def _():
        pieces = outs
        if far:
            outs[0][...] = matmul(state[...], w_project[0, :, width:]).astype(jnp.bfloat16)
            pieces = outs[1:]
        sender = outs[0] if far else senders[0]
        upper = (chip < chips // 2) if far else (chip >= chips // 2)
        start = pl.multiple_of(jnp.where(upper, half, 0), half)
        own = state[pl.ds(start, half), :]
        gathered = sum_edges(
            fanout, columns[pl.ds(start, half), :], sender[...], own, w_project[0, :, :width]
        )
        write_pieces(pieces, update_nodes(own, gathered, pair[0], pair[1]))


def write_pieces(pieces, value):
    rows = value.shape[0] // len(pieces)
    for place, piece in enumerate(pieces):
        piece[:rows, :] = value[place * rows : (place + 1) * rows]


def arrival(where, group, chips, last):
    each = chips // 2
    segment = where[0]
    chip, _ = place_of(where, group)
    crosses = lax.div(chip, each) != lax.div(segment, each)
    return crosses, jnp.logical_and(segment == last, chip == last), lax.rem(chip, each)


def far_kernel(group, chips, last, where, *refs):
    far, out = refs[:-1], refs[-1]
    crosses, _, spot = arrival(where, group, chips, last)
    for number, block in enumerate(far):

        @pl.when(jnp.logical_and(crosses, spot == number))
        def _(block=block):
            out[...] = block[...]


def near_kernel(group, chips, last, where, crossed, *refs):
    each = chips // 2
    near, kept, outs = refs[:each], refs[each : 2 * each], refs[2 * each :]
    rows = outs[0].shape[0]
    crosses, stays, spot = arrival(where, group, chips, last)
    arrives = jnp.logical_not(jnp.logical_or(crosses, stays))

    def give(block):
        for place, out in enumerate(outs):
            out[...] = block[place * rows : (place + 1) * rows, :]

    @pl.when(crosses)
    def _():
        give(crossed)

    for number in range(each):
        for blocks, chosen in ((near, arrives), (kept, stays)):

            @pl.when(jnp.logical_and(chosen, spot == number))
            def _(block=blocks[number]):
                give(block)


def prepare_kernel(where, snapshots, w_embed, w_decode, mesh_grid, ready, table_out):
    snapshot = snapshots[where[0]]
    latent = silu_by_tanh(matmul_tn(snapshot, w_embed[...])).astype(jnp.bfloat16)
    ready[...] = matmul(latent, w_decode[: latent.shape[1], :])
    mesh_rows, grid_rows = table_out.shape
    table = lax.broadcasted_iota(jnp.int32, (mesh_rows, grid_rows), 0) == mesh_grid[...]
    table_out[...] = jnp.where(table, 1.0, 0.0).astype(jnp.bfloat16)


def decode_kernel(where, ready, table, w_decode, w_output, *refs):
    blocks, out, state = refs[:-2], refs[-2], refs[-1]
    width = ready.shape[1]
    _, lane = place_of(where, len(blocks))
    for number, block in enumerate(blocks):

        @pl.when(lane == number)
        def _(block=block):
            state[...] = block[...]

    readout = matmul_tn(table[...], state[...]).astype(jnp.bfloat16)
    hidden = silu_by_tanh(ready[...] + matmul(readout, w_decode[width:, :])).astype(jnp.bfloat16)
    out[...] = matmul_nt(w_output[...], hidden).astype(jnp.bfloat16)


def call(kernel, name, shapes, inputs, places, scratch=(), room=16, flops=0):
    specs, given = [], []
    for value, place in zip(inputs, places):
        specs += [SMEM] * 2 if place == "w" else [VMEM if place == "v" else HBM]
        given += list(value) if place == "w" else [value]
    moved = sum(value.size * value.dtype.itemsize for value in given + list(shapes))

    def located(segment, place, *refs):
        kernel((segment[0], place[0]), *refs)

    return pl.pallas_call(
        located if places[0] == "w" else kernel,
        out_shape=shapes,
        in_specs=specs,
        out_specs=[VMEM] * len(shapes),
        scratch_shapes=list(scratch),
        name=name,
        compiler_params=pltpu.CompilerParams(vmem_limit_bytes=room * 1024 * 1024),
        cost_estimate=pl.CostEstimate(flops=flops, bytes_accessed=moved, transcendentals=0),
    )(*given)


def every_device(pairs, count, group):
    onward = dict(pairs)
    reached = set(onward.values())
    for first in [source for source in onward if source not in reached]:
        last = first
        while last in onward:
            last = onward[last]
        onward.update({last: last + group - 1, last + group - 1: first + group - 1, first + group - 1: first})
    alone = []
    for at in range(0, count, group):
        rest = [lane for lane in range(at, at + group) if lane not in onward]
        if len(rest) > 1:
            onward.update(zip(rest, rest[1:] + rest[:1]))
        else:
            alone += rest
    if len(alone) == 1:
        before = next(at for at in onward if at % group and onward[at] % group == 0)
        onward.update({before: alone[0], alone[0]: onward[before]})
    else:
        onward.update(zip(alone, alone[1:] + alone[:1]))
    return sorted(onward.items())


def resident(
    grid_state,
    w_embed,
    w_project,
    w_message,
    w_update,
    w_decode,
    w_output,
    grid_mesh,
    mesh_grid,
    neighbors,
    send_rows,
    halo_count,
):
    segment = lax.axis_index("segment")
    place = lax.axis_index("dom")
    segments = lax.axis_size("segment")
    parts = lax.axis_size("dom")
    samples, grid_rows, channels = grid_state.shape
    width = w_embed.shape[1]
    mesh_rows, fanout = neighbors.shape
    nodes = parts * mesh_rows
    group = parts // samples
    bf16 = jnp.bfloat16

    def device(at_segment, at_dom):
        return at_segment * parts + at_dom % parts

    def send(value, pairs):
        return lax.ppermute(value, ("segment", "dom"), every_device(pairs, segments * parts, group))

    def to_chip(value, steps):
        giver = last if steps == samples - 1 else 0
        pairs = []
        for at in range(segments):
            for dom in range(parts):
                chip, lane = divmod(dom, group)
                across = (chip ^ steps) * group + lane
                if at == giver:
                    pairs.append((device(at, dom), device(0, across)))
                elif at == 0:
                    pairs.append((device(at, dom), device(giver, dom)))
                else:
                    pairs.append((device(at, dom), device(at, chip * group + (lane + 1) % group)))
        return lax.ppermute(value, ("segment", "dom"), pairs)

    def change_lane(value, steps):
        pairs = [(at, at - at % group + (at + steps) % group) for at in range(parts)]
        return lax.ppermute(value, "dom", pairs)

    def owner(m, at_segment):
        return device(at_segment, m * group)

    own_segment, own_place, w_project = lax.optimization_barrier(
        (segment.reshape(1), place.reshape(1), w_project)
    )
    where = (own_segment, own_place)
    weights = [w_project, w_message, w_update]
    last = segments - 2
    pairs = [(owner(m, at + 1), owner(m, at)) for m in range(samples) for at in range(0, segments, 2)]
    (pair,) = call(
        functools.partial(pack_kernel, group),
        "pack",
        [jax.ShapeDtypeStruct((2, width, width), bf16)],
        [where, w_message, w_update],
        "whh",
        [pltpu.VMEM((width, width), bf16)] * 2 + [pltpu.SemaphoreType.DMA((3,))],
        room=60,
    )
    came = [send(w_project, pairs), send(pair, pairs)]
    snapshots = jnp.transpose(grid_state, (0, 2, 1))
    lists = send_rows.shape[0]

    def rows_of(value):
        return jnp.pad(value, ((0, 0), (0, 128 - value.shape[1])))

    packed = jnp.concatenate(
        [
            rows_of(neighbors.T),
            rows_of(send_rows),
            rows_of(grid_mesh.reshape(1, grid_rows)),
            rows_of(halo_count.reshape(1, lists)),
        ],
        axis=0,
    )
    payloads = call(
        functools.partial(encode_kernel, group, mesh_rows, fanout, lists),
        "encode",
        [jax.ShapeDtypeStruct((mesh_rows + 2 * fanout, width), bf16)] * samples,
        [where, snapshots, w_embed, packed],
        "wvvv",
        [pltpu.VMEM((samples * grid_rows, width), bf16)],
    )
    held = call(
        hold_kernel,
        "hold",
        [jax.ShapeDtypeStruct((width, width), bf16)] * 2 + [jax.ShapeDtypeStruct((2, width, width), bf16)],
        weights,
        "hhh",
        [pltpu.VMEM((width, width), bf16)] * 2 + [pltpu.SemaphoreType.DMA((5,))],
    )
    own_payload, *held = lax.optimization_barrier((payloads[0], *held))
    arrived = [own_payload] + [to_chip(payloads[turn], turn) for turn in range(1, samples)]
    (joined,) = call(
        join_kernel,
        "join",
        [jax.ShapeDtypeStruct((samples * (mesh_rows + 2 * fanout), width), bf16)],
        arrived,
        "v" * samples,
    )
    lanes = [joined] + [change_lane(joined, -steps) for steps in range(1, group)]
    share = group * mesh_rows
    whole, short, tall = [
        jax.ShapeDtypeStruct((rows, width), bf16) for rows in (nodes, share, share + 2 * fanout)
    ]
    columns_shape = jax.ShapeDtypeStruct((nodes, 128), bf16)
    columns, codes, state = call(
        functools.partial(index_kernel, parts, mesh_rows),
        "index",
        [columns_shape, jax.ShapeDtypeStruct((2 * fanout, width), bf16), whole],
        [where] + lanes,
        "w" + "v" * group,
        [pltpu.VMEM((fanout, nodes), jnp.int32)],
    )
    both = [pltpu.VMEM((nodes, width), bf16)] * 2
    (state,) = call(
        functools.partial(layer_kernel, group, 0, fanout, (nodes,)),
        "layer",
        [whole],
        [where, columns, state] + list(held),
        "w" + "v" * 5,
        both,
    )
    (gathered,) = call(
        functools.partial(edges_kernel, group, 0, fanout),
        "edges",
        [whole],
        [where, columns, state, came[0]],
        "wvvv",
        both[:1],
    )
    pairs = [(owner(m, 0), owner(m, last)) for m in range(samples)]
    pieces, senders = [], []
    for start in range(0, nodes, share):
        (piece,) = call(
            functools.partial(update_kernel, group, 0, start),
            "update",
            [short if start else tall],
            [where, gathered, state, codes, came[1]],
            "wvvvv",
        )
        pieces.append(send(piece, pairs))
    ready, table = call(
        prepare_kernel,
        "prepare",
        [
            jax.ShapeDtypeStruct((grid_rows, width), jnp.float32),
            jax.ShapeDtypeStruct((mesh_rows, grid_rows), bf16),
        ],
        [where, snapshots, w_embed, w_decode, mesh_grid.reshape(1, grid_rows)],
        "wvvvv",
    )
    pieces[0], ready, table = lax.optimization_barrier((pieces[0], ready, table))
    for piece in pieces[:-1]:
        if senders:
            piece, senders[-1] = lax.optimization_barrier((piece, senders[-1]))
        sender, *found = call(
            functools.partial(sender_kernel, group, last, fanout, share),
            "sender",
            [short] + [columns_shape] * (not senders),
            [where, piece, held[1]],
            "wvv",
        )
        columns = found[0] if found else columns
        senders.append(sender)
    (state,) = call(
        functools.partial(layer_kernel, group, last, fanout, (share,) * samples),
        "layer",
        [whole],
        [where, columns] + pieces + senders + list(held),
        "w" + "v" * (2 * samples + 3),
        both,
    )
    sender, *far = call(
        functools.partial(half_kernel, group, last, samples, True, fanout),
        "far_half",
        [whole] + [short] * (samples // 2),
        [where, columns, state] + came,
        "wvvvv",
    )
    near = call(
        functools.partial(half_kernel, group, last, samples, False, fanout),
        "near_half",
        [short] * (samples // 2),
        [where, columns, state, sender] + came,
        "wvvvvv",
    )
    state = far + list(near)
    each = samples // 2
    arrived = []
    for far, blocks in ((1, state[:each]), (0, state[each:])):
        for turn, block in enumerate(blocks):
            pairs = [
                (owner(m, last), device(m, ((m // each ^ far) * each + turn) * group)) for m in range(samples)
            ]
            arrived.append(send(block, [pair for pair in pairs if pair[0] != pair[1]]))
    (crossed,) = call(
        functools.partial(far_kernel, group, samples, last),
        "far",
        [jax.ShapeDtypeStruct((share, width), bf16)],
        [where] + arrived[:each],
        "w" + "v" * each,
    )
    parts_of_block = call(
        functools.partial(near_kernel, group, samples, last),
        "near",
        [jax.ShapeDtypeStruct((mesh_rows, width), bf16)] * group,
        [where, crossed] + arrived[each:] + state[each:],
        "w" + "v" * (1 + 2 * each),
    )
    handed = [parts_of_block[0]]
    for steps in range(1, group):
        handed.append(change_lane(parts_of_block[steps], steps))
    (prediction,) = call(
        decode_kernel,
        "decode",
        [jax.ShapeDtypeStruct((channels, grid_rows), bf16)],
        [where, ready, table, w_decode, w_output.T] + handed,
        "wvvvv" + "v" * group,
        [pltpu.VMEM((mesh_rows, width), bf16)],
    )
    return prediction.T.reshape(1, grid_rows, channels)


def chosen_plan(mesh, *arrays):
    segments, parts = mesh.shape["segment"], mesh.shape["dom"]
    samples, width = arrays[0].shape[0], arrays[1].shape[1]
    nodes = parts * arrays[9].shape[0]
    fits = samples == segments == 4 and parts % samples == 0 and parts > samples and nodes == width
    return (resident if fits else streamed)(*arrays)


def solution(mesh):
    return jax.shard_map(
        functools.partial(chosen_plan, mesh),
        mesh=mesh,
        in_specs=(
            P(None, "dom", None),
            P(),
            P("segment", None, None),
            P("segment", None, None),
            P("segment", None, None),
            P(),
            P(),
            P("dom"),
            P("dom"),
            P("dom", None),
            P(None, "dom"),
            P(None, "dom"),
        ),
        out_specs=P("segment", "dom", None),
        check_vma=False,
    )
```

```python
import functools

import jax
import jax.numpy as jnp
from jax import lax
from jax.experimental import pallas as pl
from jax.experimental.pallas import tpu as pltpu
from jax.sharding import PartitionSpec as P

epsilon = 1e-05
DIGIT = 256
VMEM = pl.BlockSpec(memory_space=pltpu.VMEM)
SMEM = pl.BlockSpec(memory_space=pltpu.SMEM)
HBM = pl.BlockSpec(memory_space=pltpu.HBM)


def from_behind(value, axis, steps):
    count = lax.axis_size(axis)
    pairs = [(source, (source + steps) % count) for source in range(count)]
    return lax.ppermute(value, axis, pairs)


def from_behind_2(block, axis, distance):
    devices = range(lax.axis_size(axis))
    route = [(i - distance, i) for i in devices if i - distance in devices]
    return lax.ppermute(block, axis, route)


def from_root(value, axis, source):
    kept = jnp.where(lax.axis_index(axis) == source, value, 0).astype(value.dtype)
    return lax.psum(kept, axis)


def rms_scale(values):
    return values * lax.rsqrt(jnp.mean(values * values, axis=-1, keepdims=True) + epsilon)


def streamed(
    grid_state,
    w_embed,
    w_project,
    w_message,
    w_update,
    w_decode,
    w_output,
    grid_mesh,
    mesh_grid,
    neighbors,
    send_rows,
    halo_count,
):
    segment_index = lax.axis_index("segment")
    segment_count = lax.axis_size("segment")
    final_segment = segment_count - 1
    samples, grid_rows, channels = grid_state.shape
    width = w_embed.shape[1]
    mesh_rows = neighbors.shape[0]
    fanout = neighbors.shape[1]
    halo_rows = send_rows.shape[1]
    share = samples // segment_count
    pool_table = (grid_mesh[None, :] == jnp.arange(mesh_rows, dtype=jnp.int32)[:, None]).astype(
        jnp.bfloat16
    )
    read_table = (mesh_grid[:, None] == jnp.arange(mesh_rows, dtype=jnp.int32)[None, :]).astype(
        jnp.bfloat16
    )
    valid_rows = jnp.arange(halo_rows, dtype=jnp.int32)[None, :] < halo_count[:, 0][:, None]
    source_rows = neighbors.reshape(mesh_rows * fanout)

    def embed_grid(snapshot):
        return jax.nn.silu(jnp.dot(snapshot, w_embed, preferred_element_type=jnp.float32)).astype(
            jnp.bfloat16
        )

    def encode(snapshot):
        latent = embed_grid(snapshot)
        pooled = jnp.dot(pool_table, latent, preferred_element_type=jnp.float32)
        return (rms_scale(pooled).astype(jnp.bfloat16), latent)

    def project(state, weights):
        projected = jnp.dot(state, weights[0], preferred_element_type=jnp.float32)
        return (projected[:, :width], projected[:, width:].astype(jnp.bfloat16))

    def renew(state, receiver, extended, weights):
        fetched = extended[source_rows].reshape(mesh_rows, fanout, width)
        edges = jax.nn.silu(receiver[:, None, :] + fetched.astype(jnp.float32)).astype(jnp.bfloat16)
        messages = jnp.dot(
            edges.reshape(mesh_rows * fanout, width), weights[1], preferred_element_type=jnp.float32
        )
        aggregate = (jnp.sum(messages.reshape(mesh_rows, fanout, width), axis=1) / fanout).astype(
            jnp.bfloat16
        )
        update = jax.nn.silu(
            jnp.dot(state, weights[2][:width], preferred_element_type=jnp.float32)
            + jnp.dot(aggregate, weights[2][width:], preferred_element_type=jnp.float32)
        )
        return (state.astype(jnp.float32) + rms_scale(update)).astype(jnp.bfloat16)

    def decode(state, latent):
        readout = jnp.dot(read_table, state, preferred_element_type=jnp.float32).astype(
            jnp.bfloat16
        )
        hidden = jax.nn.silu(
            jnp.dot(latent, w_decode[:width], preferred_element_type=jnp.float32)
            + jnp.dot(readout, w_decode[width:], preferred_element_type=jnp.float32)
        ).astype(jnp.bfloat16)
        return jnp.dot(hidden, w_output, preferred_element_type=jnp.float32).astype(jnp.bfloat16)

    own_weights = (w_project[0], w_message[0], w_update[0])
    empty_mesh = jnp.zeros((mesh_rows, width), jnp.bfloat16)
    empty_receiver = jnp.zeros((mesh_rows, width), jnp.float32)
    empty_grid = jnp.zeros((grid_rows, width), jnp.bfloat16)
    empty_output = jnp.zeros((grid_rows, channels), jnp.bfloat16)
    received = empty_mesh
    carried = {}
    results = [empty_output for sample in range(samples)]
    for moment in range(samples + final_segment):
        current = received
        if moment < samples:
            snapshot = grid_state[moment]
            started, latent = lax.cond(
                segment_index == 0, lambda: encode(snapshot), lambda: (empty_mesh, empty_grid)
            )
            current = jnp.where(segment_index == 0, started, received)
            carried[moment] = from_behind_2(latent, "segment", final_segment)
        active = (moment - segment_index >= 0) & (moment - segment_index < samples)
        receiver, outgoing = lax.cond(
            active, lambda: project(current, own_weights), lambda: (empty_receiver, empty_mesh)
        )
        picked = jnp.where(valid_rows[:, :, None], outgoing[send_rows], jnp.zeros((), jnp.bfloat16))
        arrived = [outgoing]
        for list_index, offset in enumerate((1, -1, 2, -2)):
            arrived.append(from_behind(picked[list_index], "dom", offset))
        extended = jnp.concatenate(arrived, axis=0)
        renewed = lax.cond(
            active, lambda: renew(current, receiver, extended, own_weights), lambda: empty_mesh
        )
        if moment >= final_segment:
            finished = moment - final_segment
            skipped = carried[finished]
            results[finished] = lax.cond(
                segment_index == final_segment,
                lambda: decode(renewed, skipped),
                lambda: empty_output,
            )
        if moment < samples + final_segment - 1:
            received = from_behind_2(renewed, "segment", 1)
    everything = from_root(jnp.stack(results), "segment", final_segment)
    return lax.dynamic_slice_in_dim(everything, segment_index * share, share, 0)


def silu_by_tanh(values):
    half = 0.5 * values
    return half + half * jnp.tanh(half)


def matmul(left, right):
    return jnp.dot(left, right, preferred_element_type=jnp.float32)


def matmul_nt(left, right):
    return lax.dot_general(left, right, (((1,), (1,)), ((), ())), preferred_element_type=jnp.float32)


def matmul_tn(left, right):
    return lax.dot_general(left, right, (((0,), (0,)), ((), ())), preferred_element_type=jnp.float32)


def place_of(where, group):
    return lax.div(where[1], group), lax.rem(where[1], group)


def owns(where, group, at_segment):
    return jnp.logical_and(where[0] == at_segment, lax.rem(where[1], group) == 0)


def fetch(sources, targets, semaphores):
    copies = [
        pltpu.make_async_copy(source, target, semaphores.at[place])
        for place, (source, target) in enumerate(zip(sources, targets))
    ]
    for copy in copies:
        copy.start()
    return copies


def encode_kernel(group, mesh_rows, fanout, lists, where, snapshots, w_embed, packed, *refs):
    payloads, latent = refs[:-1], refs[-1]
    chip, _ = place_of(where, group)
    neighbors = packed[:fanout, :mesh_rows]
    grid_rows = snapshots.shape[2]
    grid_mesh = packed[fanout + lists : fanout + lists + 1, :grid_rows]
    counts = packed[fanout + lists + 1 : fanout + lists + 2, :lists]
    width = w_embed.shape[1]
    for place in range(snapshots.shape[0]):
        found = silu_by_tanh(matmul_tn(snapshots[place], w_embed[...])).astype(jnp.bfloat16)
        latent[place * grid_rows : (place + 1) * grid_rows, :] = found
    table = lax.broadcasted_iota(jnp.int32, (mesh_rows, grid_rows), 0) == grid_mesh
    table = jnp.where(table, 1.0, 0.0).astype(jnp.bfloat16)
    block = neighbors // mesh_rows
    row = neighbors - block * mesh_rows
    halo_rows = mesh_rows
    position = lax.broadcasted_iota(jnp.int32, (1, halo_rows), 1)
    rows = []
    for list_index in range(lists):
        kept = position < counts[:, list_index : list_index + 1]
        listed = packed[fanout + list_index : fanout + list_index + 1, :halo_rows]
        rows.append(jnp.where(kept, listed, mesh_rows))
    rows.append(jnp.zeros((fanout - lists, halo_rows), jnp.int32))
    filler = jnp.zeros((fanout, 128 - mesh_rows), jnp.int32)
    pieces = [block, filler, row, filler, jnp.concatenate(rows, axis=0), filler]
    coded = jnp.concatenate(pieces + [jnp.zeros((fanout, width - 384), jnp.int32)], axis=1)
    coded = jnp.concatenate([coded, jnp.zeros_like(coded)], axis=0)
    coded = coded.astype(jnp.float32).astype(jnp.bfloat16)
    for turn, payload in enumerate(payloads):
        start = pl.multiple_of(jnp.bitwise_xor(chip, turn) * grid_rows, grid_rows)
        pooled = matmul(table, latent[pl.ds(start, grid_rows), :])
        payload[:mesh_rows, :] = rms_scale(pooled).astype(jnp.bfloat16)
        payload[mesh_rows:, :] = coded


def join_kernel(*refs):
    payloads, joined = refs[:-1], refs[-1]
    rows = payloads[0].shape[0]
    for place, payload in enumerate(payloads):
        joined[place * rows : (place + 1) * rows, :] = payload[...]


def columns_of(names):
    fanout, nodes = names.shape
    tile = min(nodes, DIGIT)
    rows = [names - number * tile for number in range(nodes // tile)]
    rows.append(jnp.zeros((128 - fanout * len(rows), nodes), jnp.float32))
    return jnp.transpose(jnp.concatenate(rows, axis=0)).astype(jnp.bfloat16)


def index_kernel(parts, mesh_rows, where, *refs):
    lanes, (columns_out, codes, state), index_out = refs[:-4], refs[-4:-1], refs[-1]
    nodes = columns_out.shape[0]
    group = len(lanes)
    rows = lanes[0].shape[0] // (parts // group)
    chip, _ = place_of(where, group)

    @pl.when(owns(where, group, 0))
    def _():
        tables = []
        for part in range(parts):
            lane, turn = lanes[part % group], jnp.bitwise_xor(chip, part // group)
            base = pl.multiple_of(turn * rows, 16)
            state[part * mesh_rows : (part + 1) * mesh_rows, :] = lane[pl.ds(base, mesh_rows), :]
            base = pl.multiple_of(turn * rows + mesh_rows, 16)
            coded = lane[pl.ds(base, rows - mesh_rows), :384].astype(jnp.float32).astype(jnp.int32)
            tables.append(coded[: coded.shape[0] // 2])
        fanout = tables[0].shape[0]
        for part in range(parts):
            block = tables[part][:, :128]
            row = tables[part][:, 128:256]
            found = part * mesh_rows + row
            for list_index, offset in enumerate((-1, 1, -2, 2)):
                source = (part + offset) % parts
                lists = tables[source][list_index : list_index + 1, 256:384]
                lists = jnp.broadcast_to(lists, (fanout, 128))
                picked = jnp.take_along_axis(lists, row, axis=1)
                picked = jnp.where(picked == mesh_rows, parts * mesh_rows, source * mesh_rows + picked)
                found = jnp.where(block == list_index + 1, picked, found)
            index_out[:, part * mesh_rows : (part + 1) * mesh_rows] = found[:, :mesh_rows]
        names = index_out[...]
        high_digit = names // DIGIT
        digits = jnp.concatenate([high_digit, names - high_digit * DIGIT], axis=0)
        codes[...] = digits.astype(jnp.float32).astype(jnp.bfloat16)
        columns_out[...] = columns_of(names.astype(jnp.float32))


def pack_kernel(group, at_segment, where, *refs):
    @pl.when(owns(where, group, at_segment))
    def _():
        for place, block in enumerate(refs[:-1]):
            refs[-1][place] = block[...]


def hold_kernel(w_project, w_message, w_update, receive, send, own, edges, message, update, semaphores):
    width = own.shape[0]
    sources = [
        w_message.at[0],
        w_update.at[0, width:],
        w_project.at[0, :, :width],
        w_project.at[0, :, width:],
        w_update.at[0, :width],
    ]
    copies = fetch(sources, [message, update, receive, send, own], semaphores)
    copies[0].wait()
    copies[1].wait()
    edges[...] = matmul(message[...], update[...]).astype(jnp.bfloat16)
    for copy in copies[2:]:
        copy.wait()


def sum_edges(fanout, columns, sender, own, w_receive):
    chunk, width = own.shape
    nodes = sender.shape[0]
    tile = min(nodes, DIGIT)
    names = lax.broadcasted_iota(jnp.int32, (chunk, tile), 1).astype(jnp.float32).astype(jnp.bfloat16)
    one_half = jnp.full((chunk, tile), 0.5, jnp.bfloat16)
    none = jnp.zeros((chunk, tile), jnp.bfloat16)
    receiver = 0.5 * matmul(own, w_receive)
    total = jnp.zeros((chunk, width), jnp.float32)
    for k in range(fanout):
        hits = []
        for number in range(nodes // tile):
            lane = number * fanout + k
            hits.append(jnp.where(columns[:, lane : lane + 1] == names, one_half, none))
        half = receiver + matmul(jnp.concatenate(hits, axis=1), sender)
        total = total + (half + half * jnp.tanh(half))
    return (total * (1.0 / fanout)).astype(jnp.bfloat16)


def update_nodes(own, gathered, w_own, w_edges):
    update = silu_by_tanh(matmul(own, w_own) + matmul(gathered, w_edges))
    return (own.astype(jnp.float32) + rms_scale(update)).astype(jnp.bfloat16)


def sender_kernel(group, at_segment, fanout, rows, where, state, w_send, sender, *columns):
    @pl.when(owns(where, group, at_segment))
    def _():
        sender[...] = matmul(state[:rows, :], w_send[...]).astype(jnp.bfloat16)
        if columns:
            digits = state[rows:, :].astype(jnp.float32)
            columns[0][...] = columns_of(digits[:fanout] * DIGIT + digits[fanout:])


def layer_kernel(group, at_segment, fanout, rows, where, columns, *refs):
    parts = len(rows)
    state, senders, refs = refs[:parts], refs[parts : 2 * parts - 1], refs[2 * parts - 1 :]
    (w_receive, w_send, w_own, w_edges), (renewed, whole, sender) = refs[:4], refs[4:]
    nodes = renewed.shape[0]
    chunk = min(nodes, 256)

    @pl.when(owns(where, group, at_segment))
    def _():
        start = 0
        for part, count in zip(state, rows):
            whole[start : start + count, :] = part[:count, :]
            start += count
        start = 0
        for part in senders:
            sender[start : start + part.shape[0], :] = part[...]
            start += part.shape[0]
        sender[start:, :] = matmul(whole[start:, :], w_send[...]).astype(jnp.bfloat16)
        for start in range(0, nodes, chunk):
            span = slice(start, start + chunk)
            gathered = sum_edges(fanout, columns[span, :], sender[...], whole[span, :], w_receive[...])
            renewed[span, :] = update_nodes(whole[span, :], gathered, w_own[...], w_edges[...])


def open_kernel(group, at_segment, fanout, rows, where, columns, *refs):
    parts = len(rows)
    state, senders, refs = refs[:parts], refs[parts : 2 * parts - 1], refs[2 * parts - 1 :]
    codes, (w_receive, w_send, w_own, w_edges), (sender, whole, piece) = refs[:-7], refs[-7:-3], refs[-3:]

    @pl.when(owns(where, group, at_segment))
    def _():
        start = 0
        for part, count in zip(state, rows):
            whole[start : start + count, :] = part[:count, :]
            start += count
        start = 0
        for part in senders:
            sender[start : start + part.shape[0], :] = part[...]
            start += part.shape[0]
        sender[start:, :] = matmul(whole[start:, :], w_send[...]).astype(jnp.bfloat16)
        below = codes[0][...] if codes else state[0][rows[0] :, :]
        count = piece.shape[0] - below.shape[0]
        own = whole[:count, :]
        gathered = sum_edges(fanout, columns[:count, :], sender[...], own, w_receive[...])
        piece[:count, :] = update_nodes(own, gathered, w_own[...], w_edges[...])
        piece[count:, :] = below


def next_kernel(group, at_segment, fanout, start, where, columns, sender, whole, *refs):
    w_receive, _, w_own, w_edges, piece = refs
    span = slice(start, start + piece.shape[0])

    @pl.when(owns(where, group, at_segment))
    def _():
        own = whole[span, :]
        gathered = sum_edges(fanout, columns[span, :], sender[...], own, w_receive[...])
        piece[...] = update_nodes(own, gathered, w_own[...], w_edges[...])


def end_kernel(group, at_segment, chips, far, begin, first, fanout, where, columns, state, *refs):
    senders, refs = (refs[:0], refs) if first else (refs[:1], refs[1:])
    (w_project, pair), outs = refs[:2], refs[2:]
    width = state.shape[1]
    half = state.shape[0] // 2
    chip, _ = place_of(where, group)

    @pl.when(owns(where, group, at_segment))
    def _():
        pieces = outs
        if first:
            outs[0][...] = matmul(state[...], w_project[0, :, width:]).astype(jnp.bfloat16)
            pieces = outs[1:]
        sender = outs[0] if first else senders[0]
        rows = sum(piece.shape[0] for piece in pieces)
        upper = (chip < chips // 2) if far else (chip >= chips // 2)
        start = pl.multiple_of(jnp.where(upper, half, 0) + begin, rows)
        own = state[pl.ds(start, rows), :]
        gathered = sum_edges(
            fanout, columns[pl.ds(start, rows), :], sender[...], own, w_project[0, :, :width]
        )
        write_pieces(pieces, update_nodes(own, gathered, pair[0], pair[1]))


def write_pieces(pieces, value):
    rows = value.shape[0] // len(pieces)
    for place, piece in enumerate(pieces):
        piece[:rows, :] = value[place * rows : (place + 1) * rows]


def arrival(where, group, chips, last):
    each = chips // 2
    segment = where[0]
    chip, _ = place_of(where, group)
    crosses = lax.div(chip, each) != lax.div(segment, each)
    return crosses, jnp.logical_and(segment == last, chip == last), lax.rem(chip, each)


def far_kernel(group, chips, last, number, where, *refs):
    block, out = refs[0], refs[-1]
    crosses, _, spot = arrival(where, group, chips, last)

    @pl.when(jnp.logical_and(crosses, spot == number))
    def _():
        out[...] = block[...]

    if number:

        @pl.when(jnp.logical_and(crosses, spot < number))
        def _():
            out[...] = refs[1][...]


def near_kernel(group, chips, last, where, crossed, *refs):
    each = chips // 2
    near, kept, outs = refs[:each], refs[each : 2 * each], refs[2 * each :]
    rows = outs[0].shape[0]
    crosses, stays, spot = arrival(where, group, chips, last)
    arrives = jnp.logical_not(jnp.logical_or(crosses, stays))

    def give(block):
        for place, out in enumerate(outs):
            out[...] = block[place * rows : (place + 1) * rows, :]

    @pl.when(crosses)
    def _():
        give(crossed)

    for number in range(each):
        for blocks, chosen in ((near, arrives), (kept, stays)):

            @pl.when(jnp.logical_and(chosen, spot == number))
            def _(block=blocks[number]):
                give(block)


def prepare_kernel(where, snapshots, w_embed, w_decode, mesh_grid, ready, table_out):
    snapshot = snapshots[where[0]]
    latent = silu_by_tanh(matmul_tn(snapshot, w_embed[...])).astype(jnp.bfloat16)
    ready[...] = matmul(latent, w_decode[: latent.shape[1], :])
    mesh_rows, grid_rows = table_out.shape
    table = lax.broadcasted_iota(jnp.int32, (mesh_rows, grid_rows), 0) == mesh_grid[...]
    table_out[...] = jnp.where(table, 1.0, 0.0).astype(jnp.bfloat16)


def decode_kernel(where, ready, table, w_decode, w_output, *refs):
    blocks, out, state = refs[:-2], refs[-2], refs[-1]
    width = ready.shape[1]
    _, lane = place_of(where, len(blocks))
    for number, block in enumerate(blocks):

        @pl.when(lane == number)
        def _(block=block):
            state[...] = block[...]

    readout = matmul_tn(table[...], state[...]).astype(jnp.bfloat16)
    hidden = silu_by_tanh(ready[...] + matmul(readout, w_decode[width:, :])).astype(jnp.bfloat16)
    out[...] = matmul_nt(w_output[...], hidden).astype(jnp.bfloat16)


def call(kernel, name, shapes, inputs, places, scratch=(), room=16, flops=0):
    specs, given = [], []
    for value, place in zip(inputs, places):
        specs += [SMEM] * 2 if place == "w" else [VMEM if place == "v" else HBM]
        given += list(value) if place == "w" else [value]
    moved = sum(value.size * value.dtype.itemsize for value in given + list(shapes))

    def located(segment, place, *refs):
        kernel((segment[0], place[0]), *refs)

    return pl.pallas_call(
        located if places[0] == "w" else kernel,
        out_shape=shapes,
        in_specs=specs,
        out_specs=[VMEM] * len(shapes),
        scratch_shapes=list(scratch),
        name=name,
        compiler_params=pltpu.CompilerParams(vmem_limit_bytes=room * 1024 * 1024),
        cost_estimate=pl.CostEstimate(flops=flops, bytes_accessed=moved, transcendentals=0),
    )(*given)


def every_device(pairs, count, group):
    onward = dict(pairs)
    reached = set(onward.values())
    for first in [source for source in onward if source not in reached]:
        last = first
        while last in onward:
            last = onward[last]
        onward.update({last: last + group - 1, last + group - 1: first + group - 1, first + group - 1: first})
    alone = []
    for at in range(0, count, group):
        rest = [lane for lane in range(at, at + group) if lane not in onward]
        if len(rest) > 1:
            onward.update(zip(rest, rest[1:] + rest[:1]))
        else:
            alone += rest
    if len(alone) == 1:
        before = next(at for at in onward if at % group and onward[at] % group == 0)
        onward.update({before: alone[0], alone[0]: onward[before]})
    else:
        onward.update(zip(alone, alone[1:] + alone[:1]))
    return sorted(onward.items())


def resident(
    grid_state,
    w_embed,
    w_project,
    w_message,
    w_update,
    w_decode,
    w_output,
    grid_mesh,
    mesh_grid,
    neighbors,
    send_rows,
    halo_count,
):
    segment = lax.axis_index("segment")
    place = lax.axis_index("dom")
    segments = lax.axis_size("segment")
    parts = lax.axis_size("dom")
    samples, grid_rows, channels = grid_state.shape
    width = w_embed.shape[1]
    mesh_rows, fanout = neighbors.shape
    nodes = parts * mesh_rows
    group = parts // samples
    bf16 = jnp.bfloat16

    def device(at_segment, at_dom):
        return at_segment * parts + at_dom % parts

    def send(value, pairs):
        return lax.ppermute(value, ("segment", "dom"), every_device(pairs, segments * parts, group))

    def to_chip(value, steps):
        giver = steps - 1
        pairs = []
        for at in range(segments):
            for dom in range(parts):
                chip, lane = divmod(dom, group)
                across = (chip ^ steps) * group + lane
                if at == giver:
                    pairs.append((device(at, dom), device(0, across)))
                elif at == 0:
                    pairs.append((device(at, dom), device(giver, dom)))
                else:
                    pairs.append((device(at, dom), device(at, chip * group + (lane + 1) % group)))
        return lax.ppermute(value, ("segment", "dom"), pairs)

    def change_lane(value, steps):
        pairs = [(at, at - at % group + (at + steps) % group) for at in range(parts)]
        return lax.ppermute(value, "dom", pairs)

    def owner(m, at_segment):
        return device(at_segment, m * group)

    own_segment, own_place, w_project = lax.optimization_barrier(
        (segment.reshape(1), place.reshape(1), w_project)
    )
    where = (own_segment, own_place)
    weights = [w_project, w_message, w_update]
    last = segments - 2
    to_last = [(owner(m, last + 1), owner(m, last)) for m in range(samples)]
    came_project = send(w_project, to_last)
    snapshots = jnp.transpose(grid_state, (0, 2, 1))
    lists = send_rows.shape[0]

    def rows_of(value):
        return jnp.pad(value, ((0, 0), (0, 128 - value.shape[1])))

    packed = jnp.concatenate(
        [
            rows_of(neighbors.T),
            rows_of(send_rows),
            rows_of(grid_mesh.reshape(1, grid_rows)),
            rows_of(halo_count.reshape(1, lists)),
        ],
        axis=0,
    )
    payloads = call(
        functools.partial(encode_kernel, group, mesh_rows, fanout, lists),
        "encode",
        [jax.ShapeDtypeStruct((mesh_rows + 2 * fanout, width), bf16)] * samples,
        [where, snapshots, w_embed, packed],
        "wvvv",
        [pltpu.VMEM((samples * grid_rows, width), bf16)],
    )
    held = call(
        hold_kernel,
        "hold",
        [jax.ShapeDtypeStruct((width, width), bf16)] * 4,
        weights,
        "hhh",
        [pltpu.VMEM((width, width), bf16)] * 2 + [pltpu.SemaphoreType.DMA((5,))],
    )
    own_payload, *held = lax.optimization_barrier((payloads[0], *held))
    arrived = [own_payload] + [to_chip(payloads[turn], turn) for turn in range(1, samples)]
    (joined,) = call(
        join_kernel,
        "join",
        [jax.ShapeDtypeStruct((samples * (mesh_rows + 2 * fanout), width), bf16)],
        arrived,
        "v" * samples,
    )
    lanes = [joined] + [change_lane(joined, -steps) for steps in range(1, group)]
    share = group * mesh_rows
    whole, short, tall = [
        jax.ShapeDtypeStruct((rows, width), bf16) for rows in (nodes, share, share + 2 * fanout)
    ]
    columns_shape = jax.ShapeDtypeStruct((nodes, 128), bf16)
    columns, codes, state = call(
        functools.partial(index_kernel, parts, mesh_rows),
        "index",
        [columns_shape, jax.ShapeDtypeStruct((2 * fanout, width), bf16), whole],
        [where] + lanes,
        "w" + "v" * group,
        [pltpu.VMEM((fanout, nodes), jnp.int32)],
    )
    columns, came_project, *held = lax.optimization_barrier((columns, came_project, *held))
    (pair,) = call(
        functools.partial(pack_kernel, group, last + 1),
        "pack",
        [jax.ShapeDtypeStruct((2, width, width), bf16)],
        [where] + held[2:],
        "wvv",
    )
    came = [came_project, send(pair, to_last)]
    pieces, senders, rows, extra = [state], [], (nodes,), [codes]
    for layer in range(last):
        pairs = [(owner(m, layer), owner(m, layer + 1)) for m in range(samples)]
        sender, joined_state, piece = call(
            functools.partial(open_kernel, group, layer, fanout, rows),
            "open",
            [whole, whole, tall],
            [where, columns] + pieces + senders + extra + held,
            "w" + "v" * (1 + len(pieces + senders + extra + held)),
        )
        sent = [send(piece, pairs)]
        for start in range(share, nodes, share):
            (piece,) = call(
                functools.partial(next_kernel, group, layer, fanout, start),
                "next",
                [short],
                [where, columns, sender, joined_state] + held,
                "w" + "v" * (3 + len(held)),
            )
            sent.append(send(piece, pairs))
        pieces, senders, rows, extra = sent, [], (share,) * samples, []
        if layer == 0:
            ready, table = call(
                prepare_kernel,
                "prepare",
                [
                    jax.ShapeDtypeStruct((grid_rows, width), jnp.float32),
                    jax.ShapeDtypeStruct((mesh_rows, grid_rows), bf16),
                ],
                [where, snapshots, w_embed, w_decode, mesh_grid.reshape(1, grid_rows)],
                "wvvvv",
            )
            pieces[0], ready, table = lax.optimization_barrier((pieces[0], ready, table))
        for piece in pieces[:-1]:
            if senders:
                piece, senders[-1] = lax.optimization_barrier((piece, senders[-1]))
            sender, *found = call(
                functools.partial(sender_kernel, group, layer + 1, fanout, share),
                "sender",
                [short] + [columns_shape] * (not senders),
                [where, piece, held[1]],
                "wvv",
            )
            columns = found[0] if found else columns
            senders.append(sender)
    (state,) = call(
        functools.partial(layer_kernel, group, last, fanout, rows),
        "layer",
        [whole],
        [where, columns] + pieces + senders + held,
        "w" + "v" * (1 + len(pieces + senders + held)),
        [pltpu.VMEM((nodes, width), bf16)] * 2,
    )
    far = []
    for begin in range(0, nodes // 2, share):
        found = call(
            functools.partial(end_kernel, group, last, samples, True, begin, not far, fanout),
            "far_part",
            [whole] * (not far) + [short],
            [where, columns, state] + ([sender] if far else []) + came,
            "w" + "v" * (5 if far else 4),
        )
        sender = found[0] if not far else sender
        far.append(found[-1])
    near = call(
        functools.partial(end_kernel, group, last, samples, False, 0, False, fanout),
        "near_half",
        [short] * (samples // 2),
        [where, columns, state, sender] + came,
        "wvvvvv",
    )
    state = far + list(near)
    each = samples // 2
    arrived = []
    for far, blocks in ((1, state[:each]), (0, state[each:])):
        for turn, block in enumerate(blocks):
            pairs = [
                (owner(m, last), device(m, ((m // each ^ far) * each + turn) * group)) for m in range(samples)
            ]
            arrived.append(send(block, [pair for pair in pairs if pair[0] != pair[1]]))
    crossed = []
    for number, block in enumerate(arrived[:each]):
        crossed = call(
            functools.partial(far_kernel, group, samples, last, number),
            "far",
            [short],
            [where, block] + list(crossed),
            "wv" + "v" * len(crossed),
        )
    parts_of_block = call(
        functools.partial(near_kernel, group, samples, last),
        "near",
        [jax.ShapeDtypeStruct((mesh_rows, width), bf16)] * group,
        [where, crossed[0]] + arrived[each:] + state[each:],
        "w" + "v" * (1 + 2 * each),
    )
    handed = [parts_of_block[0]]
    for steps in range(1, group):
        handed.append(change_lane(parts_of_block[steps], steps))
    (prediction,) = call(
        decode_kernel,
        "decode",
        [jax.ShapeDtypeStruct((channels, grid_rows), bf16)],
        [where, ready, table, w_decode, w_output.T] + handed,
        "wvvvv" + "v" * group,
        [pltpu.VMEM((mesh_rows, width), bf16)],
    )
    return prediction.T.reshape(1, grid_rows, channels)


def chosen_plan(mesh, *arrays):
    segments, parts = mesh.shape["segment"], mesh.shape["dom"]
    samples, width = arrays[0].shape[0], arrays[1].shape[1]
    nodes = parts * arrays[9].shape[0]
    fits = samples == segments == 4 and parts % samples == 0 and parts > samples and nodes == width
    return (resident if fits else streamed)(*arrays)


def solution(mesh):
    return jax.shard_map(
        functools.partial(chosen_plan, mesh),
        mesh=mesh,
        in_specs=(
            P(None, "dom", None),
            P(),
            P("segment", None, None),
            P("segment", None, None),
            P("segment", None, None),
            P(),
            P(),
            P("dom"),
            P("dom"),
            P("dom", None),
            P(None, "dom"),
            P(None, "dom"),
        ),
        out_specs=P("segment", "dom", None),
        check_vma=False,
    )
```

```python
import functools

import jax
import jax.numpy as jnp
from jax import lax
from jax.experimental import pallas as pl
from jax.experimental.pallas import tpu as pltpu
from jax.sharding import PartitionSpec as P

epsilon = 1e-05
DIGIT = 256
VMEM = pl.BlockSpec(memory_space=pltpu.VMEM)
SMEM = pl.BlockSpec(memory_space=pltpu.SMEM)
HBM = pl.BlockSpec(memory_space=pltpu.HBM)


def from_behind(value, axis, steps):
    count = lax.axis_size(axis)
    pairs = [(source, (source + steps) % count) for source in range(count)]
    return lax.ppermute(value, axis, pairs)


def from_behind_2(block, axis, distance):
    devices = range(lax.axis_size(axis))
    route = [(i - distance, i) for i in devices if i - distance in devices]
    return lax.ppermute(block, axis, route)


def from_root(value, axis, source):
    kept = jnp.where(lax.axis_index(axis) == source, value, 0).astype(value.dtype)
    return lax.psum(kept, axis)


def rms_scale(values):
    return values * lax.rsqrt(jnp.mean(values * values, axis=-1, keepdims=True) + epsilon)


def streamed(
    grid_state,
    w_embed,
    w_project,
    w_message,
    w_update,
    w_decode,
    w_output,
    grid_mesh,
    mesh_grid,
    neighbors,
    send_rows,
    halo_count,
):
    segment_index = lax.axis_index("segment")
    segment_count = lax.axis_size("segment")
    final_segment = segment_count - 1
    samples, grid_rows, channels = grid_state.shape
    width = w_embed.shape[1]
    mesh_rows = neighbors.shape[0]
    fanout = neighbors.shape[1]
    halo_rows = send_rows.shape[1]
    share = samples // segment_count
    pool_table = (grid_mesh[None, :] == jnp.arange(mesh_rows, dtype=jnp.int32)[:, None]).astype(
        jnp.bfloat16
    )
    read_table = (mesh_grid[:, None] == jnp.arange(mesh_rows, dtype=jnp.int32)[None, :]).astype(
        jnp.bfloat16
    )
    valid_rows = jnp.arange(halo_rows, dtype=jnp.int32)[None, :] < halo_count[:, 0][:, None]
    source_rows = neighbors.reshape(mesh_rows * fanout)

    def embed_grid(snapshot):
        return jax.nn.silu(jnp.dot(snapshot, w_embed, preferred_element_type=jnp.float32)).astype(
            jnp.bfloat16
        )

    def encode(snapshot):
        latent = embed_grid(snapshot)
        pooled = jnp.dot(pool_table, latent, preferred_element_type=jnp.float32)
        return (rms_scale(pooled).astype(jnp.bfloat16), latent)

    def project(state, weights):
        projected = jnp.dot(state, weights[0], preferred_element_type=jnp.float32)
        return (projected[:, :width], projected[:, width:].astype(jnp.bfloat16))

    def renew(state, receiver, extended, weights):
        fetched = extended[source_rows].reshape(mesh_rows, fanout, width)
        edges = jax.nn.silu(receiver[:, None, :] + fetched.astype(jnp.float32)).astype(jnp.bfloat16)
        messages = jnp.dot(
            edges.reshape(mesh_rows * fanout, width), weights[1], preferred_element_type=jnp.float32
        )
        aggregate = (jnp.sum(messages.reshape(mesh_rows, fanout, width), axis=1) / fanout).astype(
            jnp.bfloat16
        )
        update = jax.nn.silu(
            jnp.dot(state, weights[2][:width], preferred_element_type=jnp.float32)
            + jnp.dot(aggregate, weights[2][width:], preferred_element_type=jnp.float32)
        )
        return (state.astype(jnp.float32) + rms_scale(update)).astype(jnp.bfloat16)

    def decode(state, latent):
        readout = jnp.dot(read_table, state, preferred_element_type=jnp.float32).astype(
            jnp.bfloat16
        )
        hidden = jax.nn.silu(
            jnp.dot(latent, w_decode[:width], preferred_element_type=jnp.float32)
            + jnp.dot(readout, w_decode[width:], preferred_element_type=jnp.float32)
        ).astype(jnp.bfloat16)
        return jnp.dot(hidden, w_output, preferred_element_type=jnp.float32).astype(jnp.bfloat16)

    own_weights = (w_project[0], w_message[0], w_update[0])
    empty_mesh = jnp.zeros((mesh_rows, width), jnp.bfloat16)
    empty_receiver = jnp.zeros((mesh_rows, width), jnp.float32)
    empty_grid = jnp.zeros((grid_rows, width), jnp.bfloat16)
    empty_output = jnp.zeros((grid_rows, channels), jnp.bfloat16)
    received = empty_mesh
    carried = {}
    results = [empty_output for sample in range(samples)]
    for moment in range(samples + final_segment):
        current = received
        if moment < samples:
            snapshot = grid_state[moment]
            started, latent = lax.cond(
                segment_index == 0, lambda: encode(snapshot), lambda: (empty_mesh, empty_grid)
            )
            current = jnp.where(segment_index == 0, started, received)
            carried[moment] = from_behind_2(latent, "segment", final_segment)
        active = (moment - segment_index >= 0) & (moment - segment_index < samples)
        receiver, outgoing = lax.cond(
            active, lambda: project(current, own_weights), lambda: (empty_receiver, empty_mesh)
        )
        picked = jnp.where(valid_rows[:, :, None], outgoing[send_rows], jnp.zeros((), jnp.bfloat16))
        arrived = [outgoing]
        for list_index, offset in enumerate((1, -1, 2, -2)):
            arrived.append(from_behind(picked[list_index], "dom", offset))
        extended = jnp.concatenate(arrived, axis=0)
        renewed = lax.cond(
            active, lambda: renew(current, receiver, extended, own_weights), lambda: empty_mesh
        )
        if moment >= final_segment:
            finished = moment - final_segment
            skipped = carried[finished]
            results[finished] = lax.cond(
                segment_index == final_segment,
                lambda: decode(renewed, skipped),
                lambda: empty_output,
            )
        if moment < samples + final_segment - 1:
            received = from_behind_2(renewed, "segment", 1)
    everything = from_root(jnp.stack(results), "segment", final_segment)
    return lax.dynamic_slice_in_dim(everything, segment_index * share, share, 0)


def silu_by_tanh(values):
    half = 0.5 * values
    return half + half * jnp.tanh(half)


def matmul(left, right):
    return jnp.dot(left, right, preferred_element_type=jnp.float32)


def matmul_nt(left, right):
    return lax.dot_general(left, right, (((1,), (1,)), ((), ())), preferred_element_type=jnp.float32)


def matmul_tn(left, right):
    return lax.dot_general(left, right, (((0,), (0,)), ((), ())), preferred_element_type=jnp.float32)


def place_of(where, group):
    return lax.div(where[1], group), lax.rem(where[1], group)


def owns(where, group, at_segment):
    return jnp.logical_and(where[0] == at_segment, lax.rem(where[1], group) == 0)


def swapped_roles(where, group, at_segment):
    chip, lane = place_of(where, group)
    for number in range(2):
        here = jnp.logical_and(where[0] == at_segment + number, lane == 0)
        yield jnp.logical_and(here, lax.rem(chip, 2) == number), number


def weights_of(came, held, own):
    if own:
        return [block[...] for block in held]
    w_project, pair = came
    width = pair.shape[1]
    return [w_project[0, :, :width], w_project[0, :, width:], pair[0], pair[1]]


def fetch(sources, targets, semaphores):
    copies = [
        pltpu.make_async_copy(source, target, semaphores.at[place])
        for place, (source, target) in enumerate(zip(sources, targets))
    ]
    for copy in copies:
        copy.start()
    return copies


def encode_kernel(group, mesh_rows, fanout, lists, where, snapshots, w_embed, packed, *refs):
    payloads, latent = refs[:-1], refs[-1]
    chip, _ = place_of(where, group)
    neighbors = packed[:fanout, :mesh_rows]
    grid_rows = snapshots.shape[2]
    grid_mesh = packed[fanout + lists : fanout + lists + 1, :grid_rows]
    counts = packed[fanout + lists + 1 : fanout + lists + 2, :lists]
    width = w_embed.shape[1]
    for place in range(snapshots.shape[0]):
        found = silu_by_tanh(matmul_tn(snapshots[place], w_embed[...])).astype(jnp.bfloat16)
        latent[place * grid_rows : (place + 1) * grid_rows, :] = found
    table = lax.broadcasted_iota(jnp.int32, (mesh_rows, grid_rows), 0) == grid_mesh
    table = jnp.where(table, 1.0, 0.0).astype(jnp.bfloat16)
    block = neighbors // mesh_rows
    row = neighbors - block * mesh_rows
    halo_rows = mesh_rows
    position = lax.broadcasted_iota(jnp.int32, (1, halo_rows), 1)
    rows = []
    for list_index in range(lists):
        kept = position < counts[:, list_index : list_index + 1]
        listed = packed[fanout + list_index : fanout + list_index + 1, :halo_rows]
        rows.append(jnp.where(kept, listed, mesh_rows))
    rows.append(jnp.zeros((fanout - lists, halo_rows), jnp.int32))
    filler = jnp.zeros((fanout, 128 - mesh_rows), jnp.int32)
    pieces = [block, filler, row, filler, jnp.concatenate(rows, axis=0), filler]
    coded = jnp.concatenate(pieces + [jnp.zeros((fanout, width - 384), jnp.int32)], axis=1)
    coded = jnp.concatenate([coded, jnp.zeros_like(coded)], axis=0)
    coded = coded.astype(jnp.float32).astype(jnp.bfloat16)
    for turn, payload in enumerate(payloads):
        start = pl.multiple_of(jnp.bitwise_xor(chip, turn) * grid_rows, grid_rows)
        pooled = matmul(table, latent[pl.ds(start, grid_rows), :])
        payload[:mesh_rows, :] = rms_scale(pooled).astype(jnp.bfloat16)
        payload[mesh_rows:, :] = coded


def join_kernel(*refs):
    payloads, joined = refs[:-1], refs[-1]
    rows = payloads[0].shape[0]
    for place, payload in enumerate(payloads):
        joined[place * rows : (place + 1) * rows, :] = payload[...]


def columns_of(names):
    fanout, nodes = names.shape
    tile = min(nodes, DIGIT)
    rows = [names - number * tile for number in range(nodes // tile)]
    rows.append(jnp.zeros((128 - fanout * len(rows), nodes), jnp.float32))
    return jnp.transpose(jnp.concatenate(rows, axis=0)).astype(jnp.bfloat16)


def index_kernel(parts, mesh_rows, where, *refs):
    lanes, (columns_out, codes, state), index_out = refs[:-4], refs[-4:-1], refs[-1]
    nodes = columns_out.shape[0]
    group = len(lanes)
    rows = lanes[0].shape[0] // (parts // group)
    chip, _ = place_of(where, group)

    @pl.when(owns(where, group, 0))
    def _():
        tables = []
        for part in range(parts):
            lane, turn = lanes[part % group], jnp.bitwise_xor(chip, part // group)
            base = pl.multiple_of(turn * rows, 16)
            state[part * mesh_rows : (part + 1) * mesh_rows, :] = lane[pl.ds(base, mesh_rows), :]
            base = pl.multiple_of(turn * rows + mesh_rows, 16)
            coded = lane[pl.ds(base, rows - mesh_rows), :384].astype(jnp.float32).astype(jnp.int32)
            tables.append(coded[: coded.shape[0] // 2])
        fanout = tables[0].shape[0]
        for part in range(parts):
            block = tables[part][:, :128]
            row = tables[part][:, 128:256]
            found = part * mesh_rows + row
            for list_index, offset in enumerate((-1, 1, -2, 2)):
                source = (part + offset) % parts
                lists = tables[source][list_index : list_index + 1, 256:384]
                lists = jnp.broadcast_to(lists, (fanout, 128))
                picked = jnp.take_along_axis(lists, row, axis=1)
                picked = jnp.where(picked == mesh_rows, parts * mesh_rows, source * mesh_rows + picked)
                found = jnp.where(block == list_index + 1, picked, found)
            index_out[:, part * mesh_rows : (part + 1) * mesh_rows] = found[:, :mesh_rows]
        names = index_out[...]
        high_digit = names // DIGIT
        digits = jnp.concatenate([high_digit, names - high_digit * DIGIT], axis=0)
        codes[...] = digits.astype(jnp.float32).astype(jnp.bfloat16)
        columns_out[...] = columns_of(names.astype(jnp.float32))


def pack_kernel(group, at_segment, where, *refs):
    @pl.when(jnp.logical_or(owns(where, group, at_segment), owns(where, group, at_segment + 1)))
    def _():
        for place, block in enumerate(refs[:-1]):
            refs[-1][place] = block[...]


def hold_kernel(w_project, w_message, w_update, receive, send, own, edges, message, update, semaphores):
    width = own.shape[0]
    sources = [
        w_message.at[0],
        w_update.at[0, width:],
        w_project.at[0, :, :width],
        w_project.at[0, :, width:],
        w_update.at[0, :width],
    ]
    copies = fetch(sources, [message, update, receive, send, own], semaphores)
    copies[0].wait()
    copies[1].wait()
    edges[...] = matmul(message[...], update[...]).astype(jnp.bfloat16)
    for copy in copies[2:]:
        copy.wait()


def sum_edges(fanout, columns, sender, own, w_receive):
    chunk, width = own.shape
    nodes = sender.shape[0]
    tile = min(nodes, DIGIT)
    names = lax.broadcasted_iota(jnp.int32, (chunk, tile), 1).astype(jnp.float32).astype(jnp.bfloat16)
    one_half = jnp.full((chunk, tile), 0.5, jnp.bfloat16)
    none = jnp.zeros((chunk, tile), jnp.bfloat16)
    receiver = 0.5 * matmul(own, w_receive)
    total = jnp.zeros((chunk, width), jnp.float32)
    for k in range(fanout):
        hits = []
        for number in range(nodes // tile):
            lane = number * fanout + k
            hits.append(jnp.where(columns[:, lane : lane + 1] == names, one_half, none))
        half = receiver + matmul(jnp.concatenate(hits, axis=1), sender)
        total = total + (half + half * jnp.tanh(half))
    return (total * (1.0 / fanout)).astype(jnp.bfloat16)


def update_nodes(own, gathered, w_own, w_edges):
    update = silu_by_tanh(matmul(own, w_own) + matmul(gathered, w_edges))
    return (own.astype(jnp.float32) + rms_scale(update)).astype(jnp.bfloat16)


def sender_kernel(group, at_segment, fanout, rows, where, state, w_send, sender, *columns):
    @pl.when(owns(where, group, at_segment))
    def _():
        sender[...] = matmul(state[:rows, :], w_send[...]).astype(jnp.bfloat16)
        if columns:
            digits = state[rows:, :].astype(jnp.float32)
            columns[0][...] = columns_of(digits[:fanout] * DIGIT + digits[fanout:])


def late_sender_kernel(group, at_segment, fanout, rows, where, state, w_send, w_project, sender, *columns):
    width = state.shape[1]
    for here, number in swapped_roles(where, group, at_segment):

        @pl.when(here)
        def _(number=number):
            weights = w_project[0, :, width:] if number else w_send[...]
            sender[...] = matmul(state[:rows, :], weights).astype(jnp.bfloat16)
            if columns:
                digits = state[rows:, :].astype(jnp.float32)
                columns[0][...] = columns_of(digits[:fanout] * DIGIT + digits[fanout:])


def layer_kernel(group, at_segment, fanout, rows, where, columns, *refs):
    parts = len(rows)
    state, senders, refs = refs[:parts], refs[parts : 2 * parts - 1], refs[2 * parts - 1 :]
    held, came, (renewed, whole, sender) = refs[:4], refs[4:6], refs[6:]
    nodes = renewed.shape[0]
    chunk = min(nodes, 256)
    for here, number in swapped_roles(where, group, at_segment):

        @pl.when(here)
        def _(number=number):
            w_receive, w_send, w_own, w_edges = weights_of(came, held, number == 0)
            start = 0
            for part, count in zip(state, rows):
                whole[start : start + count, :] = part[:count, :]
                start += count
            start = 0
            for part in senders:
                sender[start : start + part.shape[0], :] = part[...]
                start += part.shape[0]
            sender[start:, :] = matmul(whole[start:, :], w_send).astype(jnp.bfloat16)
            for start in range(0, nodes, chunk):
                span = slice(start, start + chunk)
                gathered = sum_edges(fanout, columns[span, :], sender[...], whole[span, :], w_receive)
                renewed[span, :] = update_nodes(whole[span, :], gathered, w_own, w_edges)


def open_kernel(group, at_segment, fanout, rows, where, columns, *refs):
    parts = len(rows)
    state, senders, refs = refs[:parts], refs[parts : 2 * parts - 1], refs[2 * parts - 1 :]
    codes, (w_receive, w_send, w_own, w_edges), (sender, whole, piece) = refs[:-7], refs[-7:-3], refs[-3:]

    @pl.when(owns(where, group, at_segment))
    def _():
        start = 0
        for part, count in zip(state, rows):
            whole[start : start + count, :] = part[:count, :]
            start += count
        start = 0
        for part in senders:
            sender[start : start + part.shape[0], :] = part[...]
            start += part.shape[0]
        sender[start:, :] = matmul(whole[start:, :], w_send[...]).astype(jnp.bfloat16)
        below = codes[0][...] if codes else state[0][rows[0] :, :]
        count = piece.shape[0] - below.shape[0]
        own = whole[:count, :]
        gathered = sum_edges(fanout, columns[:count, :], sender[...], own, w_receive[...])
        piece[:count, :] = update_nodes(own, gathered, w_own[...], w_edges[...])
        piece[count:, :] = below


def next_kernel(group, at_segment, fanout, start, where, columns, sender, whole, *refs):
    w_receive, _, w_own, w_edges, piece = refs
    span = slice(start, start + piece.shape[0])

    @pl.when(owns(where, group, at_segment))
    def _():
        own = whole[span, :]
        gathered = sum_edges(fanout, columns[span, :], sender[...], own, w_receive[...])
        piece[...] = update_nodes(own, gathered, w_own[...], w_edges[...])


def end_kernel(group, at_segment, chips, far, begin, first, fanout, where, columns, state, *refs):
    senders, refs = (refs[:0], refs) if first else (refs[:1], refs[1:])
    held, came, outs = refs[:4], refs[4:6], refs[6:]
    half = state.shape[0] // 2
    chip, _ = place_of(where, group)
    for here, number in swapped_roles(where, group, at_segment):

        @pl.when(here)
        def _(number=number):
            w_receive, w_send, w_own, w_edges = weights_of(came, held, number == 1)
            pieces = outs
            if first:
                outs[0][...] = matmul(state[...], w_send).astype(jnp.bfloat16)
                pieces = outs[1:]
            sender = outs[0] if first else senders[0]
            rows = sum(piece.shape[0] for piece in pieces)
            upper = (chip < chips // 2) if far else (chip >= chips // 2)
            start = pl.multiple_of(jnp.where(upper, half, 0) + begin, rows)
            own = state[pl.ds(start, rows), :]
            gathered = sum_edges(fanout, columns[pl.ds(start, rows), :], sender[...], own, w_receive)
            write_pieces(pieces, update_nodes(own, gathered, w_own, w_edges))


def write_pieces(pieces, value):
    rows = value.shape[0] // len(pieces)
    for place, piece in enumerate(pieces):
        piece[:rows, :] = value[place * rows : (place + 1) * rows]


def arrival(where, group, chips, last):
    each = chips // 2
    segment = where[0]
    chip, _ = place_of(where, group)
    crosses = lax.div(chip, each) != lax.div(segment, each)
    return crosses, jnp.logical_and(segment >= last, chip == segment), lax.rem(chip, each)


def far_kernel(group, chips, last, number, where, *refs):
    block, out = refs[0], refs[-1]
    crosses, _, spot = arrival(where, group, chips, last)

    @pl.when(jnp.logical_and(crosses, spot == number))
    def _():
        out[...] = block[...]

    if number:

        @pl.when(jnp.logical_and(crosses, spot < number))
        def _():
            out[...] = refs[1][...]


def near_kernel(group, chips, last, where, crossed, *refs):
    each = chips // 2
    near, kept, outs = refs[:each], refs[each : 2 * each], refs[2 * each :]
    rows = outs[0].shape[0]
    crosses, stays, spot = arrival(where, group, chips, last)
    arrives = jnp.logical_not(jnp.logical_or(crosses, stays))

    def give(block):
        for place, out in enumerate(outs):
            out[...] = block[place * rows : (place + 1) * rows, :]

    @pl.when(crosses)
    def _():
        give(crossed)

    for number in range(each):
        for blocks, chosen in ((near, arrives), (kept, stays)):

            @pl.when(jnp.logical_and(chosen, spot == number))
            def _(block=blocks[number]):
                give(block)


def prepare_kernel(where, snapshots, w_embed, w_decode, mesh_grid, ready, table_out):
    snapshot = snapshots[where[0]]
    latent = silu_by_tanh(matmul_tn(snapshot, w_embed[...])).astype(jnp.bfloat16)
    ready[...] = matmul(latent, w_decode[: latent.shape[1], :])
    mesh_rows, grid_rows = table_out.shape
    table = lax.broadcasted_iota(jnp.int32, (mesh_rows, grid_rows), 0) == mesh_grid[...]
    table_out[...] = jnp.where(table, 1.0, 0.0).astype(jnp.bfloat16)


def decode_kernel(where, ready, table, w_decode, w_output, *refs):
    blocks, out, state = refs[:-2], refs[-2], refs[-1]
    width = ready.shape[1]
    _, lane = place_of(where, len(blocks))
    for number, block in enumerate(blocks):

        @pl.when(lane == number)
        def _(block=block):
            state[...] = block[...]

    readout = matmul_tn(table[...], state[...]).astype(jnp.bfloat16)
    hidden = silu_by_tanh(ready[...] + matmul(readout, w_decode[width:, :])).astype(jnp.bfloat16)
    out[...] = matmul_nt(w_output[...], hidden).astype(jnp.bfloat16)


def call(kernel, name, shapes, inputs, places, scratch=(), room=16, flops=0):
    specs, given = [], []
    for value, place in zip(inputs, places):
        specs += [SMEM] * 2 if place == "w" else [VMEM if place == "v" else HBM]
        given += list(value) if place == "w" else [value]
    moved = sum(value.size * value.dtype.itemsize for value in given + list(shapes))

    def located(segment, place, *refs):
        kernel((segment[0], place[0]), *refs)

    return pl.pallas_call(
        located if places[0] == "w" else kernel,
        out_shape=shapes,
        in_specs=specs,
        out_specs=[VMEM] * len(shapes),
        scratch_shapes=list(scratch),
        name=name,
        compiler_params=pltpu.CompilerParams(vmem_limit_bytes=room * 1024 * 1024),
        cost_estimate=pl.CostEstimate(flops=flops, bytes_accessed=moved, transcendentals=0),
    )(*given)


def every_device(pairs, count, group):
    onward = dict(pairs)
    reached = set(onward.values())
    for first in [source for source in onward if source not in reached]:
        last = first
        while last in onward:
            last = onward[last]
        onward.update({last: last + group - 1, last + group - 1: first + group - 1, first + group - 1: first})
    alone = []
    for at in range(0, count, group):
        rest = [lane for lane in range(at, at + group) if lane not in onward]
        if len(rest) > 1:
            onward.update(zip(rest, rest[1:] + rest[:1]))
        else:
            alone += rest
    if len(alone) == 1:
        before = next(at for at in onward if at % group and onward[at] % group == 0)
        onward.update({before: alone[0], alone[0]: onward[before]})
    else:
        onward.update(zip(alone, alone[1:] + alone[:1]))
    return sorted(onward.items())


def resident(
    grid_state,
    w_embed,
    w_project,
    w_message,
    w_update,
    w_decode,
    w_output,
    grid_mesh,
    mesh_grid,
    neighbors,
    send_rows,
    halo_count,
):
    segment = lax.axis_index("segment")
    place = lax.axis_index("dom")
    segments = lax.axis_size("segment")
    parts = lax.axis_size("dom")
    samples, grid_rows, channels = grid_state.shape
    width = w_embed.shape[1]
    mesh_rows, fanout = neighbors.shape
    nodes = parts * mesh_rows
    group = parts // samples
    bf16 = jnp.bfloat16

    def device(at_segment, at_dom):
        return at_segment * parts + at_dom % parts

    def send(value, pairs):
        return lax.ppermute(value, ("segment", "dom"), every_device(pairs, segments * parts, group))

    def to_chip(value, steps):
        giver = steps - 1
        pairs = []
        for at in range(segments):
            for dom in range(parts):
                chip, lane = divmod(dom, group)
                across = (chip ^ steps) * group + lane
                if at == giver:
                    pairs.append((device(at, dom), device(0, across)))
                elif at == 0:
                    pairs.append((device(at, dom), device(giver, dom)))
                else:
                    pairs.append((device(at, dom), device(at, chip * group + (lane + 1) % group)))
        return lax.ppermute(value, ("segment", "dom"), pairs)

    def change_lane(value, steps):
        pairs = [(at, at - at % group + (at + steps) % group) for at in range(parts)]
        return lax.ppermute(value, "dom", pairs)

    def owner(m, at_segment):
        return device(min(at_segment, last + m % 2), m * group)

    own_segment, own_place, w_project = lax.optimization_barrier(
        (segment.reshape(1), place.reshape(1), w_project)
    )
    where = (own_segment, own_place)
    weights = [w_project, w_message, w_update]
    last = segments - 2
    to_last = [(device(last + 1 - m % 2, m * group), owner(m, segments)) for m in range(samples)]
    came_project = send(w_project, to_last)
    snapshots = jnp.transpose(grid_state, (0, 2, 1))
    lists = send_rows.shape[0]

    def rows_of(value):
        return jnp.pad(value, ((0, 0), (0, 128 - value.shape[1])))

    packed = jnp.concatenate(
        [
            rows_of(neighbors.T),
            rows_of(send_rows),
            rows_of(grid_mesh.reshape(1, grid_rows)),
            rows_of(halo_count.reshape(1, lists)),
        ],
        axis=0,
    )
    payloads = call(
        functools.partial(encode_kernel, group, mesh_rows, fanout, lists),
        "encode",
        [jax.ShapeDtypeStruct((mesh_rows + 2 * fanout, width), bf16)] * samples,
        [where, snapshots, w_embed, packed],
        "wvvv",
        [pltpu.VMEM((samples * grid_rows, width), bf16)],
    )
    held = call(
        hold_kernel,
        "hold",
        [jax.ShapeDtypeStruct((width, width), bf16)] * 4,
        weights,
        "hhh",
        [pltpu.VMEM((width, width), bf16)] * 2 + [pltpu.SemaphoreType.DMA((5,))],
    )
    own_payload, *held = lax.optimization_barrier((payloads[0], *held))
    arrived = [own_payload] + [to_chip(payloads[turn], turn) for turn in range(1, samples)]
    (joined,) = call(
        join_kernel,
        "join",
        [jax.ShapeDtypeStruct((samples * (mesh_rows + 2 * fanout), width), bf16)],
        arrived,
        "v" * samples,
    )
    lanes = [joined] + [change_lane(joined, -steps) for steps in range(1, group)]
    share = group * mesh_rows
    whole, short, tall = [
        jax.ShapeDtypeStruct((rows, width), bf16) for rows in (nodes, share, share + 2 * fanout)
    ]
    columns_shape = jax.ShapeDtypeStruct((nodes, 128), bf16)
    columns, codes, state = call(
        functools.partial(index_kernel, parts, mesh_rows),
        "index",
        [columns_shape, jax.ShapeDtypeStruct((2 * fanout, width), bf16), whole],
        [where] + lanes,
        "w" + "v" * group,
        [pltpu.VMEM((fanout, nodes), jnp.int32)],
    )
    columns, came_project, *held = lax.optimization_barrier((columns, came_project, *held))
    (pair,) = call(
        functools.partial(pack_kernel, group, last),
        "pack",
        [jax.ShapeDtypeStruct((2, width, width), bf16)],
        [where] + held[2:],
        "wvv",
    )
    came = [came_project, send(pair, to_last)]
    pieces, senders, rows, extra = [state], [], (nodes,), [codes]
    for layer in range(last):
        pairs = [(owner(m, layer), owner(m, segments if layer + 1 == last else layer + 1)) for m in range(samples)]
        sender, joined_state, piece = call(
            functools.partial(open_kernel, group, layer, fanout, rows),
            "open",
            [whole, whole, tall],
            [where, columns] + pieces + senders + extra + held,
            "w" + "v" * (1 + len(pieces + senders + extra + held)),
        )
        sent = [send(piece, pairs)]
        for start in range(share, nodes, share):
            (piece,) = call(
                functools.partial(next_kernel, group, layer, fanout, start),
                "next",
                [short],
                [where, columns, sender, joined_state] + held,
                "w" + "v" * (3 + len(held)),
            )
            sent.append(send(piece, pairs))
        pieces, senders, rows, extra = sent, [], (share,) * samples, []
        if layer == 0:
            ready, table = call(
                prepare_kernel,
                "prepare",
                [
                    jax.ShapeDtypeStruct((grid_rows, width), jnp.float32),
                    jax.ShapeDtypeStruct((mesh_rows, grid_rows), bf16),
                ],
                [where, snapshots, w_embed, w_decode, mesh_grid.reshape(1, grid_rows)],
                "wvvvv",
            )
            pieces[0], ready, table = lax.optimization_barrier((pieces[0], ready, table))
        for piece in pieces[:-1]:
            if senders:
                piece, senders[-1] = lax.optimization_barrier((piece, senders[-1]))
            late = layer + 1 == last
            sender, *found = call(
                functools.partial(late_sender_kernel if late else sender_kernel, group, layer + 1, fanout, share),
                "sender",
                [short] + [columns_shape] * (not senders),
                [where, piece, held[1]] + came[:1] * late,
                "wvv" + "v" * late,
            )
            columns = found[0] if found else columns
            senders.append(sender)
    (state,) = call(
        functools.partial(layer_kernel, group, last, fanout, rows),
        "layer",
        [whole],
        [where, columns] + pieces + senders + held + came,
        "w" + "v" * (1 + len(pieces + senders + held + came)),
        [pltpu.VMEM((nodes, width), bf16)] * 2,
    )
    far = []
    for begin in range(0, nodes // 2, share):
        found = call(
            functools.partial(end_kernel, group, last, samples, True, begin, not far, fanout),
            "far_part",
            [whole] * (not far) + [short],
            [where, columns, state] + ([sender] if far else []) + held + came,
            "w" + "v" * (9 if far else 8),
        )
        sender = found[0] if not far else sender
        far.append(found[-1])
    near = call(
        functools.partial(end_kernel, group, last, samples, False, 0, False, fanout),
        "near_half",
        [short] * (samples // 2),
        [where, columns, state, sender] + held + came,
        "w" + "v" * 9,
    )
    state = far + list(near)
    each = samples // 2
    arrived = []
    for far, blocks in ((1, state[:each]), (0, state[each:])):
        for turn, block in enumerate(blocks):
            pairs = [
                (owner(m, segments), device(m, ((m // each ^ far) * each + turn) * group)) for m in range(samples)
            ]
            arrived.append(send(block, [pair for pair in pairs if pair[0] != pair[1]]))
    crossed = []
    for number, block in enumerate(arrived[:each]):
        crossed = call(
            functools.partial(far_kernel, group, samples, last, number),
            "far",
            [short],
            [where, block] + list(crossed),
            "wv" + "v" * len(crossed),
        )
    parts_of_block = call(
        functools.partial(near_kernel, group, samples, last),
        "near",
        [jax.ShapeDtypeStruct((mesh_rows, width), bf16)] * group,
        [where, crossed[0]] + arrived[each:] + state[each:],
        "w" + "v" * (1 + 2 * each),
    )
    handed = [parts_of_block[0]]
    for steps in range(1, group):
        handed.append(change_lane(parts_of_block[steps], steps))
    (prediction,) = call(
        decode_kernel,
        "decode",
        [jax.ShapeDtypeStruct((channels, grid_rows), bf16)],
        [where, ready, table, w_decode, w_output.T] + handed,
        "wvvvv" + "v" * group,
        [pltpu.VMEM((mesh_rows, width), bf16)],
    )
    return prediction.T.reshape(1, grid_rows, channels)


def chosen_plan(mesh, *arrays):
    segments, parts = mesh.shape["segment"], mesh.shape["dom"]
    samples, width = arrays[0].shape[0], arrays[1].shape[1]
    nodes = parts * arrays[9].shape[0]
    fits = samples == segments == 4 and parts % samples == 0 and parts > samples and nodes == width
    return (resident if fits else streamed)(*arrays)


def solution(mesh):
    return jax.shard_map(
        functools.partial(chosen_plan, mesh),
        mesh=mesh,
        in_specs=(
            P(None, "dom", None),
            P(),
            P("segment", None, None),
            P("segment", None, None),
            P("segment", None, None),
            P(),
            P(),
            P("dom"),
            P("dom"),
            P("dom", None),
            P(None, "dom"),
            P(None, "dom"),
        ),
        out_specs=P("segment", "dom", None),
        check_vma=False,
    )
```

```python
import functools

import jax
import jax.numpy as jnp
from jax import lax
from jax.experimental import pallas as pl
from jax.experimental.pallas import tpu as pltpu
from jax.sharding import PartitionSpec as P

epsilon = 1e-05
DIGIT = 256
VMEM = pl.BlockSpec(memory_space=pltpu.VMEM)
SMEM = pl.BlockSpec(memory_space=pltpu.SMEM)
HBM = pl.BlockSpec(memory_space=pltpu.HBM)


def from_behind(value, axis, steps):
    count = lax.axis_size(axis)
    pairs = [(source, (source + steps) % count) for source in range(count)]
    return lax.ppermute(value, axis, pairs)


def from_behind_2(block, axis, distance):
    devices = range(lax.axis_size(axis))
    route = [(i - distance, i) for i in devices if i - distance in devices]
    return lax.ppermute(block, axis, route)


def from_root(value, axis, source):
    kept = jnp.where(lax.axis_index(axis) == source, value, 0).astype(value.dtype)
    return lax.psum(kept, axis)


def rms_scale(values):
    return values * lax.rsqrt(jnp.mean(values * values, axis=-1, keepdims=True) + epsilon)


def streamed(
    grid_state,
    w_embed,
    w_project,
    w_message,
    w_update,
    w_decode,
    w_output,
    grid_mesh,
    mesh_grid,
    neighbors,
    send_rows,
    halo_count,
):
    segment_index = lax.axis_index("segment")
    segment_count = lax.axis_size("segment")
    final_segment = segment_count - 1
    samples, grid_rows, channels = grid_state.shape
    width = w_embed.shape[1]
    mesh_rows = neighbors.shape[0]
    fanout = neighbors.shape[1]
    halo_rows = send_rows.shape[1]
    share = samples // segment_count
    pool_table = (grid_mesh[None, :] == jnp.arange(mesh_rows, dtype=jnp.int32)[:, None]).astype(
        jnp.bfloat16
    )
    read_table = (mesh_grid[:, None] == jnp.arange(mesh_rows, dtype=jnp.int32)[None, :]).astype(
        jnp.bfloat16
    )
    valid_rows = jnp.arange(halo_rows, dtype=jnp.int32)[None, :] < halo_count[:, 0][:, None]
    source_rows = neighbors.reshape(mesh_rows * fanout)

    def embed_grid(snapshot):
        return jax.nn.silu(jnp.dot(snapshot, w_embed, preferred_element_type=jnp.float32)).astype(
            jnp.bfloat16
        )

    def encode(snapshot):
        latent = embed_grid(snapshot)
        pooled = jnp.dot(pool_table, latent, preferred_element_type=jnp.float32)
        return (rms_scale(pooled).astype(jnp.bfloat16), latent)

    def project(state, weights):
        projected = jnp.dot(state, weights[0], preferred_element_type=jnp.float32)
        return (projected[:, :width], projected[:, width:].astype(jnp.bfloat16))

    def renew(state, receiver, extended, weights):
        fetched = extended[source_rows].reshape(mesh_rows, fanout, width)
        edges = jax.nn.silu(receiver[:, None, :] + fetched.astype(jnp.float32)).astype(jnp.bfloat16)
        messages = jnp.dot(
            edges.reshape(mesh_rows * fanout, width), weights[1], preferred_element_type=jnp.float32
        )
        aggregate = (jnp.sum(messages.reshape(mesh_rows, fanout, width), axis=1) / fanout).astype(
            jnp.bfloat16
        )
        update = jax.nn.silu(
            jnp.dot(state, weights[2][:width], preferred_element_type=jnp.float32)
            + jnp.dot(aggregate, weights[2][width:], preferred_element_type=jnp.float32)
        )
        return (state.astype(jnp.float32) + rms_scale(update)).astype(jnp.bfloat16)

    def decode(state, latent):
        readout = jnp.dot(read_table, state, preferred_element_type=jnp.float32).astype(
            jnp.bfloat16
        )
        hidden = jax.nn.silu(
            jnp.dot(latent, w_decode[:width], preferred_element_type=jnp.float32)
            + jnp.dot(readout, w_decode[width:], preferred_element_type=jnp.float32)
        ).astype(jnp.bfloat16)
        return jnp.dot(hidden, w_output, preferred_element_type=jnp.float32).astype(jnp.bfloat16)

    own_weights = (w_project[0], w_message[0], w_update[0])
    empty_mesh = jnp.zeros((mesh_rows, width), jnp.bfloat16)
    empty_receiver = jnp.zeros((mesh_rows, width), jnp.float32)
    empty_grid = jnp.zeros((grid_rows, width), jnp.bfloat16)
    empty_output = jnp.zeros((grid_rows, channels), jnp.bfloat16)
    received = empty_mesh
    carried = {}
    results = [empty_output for sample in range(samples)]
    for moment in range(samples + final_segment):
        current = received
        if moment < samples:
            snapshot = grid_state[moment]
            started, latent = lax.cond(
                segment_index == 0, lambda: encode(snapshot), lambda: (empty_mesh, empty_grid)
            )
            current = jnp.where(segment_index == 0, started, received)
            carried[moment] = from_behind_2(latent, "segment", final_segment)
        active = (moment - segment_index >= 0) & (moment - segment_index < samples)
        receiver, outgoing = lax.cond(
            active, lambda: project(current, own_weights), lambda: (empty_receiver, empty_mesh)
        )
        picked = jnp.where(valid_rows[:, :, None], outgoing[send_rows], jnp.zeros((), jnp.bfloat16))
        arrived = [outgoing]
        for list_index, offset in enumerate((1, -1, 2, -2)):
            arrived.append(from_behind(picked[list_index], "dom", offset))
        extended = jnp.concatenate(arrived, axis=0)
        renewed = lax.cond(
            active, lambda: renew(current, receiver, extended, own_weights), lambda: empty_mesh
        )
        if moment >= final_segment:
            finished = moment - final_segment
            skipped = carried[finished]
            results[finished] = lax.cond(
                segment_index == final_segment,
                lambda: decode(renewed, skipped),
                lambda: empty_output,
            )
        if moment < samples + final_segment - 1:
            received = from_behind_2(renewed, "segment", 1)
    everything = from_root(jnp.stack(results), "segment", final_segment)
    return lax.dynamic_slice_in_dim(everything, segment_index * share, share, 0)


def silu_by_tanh(values):
    half = 0.5 * values
    return half + half * jnp.tanh(half)


def matmul(left, right):
    return jnp.dot(left, right, preferred_element_type=jnp.float32)


def matmul_nt(left, right):
    return lax.dot_general(left, right, (((1,), (1,)), ((), ())), preferred_element_type=jnp.float32)


def matmul_tn(left, right):
    return lax.dot_general(left, right, (((0,), (0,)), ((), ())), preferred_element_type=jnp.float32)


def place_of(where, group):
    return lax.div(where[1], group), lax.rem(where[1], group)


def owns(where, group, at_segment):
    return jnp.logical_and(where[0] == at_segment, lax.rem(where[1], group) == 0)


def swapped_roles(where, group, at_segment):
    chip, lane = place_of(where, group)
    for number in range(2):
        here = jnp.logical_and(where[0] == at_segment + number, lane == 0)
        yield jnp.logical_and(here, lax.rem(chip, 2) == number), number


def weights_of(came, held, own):
    if own:
        return [block[...] for block in held]
    w_project, pair = came
    width = pair.shape[1]
    return [w_project[0, :, :width], w_project[0, :, width:], pair[0], pair[1]]


def fetch(sources, targets, semaphores):
    copies = [
        pltpu.make_async_copy(source, target, semaphores.at[place])
        for place, (source, target) in enumerate(zip(sources, targets))
    ]
    for copy in copies:
        copy.start()
    return copies


def encode_kernel(group, mesh_rows, fanout, lists, where, snapshots, w_embed, packed, *refs):
    payloads, latent = refs[:-1], refs[-1]
    chip, _ = place_of(where, group)
    neighbors = packed[:fanout, :mesh_rows]
    grid_rows = snapshots.shape[2]
    grid_mesh = packed[fanout + lists : fanout + lists + 1, :grid_rows]
    counts = packed[fanout + lists + 1 : fanout + lists + 2, :lists]
    width = w_embed.shape[1]
    for place in range(snapshots.shape[0]):
        found = silu_by_tanh(matmul_tn(snapshots[place], w_embed[...])).astype(jnp.bfloat16)
        latent[place * grid_rows : (place + 1) * grid_rows, :] = found
    table = lax.broadcasted_iota(jnp.int32, (mesh_rows, grid_rows), 0) == grid_mesh
    table = jnp.where(table, 1.0, 0.0).astype(jnp.bfloat16)
    block = neighbors // mesh_rows
    row = neighbors - block * mesh_rows
    halo_rows = mesh_rows
    position = lax.broadcasted_iota(jnp.int32, (1, halo_rows), 1)
    rows = []
    for list_index in range(lists):
        kept = position < counts[:, list_index : list_index + 1]
        listed = packed[fanout + list_index : fanout + list_index + 1, :halo_rows]
        rows.append(jnp.where(kept, listed, mesh_rows))
    rows.append(jnp.zeros((fanout - lists, halo_rows), jnp.int32))
    filler = jnp.zeros((fanout, 128 - mesh_rows), jnp.int32)
    pieces = [block, filler, row, filler, jnp.concatenate(rows, axis=0), filler]
    coded = jnp.concatenate(pieces + [jnp.zeros((fanout, width - 384), jnp.int32)], axis=1)
    coded = jnp.concatenate([coded, jnp.zeros_like(coded)], axis=0)
    coded = coded.astype(jnp.float32).astype(jnp.bfloat16)
    for turn, payload in enumerate(payloads):
        start = pl.multiple_of(jnp.bitwise_xor(chip, turn) * grid_rows, grid_rows)
        pooled = matmul(table, latent[pl.ds(start, grid_rows), :])
        payload[:mesh_rows, :] = rms_scale(pooled).astype(jnp.bfloat16)
        payload[mesh_rows:, :] = coded


def join_kernel(*refs):
    payloads, joined = refs[:-1], refs[-1]
    rows = payloads[0].shape[0]
    for place, payload in enumerate(payloads):
        joined[place * rows : (place + 1) * rows, :] = payload[...]


def columns_of(names):
    fanout, nodes = names.shape
    tile = min(nodes, DIGIT)
    rows = [names - number * tile for number in range(nodes // tile)]
    rows.append(jnp.zeros((128 - fanout * len(rows), nodes), jnp.float32))
    return jnp.transpose(jnp.concatenate(rows, axis=0)).astype(jnp.bfloat16)


def index_kernel(parts, mesh_rows, where, *refs):
    lanes, (columns_out, codes, state), index_out = refs[:-4], refs[-4:-1], refs[-1]
    nodes = columns_out.shape[0]
    group = len(lanes)
    rows = lanes[0].shape[0] // (parts // group)
    chip, _ = place_of(where, group)

    @pl.when(owns(where, group, 0))
    def _():
        tables = []
        for part in range(parts):
            lane, turn = lanes[part % group], jnp.bitwise_xor(chip, part // group)
            base = pl.multiple_of(turn * rows, 16)
            state[part * mesh_rows : (part + 1) * mesh_rows, :] = lane[pl.ds(base, mesh_rows), :]
            base = pl.multiple_of(turn * rows + mesh_rows, 16)
            coded = lane[pl.ds(base, rows - mesh_rows), :384].astype(jnp.float32).astype(jnp.int32)
            tables.append(coded[: coded.shape[0] // 2])
        fanout = tables[0].shape[0]
        for part in range(parts):
            block = tables[part][:, :128]
            row = tables[part][:, 128:256]
            found = part * mesh_rows + row
            for list_index, offset in enumerate((-1, 1, -2, 2)):
                source = (part + offset) % parts
                lists = tables[source][list_index : list_index + 1, 256:384]
                lists = jnp.broadcast_to(lists, (fanout, 128))
                picked = jnp.take_along_axis(lists, row, axis=1)
                picked = jnp.where(picked == mesh_rows, parts * mesh_rows, source * mesh_rows + picked)
                found = jnp.where(block == list_index + 1, picked, found)
            index_out[:, part * mesh_rows : (part + 1) * mesh_rows] = found[:, :mesh_rows]
        names = index_out[...]
        high_digit = names // DIGIT
        digits = jnp.concatenate([high_digit, names - high_digit * DIGIT], axis=0)
        codes[...] = digits.astype(jnp.float32).astype(jnp.bfloat16)
        columns_out[...] = columns_of(names.astype(jnp.float32))


def pack_kernel(group, at_segment, where, *refs):
    @pl.when(jnp.logical_or(owns(where, group, at_segment), owns(where, group, at_segment + 1)))
    def _():
        for place, block in enumerate(refs[:-1]):
            refs[-1][place] = block[...]


def hold_kernel(w_project, w_message, w_update, receive, send, own, edges, message, update, semaphores):
    width = own.shape[0]
    sources = [
        w_message.at[0],
        w_update.at[0, width:],
        w_project.at[0, :, :width],
        w_project.at[0, :, width:],
        w_update.at[0, :width],
    ]
    copies = fetch(sources, [message, update, receive, send, own], semaphores)
    copies[0].wait()
    copies[1].wait()
    edges[...] = matmul(message[...], update[...]).astype(jnp.bfloat16)
    for copy in copies[2:]:
        copy.wait()


def sum_edges(fanout, columns, sender, own, w_receive):
    chunk, width = own.shape
    nodes = sender.shape[0]
    tile = min(nodes, DIGIT)
    names = lax.broadcasted_iota(jnp.int32, (chunk, tile), 1).astype(jnp.float32).astype(jnp.bfloat16)
    one_half = jnp.full((chunk, tile), 0.5, jnp.bfloat16)
    none = jnp.zeros((chunk, tile), jnp.bfloat16)
    receiver = 0.5 * matmul(own, w_receive)
    total = jnp.zeros((chunk, width), jnp.float32)
    for k in range(fanout):
        hits = []
        for number in range(nodes // tile):
            lane = number * fanout + k
            hits.append(jnp.where(columns[:, lane : lane + 1] == names, one_half, none))
        half = receiver + matmul(jnp.concatenate(hits, axis=1), sender)
        total = total + (half + half * jnp.tanh(half))
    return (total * (1.0 / fanout)).astype(jnp.bfloat16)


def update_nodes(own, gathered, w_own, w_edges):
    update = silu_by_tanh(matmul(own, w_own) + matmul(gathered, w_edges))
    return (own.astype(jnp.float32) + rms_scale(update)).astype(jnp.bfloat16)


def sender_kernel(group, at_segment, fanout, rows, where, state, w_send, sender, *columns):
    @pl.when(owns(where, group, at_segment))
    def _():
        sender[...] = matmul(state[:rows, :], w_send[...]).astype(jnp.bfloat16)
        if columns:
            digits = state[rows:, :].astype(jnp.float32)
            columns[0][...] = columns_of(digits[:fanout] * DIGIT + digits[fanout:])


def late_sender_kernel(group, at_segment, fanout, rows, where, state, w_send, w_project, sender, *columns):
    width = state.shape[1]
    for here, number in swapped_roles(where, group, at_segment):

        @pl.when(here)
        def _(number=number):
            weights = w_project[0, :, width:] if number else w_send[...]
            sender[...] = matmul(state[:rows, :], weights).astype(jnp.bfloat16)
            if columns:
                digits = state[rows:, :].astype(jnp.float32)
                columns[0][...] = columns_of(digits[:fanout] * DIGIT + digits[fanout:])


def roles(where, group, at_segment, late):
    return swapped_roles(where, group, at_segment) if late else [(owns(where, group, at_segment), 0)]


def early_kernel(group, at_segment, late, fanout, places, quarter, where, columns, *refs):
    count = len(places)
    senders, refs = refs[:count], refs[count:]
    (own, coded), held, came, (piece, sender) = refs[:2], refs[2:6], refs[6:-2], refs[-2:]
    rows = senders[0].shape[0]
    for here, number in roles(where, group, at_segment, late):

        @pl.when(here)
        def _(number=number):
            w_receive, _, w_own, w_edges = weights_of(came, held, number == 0)
            sender[...] = jnp.zeros_like(sender)
            for place, part in zip(places, senders):
                sender[place * rows : (place + 1) * rows, :] = part[...]
            state = own[:rows, :]
            span = slice(quarter * rows, (quarter + 1) * rows)
            gathered = sum_edges(fanout, columns[span, :], sender[...], state, w_receive)
            piece[:rows, :] = update_nodes(state, gathered, w_own, w_edges)
            if piece.shape[0] > rows:
                piece[rows:, :] = coded[rows:, :]


def layer_kernel(group, at_segment, fanout, places, quarter, where, columns, *refs):
    parts = len(places)
    state, senders, refs = refs[:parts], refs[parts : 2 * parts - 1], refs[2 * parts - 1 :]
    done, held, came, (renewed, whole, sender) = refs[0], refs[1:5], refs[5:7], refs[7:]
    rows = done.shape[0]
    spans = [slice(place * rows, (place + 1) * rows) for place in places]
    own = slice(quarter * rows, (quarter + 1) * rows)
    rest = [slice(0, own.start), slice(own.stop, renewed.shape[0])]
    for here, number in swapped_roles(where, group, at_segment):

        @pl.when(here)
        def _(number=number):
            w_receive, w_send, w_own, w_edges = weights_of(came, held, number == 0)
            for span, part in zip(spans, state):
                whole[span, :] = part[:rows, :]
            for span, part in zip(spans, senders):
                sender[span, :] = part[...]
            sender[spans[-1], :] = matmul(whole[spans[-1], :], w_send).astype(jnp.bfloat16)
            renewed[own, :] = done[...]
            for span in rest:
                if span.stop > span.start:
                    gathered = sum_edges(fanout, columns[span, :], sender[...], whole[span, :], w_receive)
                    renewed[span, :] = update_nodes(whole[span, :], gathered, w_own, w_edges)


def open_kernel(group, at_segment, fanout, places, start, where, columns, *refs):
    parts = len(places)
    state, senders, refs = refs[:parts], refs[parts : 2 * parts - 1], refs[2 * parts - 1 :]
    codes, (w_receive, w_send, w_own, w_edges), (sender, whole, piece) = refs[:-7], refs[-7:-3], refs[-3:]
    rows = whole.shape[0] // parts
    spans = [slice(place * rows, (place + 1) * rows) for place in places]

    @pl.when(owns(where, group, at_segment))
    def _():
        for span, part in zip(spans, state):
            whole[span, :] = part[:rows, :]
        for span, part in zip(spans, senders):
            sender[span, :] = part[...]
        sender[spans[-1], :] = matmul(whole[spans[-1], :], w_send[...]).astype(jnp.bfloat16)
        count = piece.shape[0] - (codes[0].shape[0] if codes else 0)
        span = slice(start, start + count)
        own = whole[span, :]
        gathered = sum_edges(fanout, columns[span, :], sender[...], own, w_receive[...])
        piece[:count, :] = update_nodes(own, gathered, w_own[...], w_edges[...])
        if codes:
            piece[count:, :] = codes[0][...]


def next_kernel(group, at_segment, fanout, start, where, columns, sender, whole, *refs):
    w_receive, _, w_own, w_edges, piece = refs
    span = slice(start, start + piece.shape[0])

    @pl.when(owns(where, group, at_segment))
    def _():
        own = whole[span, :]
        gathered = sum_edges(fanout, columns[span, :], sender[...], own, w_receive[...])
        piece[...] = update_nodes(own, gathered, w_own[...], w_edges[...])


def end_kernel(group, at_segment, chips, far, begin, first, fanout, where, columns, state, *refs):
    senders, refs = (refs[:0], refs) if first else (refs[:1], refs[1:])
    held, came, outs = refs[:4], refs[4:6], refs[6:]
    half = state.shape[0] // 2
    chip, _ = place_of(where, group)
    for here, number in swapped_roles(where, group, at_segment):

        @pl.when(here)
        def _(number=number):
            w_receive, w_send, w_own, w_edges = weights_of(came, held, number == 1)
            pieces = outs
            if first:
                outs[0][...] = matmul(state[...], w_send).astype(jnp.bfloat16)
                pieces = outs[1:]
            sender = outs[0] if first else senders[0]
            rows = sum(piece.shape[0] for piece in pieces)
            upper = (chip < chips // 2) if far else (chip >= chips // 2)
            start = pl.multiple_of(jnp.where(upper, half, 0) + begin, rows)
            own = state[pl.ds(start, rows), :]
            gathered = sum_edges(fanout, columns[pl.ds(start, rows), :], sender[...], own, w_receive)
            write_pieces(pieces, update_nodes(own, gathered, w_own, w_edges))


def write_pieces(pieces, value):
    rows = value.shape[0] // len(pieces)
    for place, piece in enumerate(pieces):
        piece[:rows, :] = value[place * rows : (place + 1) * rows]


def arrival(where, group, chips, last):
    each = chips // 2
    segment = where[0]
    chip, _ = place_of(where, group)
    crosses = lax.div(chip, each) != lax.div(segment, each)
    return crosses, jnp.logical_and(segment >= last, chip == segment), lax.rem(chip, each)


def far_kernel(group, chips, last, number, where, *refs):
    block, out = refs[0], refs[-1]
    crosses, _, spot = arrival(where, group, chips, last)

    @pl.when(jnp.logical_and(crosses, spot == number))
    def _():
        out[...] = block[...]

    if number:

        @pl.when(jnp.logical_and(crosses, spot < number))
        def _():
            out[...] = refs[1][...]


def near_kernel(group, chips, last, where, crossed, *refs):
    each = chips // 2
    near, kept, outs = refs[:each], refs[each : 2 * each], refs[2 * each :]
    rows = outs[0].shape[0]
    crosses, stays, spot = arrival(where, group, chips, last)
    arrives = jnp.logical_not(jnp.logical_or(crosses, stays))

    def give(block):
        for place, out in enumerate(outs):
            out[...] = block[place * rows : (place + 1) * rows, :]

    @pl.when(crosses)
    def _():
        give(crossed)

    for number in range(each):
        for blocks, chosen in ((near, arrives), (kept, stays)):

            @pl.when(jnp.logical_and(chosen, spot == number))
            def _(block=blocks[number]):
                give(block)


def prepare_kernel(where, snapshots, w_embed, w_decode, mesh_grid, ready, table_out):
    snapshot = snapshots[where[0]]
    latent = silu_by_tanh(matmul_tn(snapshot, w_embed[...])).astype(jnp.bfloat16)
    ready[...] = matmul(latent, w_decode[: latent.shape[1], :])
    mesh_rows, grid_rows = table_out.shape
    table = lax.broadcasted_iota(jnp.int32, (mesh_rows, grid_rows), 0) == mesh_grid[...]
    table_out[...] = jnp.where(table, 1.0, 0.0).astype(jnp.bfloat16)


def decode_kernel(where, ready, table, w_decode, w_output, *refs):
    blocks, out, state = refs[:-2], refs[-2], refs[-1]
    width = ready.shape[1]
    _, lane = place_of(where, len(blocks))
    for number, block in enumerate(blocks):

        @pl.when(lane == number)
        def _(block=block):
            state[...] = block[...]

    readout = matmul_tn(table[...], state[...]).astype(jnp.bfloat16)
    hidden = silu_by_tanh(ready[...] + matmul(readout, w_decode[width:, :])).astype(jnp.bfloat16)
    out[...] = matmul_nt(w_output[...], hidden).astype(jnp.bfloat16)


def call(kernel, name, shapes, inputs, places, scratch=(), room=16, flops=0):
    specs, given = [], []
    for value, place in zip(inputs, places):
        specs += [SMEM] * 2 if place == "w" else [VMEM if place == "v" else HBM]
        given += list(value) if place == "w" else [value]
    moved = sum(value.size * value.dtype.itemsize for value in given + list(shapes))

    def located(segment, place, *refs):
        kernel((segment[0], place[0]), *refs)

    return pl.pallas_call(
        located if places[0] == "w" else kernel,
        out_shape=shapes,
        in_specs=specs,
        out_specs=[VMEM] * len(shapes),
        scratch_shapes=list(scratch),
        name=name,
        compiler_params=pltpu.CompilerParams(vmem_limit_bytes=room * 1024 * 1024),
        cost_estimate=pl.CostEstimate(flops=flops, bytes_accessed=moved, transcendentals=0),
    )(*given)


def every_device(pairs, count, group):
    onward = dict(pairs)
    reached = set(onward.values())
    for first in [source for source in onward if source not in reached]:
        last = first
        while last in onward:
            last = onward[last]
        onward.update({last: last + group - 1, last + group - 1: first + group - 1, first + group - 1: first})
    alone = []
    for at in range(0, count, group):
        rest = [lane for lane in range(at, at + group) if lane not in onward]
        if len(rest) > 1:
            onward.update(zip(rest, rest[1:] + rest[:1]))
        else:
            alone += rest
    if len(alone) == 1:
        before = next(at for at in onward if at % group and onward[at] % group == 0)
        onward.update({before: alone[0], alone[0]: onward[before]})
    else:
        onward.update(zip(alone, alone[1:] + alone[:1]))
    return sorted(onward.items())


def resident(
    grid_state,
    w_embed,
    w_project,
    w_message,
    w_update,
    w_decode,
    w_output,
    grid_mesh,
    mesh_grid,
    neighbors,
    send_rows,
    halo_count,
):
    segment = lax.axis_index("segment")
    place = lax.axis_index("dom")
    segments = lax.axis_size("segment")
    parts = lax.axis_size("dom")
    samples, grid_rows, channels = grid_state.shape
    width = w_embed.shape[1]
    mesh_rows, fanout = neighbors.shape
    nodes = parts * mesh_rows
    group = parts // samples
    bf16 = jnp.bfloat16

    def device(at_segment, at_dom):
        return at_segment * parts + at_dom % parts

    def send(value, pairs):
        return lax.ppermute(value, ("segment", "dom"), every_device(pairs, segments * parts, group))

    def to_chip(value, steps):
        giver = steps - 1
        pairs = []
        for at in range(segments):
            for dom in range(parts):
                chip, lane = divmod(dom, group)
                across = (chip ^ steps) * group + lane
                if at == giver:
                    pairs.append((device(at, dom), device(0, across)))
                elif at == 0:
                    pairs.append((device(at, dom), device(giver, dom)))
                else:
                    pairs.append((device(at, dom), device(at, chip * group + (lane + 1) % group)))
        return lax.ppermute(value, ("segment", "dom"), pairs)

    def change_lane(value, steps):
        pairs = [(at, at - at % group + (at + steps) % group) for at in range(parts)]
        return lax.ppermute(value, "dom", pairs)

    def owner(m, at_segment):
        return device(min(at_segment, last + m % 2), m * group)

    own_segment, own_place, w_project = lax.optimization_barrier(
        (segment.reshape(1), place.reshape(1), w_project)
    )
    where = (own_segment, own_place)
    weights = [w_project, w_message, w_update]
    last = segments - 2
    to_last = [(device(last + 1 - m % 2, m * group), owner(m, segments)) for m in range(samples)]
    came_project = send(w_project, to_last)
    snapshots = jnp.transpose(grid_state, (0, 2, 1))
    lists = send_rows.shape[0]

    def rows_of(value):
        return jnp.pad(value, ((0, 0), (0, 128 - value.shape[1])))

    packed = jnp.concatenate(
        [
            rows_of(neighbors.T),
            rows_of(send_rows),
            rows_of(grid_mesh.reshape(1, grid_rows)),
            rows_of(halo_count.reshape(1, lists)),
        ],
        axis=0,
    )
    payloads = call(
        functools.partial(encode_kernel, group, mesh_rows, fanout, lists),
        "encode",
        [jax.ShapeDtypeStruct((mesh_rows + 2 * fanout, width), bf16)] * samples,
        [where, snapshots, w_embed, packed],
        "wvvv",
        [pltpu.VMEM((samples * grid_rows, width), bf16)],
    )
    held = call(
        hold_kernel,
        "hold",
        [jax.ShapeDtypeStruct((width, width), bf16)] * 4,
        weights,
        "hhh",
        [pltpu.VMEM((width, width), bf16)] * 2 + [pltpu.SemaphoreType.DMA((5,))],
    )
    own_payload, *held = lax.optimization_barrier((payloads[0], *held))
    arrived = [own_payload] + [to_chip(payloads[turn], turn) for turn in range(1, samples)]
    (joined,) = call(
        join_kernel,
        "join",
        [jax.ShapeDtypeStruct((samples * (mesh_rows + 2 * fanout), width), bf16)],
        arrived,
        "v" * samples,
    )
    lanes = [joined] + [change_lane(joined, -steps) for steps in range(1, group)]
    share = group * mesh_rows
    whole, short, tall = [
        jax.ShapeDtypeStruct((rows, width), bf16) for rows in (nodes, share, share + 2 * fanout)
    ]
    columns_shape = jax.ShapeDtypeStruct((nodes, 128), bf16)
    columns, codes, state = call(
        functools.partial(index_kernel, parts, mesh_rows),
        "index",
        [columns_shape, jax.ShapeDtypeStruct((2 * fanout, width), bf16), whole],
        [where] + lanes,
        "w" + "v" * group,
        [pltpu.VMEM((fanout, nodes), jnp.int32)],
    )
    columns, came_project, *held = lax.optimization_barrier((columns, came_project, *held))
    (pair,) = call(
        functools.partial(pack_kernel, group, last),
        "pack",
        [jax.ShapeDtypeStruct((2, width, width), bf16)],
        [where] + held[2:],
        "wvv",
    )
    came = [came_project, send(pair, to_last)]
    pieces, senders, places, early = [state], [], (0,), []
    for layer in range(last + 1):
        late = layer == last
        pairs = [(owner(m, layer), owner(m, segments if layer + 1 == last else layer + 1)) for m in range(samples)]
        if layer == 0:
            order, sent = list(range(samples)), []
        else:
            first = places[1]
            order = [first] + [(first + step) % samples for step in range(1, samples)]
            (piece,) = call(
                functools.partial(early_kernel, group, layer, late, fanout, places[:-1], first),
                "early",
                [short if late else tall],
                [where, columns] + senders + [pieces[1], pieces[0]] + held + came * late,
                "w" + "v" * (3 + len(senders + held + came * late)),
                [pltpu.VMEM((nodes, width), bf16)],
            )
            if late:
                pieces[-1], piece = lax.optimization_barrier((pieces[-1], piece))
                break
            sent = [send(piece, pairs)]
            pieces[-1], columns = lax.optimization_barrier((pieces[-1], columns))
        start = order[len(sent)] * share
        extra = [codes] * (layer == 0)
        sender, joined_state, piece = call(
            functools.partial(open_kernel, group, layer, fanout, places, start),
            "open",
            [whole, whole, tall if layer == 0 else short],
            [where, columns] + pieces + senders + extra + held,
            "w" + "v" * (1 + len(pieces + senders + extra + held)),
        )
        sent.append(send(piece, pairs))
        for place_sent in order[len(sent) :]:
            (piece,) = call(
                functools.partial(next_kernel, group, layer, fanout, place_sent * share),
                "next",
                [short],
                [where, columns, sender, joined_state] + held,
                "w" + "v" * (3 + len(held)),
            )
            sent.append(send(piece, pairs))
        pieces, senders, places = sent, [], tuple(order)
        if layer == 0:
            ready, table = call(
                prepare_kernel,
                "prepare",
                [
                    jax.ShapeDtypeStruct((grid_rows, width), jnp.float32),
                    jax.ShapeDtypeStruct((mesh_rows, grid_rows), bf16),
                ],
                [where, snapshots, w_embed, w_decode, mesh_grid.reshape(1, grid_rows)],
                "wvvvv",
            )
            pieces[0], ready, table = lax.optimization_barrier((pieces[0], ready, table))
        for number, part in enumerate(pieces[:-1]):
            if senders:
                part, senders[-1] = lax.optimization_barrier((part, senders[-1]))
                pieces[number] = part
            late = layer + 1 == last
            sender, *found = call(
                functools.partial(late_sender_kernel if late else sender_kernel, group, layer + 1, fanout, share),
                "sender",
                [short] + [columns_shape] * (not senders),
                [where, part, held[1]] + came[:1] * late,
                "wvv" + "v" * late,
            )
            columns = found[0] if found else columns
            senders.append(sender)
    (state,) = call(
        functools.partial(layer_kernel, group, last, fanout, places, order[0]),
        "layer",
        [whole],
        [where, columns] + pieces + senders + [piece] + held + came,
        "w" + "v" * (2 + len(pieces + senders + held + came)),
        [pltpu.VMEM((nodes, width), bf16)] * 2,
    )
    far = []
    for begin in range(0, nodes // 2, share):
        found = call(
            functools.partial(end_kernel, group, last, samples, True, begin, not far, fanout),
            "far_part",
            [whole] * (not far) + [short],
            [where, columns, state] + ([sender] if far else []) + held + came,
            "w" + "v" * (9 if far else 8),
        )
        sender = found[0] if not far else sender
        far.append(found[-1])
    near = []
    for begin in range(0, nodes // 2, share):
        near += call(
            functools.partial(end_kernel, group, last, samples, False, begin, False, fanout),
            "near_part",
            [short],
            [where, columns, state, sender] + held + came,
            "w" + "v" * 9,
        )
    state = far + list(near)
    each = samples // 2
    arrived = []
    for far, blocks in ((1, state[:each]), (0, state[each:])):
        for turn, block in enumerate(blocks):
            pairs = [
                (owner(m, segments), device(m, ((m // each ^ far) * each + turn) * group)) for m in range(samples)
            ]
            arrived.append(send(block, [pair for pair in pairs if pair[0] != pair[1]]))
    crossed = []
    for number, block in enumerate(arrived[:each]):
        crossed = call(
            functools.partial(far_kernel, group, samples, last, number),
            "far",
            [short],
            [where, block] + list(crossed),
            "wv" + "v" * len(crossed),
        )
    parts_of_block = call(
        functools.partial(near_kernel, group, samples, last),
        "near",
        [jax.ShapeDtypeStruct((mesh_rows, width), bf16)] * group,
        [where, crossed[0]] + arrived[each:] + state[each:],
        "w" + "v" * (1 + 2 * each),
    )
    handed = [parts_of_block[0]]
    for steps in range(1, group):
        handed.append(change_lane(parts_of_block[steps], steps))
    (prediction,) = call(
        decode_kernel,
        "decode",
        [jax.ShapeDtypeStruct((channels, grid_rows), bf16)],
        [where, ready, table, w_decode, w_output.T] + handed,
        "wvvvv" + "v" * group,
        [pltpu.VMEM((mesh_rows, width), bf16)],
    )
    return prediction.T.reshape(1, grid_rows, channels)


def chosen_plan(mesh, *arrays):
    segments, parts = mesh.shape["segment"], mesh.shape["dom"]
    samples, width = arrays[0].shape[0], arrays[1].shape[1]
    nodes = parts * arrays[9].shape[0]
    fits = samples == segments == 4 and parts % samples == 0 and parts > samples and nodes == width
    return (resident if fits else streamed)(*arrays)


def solution(mesh):
    return jax.shard_map(
        functools.partial(chosen_plan, mesh),
        mesh=mesh,
        in_specs=(
            P(None, "dom", None),
            P(),
            P("segment", None, None),
            P("segment", None, None),
            P("segment", None, None),
            P(),
            P(),
            P("dom"),
            P("dom"),
            P("dom", None),
            P(None, "dom"),
            P(None, "dom"),
        ),
        out_specs=P("segment", "dom", None),
        check_vma=False,
    )
```

```python
import functools

import jax
import jax.numpy as jnp
from jax import lax
from jax.experimental import pallas as pl
from jax.experimental.pallas import tpu as pltpu
from jax.sharding import PartitionSpec as P

epsilon = 1e-05
DIGIT = 256
VMEM = pl.BlockSpec(memory_space=pltpu.VMEM)
SMEM = pl.BlockSpec(memory_space=pltpu.SMEM)
HBM = pl.BlockSpec(memory_space=pltpu.HBM)


def from_behind(value, axis, steps):
    count = lax.axis_size(axis)
    pairs = [(source, (source + steps) % count) for source in range(count)]
    return lax.ppermute(value, axis, pairs)


def from_behind_2(block, axis, distance):
    devices = range(lax.axis_size(axis))
    route = [(i - distance, i) for i in devices if i - distance in devices]
    return lax.ppermute(block, axis, route)


def from_root(value, axis, source):
    kept = jnp.where(lax.axis_index(axis) == source, value, 0).astype(value.dtype)
    return lax.psum(kept, axis)


def rms_scale(values):
    return values * lax.rsqrt(jnp.mean(values * values, axis=-1, keepdims=True) + epsilon)


def streamed(
    grid_state,
    w_embed,
    w_project,
    w_message,
    w_update,
    w_decode,
    w_output,
    grid_mesh,
    mesh_grid,
    neighbors,
    send_rows,
    halo_count,
):
    segment_index = lax.axis_index("segment")
    segment_count = lax.axis_size("segment")
    final_segment = segment_count - 1
    samples, grid_rows, channels = grid_state.shape
    width = w_embed.shape[1]
    mesh_rows = neighbors.shape[0]
    fanout = neighbors.shape[1]
    halo_rows = send_rows.shape[1]
    share = samples // segment_count
    pool_table = (grid_mesh[None, :] == jnp.arange(mesh_rows, dtype=jnp.int32)[:, None]).astype(
        jnp.bfloat16
    )
    read_table = (mesh_grid[:, None] == jnp.arange(mesh_rows, dtype=jnp.int32)[None, :]).astype(
        jnp.bfloat16
    )
    valid_rows = jnp.arange(halo_rows, dtype=jnp.int32)[None, :] < halo_count[:, 0][:, None]
    source_rows = neighbors.reshape(mesh_rows * fanout)

    def embed_grid(snapshot):
        return jax.nn.silu(jnp.dot(snapshot, w_embed, preferred_element_type=jnp.float32)).astype(
            jnp.bfloat16
        )

    def encode(snapshot):
        latent = embed_grid(snapshot)
        pooled = jnp.dot(pool_table, latent, preferred_element_type=jnp.float32)
        return (rms_scale(pooled).astype(jnp.bfloat16), latent)

    def project(state, weights):
        projected = jnp.dot(state, weights[0], preferred_element_type=jnp.float32)
        return (projected[:, :width], projected[:, width:].astype(jnp.bfloat16))

    def renew(state, receiver, extended, weights):
        fetched = extended[source_rows].reshape(mesh_rows, fanout, width)
        edges = jax.nn.silu(receiver[:, None, :] + fetched.astype(jnp.float32)).astype(jnp.bfloat16)
        messages = jnp.dot(
            edges.reshape(mesh_rows * fanout, width), weights[1], preferred_element_type=jnp.float32
        )
        aggregate = (jnp.sum(messages.reshape(mesh_rows, fanout, width), axis=1) / fanout).astype(
            jnp.bfloat16
        )
        update = jax.nn.silu(
            jnp.dot(state, weights[2][:width], preferred_element_type=jnp.float32)
            + jnp.dot(aggregate, weights[2][width:], preferred_element_type=jnp.float32)
        )
        return (state.astype(jnp.float32) + rms_scale(update)).astype(jnp.bfloat16)

    def decode(state, latent):
        readout = jnp.dot(read_table, state, preferred_element_type=jnp.float32).astype(
            jnp.bfloat16
        )
        hidden = jax.nn.silu(
            jnp.dot(latent, w_decode[:width], preferred_element_type=jnp.float32)
            + jnp.dot(readout, w_decode[width:], preferred_element_type=jnp.float32)
        ).astype(jnp.bfloat16)
        return jnp.dot(hidden, w_output, preferred_element_type=jnp.float32).astype(jnp.bfloat16)

    own_weights = (w_project[0], w_message[0], w_update[0])
    empty_mesh = jnp.zeros((mesh_rows, width), jnp.bfloat16)
    empty_receiver = jnp.zeros((mesh_rows, width), jnp.float32)
    empty_grid = jnp.zeros((grid_rows, width), jnp.bfloat16)
    empty_output = jnp.zeros((grid_rows, channels), jnp.bfloat16)
    received = empty_mesh
    carried = {}
    results = [empty_output for sample in range(samples)]
    for moment in range(samples + final_segment):
        current = received
        if moment < samples:
            snapshot = grid_state[moment]
            started, latent = lax.cond(
                segment_index == 0, lambda: encode(snapshot), lambda: (empty_mesh, empty_grid)
            )
            current = jnp.where(segment_index == 0, started, received)
            carried[moment] = from_behind_2(latent, "segment", final_segment)
        active = (moment - segment_index >= 0) & (moment - segment_index < samples)
        receiver, outgoing = lax.cond(
            active, lambda: project(current, own_weights), lambda: (empty_receiver, empty_mesh)
        )
        picked = jnp.where(valid_rows[:, :, None], outgoing[send_rows], jnp.zeros((), jnp.bfloat16))
        arrived = [outgoing]
        for list_index, offset in enumerate((1, -1, 2, -2)):
            arrived.append(from_behind(picked[list_index], "dom", offset))
        extended = jnp.concatenate(arrived, axis=0)
        renewed = lax.cond(
            active, lambda: renew(current, receiver, extended, own_weights), lambda: empty_mesh
        )
        if moment >= final_segment:
            finished = moment - final_segment
            skipped = carried[finished]
            results[finished] = lax.cond(
                segment_index == final_segment,
                lambda: decode(renewed, skipped),
                lambda: empty_output,
            )
        if moment < samples + final_segment - 1:
            received = from_behind_2(renewed, "segment", 1)
    everything = from_root(jnp.stack(results), "segment", final_segment)
    return lax.dynamic_slice_in_dim(everything, segment_index * share, share, 0)


def silu_by_tanh(values):
    half = 0.5 * values
    return half + half * jnp.tanh(half)


def matmul(left, right):
    return jnp.dot(left, right, preferred_element_type=jnp.float32)


def matmul_nt(left, right):
    return lax.dot_general(left, right, (((1,), (1,)), ((), ())), preferred_element_type=jnp.float32)


def matmul_tn(left, right):
    return lax.dot_general(left, right, (((0,), (0,)), ((), ())), preferred_element_type=jnp.float32)


def place_of(where, group):
    return lax.div(where[1], group), lax.rem(where[1], group)


def owns(where, group, at_segment):
    return jnp.logical_and(where[0] == at_segment, lax.rem(where[1], group) == 0)


def swapped_roles(where, group, at_segment):
    chip, lane = place_of(where, group)
    for number in range(2):
        here = jnp.logical_and(where[0] == at_segment + number, lane == 0)
        yield jnp.logical_and(here, lax.rem(chip, 2) == number), number


def weights_of(came, held, own):
    if own:
        return [block[...] for block in held]
    w_project, pair = came
    width = pair.shape[1]
    return [w_project[0, :, :width], w_project[0, :, width:], pair[0], pair[1]]


def fetch(sources, targets, semaphores):
    copies = [
        pltpu.make_async_copy(source, target, semaphores.at[place])
        for place, (source, target) in enumerate(zip(sources, targets))
    ]
    for copy in copies:
        copy.start()
    return copies


def encode_kernel(group, mesh_rows, fanout, lists, where, snapshots, w_embed, packed, *refs):
    payloads, latent = refs[:-1], refs[-1]
    chip, _ = place_of(where, group)
    neighbors = packed[:fanout, :mesh_rows]
    grid_rows = snapshots.shape[2]
    grid_mesh = packed[fanout + lists : fanout + lists + 1, :grid_rows]
    counts = packed[fanout + lists + 1 : fanout + lists + 2, :lists]
    width = w_embed.shape[1]
    for place in range(snapshots.shape[0]):
        found = silu_by_tanh(matmul_tn(snapshots[place], w_embed[...])).astype(jnp.bfloat16)
        latent[place * grid_rows : (place + 1) * grid_rows, :] = found
    table = lax.broadcasted_iota(jnp.int32, (mesh_rows, grid_rows), 0) == grid_mesh
    table = jnp.where(table, 1.0, 0.0).astype(jnp.bfloat16)
    block = neighbors // mesh_rows
    row = neighbors - block * mesh_rows
    halo_rows = mesh_rows
    position = lax.broadcasted_iota(jnp.int32, (1, halo_rows), 1)
    rows = []
    for list_index in range(lists):
        kept = position < counts[:, list_index : list_index + 1]
        listed = packed[fanout + list_index : fanout + list_index + 1, :halo_rows]
        rows.append(jnp.where(kept, listed, mesh_rows))
    rows.append(jnp.zeros((fanout - lists, halo_rows), jnp.int32))
    filler = jnp.zeros((fanout, 128 - mesh_rows), jnp.int32)
    pieces = [block, filler, row, filler, jnp.concatenate(rows, axis=0), filler]
    coded = jnp.concatenate(pieces + [jnp.zeros((fanout, width - 384), jnp.int32)], axis=1)
    coded = jnp.concatenate([coded, jnp.zeros_like(coded)], axis=0)
    coded = coded.astype(jnp.float32).astype(jnp.bfloat16)
    for turn, payload in enumerate(payloads):
        start = pl.multiple_of(jnp.bitwise_xor(chip, turn) * grid_rows, grid_rows)
        pooled = matmul(table, latent[pl.ds(start, grid_rows), :])
        payload[:mesh_rows, :] = rms_scale(pooled).astype(jnp.bfloat16)
        payload[mesh_rows:, :] = coded


def join_kernel(*refs):
    payloads, joined = refs[:-1], refs[-1]
    rows = payloads[0].shape[0]
    for place, payload in enumerate(payloads):
        joined[place * rows : (place + 1) * rows, :] = payload[...]


def columns_of(names):
    fanout, nodes = names.shape
    tile = min(nodes, DIGIT)
    rows = [names - number * tile for number in range(nodes // tile)]
    rows.append(jnp.zeros((128 - fanout * len(rows), nodes), jnp.float32))
    return jnp.transpose(jnp.concatenate(rows, axis=0)).astype(jnp.bfloat16)


def index_kernel(parts, mesh_rows, where, *refs):
    lanes, (columns_out, codes, state), index_out = refs[:-4], refs[-4:-1], refs[-1]
    nodes = columns_out.shape[0]
    group = len(lanes)
    rows = lanes[0].shape[0] // (parts // group)
    chip, _ = place_of(where, group)

    @pl.when(owns(where, group, 0))
    def _():
        tables = []
        for part in range(parts):
            lane, turn = lanes[part % group], jnp.bitwise_xor(chip, part // group)
            base = pl.multiple_of(turn * rows, 16)
            state[part * mesh_rows : (part + 1) * mesh_rows, :] = lane[pl.ds(base, mesh_rows), :]
            base = pl.multiple_of(turn * rows + mesh_rows, 16)
            coded = lane[pl.ds(base, rows - mesh_rows), :384].astype(jnp.float32).astype(jnp.int32)
            tables.append(coded[: coded.shape[0] // 2])
        fanout = tables[0].shape[0]
        for part in range(parts):
            block = tables[part][:, :128]
            row = tables[part][:, 128:256]
            found = part * mesh_rows + row
            for list_index, offset in enumerate((-1, 1, -2, 2)):
                source = (part + offset) % parts
                lists = tables[source][list_index : list_index + 1, 256:384]
                lists = jnp.broadcast_to(lists, (fanout, 128))
                picked = jnp.take_along_axis(lists, row, axis=1)
                picked = jnp.where(picked == mesh_rows, parts * mesh_rows, source * mesh_rows + picked)
                found = jnp.where(block == list_index + 1, picked, found)
            index_out[:, part * mesh_rows : (part + 1) * mesh_rows] = found[:, :mesh_rows]
        names = index_out[...]
        high_digit = names // DIGIT
        digits = jnp.concatenate([high_digit, names - high_digit * DIGIT], axis=0)
        codes[...] = digits.astype(jnp.float32).astype(jnp.bfloat16)
        columns_out[...] = columns_of(names.astype(jnp.float32))


def pack_kernel(group, at_segment, where, *refs):
    @pl.when(jnp.logical_or(owns(where, group, at_segment), owns(where, group, at_segment + 1)))
    def _():
        for place, block in enumerate(refs[:-1]):
            refs[-1][place] = block[...]


def hold_kernel(w_project, w_message, w_update, receive, send, own, edges, message, update, semaphores):
    width = own.shape[0]
    sources = [
        w_message.at[0],
        w_update.at[0, width:],
        w_project.at[0, :, :width],
        w_project.at[0, :, width:],
        w_update.at[0, :width],
    ]
    copies = fetch(sources, [message, update, receive, send, own], semaphores)
    copies[0].wait()
    copies[1].wait()
    edges[...] = matmul(message[...], update[...]).astype(jnp.bfloat16)
    for copy in copies[2:]:
        copy.wait()


def sum_edges(fanout, columns, sender, own, w_receive):
    chunk, width = own.shape
    nodes = sender.shape[0]
    tile = min(nodes, DIGIT)
    names = lax.broadcasted_iota(jnp.int32, (chunk, tile), 1).astype(jnp.float32).astype(jnp.bfloat16)
    one_half = jnp.full((chunk, tile), 0.5, jnp.bfloat16)
    none = jnp.zeros((chunk, tile), jnp.bfloat16)
    receiver = 0.5 * matmul(own, w_receive)
    total = jnp.zeros((chunk, width), jnp.float32)
    for k in range(fanout):
        hits = []
        for number in range(nodes // tile):
            lane = number * fanout + k
            hits.append(jnp.where(columns[:, lane : lane + 1] == names, one_half, none))
        half = (receiver + matmul(jnp.concatenate(hits, axis=1), sender)).astype(jnp.bfloat16)
        total = total + (half + half * jnp.tanh(half)).astype(jnp.float32)
    return (total * (1.0 / fanout)).astype(jnp.bfloat16)


def update_nodes(own, gathered, w_own, w_edges):
    update = silu_by_tanh(matmul(own, w_own) + matmul(gathered, w_edges))
    return (own.astype(jnp.float32) + rms_scale(update)).astype(jnp.bfloat16)


def sender_kernel(group, at_segment, fanout, rows, where, state, w_send, sender, *columns):
    @pl.when(owns(where, group, at_segment))
    def _():
        sender[...] = matmul(state[:rows, :], w_send[...]).astype(jnp.bfloat16)
        if columns:
            digits = state[rows:, :].astype(jnp.float32)
            columns[0][...] = columns_of(digits[:fanout] * DIGIT + digits[fanout:])


def late_sender_kernel(group, at_segment, fanout, rows, where, state, w_send, w_project, sender, *columns):
    width = state.shape[1]
    for here, number in swapped_roles(where, group, at_segment):

        @pl.when(here)
        def _(number=number):
            weights = w_project[0, :, width:] if number else w_send[...]
            sender[...] = matmul(state[:rows, :], weights).astype(jnp.bfloat16)
            if columns:
                digits = state[rows:, :].astype(jnp.float32)
                columns[0][...] = columns_of(digits[:fanout] * DIGIT + digits[fanout:])


def roles(where, group, at_segment, late):
    return swapped_roles(where, group, at_segment) if late else [(owns(where, group, at_segment), 0)]


def early_kernel(group, at_segment, late, fanout, places, quarter, where, columns, *refs):
    count = len(places)
    senders, refs = refs[:count], refs[count:]
    (own, coded), held, came, (piece, sender) = refs[:2], refs[2:6], refs[6:-2], refs[-2:]
    rows = senders[0].shape[0]
    for here, number in roles(where, group, at_segment, late):

        @pl.when(here)
        def _(number=number):
            w_receive, _, w_own, w_edges = weights_of(came, held, number == 0)
            sender[...] = jnp.zeros_like(sender)
            for place, part in zip(places, senders):
                sender[place * rows : (place + 1) * rows, :] = part[...]
            state = own[:rows, :]
            span = slice(quarter * rows, (quarter + 1) * rows)
            gathered = sum_edges(fanout, columns[span, :], sender[...], state, w_receive)
            piece[:rows, :] = update_nodes(state, gathered, w_own, w_edges)
            if piece.shape[0] > rows:
                piece[rows:, :] = coded[rows:, :]


def layer_kernel(group, at_segment, fanout, places, quarter, where, columns, *refs):
    parts = len(places)
    state, senders, refs = refs[:parts], refs[parts : 2 * parts - 1], refs[2 * parts - 1 :]
    done, held, came, (renewed, whole, sender) = refs[0], refs[1:5], refs[5:7], refs[7:]
    rows = done.shape[0]
    spans = [slice(place * rows, (place + 1) * rows) for place in places]
    own = slice(quarter * rows, (quarter + 1) * rows)
    rest = [slice(0, own.start), slice(own.stop, renewed.shape[0])]
    for here, number in swapped_roles(where, group, at_segment):

        @pl.when(here)
        def _(number=number):
            w_receive, w_send, w_own, w_edges = weights_of(came, held, number == 0)
            for span, part in zip(spans, state):
                whole[span, :] = part[:rows, :]
            for span, part in zip(spans, senders):
                sender[span, :] = part[...]
            sender[spans[-1], :] = matmul(whole[spans[-1], :], w_send).astype(jnp.bfloat16)
            renewed[own, :] = done[...]
            for span in rest:
                if span.stop > span.start:
                    gathered = sum_edges(fanout, columns[span, :], sender[...], whole[span, :], w_receive)
                    renewed[span, :] = update_nodes(whole[span, :], gathered, w_own, w_edges)


def open_kernel(group, at_segment, fanout, places, start, where, columns, *refs):
    parts = len(places)
    state, senders, refs = refs[:parts], refs[parts : 2 * parts - 1], refs[2 * parts - 1 :]
    codes, (w_receive, w_send, w_own, w_edges), (sender, whole, piece) = refs[:-7], refs[-7:-3], refs[-3:]
    rows = whole.shape[0] // parts
    spans = [slice(place * rows, (place + 1) * rows) for place in places]

    @pl.when(owns(where, group, at_segment))
    def _():
        for span, part in zip(spans, state):
            whole[span, :] = part[:rows, :]
        for span, part in zip(spans, senders):
            sender[span, :] = part[...]
        sender[spans[-1], :] = matmul(whole[spans[-1], :], w_send[...]).astype(jnp.bfloat16)
        count = piece.shape[0] - (codes[0].shape[0] if codes else 0)
        span = slice(start, start + count)
        own = whole[span, :]
        gathered = sum_edges(fanout, columns[span, :], sender[...], own, w_receive[...])
        piece[:count, :] = update_nodes(own, gathered, w_own[...], w_edges[...])
        if codes:
            piece[count:, :] = codes[0][...]


def next_kernel(group, at_segment, fanout, start, where, columns, sender, whole, *refs):
    w_receive, _, w_own, w_edges, piece = refs
    span = slice(start, start + piece.shape[0])

    @pl.when(owns(where, group, at_segment))
    def _():
        own = whole[span, :]
        gathered = sum_edges(fanout, columns[span, :], sender[...], own, w_receive[...])
        piece[...] = update_nodes(own, gathered, w_own[...], w_edges[...])


def end_kernel(group, at_segment, chips, far, begin, first, fanout, where, columns, state, *refs):
    senders, refs = (refs[:0], refs) if first else (refs[:1], refs[1:])
    held, came, outs = refs[:4], refs[4:6], refs[6:]
    half = state.shape[0] // 2
    chip, _ = place_of(where, group)
    for here, number in swapped_roles(where, group, at_segment):

        @pl.when(here)
        def _(number=number):
            w_receive, w_send, w_own, w_edges = weights_of(came, held, number == 1)
            pieces = outs
            if first:
                outs[0][...] = matmul(state[...], w_send).astype(jnp.bfloat16)
                pieces = outs[1:]
            sender = outs[0] if first else senders[0]
            rows = sum(piece.shape[0] for piece in pieces)
            upper = (chip < chips // 2) if far else (chip >= chips // 2)
            start = pl.multiple_of(jnp.where(upper, half, 0) + begin, rows)
            own = state[pl.ds(start, rows), :]
            gathered = sum_edges(fanout, columns[pl.ds(start, rows), :], sender[...], own, w_receive)
            write_pieces(pieces, update_nodes(own, gathered, w_own, w_edges))


def write_pieces(pieces, value):
    rows = value.shape[0] // len(pieces)
    for place, piece in enumerate(pieces):
        piece[:rows, :] = value[place * rows : (place + 1) * rows]


def arrival(where, group, chips, last):
    each = chips // 2
    segment = where[0]
    chip, _ = place_of(where, group)
    crosses = lax.div(chip, each) != lax.div(segment, each)
    return crosses, jnp.logical_and(segment >= last, chip == segment), lax.rem(chip, each)


def far_kernel(group, chips, last, number, where, *refs):
    block, out = refs[0], refs[-1]
    crosses, _, spot = arrival(where, group, chips, last)

    @pl.when(jnp.logical_and(crosses, spot == number))
    def _():
        out[...] = block[...]

    if number:

        @pl.when(jnp.logical_and(crosses, spot < number))
        def _():
            out[...] = refs[1][...]


def near_kernel(group, chips, last, where, crossed, *refs):
    each = chips // 2
    near, kept, outs = refs[:each], refs[each : 2 * each], refs[2 * each :]
    rows = outs[0].shape[0]
    crosses, stays, spot = arrival(where, group, chips, last)
    arrives = jnp.logical_not(jnp.logical_or(crosses, stays))

    def give(block):
        for place, out in enumerate(outs):
            out[...] = block[place * rows : (place + 1) * rows, :]

    @pl.when(crosses)
    def _():
        give(crossed)

    for number in range(each):
        for blocks, chosen in ((near, arrives), (kept, stays)):

            @pl.when(jnp.logical_and(chosen, spot == number))
            def _(block=blocks[number]):
                give(block)


def prepare_kernel(where, snapshots, w_embed, w_decode, mesh_grid, ready, table_out):
    snapshot = snapshots[where[0]]
    latent = silu_by_tanh(matmul_tn(snapshot, w_embed[...])).astype(jnp.bfloat16)
    ready[...] = matmul(latent, w_decode[: latent.shape[1], :])
    mesh_rows, grid_rows = table_out.shape
    table = lax.broadcasted_iota(jnp.int32, (mesh_rows, grid_rows), 0) == mesh_grid[...]
    table_out[...] = jnp.where(table, 1.0, 0.0).astype(jnp.bfloat16)


def decode_kernel(where, ready, table, w_decode, w_output, *refs):
    blocks, out, state = refs[:-2], refs[-2], refs[-1]
    width = ready.shape[1]
    _, lane = place_of(where, len(blocks))
    for number, block in enumerate(blocks):

        @pl.when(lane == number)
        def _(block=block):
            state[...] = block[...]

    readout = matmul_tn(table[...], state[...]).astype(jnp.bfloat16)
    hidden = silu_by_tanh(ready[...] + matmul(readout, w_decode[width:, :])).astype(jnp.bfloat16)
    out[...] = matmul_nt(w_output[...], hidden).astype(jnp.bfloat16)


def call(kernel, name, shapes, inputs, places, scratch=(), room=16, flops=0):
    specs, given = [], []
    for value, place in zip(inputs, places):
        specs += [SMEM] * 2 if place == "w" else [VMEM if place == "v" else HBM]
        given += list(value) if place == "w" else [value]
    moved = sum(value.size * value.dtype.itemsize for value in given + list(shapes))

    def located(segment, place, *refs):
        kernel((segment[0], place[0]), *refs)

    return pl.pallas_call(
        located if places[0] == "w" else kernel,
        out_shape=shapes,
        in_specs=specs,
        out_specs=[VMEM] * len(shapes),
        scratch_shapes=list(scratch),
        name=name,
        compiler_params=pltpu.CompilerParams(vmem_limit_bytes=room * 1024 * 1024),
        cost_estimate=pl.CostEstimate(flops=flops, bytes_accessed=moved, transcendentals=0),
    )(*given)


def every_device(pairs, count, group):
    onward = dict(pairs)
    reached = set(onward.values())
    for first in [source for source in onward if source not in reached]:
        last = first
        while last in onward:
            last = onward[last]
        onward.update({last: last + group - 1, last + group - 1: first + group - 1, first + group - 1: first})
    alone = []
    for at in range(0, count, group):
        rest = [lane for lane in range(at, at + group) if lane not in onward]
        if len(rest) > 1:
            onward.update(zip(rest, rest[1:] + rest[:1]))
        else:
            alone += rest
    if len(alone) == 1:
        before = next(at for at in onward if at % group and onward[at] % group == 0)
        onward.update({before: alone[0], alone[0]: onward[before]})
    else:
        onward.update(zip(alone, alone[1:] + alone[:1]))
    return sorted(onward.items())


def resident(
    grid_state,
    w_embed,
    w_project,
    w_message,
    w_update,
    w_decode,
    w_output,
    grid_mesh,
    mesh_grid,
    neighbors,
    send_rows,
    halo_count,
):
    segment = lax.axis_index("segment")
    place = lax.axis_index("dom")
    segments = lax.axis_size("segment")
    parts = lax.axis_size("dom")
    samples, grid_rows, channels = grid_state.shape
    width = w_embed.shape[1]
    mesh_rows, fanout = neighbors.shape
    nodes = parts * mesh_rows
    group = parts // samples
    bf16 = jnp.bfloat16

    def device(at_segment, at_dom):
        return at_segment * parts + at_dom % parts

    def send(value, pairs):
        return lax.ppermute(value, ("segment", "dom"), every_device(pairs, segments * parts, group))

    def to_chip(value, steps):
        giver = steps - 1
        pairs = []
        for at in range(segments):
            for dom in range(parts):
                chip, lane = divmod(dom, group)
                across = (chip ^ steps) * group + lane
                if at == giver:
                    pairs.append((device(at, dom), device(0, across)))
                elif at == 0:
                    pairs.append((device(at, dom), device(giver, dom)))
                else:
                    pairs.append((device(at, dom), device(at, chip * group + (lane + 1) % group)))
        return lax.ppermute(value, ("segment", "dom"), pairs)

    def change_lane(value, steps):
        pairs = [(at, at - at % group + (at + steps) % group) for at in range(parts)]
        return lax.ppermute(value, "dom", pairs)

    def owner(m, at_segment):
        return device(min(at_segment, last + m % 2), m * group)

    own_segment, own_place, w_project = lax.optimization_barrier(
        (segment.reshape(1), place.reshape(1), w_project)
    )
    where = (own_segment, own_place)
    weights = [w_project, w_message, w_update]
    last = segments - 2
    to_last = [(device(last + 1 - m % 2, m * group), owner(m, segments)) for m in range(samples)]
    came_project = send(w_project, to_last)
    snapshots = jnp.transpose(grid_state, (0, 2, 1))
    lists = send_rows.shape[0]

    def rows_of(value):
        return jnp.pad(value, ((0, 0), (0, 128 - value.shape[1])))

    packed = jnp.concatenate(
        [
            rows_of(neighbors.T),
            rows_of(send_rows),
            rows_of(grid_mesh.reshape(1, grid_rows)),
            rows_of(halo_count.reshape(1, lists)),
        ],
        axis=0,
    )
    payloads = call(
        functools.partial(encode_kernel, group, mesh_rows, fanout, lists),
        "encode",
        [jax.ShapeDtypeStruct((mesh_rows + 2 * fanout, width), bf16)] * samples,
        [where, snapshots, w_embed, packed],
        "wvvv",
        [pltpu.VMEM((samples * grid_rows, width), bf16)],
    )
    held = call(
        hold_kernel,
        "hold",
        [jax.ShapeDtypeStruct((width, width), bf16)] * 4,
        weights,
        "hhh",
        [pltpu.VMEM((width, width), bf16)] * 2 + [pltpu.SemaphoreType.DMA((5,))],
    )
    own_payload, *held = lax.optimization_barrier((payloads[0], *held))
    arrived = [own_payload] + [to_chip(payloads[turn], turn) for turn in range(1, samples)]
    (joined,) = call(
        join_kernel,
        "join",
        [jax.ShapeDtypeStruct((samples * (mesh_rows + 2 * fanout), width), bf16)],
        arrived,
        "v" * samples,
    )
    lanes = [joined] + [change_lane(joined, -steps) for steps in range(1, group)]
    share = group * mesh_rows
    whole, short, tall = [
        jax.ShapeDtypeStruct((rows, width), bf16) for rows in (nodes, share, share + 2 * fanout)
    ]
    columns_shape = jax.ShapeDtypeStruct((nodes, 128), bf16)
    columns, codes, state = call(
        functools.partial(index_kernel, parts, mesh_rows),
        "index",
        [columns_shape, jax.ShapeDtypeStruct((2 * fanout, width), bf16), whole],
        [where] + lanes,
        "w" + "v" * group,
        [pltpu.VMEM((fanout, nodes), jnp.int32)],
    )
    columns, came_project, *held = lax.optimization_barrier((columns, came_project, *held))
    (pair,) = call(
        functools.partial(pack_kernel, group, last),
        "pack",
        [jax.ShapeDtypeStruct((2, width, width), bf16)],
        [where] + held[2:],
        "wvv",
    )
    came = [came_project, send(pair, to_last)]
    pieces, senders, places, early = [state], [], (0,), []
    for layer in range(last + 1):
        late = layer == last
        pairs = [(owner(m, layer), owner(m, segments if layer + 1 == last else layer + 1)) for m in range(samples)]
        if layer == 0:
            order, sent = list(range(samples)), []
        else:
            first = places[1]
            order = [first] + [(first + step) % samples for step in range(1, samples)]
            (piece,) = call(
                functools.partial(early_kernel, group, layer, late, fanout, places[:-1], first),
                "early",
                [short if late else tall],
                [where, columns] + senders + [pieces[1], pieces[0]] + held + came * late,
                "w" + "v" * (3 + len(senders + held + came * late)),
                [pltpu.VMEM((nodes, width), bf16)],
            )
            if late:
                pieces[-1], piece = lax.optimization_barrier((pieces[-1], piece))
                break
            sent = [send(piece, pairs)]
            pieces[-1], columns = lax.optimization_barrier((pieces[-1], columns))
        start = order[len(sent)] * share
        extra = [codes] * (layer == 0)
        sender, joined_state, piece = call(
            functools.partial(open_kernel, group, layer, fanout, places, start),
            "open",
            [whole, whole, tall if layer == 0 else short],
            [where, columns] + pieces + senders + extra + held,
            "w" + "v" * (1 + len(pieces + senders + extra + held)),
        )
        sent.append(send(piece, pairs))
        for place_sent in order[len(sent) :]:
            (piece,) = call(
                functools.partial(next_kernel, group, layer, fanout, place_sent * share),
                "next",
                [short],
                [where, columns, sender, joined_state] + held,
                "w" + "v" * (3 + len(held)),
            )
            sent.append(send(piece, pairs))
        pieces, senders, places = sent, [], tuple(order)
        if layer == 0:
            ready, table = call(
                prepare_kernel,
                "prepare",
                [
                    jax.ShapeDtypeStruct((grid_rows, width), jnp.float32),
                    jax.ShapeDtypeStruct((mesh_rows, grid_rows), bf16),
                ],
                [where, snapshots, w_embed, w_decode, mesh_grid.reshape(1, grid_rows)],
                "wvvvv",
            )
            pieces[0], ready, table = lax.optimization_barrier((pieces[0], ready, table))
        for number, part in enumerate(pieces[:-1]):
            if senders:
                part, senders[-1] = lax.optimization_barrier((part, senders[-1]))
                pieces[number] = part
            late = layer + 1 == last
            sender, *found = call(
                functools.partial(late_sender_kernel if late else sender_kernel, group, layer + 1, fanout, share),
                "sender",
                [short] + [columns_shape] * (not senders),
                [where, part, held[1]] + came[:1] * late,
                "wvv" + "v" * late,
            )
            columns = found[0] if found else columns
            senders.append(sender)
    (state,) = call(
        functools.partial(layer_kernel, group, last, fanout, places, order[0]),
        "layer",
        [whole],
        [where, columns] + pieces + senders + [piece] + held + came,
        "w" + "v" * (2 + len(pieces + senders + held + came)),
        [pltpu.VMEM((nodes, width), bf16)] * 2,
    )
    far = []
    for begin in range(0, nodes // 2, share):
        found = call(
            functools.partial(end_kernel, group, last, samples, True, begin, not far, fanout),
            "far_part",
            [whole] * (not far) + [short],
            [where, columns, state] + ([sender] if far else []) + held + came,
            "w" + "v" * (9 if far else 8),
        )
        sender = found[0] if not far else sender
        far.append(found[-1])
    near = []
    for begin in range(0, nodes // 2, share):
        near += call(
            functools.partial(end_kernel, group, last, samples, False, begin, False, fanout),
            "near_part",
            [short],
            [where, columns, state, sender] + held + came,
            "w" + "v" * 9,
        )
    state = far + list(near)
    each = samples // 2
    arrived = []
    for far, blocks in ((1, state[:each]), (0, state[each:])):
        for turn, block in enumerate(blocks):
            pairs = [
                (owner(m, segments), device(m, ((m // each ^ far) * each + turn) * group)) for m in range(samples)
            ]
            arrived.append(send(block, [pair for pair in pairs if pair[0] != pair[1]]))
    crossed = []
    for number, block in enumerate(arrived[:each]):
        crossed = call(
            functools.partial(far_kernel, group, samples, last, number),
            "far",
            [short],
            [where, block] + list(crossed),
            "wv" + "v" * len(crossed),
        )
    parts_of_block = call(
        functools.partial(near_kernel, group, samples, last),
        "near",
        [jax.ShapeDtypeStruct((mesh_rows, width), bf16)] * group,
        [where, crossed[0]] + arrived[each:] + state[each:],
        "w" + "v" * (1 + 2 * each),
    )
    handed = [parts_of_block[0]]
    for steps in range(1, group):
        handed.append(change_lane(parts_of_block[steps], steps))
    (prediction,) = call(
        decode_kernel,
        "decode",
        [jax.ShapeDtypeStruct((channels, grid_rows), bf16)],
        [where, ready, table, w_decode, w_output.T] + handed,
        "wvvvv" + "v" * group,
        [pltpu.VMEM((mesh_rows, width), bf16)],
    )
    return prediction.T.reshape(1, grid_rows, channels)


def chosen_plan(mesh, *arrays):
    segments, parts = mesh.shape["segment"], mesh.shape["dom"]
    samples, width = arrays[0].shape[0], arrays[1].shape[1]
    nodes = parts * arrays[9].shape[0]
    fits = samples == segments == 4 and parts % samples == 0 and parts > samples and nodes == width
    return (resident if fits else streamed)(*arrays)


def solution(mesh):
    return jax.shard_map(
        functools.partial(chosen_plan, mesh),
        mesh=mesh,
        in_specs=(
            P(None, "dom", None),
            P(),
            P("segment", None, None),
            P("segment", None, None),
            P("segment", None, None),
            P(),
            P(),
            P("dom"),
            P("dom"),
            P("dom", None),
            P(None, "dom"),
            P(None, "dom"),
        ),
        out_specs=P("segment", "dom", None),
        check_vma=False,
    )
```

```python
import functools

import jax
import jax.numpy as jnp
from jax import lax
from jax.experimental import pallas as pl
from jax.experimental.pallas import tpu as pltpu
from jax.sharding import PartitionSpec as P

epsilon = 1e-05
DIGIT = 256
VMEM = pl.BlockSpec(memory_space=pltpu.VMEM)
SMEM = pl.BlockSpec(memory_space=pltpu.SMEM)
HBM = pl.BlockSpec(memory_space=pltpu.HBM)


def from_behind(value, axis, steps):
    count = lax.axis_size(axis)
    pairs = [(source, (source + steps) % count) for source in range(count)]
    return lax.ppermute(value, axis, pairs)


def from_behind_2(block, axis, distance):
    devices = range(lax.axis_size(axis))
    route = [(i - distance, i) for i in devices if i - distance in devices]
    return lax.ppermute(block, axis, route)


def from_root(value, axis, source):
    kept = jnp.where(lax.axis_index(axis) == source, value, 0).astype(value.dtype)
    return lax.psum(kept, axis)


def rms_scale(values):
    return values * lax.rsqrt(jnp.mean(values * values, axis=-1, keepdims=True) + epsilon)


def streamed(
    grid_state,
    w_embed,
    w_project,
    w_message,
    w_update,
    w_decode,
    w_output,
    grid_mesh,
    mesh_grid,
    neighbors,
    send_rows,
    halo_count,
):
    segment_index = lax.axis_index("segment")
    segment_count = lax.axis_size("segment")
    final_segment = segment_count - 1
    samples, grid_rows, channels = grid_state.shape
    width = w_embed.shape[1]
    mesh_rows = neighbors.shape[0]
    fanout = neighbors.shape[1]
    halo_rows = send_rows.shape[1]
    share = samples // segment_count
    pool_table = (grid_mesh[None, :] == jnp.arange(mesh_rows, dtype=jnp.int32)[:, None]).astype(
        jnp.bfloat16
    )
    read_table = (mesh_grid[:, None] == jnp.arange(mesh_rows, dtype=jnp.int32)[None, :]).astype(
        jnp.bfloat16
    )
    valid_rows = jnp.arange(halo_rows, dtype=jnp.int32)[None, :] < halo_count[:, 0][:, None]
    source_rows = neighbors.reshape(mesh_rows * fanout)

    def embed_grid(snapshot):
        return jax.nn.silu(jnp.dot(snapshot, w_embed, preferred_element_type=jnp.float32)).astype(
            jnp.bfloat16
        )

    def encode(snapshot):
        latent = embed_grid(snapshot)
        pooled = jnp.dot(pool_table, latent, preferred_element_type=jnp.float32)
        return (rms_scale(pooled).astype(jnp.bfloat16), latent)

    def project(state, weights):
        projected = jnp.dot(state, weights[0], preferred_element_type=jnp.float32)
        return (projected[:, :width], projected[:, width:].astype(jnp.bfloat16))

    def renew(state, receiver, extended, weights):
        fetched = extended[source_rows].reshape(mesh_rows, fanout, width)
        edges = jax.nn.silu(receiver[:, None, :] + fetched.astype(jnp.float32)).astype(jnp.bfloat16)
        messages = jnp.dot(
            edges.reshape(mesh_rows * fanout, width), weights[1], preferred_element_type=jnp.float32
        )
        aggregate = (jnp.sum(messages.reshape(mesh_rows, fanout, width), axis=1) / fanout).astype(
            jnp.bfloat16
        )
        update = jax.nn.silu(
            jnp.dot(state, weights[2][:width], preferred_element_type=jnp.float32)
            + jnp.dot(aggregate, weights[2][width:], preferred_element_type=jnp.float32)
        )
        return (state.astype(jnp.float32) + rms_scale(update)).astype(jnp.bfloat16)

    def decode(state, latent):
        readout = jnp.dot(read_table, state, preferred_element_type=jnp.float32).astype(
            jnp.bfloat16
        )
        hidden = jax.nn.silu(
            jnp.dot(latent, w_decode[:width], preferred_element_type=jnp.float32)
            + jnp.dot(readout, w_decode[width:], preferred_element_type=jnp.float32)
        ).astype(jnp.bfloat16)
        return jnp.dot(hidden, w_output, preferred_element_type=jnp.float32).astype(jnp.bfloat16)

    own_weights = (w_project[0], w_message[0], w_update[0])
    empty_mesh = jnp.zeros((mesh_rows, width), jnp.bfloat16)
    empty_receiver = jnp.zeros((mesh_rows, width), jnp.float32)
    empty_grid = jnp.zeros((grid_rows, width), jnp.bfloat16)
    empty_output = jnp.zeros((grid_rows, channels), jnp.bfloat16)
    received = empty_mesh
    carried = {}
    results = [empty_output for sample in range(samples)]
    for moment in range(samples + final_segment):
        current = received
        if moment < samples:
            snapshot = grid_state[moment]
            started, latent = lax.cond(
                segment_index == 0, lambda: encode(snapshot), lambda: (empty_mesh, empty_grid)
            )
            current = jnp.where(segment_index == 0, started, received)
            carried[moment] = from_behind_2(latent, "segment", final_segment)
        active = (moment - segment_index >= 0) & (moment - segment_index < samples)
        receiver, outgoing = lax.cond(
            active, lambda: project(current, own_weights), lambda: (empty_receiver, empty_mesh)
        )
        picked = jnp.where(valid_rows[:, :, None], outgoing[send_rows], jnp.zeros((), jnp.bfloat16))
        arrived = [outgoing]
        for list_index, offset in enumerate((1, -1, 2, -2)):
            arrived.append(from_behind(picked[list_index], "dom", offset))
        extended = jnp.concatenate(arrived, axis=0)
        renewed = lax.cond(
            active, lambda: renew(current, receiver, extended, own_weights), lambda: empty_mesh
        )
        if moment >= final_segment:
            finished = moment - final_segment
            skipped = carried[finished]
            results[finished] = lax.cond(
                segment_index == final_segment,
                lambda: decode(renewed, skipped),
                lambda: empty_output,
            )
        if moment < samples + final_segment - 1:
            received = from_behind_2(renewed, "segment", 1)
    everything = from_root(jnp.stack(results), "segment", final_segment)
    return lax.dynamic_slice_in_dim(everything, segment_index * share, share, 0)


def silu_by_tanh(values):
    half = 0.5 * values
    return half + half * jnp.tanh(half)


def matmul(left, right):
    return jnp.dot(left, right, preferred_element_type=jnp.float32)


def matmul_nt(left, right):
    return lax.dot_general(left, right, (((1,), (1,)), ((), ())), preferred_element_type=jnp.float32)


def matmul_tn(left, right):
    return lax.dot_general(left, right, (((0,), (0,)), ((), ())), preferred_element_type=jnp.float32)


def place_of(where, group):
    return lax.div(where[1], group), lax.rem(where[1], group)


def owns(where, group, at_segment):
    return jnp.logical_and(where[0] == at_segment, lax.rem(where[1], group) == 0)


def swapped_roles(where, group, at_segment):
    chip, lane = place_of(where, group)
    for number in range(2):
        here = jnp.logical_and(where[0] == at_segment + number, lane == 0)
        yield jnp.logical_and(here, lax.rem(chip, 2) == number), number


def weights_of(came, held, own):
    if own:
        return [block[...] for block in held]
    w_project, pair = came
    width = pair.shape[1]
    return [w_project[0, :, :width], w_project[0, :, width:], pair[0], pair[1]]


def fetch(sources, targets, semaphores):
    copies = [
        pltpu.make_async_copy(source, target, semaphores.at[place])
        for place, (source, target) in enumerate(zip(sources, targets))
    ]
    for copy in copies:
        copy.start()
    return copies


def encode_kernel(group, mesh_rows, fanout, lists, where, snapshots, w_embed, packed, *refs):
    payloads, latent = refs[:-1], refs[-1]
    chip, _ = place_of(where, group)
    neighbors = packed[:fanout, :mesh_rows]
    grid_rows = snapshots.shape[2]
    grid_mesh = packed[fanout + lists : fanout + lists + 1, :grid_rows]
    counts = packed[fanout + lists + 1 : fanout + lists + 2, :lists]
    width = w_embed.shape[1]
    for place in range(snapshots.shape[0]):
        found = silu_by_tanh(matmul_tn(snapshots[place], w_embed[...])).astype(jnp.bfloat16)
        latent[place * grid_rows : (place + 1) * grid_rows, :] = found
    table = lax.broadcasted_iota(jnp.int32, (mesh_rows, grid_rows), 0) == grid_mesh
    table = jnp.where(table, 1.0, 0.0).astype(jnp.bfloat16)
    block = neighbors // mesh_rows
    row = neighbors - block * mesh_rows
    halo_rows = mesh_rows
    position = lax.broadcasted_iota(jnp.int32, (1, halo_rows), 1)
    rows = []
    for list_index in range(lists):
        kept = position < counts[:, list_index : list_index + 1]
        listed = packed[fanout + list_index : fanout + list_index + 1, :halo_rows]
        rows.append(jnp.where(kept, listed, mesh_rows))
    rows.append(jnp.zeros((fanout - lists, halo_rows), jnp.int32))
    filler = jnp.zeros((fanout, 128 - mesh_rows), jnp.int32)
    pieces = [block, filler, row, filler, jnp.concatenate(rows, axis=0), filler]
    coded = jnp.concatenate(pieces + [jnp.zeros((fanout, width - 384), jnp.int32)], axis=1)
    coded = jnp.concatenate([coded, jnp.zeros_like(coded)], axis=0)
    coded = coded.astype(jnp.float32).astype(jnp.bfloat16)
    for turn, payload in enumerate(payloads):
        start = pl.multiple_of(jnp.bitwise_xor(chip, turn) * grid_rows, grid_rows)
        pooled = matmul(table, latent[pl.ds(start, grid_rows), :])
        payload[:mesh_rows, :] = rms_scale(pooled).astype(jnp.bfloat16)
        payload[mesh_rows:, :] = coded


def join_kernel(*refs):
    payloads, joined = refs[:-1], refs[-1]
    rows = payloads[0].shape[0]
    for place, payload in enumerate(payloads):
        joined[place * rows : (place + 1) * rows, :] = payload[...]


def columns_of(names):
    fanout, nodes = names.shape
    tile = min(nodes, DIGIT)
    rows = [names - number * tile for number in range(nodes // tile)]
    rows.append(jnp.zeros((128 - fanout * len(rows), nodes), jnp.float32))
    return jnp.transpose(jnp.concatenate(rows, axis=0)).astype(jnp.bfloat16)


def index_kernel(parts, mesh_rows, where, *refs):
    lanes, (columns_out, codes, state), index_out = refs[:-4], refs[-4:-1], refs[-1]
    nodes = columns_out.shape[0]
    group = len(lanes)
    rows = lanes[0].shape[0] // (parts // group)
    chip, _ = place_of(where, group)

    @pl.when(owns(where, group, 0))
    def _():
        tables = []
        for part in range(parts):
            lane, turn = lanes[part % group], jnp.bitwise_xor(chip, part // group)
            base = pl.multiple_of(turn * rows, 16)
            state[part * mesh_rows : (part + 1) * mesh_rows, :] = lane[pl.ds(base, mesh_rows), :]
            base = pl.multiple_of(turn * rows + mesh_rows, 16)
            coded = lane[pl.ds(base, rows - mesh_rows), :384].astype(jnp.float32).astype(jnp.int32)
            tables.append(coded[: coded.shape[0] // 2])
        fanout = tables[0].shape[0]
        for part in range(parts):
            block = tables[part][:, :128]
            row = tables[part][:, 128:256]
            found = part * mesh_rows + row
            for list_index, offset in enumerate((-1, 1, -2, 2)):
                source = (part + offset) % parts
                lists = tables[source][list_index : list_index + 1, 256:384]
                lists = jnp.broadcast_to(lists, (fanout, 128))
                picked = jnp.take_along_axis(lists, row, axis=1)
                picked = jnp.where(picked == mesh_rows, parts * mesh_rows, source * mesh_rows + picked)
                found = jnp.where(block == list_index + 1, picked, found)
            index_out[:, part * mesh_rows : (part + 1) * mesh_rows] = found[:, :mesh_rows]
        names = index_out[...]
        high_digit = names // DIGIT
        digits = jnp.concatenate([high_digit, names - high_digit * DIGIT], axis=0)
        codes[...] = digits.astype(jnp.float32).astype(jnp.bfloat16)
        columns_out[...] = columns_of(names.astype(jnp.float32))


def pack_kernel(group, at_segment, where, *refs):
    @pl.when(jnp.logical_or(owns(where, group, at_segment), owns(where, group, at_segment + 1)))
    def _():
        for place, block in enumerate(refs[:-1]):
            refs[-1][place] = block[...]


def hold_kernel(w_project, w_message, w_update, receive, send, own, edges, message, update, semaphores):
    width = own.shape[0]
    sources = [
        w_message.at[0],
        w_update.at[0, width:],
        w_project.at[0, :, :width],
        w_project.at[0, :, width:],
        w_update.at[0, :width],
    ]
    copies = fetch(sources, [message, update, receive, send, own], semaphores)
    copies[0].wait()
    copies[1].wait()
    edges[...] = matmul(message[...], update[...]).astype(jnp.bfloat16)
    for copy in copies[2:]:
        copy.wait()


def sum_edges(fanout, columns, sender, own, w_receive):
    chunk, width = own.shape
    nodes = sender.shape[0]
    tile = min(nodes, DIGIT)
    names = lax.broadcasted_iota(jnp.int32, (chunk, tile), 1).astype(jnp.float32).astype(jnp.bfloat16)
    one_half = jnp.full((chunk, tile), 0.5, jnp.bfloat16)
    none = jnp.zeros((chunk, tile), jnp.bfloat16)
    receiver = 0.5 * matmul(own, w_receive)
    total = jnp.zeros((chunk, width), jnp.float32)
    for k in range(fanout):
        hits = []
        for number in range(nodes // tile):
            lane = number * fanout + k
            hits.append(jnp.where(columns[:, lane : lane + 1] == names, one_half, none))
        half = receiver + matmul(jnp.concatenate(hits, axis=1), sender)
        total = total + (half + half * jnp.tanh(half))
    return (total * (1.0 / fanout)).astype(jnp.bfloat16)


def update_nodes(own, gathered, w_own, w_edges):
    update = silu_by_tanh(matmul(own, w_own) + matmul(gathered, w_edges))
    return (own.astype(jnp.float32) + rms_scale(update)).astype(jnp.bfloat16)


def sender_kernel(group, at_segment, fanout, rows, where, state, w_send, sender, *columns):
    @pl.when(owns(where, group, at_segment))
    def _():
        sender[...] = matmul(state[:rows, :], w_send[...]).astype(jnp.bfloat16)
        if columns:
            digits = state[rows:, :].astype(jnp.float32)
            columns[0][...] = columns_of(digits[:fanout] * DIGIT + digits[fanout:])


def late_sender_kernel(group, at_segment, fanout, rows, where, state, w_send, w_project, sender, *columns):
    width = state.shape[1]
    for here, number in swapped_roles(where, group, at_segment):

        @pl.when(here)
        def _(number=number):
            weights = w_project[0, :, width:] if number else w_send[...]
            sender[...] = matmul(state[:rows, :], weights).astype(jnp.bfloat16)
            if columns:
                digits = state[rows:, :].astype(jnp.float32)
                columns[0][...] = columns_of(digits[:fanout] * DIGIT + digits[fanout:])


def roles(where, group, at_segment, late):
    return swapped_roles(where, group, at_segment) if late else [(owns(where, group, at_segment), 0)]


def early_kernel(group, at_segment, late, fanout, places, quarter, where, columns, *refs):
    count = len(places)
    senders, refs = refs[:count], refs[count:]
    (own, coded), held, came, (piece, sender) = refs[:2], refs[2:6], refs[6:-2], refs[-2:]
    rows = senders[0].shape[0]
    for here, number in roles(where, group, at_segment, late):

        @pl.when(here)
        def _(number=number):
            w_receive, _, w_own, w_edges = weights_of(came, held, number == 0)
            sender[...] = jnp.zeros_like(sender)
            for place, part in zip(places, senders):
                sender[place * rows : (place + 1) * rows, :] = part[...]
            state = own[:rows, :]
            span = slice(quarter * rows, (quarter + 1) * rows)
            gathered = sum_edges(fanout, columns[span, :], sender[...], state, w_receive)
            piece[:rows, :] = update_nodes(state, gathered, w_own, w_edges)
            if piece.shape[0] > rows:
                piece[rows:, :] = coded[rows:, :]


def layer_kernel(group, at_segment, fanout, places, quarter, where, columns, *refs):
    parts = len(places)
    state, senders, refs = refs[:parts], refs[parts : 2 * parts - 1], refs[2 * parts - 1 :]
    done, held, came, (renewed, whole, sender) = refs[0], refs[1:5], refs[5:7], refs[7:]
    rows = done.shape[0]
    spans = [slice(place * rows, (place + 1) * rows) for place in places]
    own = slice(quarter * rows, (quarter + 1) * rows)
    rest = [slice(0, own.start), slice(own.stop, renewed.shape[0])]
    for here, number in swapped_roles(where, group, at_segment):

        @pl.when(here)
        def _(number=number):
            w_receive, w_send, w_own, w_edges = weights_of(came, held, number == 0)
            for span, part in zip(spans, state):
                whole[span, :] = part[:rows, :]
            for span, part in zip(spans, senders):
                sender[span, :] = part[...]
            sender[spans[-1], :] = matmul(whole[spans[-1], :], w_send).astype(jnp.bfloat16)
            renewed[own, :] = done[...]
            for span in rest:
                if span.stop > span.start:
                    gathered = sum_edges(fanout, columns[span, :], sender[...], whole[span, :], w_receive)
                    renewed[span, :] = update_nodes(whole[span, :], gathered, w_own, w_edges)


def open_kernel(group, at_segment, fanout, places, start, where, columns, *refs):
    parts = len(places)
    state, senders, refs = refs[:parts], refs[parts : 2 * parts - 1], refs[2 * parts - 1 :]
    codes, (w_receive, w_send, w_own, w_edges), (sender, whole, piece) = refs[:-7], refs[-7:-3], refs[-3:]
    rows = whole.shape[0] // parts
    spans = [slice(place * rows, (place + 1) * rows) for place in places]

    @pl.when(owns(where, group, at_segment))
    def _():
        for span, part in zip(spans, state):
            whole[span, :] = part[:rows, :]
        for span, part in zip(spans, senders):
            sender[span, :] = part[...]
        sender[spans[-1], :] = matmul(whole[spans[-1], :], w_send[...]).astype(jnp.bfloat16)
        count = piece.shape[0] - (codes[0].shape[0] if codes else 0)
        span = slice(start, start + count)
        own = whole[span, :]
        gathered = sum_edges(fanout, columns[span, :], sender[...], own, w_receive[...])
        piece[:count, :] = update_nodes(own, gathered, w_own[...], w_edges[...])
        if codes:
            piece[count:, :] = codes[0][...]


def next_kernel(group, at_segment, fanout, start, where, columns, sender, whole, *refs):
    w_receive, _, w_own, w_edges, piece = refs
    span = slice(start, start + piece.shape[0])

    @pl.when(owns(where, group, at_segment))
    def _():
        own = whole[span, :]
        gathered = sum_edges(fanout, columns[span, :], sender[...], own, w_receive[...])
        piece[...] = update_nodes(own, gathered, w_own[...], w_edges[...])


def end_kernel(group, at_segment, chips, far, begin, first, fanout, where, columns, state, *refs):
    senders, refs = (refs[:0], refs) if first else (refs[:1], refs[1:])
    held, came, outs = refs[:4], refs[4:6], refs[6:]
    half = state.shape[0] // 2
    chip, _ = place_of(where, group)
    for here, number in swapped_roles(where, group, at_segment):

        @pl.when(here)
        def _(number=number):
            w_receive, w_send, w_own, w_edges = weights_of(came, held, number == 1)
            pieces = outs
            if first:
                outs[0][...] = matmul(state[...], w_send).astype(jnp.bfloat16)
                pieces = outs[1:]
            sender = outs[0] if first else senders[0]
            rows = sum(piece.shape[0] for piece in pieces)
            if far:
                start = jnp.where(chip < chips // 2, half, 0) + begin
            else:
                start = (chip if begin else jnp.bitwise_xor(chip, 1)) * rows
            start = pl.multiple_of(start, rows)
            own = state[pl.ds(start, rows), :]
            gathered = sum_edges(fanout, columns[pl.ds(start, rows), :], sender[...], own, w_receive)
            write_pieces(pieces, update_nodes(own, gathered, w_own, w_edges))


def write_pieces(pieces, value):
    rows = value.shape[0] // len(pieces)
    for place, piece in enumerate(pieces):
        piece[:rows, :] = value[place * rows : (place + 1) * rows]


def arrival(where, group, chips):
    each = chips // 2
    chip, _ = place_of(where, group)
    return lax.div(chip, each) != lax.div(where[0], each), lax.rem(chip, each)


def far_kernel(group, chips, last, number, where, *refs):
    block, out = refs[0], refs[-1]
    crosses, spot = arrival(where, group, chips)

    @pl.when(jnp.logical_and(crosses, spot == number))
    def _():
        out[...] = block[...]

    if number:

        @pl.when(jnp.logical_and(crosses, spot < number))
        def _():
            out[...] = refs[1][...]


def near_kernel(group, chips, last, where, crossed, beside, same, kept, *outs):
    rows = outs[0].shape[0]
    crosses, _ = arrival(where, group, chips)
    chip, _ = place_of(where, group)
    own = chip == where[0]
    stays = jnp.logical_and(own, chip >= last)
    chosen = [
        (crossed, crosses),
        (beside, jnp.logical_not(jnp.logical_or(crosses, own))),
        (same, jnp.logical_and(own, chip < last)),
        (kept, stays),
    ]
    for block, here in chosen:

        @pl.when(here)
        def _(block=block):
            for place, out in enumerate(outs):
                out[...] = block[place * rows : (place + 1) * rows, :]


def prepare_kernel(where, snapshots, w_embed, w_decode, mesh_grid, ready, table_out):
    snapshot = snapshots[where[0]]
    latent = silu_by_tanh(matmul_tn(snapshot, w_embed[...])).astype(jnp.bfloat16)
    ready[...] = matmul(latent, w_decode[: latent.shape[1], :])
    mesh_rows, grid_rows = table_out.shape
    table = lax.broadcasted_iota(jnp.int32, (mesh_rows, grid_rows), 0) == mesh_grid[...]
    table_out[...] = jnp.where(table, 1.0, 0.0).astype(jnp.bfloat16)


def decode_kernel(where, ready, table, w_decode, w_output, *refs):
    blocks, out, state = refs[:-2], refs[-2], refs[-1]
    width = ready.shape[1]
    _, lane = place_of(where, len(blocks))
    for number, block in enumerate(blocks):

        @pl.when(lane == number)
        def _(block=block):
            state[...] = block[...]

    readout = matmul_tn(table[...], state[...]).astype(jnp.bfloat16)
    hidden = silu_by_tanh(ready[...] + matmul(readout, w_decode[width:, :])).astype(jnp.bfloat16)
    out[...] = matmul_nt(w_output[...], hidden).astype(jnp.bfloat16)


def call(kernel, name, shapes, inputs, places, scratch=(), room=16, flops=0):
    specs, given = [], []
    for value, place in zip(inputs, places):
        specs += [SMEM] * 2 if place == "w" else [VMEM if place == "v" else HBM]
        given += list(value) if place == "w" else [value]
    moved = sum(value.size * value.dtype.itemsize for value in given + list(shapes))

    def located(segment, place, *refs):
        kernel((segment[0], place[0]), *refs)

    return pl.pallas_call(
        located if places[0] == "w" else kernel,
        out_shape=shapes,
        in_specs=specs,
        out_specs=[VMEM] * len(shapes),
        scratch_shapes=list(scratch),
        name=name,
        compiler_params=pltpu.CompilerParams(vmem_limit_bytes=room * 1024 * 1024),
        cost_estimate=pl.CostEstimate(flops=flops, bytes_accessed=moved, transcendentals=0),
    )(*given)


def every_device(pairs, count, group):
    onward = dict(pairs)
    reached = set(onward.values())
    for first in [source for source in onward if source not in reached]:
        last = first
        while last in onward:
            last = onward[last]
        onward.update({last: last + group - 1, last + group - 1: first + group - 1, first + group - 1: first})
    alone = []
    for at in range(0, count, group):
        rest = [lane for lane in range(at, at + group) if lane not in onward]
        if len(rest) > 1:
            onward.update(zip(rest, rest[1:] + rest[:1]))
        else:
            alone += rest
    if len(alone) == 1:
        before = next(at for at in onward if at % group and onward[at] % group == 0)
        onward.update({before: alone[0], alone[0]: onward[before]})
    else:
        onward.update(zip(alone, alone[1:] + alone[:1]))
    return sorted(onward.items())


def resident(
    grid_state,
    w_embed,
    w_project,
    w_message,
    w_update,
    w_decode,
    w_output,
    grid_mesh,
    mesh_grid,
    neighbors,
    send_rows,
    halo_count,
):
    segment = lax.axis_index("segment")
    place = lax.axis_index("dom")
    segments = lax.axis_size("segment")
    parts = lax.axis_size("dom")
    samples, grid_rows, channels = grid_state.shape
    width = w_embed.shape[1]
    mesh_rows, fanout = neighbors.shape
    nodes = parts * mesh_rows
    group = parts // samples
    bf16 = jnp.bfloat16

    def device(at_segment, at_dom):
        return at_segment * parts + at_dom % parts

    def send(value, pairs):
        return lax.ppermute(value, ("segment", "dom"), every_device(pairs, segments * parts, group))

    def to_chip(value, steps):
        giver = steps - 1
        pairs = []
        for at in range(segments):
            for dom in range(parts):
                chip, lane = divmod(dom, group)
                across = (chip ^ steps) * group + lane
                if at == giver:
                    pairs.append((device(at, dom), device(0, across)))
                elif at == 0:
                    pairs.append((device(at, dom), device(giver, dom)))
                else:
                    pairs.append((device(at, dom), device(at, chip * group + (lane + 1) % group)))
        return lax.ppermute(value, ("segment", "dom"), pairs)

    def change_lane(value, steps):
        pairs = [(at, at - at % group + (at + steps) % group) for at in range(parts)]
        return lax.ppermute(value, "dom", pairs)

    def owner(m, at_segment):
        return device(min(at_segment, last + m % 2), m * group)

    own_segment, own_place, w_project = lax.optimization_barrier(
        (segment.reshape(1), place.reshape(1), w_project)
    )
    where = (own_segment, own_place)
    weights = [w_project, w_message, w_update]
    last = segments - 2
    to_last = [(device(last + 1 - m % 2, m * group), owner(m, segments)) for m in range(samples)]
    came_project = send(w_project, to_last)
    snapshots = jnp.transpose(grid_state, (0, 2, 1))
    lists = send_rows.shape[0]

    def rows_of(value):
        return jnp.pad(value, ((0, 0), (0, 128 - value.shape[1])))

    packed = jnp.concatenate(
        [
            rows_of(neighbors.T),
            rows_of(send_rows),
            rows_of(grid_mesh.reshape(1, grid_rows)),
            rows_of(halo_count.reshape(1, lists)),
        ],
        axis=0,
    )
    payloads = call(
        functools.partial(encode_kernel, group, mesh_rows, fanout, lists),
        "encode",
        [jax.ShapeDtypeStruct((mesh_rows + 2 * fanout, width), bf16)] * samples,
        [where, snapshots, w_embed, packed],
        "wvvv",
        [pltpu.VMEM((samples * grid_rows, width), bf16)],
    )
    held = call(
        hold_kernel,
        "hold",
        [jax.ShapeDtypeStruct((width, width), bf16)] * 4,
        weights,
        "hhh",
        [pltpu.VMEM((width, width), bf16)] * 2 + [pltpu.SemaphoreType.DMA((5,))],
    )
    own_payload, *held = lax.optimization_barrier((payloads[0], *held))
    arrived = [own_payload] + [to_chip(payloads[turn], turn) for turn in range(1, samples)]
    (joined,) = call(
        join_kernel,
        "join",
        [jax.ShapeDtypeStruct((samples * (mesh_rows + 2 * fanout), width), bf16)],
        arrived,
        "v" * samples,
    )
    lanes = [joined] + [change_lane(joined, -steps) for steps in range(1, group)]
    share = group * mesh_rows
    whole, short, tall = [
        jax.ShapeDtypeStruct((rows, width), bf16) for rows in (nodes, share, share + 2 * fanout)
    ]
    columns_shape = jax.ShapeDtypeStruct((nodes, 128), bf16)
    columns, codes, state = call(
        functools.partial(index_kernel, parts, mesh_rows),
        "index",
        [columns_shape, jax.ShapeDtypeStruct((2 * fanout, width), bf16), whole],
        [where] + lanes,
        "w" + "v" * group,
        [pltpu.VMEM((fanout, nodes), jnp.int32)],
    )
    columns, came_project, *held = lax.optimization_barrier((columns, came_project, *held))
    (pair,) = call(
        functools.partial(pack_kernel, group, last),
        "pack",
        [jax.ShapeDtypeStruct((2, width, width), bf16)],
        [where] + held[2:],
        "wvv",
    )
    came = [came_project, send(pair, to_last)]
    pieces, senders, places, early = [state], [], (0,), []
    for layer in range(last + 1):
        late = layer == last
        pairs = [(owner(m, layer), owner(m, segments if layer + 1 == last else layer + 1)) for m in range(samples)]
        if layer == 0:
            order, sent = list(range(samples)), []
        else:
            first = places[1]
            order = [first] + [(first + step) % samples for step in range(1, samples)]
            (piece,) = call(
                functools.partial(early_kernel, group, layer, late, fanout, places[:-1], first),
                "early",
                [short if late else tall],
                [where, columns] + senders + [pieces[1], pieces[0]] + held + came * late,
                "w" + "v" * (3 + len(senders + held + came * late)),
                [pltpu.VMEM((nodes, width), bf16)],
            )
            if late:
                pieces[-1], piece = lax.optimization_barrier((pieces[-1], piece))
                break
            sent = [send(piece, pairs)]
            pieces[-1], columns = lax.optimization_barrier((pieces[-1], columns))
        start = order[len(sent)] * share
        extra = [codes] * (layer == 0)
        sender, joined_state, piece = call(
            functools.partial(open_kernel, group, layer, fanout, places, start),
            "open",
            [whole, whole, tall if layer == 0 else short],
            [where, columns] + pieces + senders + extra + held,
            "w" + "v" * (1 + len(pieces + senders + extra + held)),
        )
        sent.append(send(piece, pairs))
        for place_sent in order[len(sent) :]:
            (piece,) = call(
                functools.partial(next_kernel, group, layer, fanout, place_sent * share),
                "next",
                [short],
                [where, columns, sender, joined_state] + held,
                "w" + "v" * (3 + len(held)),
            )
            sent.append(send(piece, pairs))
        pieces, senders, places = sent, [], tuple(order)
        if layer == 0:
            ready, table = call(
                prepare_kernel,
                "prepare",
                [
                    jax.ShapeDtypeStruct((grid_rows, width), jnp.float32),
                    jax.ShapeDtypeStruct((mesh_rows, grid_rows), bf16),
                ],
                [where, snapshots, w_embed, w_decode, mesh_grid.reshape(1, grid_rows)],
                "wvvvv",
            )
            pieces[0], ready, table = lax.optimization_barrier((pieces[0], ready, table))
        for number, part in enumerate(pieces[:-1]):
            if senders:
                part, senders[-1] = lax.optimization_barrier((part, senders[-1]))
                pieces[number] = part
            late = layer + 1 == last
            sender, *found = call(
                functools.partial(late_sender_kernel if late else sender_kernel, group, layer + 1, fanout, share),
                "sender",
                [short] + [columns_shape] * (not senders),
                [where, part, held[1]] + came[:1] * late,
                "wvv" + "v" * late,
            )
            columns = found[0] if found else columns
            senders.append(sender)
    (state,) = call(
        functools.partial(layer_kernel, group, last, fanout, places, order[0]),
        "layer",
        [whole],
        [where, columns] + pieces + senders + [piece] + held + came,
        "w" + "v" * (2 + len(pieces + senders + held + came)),
        [pltpu.VMEM((nodes, width), bf16)] * 2,
    )
    far = []
    for begin in range(0, nodes // 2, share):
        found = call(
            functools.partial(end_kernel, group, last, samples, True, begin, not far, fanout),
            "far_part",
            [whole] * (not far) + [short],
            [where, columns, state] + ([sender] if far else []) + held + came,
            "w" + "v" * (9 if far else 8),
        )
        sender = found[0] if not far else sender
        far.append(found[-1])
    near = []
    for begin in range(0, nodes // 2, share):
        near += call(
            functools.partial(end_kernel, group, last, samples, False, begin, False, fanout),
            "near_part",
            [short],
            [where, columns, state, sender] + held + came,
            "w" + "v" * 9,
        )
    state = far + list(near)
    each = samples // 2
    arrived = []
    for far, blocks in ((1, state[:each]), (0, state[each:])):
        for turn, block in enumerate(blocks):
            chips = [(m // each ^ 1) * each + turn if far else m ^ (1 - turn) for m in range(samples)]
            pairs = [(owner(m, segments), device(m, chips[m] * group)) for m in range(samples)]
            arrived.append(send(block, [pair for pair in pairs if pair[0] != pair[1]]))
    crossed = []
    for number, block in enumerate(arrived[:each]):
        crossed = call(
            functools.partial(far_kernel, group, samples, last, number),
            "far",
            [short],
            [where, block] + list(crossed),
            "wv" + "v" * len(crossed),
        )
    parts_of_block = call(
        functools.partial(near_kernel, group, samples, last),
        "near",
        [jax.ShapeDtypeStruct((mesh_rows, width), bf16)] * group,
        [where, crossed[0]] + arrived[each:] + state[-1:],
        "w" + "v" * (2 + each),
    )
    handed = [parts_of_block[0]]
    for steps in range(1, group):
        handed.append(change_lane(parts_of_block[steps], steps))
    (prediction,) = call(
        decode_kernel,
        "decode",
        [jax.ShapeDtypeStruct((channels, grid_rows), bf16)],
        [where, ready, table, w_decode, w_output.T] + handed,
        "wvvvv" + "v" * group,
        [pltpu.VMEM((mesh_rows, width), bf16)],
    )
    return prediction.T.reshape(1, grid_rows, channels)


def chosen_plan(mesh, *arrays):
    segments, parts = mesh.shape["segment"], mesh.shape["dom"]
    samples, width = arrays[0].shape[0], arrays[1].shape[1]
    nodes = parts * arrays[9].shape[0]
    fits = samples == segments == 4 and parts == 2 * samples and nodes == width
    return (resident if fits else streamed)(*arrays)


def solution(mesh):
    return jax.shard_map(
        functools.partial(chosen_plan, mesh),
        mesh=mesh,
        in_specs=(
            P(None, "dom", None),
            P(),
            P("segment", None, None),
            P("segment", None, None),
            P("segment", None, None),
            P(),
            P(),
            P("dom"),
            P("dom"),
            P("dom", None),
            P(None, "dom"),
            P(None, "dom"),
        ),
        out_specs=P("segment", "dom", None),
        check_vma=False,
    )
```

```python
import functools

import jax
import jax.numpy as jnp
from jax import lax
from jax.experimental import pallas as pl
from jax.experimental.pallas import tpu as pltpu
from jax.sharding import PartitionSpec as P

epsilon = 1e-05
DIGIT = 256
VMEM = pl.BlockSpec(memory_space=pltpu.VMEM)
SMEM = pl.BlockSpec(memory_space=pltpu.SMEM)
HBM = pl.BlockSpec(memory_space=pltpu.HBM)


def from_behind(value, axis, steps):
    count = lax.axis_size(axis)
    pairs = [(source, (source + steps) % count) for source in range(count)]
    return lax.ppermute(value, axis, pairs)


def from_behind_2(block, axis, distance):
    devices = range(lax.axis_size(axis))
    route = [(i - distance, i) for i in devices if i - distance in devices]
    return lax.ppermute(block, axis, route)


def from_root(value, axis, source):
    kept = jnp.where(lax.axis_index(axis) == source, value, 0).astype(value.dtype)
    return lax.psum(kept, axis)


def rms_scale(values):
    return values * lax.rsqrt(jnp.mean(values * values, axis=-1, keepdims=True) + epsilon)


def streamed(
    grid_state,
    w_embed,
    w_project,
    w_message,
    w_update,
    w_decode,
    w_output,
    grid_mesh,
    mesh_grid,
    neighbors,
    send_rows,
    halo_count,
):
    segment_index = lax.axis_index("segment")
    segment_count = lax.axis_size("segment")
    final_segment = segment_count - 1
    samples, grid_rows, channels = grid_state.shape
    width = w_embed.shape[1]
    mesh_rows = neighbors.shape[0]
    fanout = neighbors.shape[1]
    halo_rows = send_rows.shape[1]
    share = samples // segment_count
    pool_table = (grid_mesh[None, :] == jnp.arange(mesh_rows, dtype=jnp.int32)[:, None]).astype(
        jnp.bfloat16
    )
    read_table = (mesh_grid[:, None] == jnp.arange(mesh_rows, dtype=jnp.int32)[None, :]).astype(
        jnp.bfloat16
    )
    valid_rows = jnp.arange(halo_rows, dtype=jnp.int32)[None, :] < halo_count[:, 0][:, None]
    source_rows = neighbors.reshape(mesh_rows * fanout)

    def embed_grid(snapshot):
        return jax.nn.silu(jnp.dot(snapshot, w_embed, preferred_element_type=jnp.float32)).astype(
            jnp.bfloat16
        )

    def encode(snapshot):
        latent = embed_grid(snapshot)
        pooled = jnp.dot(pool_table, latent, preferred_element_type=jnp.float32)
        return (rms_scale(pooled).astype(jnp.bfloat16), latent)

    def project(state, weights):
        projected = jnp.dot(state, weights[0], preferred_element_type=jnp.float32)
        return (projected[:, :width], projected[:, width:].astype(jnp.bfloat16))

    def renew(state, receiver, extended, weights):
        fetched = extended[source_rows].reshape(mesh_rows, fanout, width)
        edges = jax.nn.silu(receiver[:, None, :] + fetched.astype(jnp.float32)).astype(jnp.bfloat16)
        messages = jnp.dot(
            edges.reshape(mesh_rows * fanout, width), weights[1], preferred_element_type=jnp.float32
        )
        aggregate = (jnp.sum(messages.reshape(mesh_rows, fanout, width), axis=1) / fanout).astype(
            jnp.bfloat16
        )
        update = jax.nn.silu(
            jnp.dot(state, weights[2][:width], preferred_element_type=jnp.float32)
            + jnp.dot(aggregate, weights[2][width:], preferred_element_type=jnp.float32)
        )
        return (state.astype(jnp.float32) + rms_scale(update)).astype(jnp.bfloat16)

    def decode(state, latent):
        readout = jnp.dot(read_table, state, preferred_element_type=jnp.float32).astype(
            jnp.bfloat16
        )
        hidden = jax.nn.silu(
            jnp.dot(latent, w_decode[:width], preferred_element_type=jnp.float32)
            + jnp.dot(readout, w_decode[width:], preferred_element_type=jnp.float32)
        ).astype(jnp.bfloat16)
        return jnp.dot(hidden, w_output, preferred_element_type=jnp.float32).astype(jnp.bfloat16)

    own_weights = (w_project[0], w_message[0], w_update[0])
    empty_mesh = jnp.zeros((mesh_rows, width), jnp.bfloat16)
    empty_receiver = jnp.zeros((mesh_rows, width), jnp.float32)
    empty_grid = jnp.zeros((grid_rows, width), jnp.bfloat16)
    empty_output = jnp.zeros((grid_rows, channels), jnp.bfloat16)
    received = empty_mesh
    carried = {}
    results = [empty_output for sample in range(samples)]
    for moment in range(samples + final_segment):
        current = received
        if moment < samples:
            snapshot = grid_state[moment]
            started, latent = lax.cond(
                segment_index == 0, lambda: encode(snapshot), lambda: (empty_mesh, empty_grid)
            )
            current = jnp.where(segment_index == 0, started, received)
            carried[moment] = from_behind_2(latent, "segment", final_segment)
        active = (moment - segment_index >= 0) & (moment - segment_index < samples)
        receiver, outgoing = lax.cond(
            active, lambda: project(current, own_weights), lambda: (empty_receiver, empty_mesh)
        )
        picked = jnp.where(valid_rows[:, :, None], outgoing[send_rows], jnp.zeros((), jnp.bfloat16))
        arrived = [outgoing]
        for list_index, offset in enumerate((1, -1, 2, -2)):
            arrived.append(from_behind(picked[list_index], "dom", offset))
        extended = jnp.concatenate(arrived, axis=0)
        renewed = lax.cond(
            active, lambda: renew(current, receiver, extended, own_weights), lambda: empty_mesh
        )
        if moment >= final_segment:
            finished = moment - final_segment
            skipped = carried[finished]
            results[finished] = lax.cond(
                segment_index == final_segment,
                lambda: decode(renewed, skipped),
                lambda: empty_output,
            )
        if moment < samples + final_segment - 1:
            received = from_behind_2(renewed, "segment", 1)
    everything = from_root(jnp.stack(results), "segment", final_segment)
    return lax.dynamic_slice_in_dim(everything, segment_index * share, share, 0)


def silu_by_tanh(values):
    half = 0.5 * values
    return half + half * jnp.tanh(half)


def matmul(left, right):
    return jnp.dot(left, right, preferred_element_type=jnp.float32)


def matmul_nt(left, right):
    return lax.dot_general(left, right, (((1,), (1,)), ((), ())), preferred_element_type=jnp.float32)


def matmul_tn(left, right):
    return lax.dot_general(left, right, (((0,), (0,)), ((), ())), preferred_element_type=jnp.float32)


def place_of(where, group):
    return lax.div(where[1], group), lax.rem(where[1], group)


def owns(where, group, at_segment):
    return jnp.logical_and(where[0] == at_segment, lax.rem(where[1], group) == 0)


def swapped_roles(where, group, at_segment):
    chip, lane = place_of(where, group)
    for number in range(2):
        here = jnp.logical_and(where[0] == at_segment + number, lane == 0)
        yield jnp.logical_and(here, lax.rem(chip, 2) == number), number


def weights_of(came, held, own):
    if own:
        return [block[...] for block in held]
    w_project, pair = came
    width = pair.shape[1]
    return [w_project[0, :, :width], w_project[0, :, width:], pair[0], pair[1]]


def fetch(sources, targets, semaphores):
    copies = [
        pltpu.make_async_copy(source, target, semaphores.at[place])
        for place, (source, target) in enumerate(zip(sources, targets))
    ]
    for copy in copies:
        copy.start()
    return copies


def encode_kernel(group, mesh_rows, fanout, lists, where, snapshots, w_embed, packed, *refs):
    payloads, latent = refs[:-1], refs[-1]
    chip, _ = place_of(where, group)
    neighbors = packed[:fanout, :mesh_rows]
    grid_rows = snapshots.shape[2]
    grid_mesh = packed[fanout + lists : fanout + lists + 1, :grid_rows]
    counts = packed[fanout + lists + 1 : fanout + lists + 2, :lists]
    width = w_embed.shape[1]
    for place in range(snapshots.shape[0]):
        found = silu_by_tanh(matmul_tn(snapshots[place], w_embed[...])).astype(jnp.bfloat16)
        latent[place * grid_rows : (place + 1) * grid_rows, :] = found
    table = lax.broadcasted_iota(jnp.int32, (mesh_rows, grid_rows), 0) == grid_mesh
    table = jnp.where(table, 1.0, 0.0).astype(jnp.bfloat16)
    block = neighbors // mesh_rows
    row = neighbors - block * mesh_rows
    halo_rows = mesh_rows
    position = lax.broadcasted_iota(jnp.int32, (1, halo_rows), 1)
    rows = []
    for list_index in range(lists):
        kept = position < counts[:, list_index : list_index + 1]
        listed = packed[fanout + list_index : fanout + list_index + 1, :halo_rows]
        rows.append(jnp.where(kept, listed, mesh_rows))
    rows.append(jnp.zeros((fanout - lists, halo_rows), jnp.int32))
    filler = jnp.zeros((fanout, 128 - mesh_rows), jnp.int32)
    pieces = [block, filler, row, filler, jnp.concatenate(rows, axis=0), filler]
    coded = jnp.concatenate(pieces + [jnp.zeros((fanout, width - 384), jnp.int32)], axis=1)
    coded = jnp.concatenate([coded, jnp.zeros_like(coded)], axis=0)
    coded = coded.astype(jnp.float32).astype(jnp.bfloat16)
    for turn, payload in enumerate(payloads):
        start = pl.multiple_of(jnp.bitwise_xor(chip, turn) * grid_rows, grid_rows)
        pooled = matmul(table, latent[pl.ds(start, grid_rows), :])
        payload[:mesh_rows, :] = rms_scale(pooled).astype(jnp.bfloat16)
        payload[mesh_rows:, :] = coded


def join_kernel(places, *refs):
    payloads, joined = refs[:-1], refs[-1]
    rows = payloads[0].shape[0]
    for place, payload in zip(places, payloads):
        joined[place * rows : (place + 1) * rows, :] = payload[...]


def columns_of(names):
    fanout, nodes = names.shape
    tile = min(nodes, DIGIT)
    rows = [names - number * tile for number in range(nodes // tile)]
    rows.append(jnp.zeros((128 - fanout * len(rows), nodes), jnp.float32))
    return jnp.transpose(jnp.concatenate(rows, axis=0)).astype(jnp.bfloat16)


def index_kernel(parts, mesh_rows, where, *refs):
    lanes, (columns_out, codes, state), index_out = refs[:-4], refs[-4:-1], refs[-1]
    nodes = columns_out.shape[0]
    group = len(lanes)
    rows = lanes[0].shape[0] // (parts // group)
    chip, _ = place_of(where, group)

    @pl.when(owns(where, group, 0))
    def _():
        tables = []
        for part in range(parts):
            lane, turn = lanes[part % group], jnp.bitwise_xor(chip, part // group)
            base = pl.multiple_of(turn * rows, 16)
            state[part * mesh_rows : (part + 1) * mesh_rows, :] = lane[pl.ds(base, mesh_rows), :]
            base = pl.multiple_of(turn * rows + mesh_rows, 16)
            coded = lane[pl.ds(base, rows - mesh_rows), :384].astype(jnp.float32).astype(jnp.int32)
            tables.append(coded[: coded.shape[0] // 2])
        fanout = tables[0].shape[0]
        for part in range(parts):
            block = tables[part][:, :128]
            row = tables[part][:, 128:256]
            found = part * mesh_rows + row
            for list_index, offset in enumerate((-1, 1, -2, 2)):
                source = (part + offset) % parts
                lists = tables[source][list_index : list_index + 1, 256:384]
                lists = jnp.broadcast_to(lists, (fanout, 128))
                picked = jnp.take_along_axis(lists, row, axis=1)
                picked = jnp.where(picked == mesh_rows, parts * mesh_rows, source * mesh_rows + picked)
                found = jnp.where(block == list_index + 1, picked, found)
            index_out[:, part * mesh_rows : (part + 1) * mesh_rows] = found[:, :mesh_rows]
        names = index_out[...]
        high_digit = names // DIGIT
        digits = jnp.concatenate([high_digit, names - high_digit * DIGIT], axis=0)
        codes[...] = digits.astype(jnp.float32).astype(jnp.bfloat16)
        columns_out[...] = columns_of(names.astype(jnp.float32))


def pack_kernel(group, at_segment, where, *refs):
    @pl.when(jnp.logical_or(owns(where, group, at_segment), owns(where, group, at_segment + 1)))
    def _():
        for place, block in enumerate(refs[:-1]):
            refs[-1][place] = block[...]


def hold_kernel(w_project, w_message, w_update, receive, send, own, edges, message, update, semaphores):
    width = own.shape[0]
    sources = [
        w_message.at[0],
        w_update.at[0, width:],
        w_project.at[0, :, :width],
        w_project.at[0, :, width:],
        w_update.at[0, :width],
    ]
    copies = fetch(sources, [message, update, receive, send, own], semaphores)
    copies[0].wait()
    copies[1].wait()
    edges[...] = matmul(message[...], update[...]).astype(jnp.bfloat16)
    for copy in copies[2:]:
        copy.wait()


def sum_edges(fanout, columns, sender, own, w_receive):
    chunk, width = own.shape
    nodes = sender.shape[0]
    tile = min(nodes, DIGIT)
    names = lax.broadcasted_iota(jnp.int32, (chunk, tile), 1).astype(jnp.float32).astype(jnp.bfloat16)
    one_half = jnp.full((chunk, tile), 0.5, jnp.bfloat16)
    none = jnp.zeros((chunk, tile), jnp.bfloat16)
    receiver = 0.5 * matmul(own, w_receive)
    total = jnp.zeros((chunk, width), jnp.float32)
    for k in range(fanout):
        hits = []
        for number in range(nodes // tile):
            lane = number * fanout + k
            hits.append(jnp.where(columns[:, lane : lane + 1] == names, one_half, none))
        half = receiver + matmul(jnp.concatenate(hits, axis=1), sender)
        total = total + (half + half * jnp.tanh(half))
    return (total * (1.0 / fanout)).astype(jnp.bfloat16)


def update_nodes(own, gathered, w_own, w_edges):
    update = silu_by_tanh(matmul(own, w_own) + matmul(gathered, w_edges))
    return (own.astype(jnp.float32) + rms_scale(update)).astype(jnp.bfloat16)


def sender_kernel(group, at_segment, fanout, rows, where, state, w_send, sender, *columns):
    @pl.when(owns(where, group, at_segment))
    def _():
        sender[...] = matmul(state[:rows, :], w_send[...]).astype(jnp.bfloat16)
        if columns:
            digits = state[rows:, :].astype(jnp.float32)
            columns[0][...] = columns_of(digits[:fanout] * DIGIT + digits[fanout:])


def late_sender_kernel(group, at_segment, fanout, rows, where, state, w_send, w_project, sender, *columns):
    width = state.shape[1]
    for here, number in swapped_roles(where, group, at_segment):

        @pl.when(here)
        def _(number=number):
            weights = w_project[0, :, width:] if number else w_send[...]
            sender[...] = matmul(state[:rows, :], weights).astype(jnp.bfloat16)
            if columns:
                digits = state[rows:, :].astype(jnp.float32)
                columns[0][...] = columns_of(digits[:fanout] * DIGIT + digits[fanout:])


def roles(where, group, at_segment, late):
    return swapped_roles(where, group, at_segment) if late else [(owns(where, group, at_segment), 0)]


def early_kernel(group, at_segment, late, fanout, places, quarter, where, columns, *refs):
    count = len(places)
    senders, refs = refs[:count], refs[count:]
    (own, coded), held, came, (piece, sender) = refs[:2], refs[2:6], refs[6:-2], refs[-2:]
    rows = senders[0].shape[0]
    for here, number in roles(where, group, at_segment, late):

        @pl.when(here)
        def _(number=number):
            w_receive, _, w_own, w_edges = weights_of(came, held, number == 0)
            sender[...] = jnp.zeros_like(sender)
            for place, part in zip(places, senders):
                sender[place * rows : (place + 1) * rows, :] = part[...]
            state = own[:rows, :]
            span = slice(quarter * rows, (quarter + 1) * rows)
            gathered = sum_edges(fanout, columns[span, :], sender[...], state, w_receive)
            piece[:rows, :] = update_nodes(state, gathered, w_own, w_edges)
            if piece.shape[0] > rows:
                piece[rows:, :] = coded[rows:, :]


def layer_kernel(group, at_segment, fanout, places, quarter, where, columns, *refs):
    parts = len(places)
    state, senders, refs = refs[:parts], refs[parts : 2 * parts - 1], refs[2 * parts - 1 :]
    done, held, came, (renewed, whole, sender) = refs[0], refs[1:5], refs[5:7], refs[7:]
    rows = done.shape[0]
    spans = [slice(place * rows, (place + 1) * rows) for place in places]
    own = slice(quarter * rows, (quarter + 1) * rows)
    rest = [slice(0, own.start), slice(own.stop, renewed.shape[0])]
    for here, number in swapped_roles(where, group, at_segment):

        @pl.when(here)
        def _(number=number):
            w_receive, w_send, w_own, w_edges = weights_of(came, held, number == 0)
            for span, part in zip(spans, state):
                whole[span, :] = part[:rows, :]
            for span, part in zip(spans, senders):
                sender[span, :] = part[...]
            sender[spans[-1], :] = matmul(whole[spans[-1], :], w_send).astype(jnp.bfloat16)
            renewed[own, :] = done[...]
            for span in rest:
                if span.stop > span.start:
                    gathered = sum_edges(fanout, columns[span, :], sender[...], whole[span, :], w_receive)
                    renewed[span, :] = update_nodes(whole[span, :], gathered, w_own, w_edges)


def open_kernel(group, at_segment, fanout, places, start, where, columns, *refs):
    parts = len(places)
    state, senders, refs = refs[:parts], refs[parts : 2 * parts - 1], refs[2 * parts - 1 :]
    codes, (w_receive, w_send, w_own, w_edges), (sender, whole, piece) = refs[:-7], refs[-7:-3], refs[-3:]
    rows = whole.shape[0] // parts
    spans = [slice(place * rows, (place + 1) * rows) for place in places]

    @pl.when(owns(where, group, at_segment))
    def _():
        for span, part in zip(spans, state):
            whole[span, :] = part[:rows, :]
        for span, part in zip(spans, senders):
            sender[span, :] = part[...]
        sender[spans[-1], :] = matmul(whole[spans[-1], :], w_send[...]).astype(jnp.bfloat16)
        count = piece.shape[0] - (codes[0].shape[0] if codes else 0)
        span = slice(start, start + count)
        own = whole[span, :]
        gathered = sum_edges(fanout, columns[span, :], sender[...], own, w_receive[...])
        piece[:count, :] = update_nodes(own, gathered, w_own[...], w_edges[...])
        if codes:
            piece[count:, :] = codes[0][...]


def next_kernel(group, at_segment, fanout, start, where, columns, sender, whole, *refs):
    w_receive, _, w_own, w_edges, piece = refs
    span = slice(start, start + piece.shape[0])

    @pl.when(owns(where, group, at_segment))
    def _():
        own = whole[span, :]
        gathered = sum_edges(fanout, columns[span, :], sender[...], own, w_receive[...])
        piece[...] = update_nodes(own, gathered, w_own[...], w_edges[...])


def end_kernel(group, at_segment, chips, far, begin, first, fanout, where, columns, state, *refs):
    senders, refs = (refs[:0], refs) if first else (refs[:1], refs[1:])
    held, came, outs = refs[:4], refs[4:6], refs[6:]
    half = state.shape[0] // 2
    chip, _ = place_of(where, group)
    for here, number in swapped_roles(where, group, at_segment):

        @pl.when(here)
        def _(number=number):
            w_receive, w_send, w_own, w_edges = weights_of(came, held, number == 1)
            pieces = outs
            if first:
                outs[0][...] = matmul(state[...], w_send).astype(jnp.bfloat16)
                pieces = outs[1:]
            sender = outs[0] if first else senders[0]
            rows = sum(piece.shape[0] for piece in pieces)
            upper = (chip < chips // 2) if far else (chip >= chips // 2)
            start = pl.multiple_of(jnp.where(upper, half, 0) + begin, rows)
            own = state[pl.ds(start, rows), :]
            gathered = sum_edges(fanout, columns[pl.ds(start, rows), :], sender[...], own, w_receive)
            write_pieces(pieces, update_nodes(own, gathered, w_own, w_edges))


def write_pieces(pieces, value):
    rows = value.shape[0] // len(pieces)
    for place, piece in enumerate(pieces):
        piece[:rows, :] = value[place * rows : (place + 1) * rows]


def arrival(where, group, chips, last):
    each = chips // 2
    segment = where[0]
    chip, _ = place_of(where, group)
    crosses = lax.div(chip, each) != lax.div(segment, each)
    return crosses, jnp.logical_and(segment >= last, chip == segment), lax.rem(chip, each)


def far_kernel(group, chips, last, number, where, *refs):
    block, out = refs[0], refs[-1]
    crosses, _, spot = arrival(where, group, chips, last)

    @pl.when(jnp.logical_and(crosses, spot == number))
    def _():
        out[...] = block[...]

    if number:

        @pl.when(jnp.logical_and(crosses, spot < number))
        def _():
            out[...] = refs[1][...]


def near_kernel(group, chips, last, where, crossed, *refs):
    each = chips // 2
    near, kept, outs = refs[:each], refs[each : 2 * each], refs[2 * each :]
    rows = outs[0].shape[0]
    crosses, stays, spot = arrival(where, group, chips, last)
    arrives = jnp.logical_not(jnp.logical_or(crosses, stays))

    def give(block):
        for place, out in enumerate(outs):
            out[...] = block[place * rows : (place + 1) * rows, :]

    @pl.when(crosses)
    def _():
        give(crossed)

    for number in range(each):
        for blocks, chosen in ((near, arrives), (kept, stays)):

            @pl.when(jnp.logical_and(chosen, spot == number))
            def _(block=blocks[number]):
                give(block)


def prepare_kernel(where, snapshots, w_embed, w_decode, mesh_grid, ready, table_out):
    snapshot = snapshots[where[0]]
    latent = silu_by_tanh(matmul_tn(snapshot, w_embed[...])).astype(jnp.bfloat16)
    ready[...] = matmul(latent, w_decode[: latent.shape[1], :])
    mesh_rows, grid_rows = table_out.shape
    table = lax.broadcasted_iota(jnp.int32, (mesh_rows, grid_rows), 0) == mesh_grid[...]
    table_out[...] = jnp.where(table, 1.0, 0.0).astype(jnp.bfloat16)


def decode_kernel(where, ready, table, w_decode, w_output, *refs):
    blocks, out, state = refs[:-2], refs[-2], refs[-1]
    width = ready.shape[1]
    _, lane = place_of(where, len(blocks))
    for number, block in enumerate(blocks):

        @pl.when(lane == number)
        def _(block=block):
            state[...] = block[...]

    readout = matmul_tn(table[...], state[...]).astype(jnp.bfloat16)
    hidden = silu_by_tanh(ready[...] + matmul(readout, w_decode[width:, :])).astype(jnp.bfloat16)
    out[...] = matmul_nt(w_output[...], hidden).astype(jnp.bfloat16)


def call(kernel, name, shapes, inputs, places, scratch=(), room=16, flops=0):
    specs, given = [], []
    for value, place in zip(inputs, places):
        specs += [SMEM] * 2 if place == "w" else [VMEM if place == "v" else HBM]
        given += list(value) if place == "w" else [value]
    moved = sum(value.size * value.dtype.itemsize for value in given + list(shapes))

    def located(segment, place, *refs):
        kernel((segment[0], place[0]), *refs)

    return pl.pallas_call(
        located if places[0] == "w" else kernel,
        out_shape=shapes,
        in_specs=specs,
        out_specs=[VMEM] * len(shapes),
        scratch_shapes=list(scratch),
        name=name,
        compiler_params=pltpu.CompilerParams(vmem_limit_bytes=room * 1024 * 1024),
        cost_estimate=pl.CostEstimate(flops=flops, bytes_accessed=moved, transcendentals=0),
    )(*given)


def every_device(pairs, count, group):
    onward = dict(pairs)
    reached = set(onward.values())
    for first in [source for source in onward if source not in reached]:
        last = first
        while last in onward:
            last = onward[last]
        onward.update({last: last + group - 1, last + group - 1: first + group - 1, first + group - 1: first})
    alone = []
    for at in range(0, count, group):
        rest = [lane for lane in range(at, at + group) if lane not in onward]
        if len(rest) > 1:
            onward.update(zip(rest, rest[1:] + rest[:1]))
        else:
            alone += rest
    if len(alone) == 1:
        before = next(at for at in onward if at % group and onward[at] % group == 0)
        onward.update({before: alone[0], alone[0]: onward[before]})
    else:
        onward.update(zip(alone, alone[1:] + alone[:1]))
    return sorted(onward.items())


def resident(
    grid_state,
    w_embed,
    w_project,
    w_message,
    w_update,
    w_decode,
    w_output,
    grid_mesh,
    mesh_grid,
    neighbors,
    send_rows,
    halo_count,
):
    segment = lax.axis_index("segment")
    place = lax.axis_index("dom")
    segments = lax.axis_size("segment")
    parts = lax.axis_size("dom")
    samples, grid_rows, channels = grid_state.shape
    width = w_embed.shape[1]
    mesh_rows, fanout = neighbors.shape
    nodes = parts * mesh_rows
    group = parts // samples
    bf16 = jnp.bfloat16

    def device(at_segment, at_dom):
        return at_segment * parts + at_dom % parts

    def send(value, pairs):
        return lax.ppermute(value, ("segment", "dom"), every_device(pairs, segments * parts, group))

    def to_chip(value, steps):
        giver = steps - 1
        pairs = []
        for at in range(segments):
            for dom in range(parts):
                chip, lane = divmod(dom, group)
                across = (chip ^ steps) * group + lane
                if at == giver:
                    pairs.append((device(at, dom), device(0, across)))
                elif at == 0:
                    pairs.append((device(at, dom), device(giver, dom)))
                else:
                    pairs.append((device(at, dom), device(at, chip * group + (lane + 1) % group)))
        return lax.ppermute(value, ("segment", "dom"), pairs)

    def change_lane(value, steps):
        pairs = [(at, at - at % group + (at + steps) % group) for at in range(parts)]
        return lax.ppermute(value, "dom", pairs)

    def owner(m, at_segment):
        return device(min(at_segment, last + m % 2), m * group)

    own_segment, own_place, w_project = lax.optimization_barrier(
        (segment.reshape(1), place.reshape(1), w_project)
    )
    where = (own_segment, own_place)
    weights = [w_project, w_message, w_update]
    last = segments - 2
    to_last = [(device(last + 1 - m % 2, m * group), owner(m, segments)) for m in range(samples)]
    came_project = send(w_project, to_last)
    snapshots = jnp.transpose(grid_state, (0, 2, 1))
    lists = send_rows.shape[0]

    def rows_of(value):
        return jnp.pad(value, ((0, 0), (0, 128 - value.shape[1])))

    packed = jnp.concatenate(
        [
            rows_of(neighbors.T),
            rows_of(send_rows),
            rows_of(grid_mesh.reshape(1, grid_rows)),
            rows_of(halo_count.reshape(1, lists)),
        ],
        axis=0,
    )
    payloads = call(
        functools.partial(encode_kernel, group, mesh_rows, fanout, lists),
        "encode",
        [jax.ShapeDtypeStruct((mesh_rows + 2 * fanout, width), bf16)] * samples,
        [where, snapshots, w_embed, packed],
        "wvvv",
        [pltpu.VMEM((samples * grid_rows, width), bf16)],
    )
    held = call(
        hold_kernel,
        "hold",
        [jax.ShapeDtypeStruct((width, width), bf16)] * 4,
        weights,
        "hhh",
        [pltpu.VMEM((width, width), bf16)] * 2 + [pltpu.SemaphoreType.DMA((5,))],
    )
    own_payload, *held = lax.optimization_barrier((payloads[0], *held))
    longest_first = sorted(range(1, samples), key=lambda turn: (turn < samples // 2, turn))
    arrived = [to_chip(payloads[turn], turn) for turn in longest_first] + [own_payload]
    (joined,) = call(
        functools.partial(join_kernel, longest_first + [0]),
        "join",
        [jax.ShapeDtypeStruct((samples * (mesh_rows + 2 * fanout), width), bf16)],
        arrived,
        "v" * samples,
    )
    lanes = [joined] + [change_lane(joined, -steps) for steps in range(1, group)]
    share = group * mesh_rows
    whole, short, tall = [
        jax.ShapeDtypeStruct((rows, width), bf16) for rows in (nodes, share, share + 2 * fanout)
    ]
    columns_shape = jax.ShapeDtypeStruct((nodes, 128), bf16)
    columns, codes, state = call(
        functools.partial(index_kernel, parts, mesh_rows),
        "index",
        [columns_shape, jax.ShapeDtypeStruct((2 * fanout, width), bf16), whole],
        [where] + lanes,
        "w" + "v" * group,
        [pltpu.VMEM((fanout, nodes), jnp.int32)],
    )
    columns, came_project, *held = lax.optimization_barrier((columns, came_project, *held))
    (pair,) = call(
        functools.partial(pack_kernel, group, last),
        "pack",
        [jax.ShapeDtypeStruct((2, width, width), bf16)],
        [where] + held[2:],
        "wvv",
    )
    came = [came_project, send(pair, to_last)]
    pieces, senders, places, early = [state], [], (0,), []
    for layer in range(last + 1):
        late = layer == last
        pairs = [(owner(m, layer), owner(m, segments if layer + 1 == last else layer + 1)) for m in range(samples)]
        if layer == 0:
            order, sent = list(range(samples)), []
        else:
            first = places[1]
            order = [first] + [(first + step) % samples for step in range(1, samples)]
            (piece,) = call(
                functools.partial(early_kernel, group, layer, late, fanout, places[:-1], first),
                "early",
                [short if late else tall],
                [where, columns] + senders + [pieces[1], pieces[0]] + held + came * late,
                "w" + "v" * (3 + len(senders + held + came * late)),
                [pltpu.VMEM((nodes, width), bf16)],
            )
            if late:
                pieces[-1], piece = lax.optimization_barrier((pieces[-1], piece))
                break
            sent = [send(piece, pairs)]
            pieces[-1], columns = lax.optimization_barrier((pieces[-1], columns))
        start = order[len(sent)] * share
        extra = [codes] * (layer == 0)
        sender, joined_state, piece = call(
            functools.partial(open_kernel, group, layer, fanout, places, start),
            "open",
            [whole, whole, tall if layer == 0 else short],
            [where, columns] + pieces + senders + extra + held,
            "w" + "v" * (1 + len(pieces + senders + extra + held)),
        )
        sent.append(send(piece, pairs))
        for place_sent in order[len(sent) :]:
            (piece,) = call(
                functools.partial(next_kernel, group, layer, fanout, place_sent * share),
                "next",
                [short],
                [where, columns, sender, joined_state] + held,
                "w" + "v" * (3 + len(held)),
            )
            sent.append(send(piece, pairs))
        pieces, senders, places = sent, [], tuple(order)
        if layer == 0:
            ready, table = call(
                prepare_kernel,
                "prepare",
                [
                    jax.ShapeDtypeStruct((grid_rows, width), jnp.float32),
                    jax.ShapeDtypeStruct((mesh_rows, grid_rows), bf16),
                ],
                [where, snapshots, w_embed, w_decode, mesh_grid.reshape(1, grid_rows)],
                "wvvvv",
            )
            pieces[0], ready, table = lax.optimization_barrier((pieces[0], ready, table))
        for number, part in enumerate(pieces[:-1]):
            if senders:
                part, senders[-1] = lax.optimization_barrier((part, senders[-1]))
                pieces[number] = part
            late = layer + 1 == last
            sender, *found = call(
                functools.partial(late_sender_kernel if late else sender_kernel, group, layer + 1, fanout, share),
                "sender",
                [short] + [columns_shape] * (not senders),
                [where, part, held[1]] + came[:1] * late,
                "wvv" + "v" * late,
            )
            columns = found[0] if found else columns
            senders.append(sender)
    (state,) = call(
        functools.partial(layer_kernel, group, last, fanout, places, order[0]),
        "layer",
        [whole],
        [where, columns] + pieces + senders + [piece] + held + came,
        "w" + "v" * (2 + len(pieces + senders + held + came)),
        [pltpu.VMEM((nodes, width), bf16)] * 2,
    )
    far = []
    for begin in range(0, nodes // 2, share):
        found = call(
            functools.partial(end_kernel, group, last, samples, True, begin, not far, fanout),
            "far_part",
            [whole] * (not far) + [short],
            [where, columns, state] + ([sender] if far else []) + held + came,
            "w" + "v" * (9 if far else 8),
        )
        sender = found[0] if not far else sender
        far.append(found[-1])
    near = []
    for begin in range(0, nodes // 2, share):
        near += call(
            functools.partial(end_kernel, group, last, samples, False, begin, False, fanout),
            "near_part",
            [short],
            [where, columns, state, sender] + held + came,
            "w" + "v" * 9,
        )
    state = far + list(near)
    each = samples // 2
    arrived = []
    for far, blocks in ((1, state[:each]), (0, state[each:])):
        for turn, block in enumerate(blocks):
            pairs = [
                (owner(m, segments), device(m, ((m // each ^ far) * each + turn) * group)) for m in range(samples)
            ]
            arrived.append(send(block, [pair for pair in pairs if pair[0] != pair[1]]))
    crossed = []
    for number, block in enumerate(arrived[:each]):
        crossed = call(
            functools.partial(far_kernel, group, samples, last, number),
            "far",
            [short],
            [where, block] + list(crossed),
            "wv" + "v" * len(crossed),
        )
    parts_of_block = call(
        functools.partial(near_kernel, group, samples, last),
        "near",
        [jax.ShapeDtypeStruct((mesh_rows, width), bf16)] * group,
        [where, crossed[0]] + arrived[each:] + state[each:],
        "w" + "v" * (1 + 2 * each),
    )
    handed = [parts_of_block[0]]
    for steps in range(1, group):
        handed.append(change_lane(parts_of_block[steps], steps))
    (prediction,) = call(
        decode_kernel,
        "decode",
        [jax.ShapeDtypeStruct((channels, grid_rows), bf16)],
        [where, ready, table, w_decode, w_output.T] + handed,
        "wvvvv" + "v" * group,
        [pltpu.VMEM((mesh_rows, width), bf16)],
    )
    return prediction.T.reshape(1, grid_rows, channels)


def chosen_plan(mesh, *arrays):
    segments, parts = mesh.shape["segment"], mesh.shape["dom"]
    samples, width = arrays[0].shape[0], arrays[1].shape[1]
    nodes = parts * arrays[9].shape[0]
    fits = samples == segments == 4 and parts % samples == 0 and parts > samples and nodes == width
    return (resident if fits else streamed)(*arrays)


def solution(mesh):
    return jax.shard_map(
        functools.partial(chosen_plan, mesh),
        mesh=mesh,
        in_specs=(
            P(None, "dom", None),
            P(),
            P("segment", None, None),
            P("segment", None, None),
            P("segment", None, None),
            P(),
            P(),
            P("dom"),
            P("dom"),
            P("dom", None),
            P(None, "dom"),
            P(None, "dom"),
        ),
        out_specs=P("segment", "dom", None),
        check_vma=False,
    )
```

```python
import functools

import jax
import jax.numpy as jnp
from jax import lax
from jax.experimental import pallas as pl
from jax.experimental.pallas import tpu as pltpu
from jax.sharding import PartitionSpec as P

epsilon = 1e-05
DIGIT = 256
VMEM = pl.BlockSpec(memory_space=pltpu.VMEM)
SMEM = pl.BlockSpec(memory_space=pltpu.SMEM)
HBM = pl.BlockSpec(memory_space=pltpu.HBM)


def from_behind(value, axis, steps):
    count = lax.axis_size(axis)
    pairs = [(source, (source + steps) % count) for source in range(count)]
    return lax.ppermute(value, axis, pairs)


def from_behind_2(block, axis, distance):
    devices = range(lax.axis_size(axis))
    route = [(i - distance, i) for i in devices if i - distance in devices]
    return lax.ppermute(block, axis, route)


def from_root(value, axis, source):
    kept = jnp.where(lax.axis_index(axis) == source, value, 0).astype(value.dtype)
    return lax.psum(kept, axis)


def rms_scale(values):
    return values * lax.rsqrt(jnp.mean(values * values, axis=-1, keepdims=True) + epsilon)


def streamed(
    grid_state,
    w_embed,
    w_project,
    w_message,
    w_update,
    w_decode,
    w_output,
    grid_mesh,
    mesh_grid,
    neighbors,
    send_rows,
    halo_count,
):
    segment_index = lax.axis_index("segment")
    segment_count = lax.axis_size("segment")
    final_segment = segment_count - 1
    samples, grid_rows, channels = grid_state.shape
    width = w_embed.shape[1]
    mesh_rows = neighbors.shape[0]
    fanout = neighbors.shape[1]
    halo_rows = send_rows.shape[1]
    share = samples // segment_count
    pool_table = (grid_mesh[None, :] == jnp.arange(mesh_rows, dtype=jnp.int32)[:, None]).astype(
        jnp.bfloat16
    )
    read_table = (mesh_grid[:, None] == jnp.arange(mesh_rows, dtype=jnp.int32)[None, :]).astype(
        jnp.bfloat16
    )
    valid_rows = jnp.arange(halo_rows, dtype=jnp.int32)[None, :] < halo_count[:, 0][:, None]
    source_rows = neighbors.reshape(mesh_rows * fanout)

    def embed_grid(snapshot):
        return jax.nn.silu(jnp.dot(snapshot, w_embed, preferred_element_type=jnp.float32)).astype(
            jnp.bfloat16
        )

    def encode(snapshot):
        latent = embed_grid(snapshot)
        pooled = jnp.dot(pool_table, latent, preferred_element_type=jnp.float32)
        return (rms_scale(pooled).astype(jnp.bfloat16), latent)

    def project(state, weights):
        projected = jnp.dot(state, weights[0], preferred_element_type=jnp.float32)
        return (projected[:, :width], projected[:, width:].astype(jnp.bfloat16))

    def renew(state, receiver, extended, weights):
        fetched = extended[source_rows].reshape(mesh_rows, fanout, width)
        edges = jax.nn.silu(receiver[:, None, :] + fetched.astype(jnp.float32)).astype(jnp.bfloat16)
        messages = jnp.dot(
            edges.reshape(mesh_rows * fanout, width), weights[1], preferred_element_type=jnp.float32
        )
        aggregate = (jnp.sum(messages.reshape(mesh_rows, fanout, width), axis=1) / fanout).astype(
            jnp.bfloat16
        )
        update = jax.nn.silu(
            jnp.dot(state, weights[2][:width], preferred_element_type=jnp.float32)
            + jnp.dot(aggregate, weights[2][width:], preferred_element_type=jnp.float32)
        )
        return (state.astype(jnp.float32) + rms_scale(update)).astype(jnp.bfloat16)

    def decode(state, latent):
        readout = jnp.dot(read_table, state, preferred_element_type=jnp.float32).astype(
            jnp.bfloat16
        )
        hidden = jax.nn.silu(
            jnp.dot(latent, w_decode[:width], preferred_element_type=jnp.float32)
            + jnp.dot(readout, w_decode[width:], preferred_element_type=jnp.float32)
        ).astype(jnp.bfloat16)
        return jnp.dot(hidden, w_output, preferred_element_type=jnp.float32).astype(jnp.bfloat16)

    own_weights = (w_project[0], w_message[0], w_update[0])
    empty_mesh = jnp.zeros((mesh_rows, width), jnp.bfloat16)
    empty_receiver = jnp.zeros((mesh_rows, width), jnp.float32)
    empty_grid = jnp.zeros((grid_rows, width), jnp.bfloat16)
    empty_output = jnp.zeros((grid_rows, channels), jnp.bfloat16)
    received = empty_mesh
    carried = {}
    results = [empty_output for sample in range(samples)]
    for moment in range(samples + final_segment):
        current = received
        if moment < samples:
            snapshot = grid_state[moment]
            started, latent = lax.cond(
                segment_index == 0, lambda: encode(snapshot), lambda: (empty_mesh, empty_grid)
            )
            current = jnp.where(segment_index == 0, started, received)
            carried[moment] = from_behind_2(latent, "segment", final_segment)
        active = (moment - segment_index >= 0) & (moment - segment_index < samples)
        receiver, outgoing = lax.cond(
            active, lambda: project(current, own_weights), lambda: (empty_receiver, empty_mesh)
        )
        picked = jnp.where(valid_rows[:, :, None], outgoing[send_rows], jnp.zeros((), jnp.bfloat16))
        arrived = [outgoing]
        for list_index, offset in enumerate((1, -1, 2, -2)):
            arrived.append(from_behind(picked[list_index], "dom", offset))
        extended = jnp.concatenate(arrived, axis=0)
        renewed = lax.cond(
            active, lambda: renew(current, receiver, extended, own_weights), lambda: empty_mesh
        )
        if moment >= final_segment:
            finished = moment - final_segment
            skipped = carried[finished]
            results[finished] = lax.cond(
                segment_index == final_segment,
                lambda: decode(renewed, skipped),
                lambda: empty_output,
            )
        if moment < samples + final_segment - 1:
            received = from_behind_2(renewed, "segment", 1)
    everything = from_root(jnp.stack(results), "segment", final_segment)
    return lax.dynamic_slice_in_dim(everything, segment_index * share, share, 0)


def silu_by_tanh(values):
    half = 0.5 * values
    return half + half * jnp.tanh(half)


def matmul(left, right):
    return jnp.dot(left, right, preferred_element_type=jnp.float32)


def matmul_nt(left, right):
    return lax.dot_general(left, right, (((1,), (1,)), ((), ())), preferred_element_type=jnp.float32)


def matmul_tn(left, right):
    return lax.dot_general(left, right, (((0,), (0,)), ((), ())), preferred_element_type=jnp.float32)


def place_of(where, group):
    return lax.div(where[1], group), lax.rem(where[1], group)


def owns(where, group, at_segment):
    return jnp.logical_and(where[0] == at_segment, lax.rem(where[1], group) == 0)


def swapped_roles(where, group, at_segment):
    chip, lane = place_of(where, group)
    for number in range(2):
        here = jnp.logical_and(where[0] == at_segment + number, lane == 0)
        yield jnp.logical_and(here, lax.rem(chip, 2) == number), number


def weights_of(came, held, own):
    if own:
        return [block[...] for block in held]
    w_project, pair = came
    width = pair.shape[1]
    return [w_project[0, :, :width], w_project[0, :, width:], pair[0], pair[1]]


def fetch(sources, targets, semaphores):
    copies = [
        pltpu.make_async_copy(source, target, semaphores.at[place])
        for place, (source, target) in enumerate(zip(sources, targets))
    ]
    for copy in copies:
        copy.start()
    return copies


def encode_kernel(group, mesh_rows, fanout, lists, where, snapshots, w_embed, packed, *refs):
    payloads, latent = refs[:-1], refs[-1]
    chip, _ = place_of(where, group)
    neighbors = packed[:fanout, :mesh_rows]
    grid_rows = snapshots.shape[2]
    grid_mesh = packed[fanout + lists : fanout + lists + 1, :grid_rows]
    counts = packed[fanout + lists + 1 : fanout + lists + 2, :lists]
    width = w_embed.shape[1]
    for place in range(snapshots.shape[0]):
        found = silu_by_tanh(matmul_tn(snapshots[place], w_embed[...])).astype(jnp.bfloat16)
        latent[place * grid_rows : (place + 1) * grid_rows, :] = found
    table = lax.broadcasted_iota(jnp.int32, (mesh_rows, grid_rows), 0) == grid_mesh
    table = jnp.where(table, 1.0, 0.0).astype(jnp.bfloat16)
    block = neighbors // mesh_rows
    row = neighbors - block * mesh_rows
    halo_rows = mesh_rows
    position = lax.broadcasted_iota(jnp.int32, (1, halo_rows), 1)
    rows = []
    for list_index in range(lists):
        kept = position < counts[:, list_index : list_index + 1]
        listed = packed[fanout + list_index : fanout + list_index + 1, :halo_rows]
        rows.append(jnp.where(kept, listed, mesh_rows))
    rows.append(jnp.zeros((fanout - lists, halo_rows), jnp.int32))
    filler = jnp.zeros((fanout, 128 - mesh_rows), jnp.int32)
    pieces = [block, filler, row, filler, jnp.concatenate(rows, axis=0), filler]
    coded = jnp.concatenate(pieces + [jnp.zeros((fanout, width - 384), jnp.int32)], axis=1)
    coded = jnp.concatenate([coded, jnp.zeros_like(coded)], axis=0)
    coded = coded.astype(jnp.float32).astype(jnp.bfloat16)
    for turn, payload in enumerate(payloads):
        start = pl.multiple_of(jnp.bitwise_xor(chip, turn) * grid_rows, grid_rows)
        pooled = matmul(table, latent[pl.ds(start, grid_rows), :])
        payload[:mesh_rows, :] = rms_scale(pooled).astype(jnp.bfloat16)
        payload[mesh_rows:, :] = coded


def join_kernel(places, *refs):
    payloads, joined = refs[:-1], refs[-1]
    rows = payloads[0].shape[0]
    for place, payload in zip(places, payloads):
        joined[place * rows : (place + 1) * rows, :] = payload[...]


def columns_of(names):
    fanout, nodes = names.shape
    tile = min(nodes, DIGIT)
    rows = [names - number * tile for number in range(nodes // tile)]
    rows.append(jnp.zeros((128 - fanout * len(rows), nodes), jnp.float32))
    return jnp.transpose(jnp.concatenate(rows, axis=0)).astype(jnp.bfloat16)


def index_kernel(parts, mesh_rows, where, *refs):
    lanes, (columns_out, codes, state), index_out = refs[:-4], refs[-4:-1], refs[-1]
    nodes = columns_out.shape[0]
    group = len(lanes)
    rows = lanes[0].shape[0] // (parts // group)
    chip, _ = place_of(where, group)

    @pl.when(owns(where, group, 0))
    def _():
        tables = []
        for part in range(parts):
            lane, turn = lanes[part % group], jnp.bitwise_xor(chip, part // group)
            base = pl.multiple_of(turn * rows, 16)
            state[part * mesh_rows : (part + 1) * mesh_rows, :] = lane[pl.ds(base, mesh_rows), :]
            base = pl.multiple_of(turn * rows + mesh_rows, 16)
            coded = lane[pl.ds(base, rows - mesh_rows), :384].astype(jnp.float32).astype(jnp.int32)
            tables.append(coded[: coded.shape[0] // 2])
        fanout = tables[0].shape[0]
        for part in range(parts):
            block = tables[part][:, :128]
            row = tables[part][:, 128:256]
            found = part * mesh_rows + row
            for list_index, offset in enumerate((-1, 1, -2, 2)):
                source = (part + offset) % parts
                lists = tables[source][list_index : list_index + 1, 256:384]
                lists = jnp.broadcast_to(lists, (fanout, 128))
                picked = jnp.take_along_axis(lists, row, axis=1)
                picked = jnp.where(picked == mesh_rows, parts * mesh_rows, source * mesh_rows + picked)
                found = jnp.where(block == list_index + 1, picked, found)
            index_out[:, part * mesh_rows : (part + 1) * mesh_rows] = found[:, :mesh_rows]
        names = index_out[...]
        high_digit = names // DIGIT
        digits = jnp.concatenate([high_digit, names - high_digit * DIGIT], axis=0)
        codes[...] = digits.astype(jnp.float32).astype(jnp.bfloat16)
        columns_out[...] = columns_of(names.astype(jnp.float32))


def pack_kernel(group, at_segment, where, *refs):
    @pl.when(jnp.logical_or(owns(where, group, at_segment), owns(where, group, at_segment + 1)))
    def _():
        for place, block in enumerate(refs[:-1]):
            refs[-1][place] = block[...]


def hold_kernel(w_project, w_message, w_update, receive, send, own, edges, message, update, semaphores):
    width = own.shape[0]
    sources = [
        w_message.at[0],
        w_update.at[0, width:],
        w_project.at[0, :, :width],
        w_project.at[0, :, width:],
        w_update.at[0, :width],
    ]
    copies = fetch(sources, [message, update, receive, send, own], semaphores)
    copies[0].wait()
    copies[1].wait()
    edges[...] = matmul(message[...], update[...]).astype(jnp.bfloat16)
    for copy in copies[2:]:
        copy.wait()


def sum_edges(fanout, columns, sender, own, w_receive):
    chunk, width = own.shape
    nodes = sender.shape[0]
    tile = min(nodes, DIGIT)
    names = lax.broadcasted_iota(jnp.int32, (chunk, tile), 1).astype(jnp.float32).astype(jnp.bfloat16)
    one_half = jnp.full((chunk, tile), 0.5, jnp.bfloat16)
    none = jnp.zeros((chunk, tile), jnp.bfloat16)
    receiver = 0.5 * matmul(own, w_receive)
    total = jnp.zeros((chunk, width), jnp.float32)
    for k in range(fanout):
        hits = []
        for number in range(nodes // tile):
            lane = number * fanout + k
            hits.append(jnp.where(columns[:, lane : lane + 1] == names, one_half, none))
        half = receiver + matmul(jnp.concatenate(hits, axis=1), sender)
        total = total + (half + half * jnp.tanh(half))
    return (total * (1.0 / fanout)).astype(jnp.bfloat16)


def update_nodes(own, gathered, w_own, w_edges):
    update = silu_by_tanh(matmul(own, w_own) + matmul(gathered, w_edges))
    return (own.astype(jnp.float32) + rms_scale(update)).astype(jnp.bfloat16)


def sender_kernel(group, at_segment, fanout, rows, where, state, w_send, sender, *columns):
    @pl.when(owns(where, group, at_segment))
    def _():
        sender[...] = matmul(state[:rows, :], w_send[...]).astype(jnp.bfloat16)
        if columns:
            digits = state[rows:, :].astype(jnp.float32)
            columns[0][...] = columns_of(digits[:fanout] * DIGIT + digits[fanout:])


def late_sender_kernel(group, at_segment, fanout, rows, where, state, w_send, w_project, sender, *columns):
    width = state.shape[1]
    for here, number in swapped_roles(where, group, at_segment):

        @pl.when(here)
        def _(number=number):
            weights = w_project[0, :, width:] if number else w_send[...]
            sender[...] = matmul(state[:rows, :], weights).astype(jnp.bfloat16)
            if columns:
                digits = state[rows:, :].astype(jnp.float32)
                columns[0][...] = columns_of(digits[:fanout] * DIGIT + digits[fanout:])


def roles(where, group, at_segment, late):
    return swapped_roles(where, group, at_segment) if late else [(owns(where, group, at_segment), 0)]


def early_kernel(group, at_segment, late, fanout, places, quarter, where, columns, *refs):
    count = len(places)
    senders, refs = refs[:count], refs[count:]
    (own, coded), held, came, (piece, sender) = refs[:2], refs[2:6], refs[6:-2], refs[-2:]
    rows = senders[0].shape[0]
    for here, number in roles(where, group, at_segment, late):

        @pl.when(here)
        def _(number=number):
            w_receive, _, w_own, w_edges = weights_of(came, held, number == 0)
            sender[...] = jnp.zeros_like(sender)
            for place, part in zip(places, senders):
                sender[place * rows : (place + 1) * rows, :] = part[...]
            state = own[:rows, :]
            span = slice(quarter * rows, (quarter + 1) * rows)
            gathered = sum_edges(fanout, columns[span, :], sender[...], state, w_receive)
            piece[:rows, :] = update_nodes(state, gathered, w_own, w_edges)
            if piece.shape[0] > rows:
                piece[rows:, :] = coded[rows:, :]


def layer_kernel(group, at_segment, fanout, places, quarter, where, columns, *refs):
    parts = len(places)
    state, senders, refs = refs[:parts], refs[parts : 2 * parts - 1], refs[2 * parts - 1 :]
    done, held, came, (renewed, whole, sender) = refs[0], refs[1:5], refs[5:7], refs[7:]
    rows = done.shape[0]
    spans = [slice(place * rows, (place + 1) * rows) for place in places]
    own = slice(quarter * rows, (quarter + 1) * rows)
    rest = [slice(0, own.start), slice(own.stop, renewed.shape[0])]
    for here, number in swapped_roles(where, group, at_segment):

        @pl.when(here)
        def _(number=number):
            w_receive, w_send, w_own, w_edges = weights_of(came, held, number == 0)
            for span, part in zip(spans, state):
                whole[span, :] = part[:rows, :]
            for span, part in zip(spans, senders):
                sender[span, :] = part[...]
            sender[spans[-1], :] = matmul(whole[spans[-1], :], w_send).astype(jnp.bfloat16)
            renewed[own, :] = done[...]
            for span in rest:
                if span.stop > span.start:
                    gathered = sum_edges(fanout, columns[span, :], sender[...], whole[span, :], w_receive)
                    renewed[span, :] = update_nodes(whole[span, :], gathered, w_own, w_edges)


def open_kernel(group, at_segment, fanout, places, start, where, columns, *refs):
    parts = len(places)
    state, senders, refs = refs[:parts], refs[parts : 2 * parts - 1], refs[2 * parts - 1 :]
    codes, (w_receive, w_send, w_own, w_edges), (sender, whole, piece) = refs[:-7], refs[-7:-3], refs[-3:]
    rows = whole.shape[0] // parts
    spans = [slice(place * rows, (place + 1) * rows) for place in places]

    @pl.when(owns(where, group, at_segment))
    def _():
        for span, part in zip(spans, state):
            whole[span, :] = part[:rows, :]
        for span, part in zip(spans, senders):
            sender[span, :] = part[...]
        sender[spans[-1], :] = matmul(whole[spans[-1], :], w_send[...]).astype(jnp.bfloat16)
        count = piece.shape[0] - (codes[0].shape[0] if codes else 0)
        span = slice(start, start + count)
        own = whole[span, :]
        gathered = sum_edges(fanout, columns[span, :], sender[...], own, w_receive[...])
        piece[:count, :] = update_nodes(own, gathered, w_own[...], w_edges[...])
        if codes:
            piece[count:, :] = codes[0][...]


def next_kernel(group, at_segment, fanout, start, where, columns, sender, whole, *refs):
    w_receive, _, w_own, w_edges, piece = refs
    span = slice(start, start + piece.shape[0])

    @pl.when(owns(where, group, at_segment))
    def _():
        own = whole[span, :]
        gathered = sum_edges(fanout, columns[span, :], sender[...], own, w_receive[...])
        piece[...] = update_nodes(own, gathered, w_own[...], w_edges[...])


def end_kernel(group, at_segment, chips, far, begin, first, fanout, where, columns, state, *refs):
    senders, refs = (refs[:0], refs) if first else (refs[:1], refs[1:])
    held, came, outs = refs[:4], refs[4:6], refs[6:]
    half = state.shape[0] // 2
    chip, _ = place_of(where, group)
    for here, number in swapped_roles(where, group, at_segment):

        @pl.when(here)
        def _(number=number):
            w_receive, w_send, w_own, w_edges = weights_of(came, held, number == 1)
            pieces = outs
            if first:
                outs[0][...] = matmul(state[...], w_send).astype(jnp.bfloat16)
                pieces = outs[1:]
            sender = outs[0] if first else senders[0]
            rows = sum(piece.shape[0] for piece in pieces)
            upper = (chip < chips // 2) if far else (chip >= chips // 2)
            start = pl.multiple_of(jnp.where(upper, half, 0) + begin, rows)
            own = state[pl.ds(start, rows), :]
            gathered = sum_edges(fanout, columns[pl.ds(start, rows), :], sender[...], own, w_receive)
            write_pieces(pieces, update_nodes(own, gathered, w_own, w_edges))


def write_pieces(pieces, value):
    rows = value.shape[0] // len(pieces)
    for place, piece in enumerate(pieces):
        piece[:rows, :] = value[place * rows : (place + 1) * rows]


def arrival(where, group, chips, last):
    each = chips // 2
    segment = where[0]
    chip, _ = place_of(where, group)
    crosses = lax.div(chip, each) != lax.div(segment, each)
    return crosses, jnp.logical_and(segment >= last, chip == segment), lax.rem(chip, each)


def far_kernel(group, chips, last, number, where, *refs):
    block, out = refs[0], refs[-1]
    crosses, _, spot = arrival(where, group, chips, last)

    @pl.when(jnp.logical_and(crosses, spot == number))
    def _():
        out[...] = block[...]

    if number:

        @pl.when(jnp.logical_and(crosses, spot < number))
        def _():
            out[...] = refs[1][...]


def near_kernel(group, chips, last, where, crossed, *refs):
    each = chips // 2
    near, kept, outs = refs[:each], refs[each : 2 * each], refs[2 * each :]
    rows = outs[0].shape[0]
    crosses, stays, spot = arrival(where, group, chips, last)
    arrives = jnp.logical_not(jnp.logical_or(crosses, stays))

    def give(block):
        for place, out in enumerate(outs):
            out[...] = block[place * rows : (place + 1) * rows, :]

    @pl.when(crosses)
    def _():
        give(crossed)

    for number in range(each):
        for blocks, chosen in ((near, arrives), (kept, stays)):

            @pl.when(jnp.logical_and(chosen, spot == number))
            def _(block=blocks[number]):
                give(block)


def prepare_kernel(where, snapshots, w_embed, w_decode, mesh_grid, ready, table_out):
    snapshot = snapshots[where[0]]
    latent = silu_by_tanh(matmul_tn(snapshot, w_embed[...])).astype(jnp.bfloat16)
    ready[...] = matmul(latent, w_decode[: latent.shape[1], :])
    mesh_rows, grid_rows = table_out.shape
    table = lax.broadcasted_iota(jnp.int32, (mesh_rows, grid_rows), 0) == mesh_grid[...]
    table_out[...] = jnp.where(table, 1.0, 0.0).astype(jnp.bfloat16)


def decode_kernel(where, ready, table, w_decode, w_output, *refs):
    blocks, out, state = refs[:-2], refs[-2], refs[-1]
    width = ready.shape[1]
    _, lane = place_of(where, len(blocks))
    for number, block in enumerate(blocks):

        @pl.when(lane == number)
        def _(block=block):
            state[...] = block[...]

    readout = matmul_tn(table[...], state[...]).astype(jnp.bfloat16)
    hidden = silu_by_tanh(ready[...] + matmul(readout, w_decode[width:, :])).astype(jnp.bfloat16)
    out[...] = matmul_nt(w_output[...], hidden).astype(jnp.bfloat16)


def call(kernel, name, shapes, inputs, places, scratch=(), room=16, flops=0):
    specs, given = [], []
    for value, place in zip(inputs, places):
        specs += [SMEM] * 2 if place == "w" else [VMEM if place == "v" else HBM]
        given += list(value) if place == "w" else [value]
    moved = sum(value.size * value.dtype.itemsize for value in given + list(shapes))

    def located(segment, place, *refs):
        kernel((segment[0], place[0]), *refs)

    return pl.pallas_call(
        located if places[0] == "w" else kernel,
        out_shape=shapes,
        in_specs=specs,
        out_specs=[VMEM] * len(shapes),
        scratch_shapes=list(scratch),
        name=name,
        compiler_params=pltpu.CompilerParams(vmem_limit_bytes=room * 1024 * 1024),
        cost_estimate=pl.CostEstimate(flops=flops, bytes_accessed=moved, transcendentals=0),
    )(*given)


def every_device(pairs, count, group):
    onward = dict(pairs)
    reached = set(onward.values())
    for first in [source for source in onward if source not in reached]:
        last = first
        while last in onward:
            last = onward[last]
        onward.update({last: last + group - 1, last + group - 1: first + group - 1, first + group - 1: first})
    alone = []
    for at in range(0, count, group):
        rest = [lane for lane in range(at, at + group) if lane not in onward]
        if len(rest) > 1:
            onward.update(zip(rest, rest[1:] + rest[:1]))
        else:
            alone += rest
    if len(alone) == 1:
        before = next(at for at in onward if at % group and onward[at] % group == 0)
        onward.update({before: alone[0], alone[0]: onward[before]})
    else:
        onward.update(zip(alone, alone[1:] + alone[:1]))
    return sorted(onward.items())


def resident(
    grid_state,
    w_embed,
    w_project,
    w_message,
    w_update,
    w_decode,
    w_output,
    grid_mesh,
    mesh_grid,
    neighbors,
    send_rows,
    halo_count,
):
    segment = lax.axis_index("segment")
    place = lax.axis_index("dom")
    segments = lax.axis_size("segment")
    parts = lax.axis_size("dom")
    samples, grid_rows, channels = grid_state.shape
    width = w_embed.shape[1]
    mesh_rows, fanout = neighbors.shape
    nodes = parts * mesh_rows
    group = parts // samples
    bf16 = jnp.bfloat16

    def device(at_segment, at_dom):
        return at_segment * parts + at_dom % parts

    def send(value, pairs):
        return lax.ppermute(value, ("segment", "dom"), every_device(pairs, segments * parts, group))

    def to_chip(value, steps):
        giver = steps - 1
        pairs = []
        for at in range(segments):
            for dom in range(parts):
                chip, lane = divmod(dom, group)
                across = (chip ^ steps) * group + lane
                if at == giver:
                    pairs.append((device(at, dom), device(0, across)))
                elif at == 0:
                    pairs.append((device(at, dom), device(giver, dom)))
                else:
                    pairs.append((device(at, dom), device(at, chip * group + (lane + 1) % group)))
        return lax.ppermute(value, ("segment", "dom"), pairs)

    def change_lane(value, steps):
        pairs = [(at, at - at % group + (at + steps) % group) for at in range(parts)]
        return lax.ppermute(value, "dom", pairs)

    def owner(m, at_segment):
        return device(min(at_segment, last + m % 2), m * group)

    own_segment, own_place, w_project = lax.optimization_barrier(
        (segment.reshape(1), place.reshape(1), w_project)
    )
    where = (own_segment, own_place)
    weights = [w_project, w_message, w_update]
    last = segments - 2
    to_last = [(device(last + 1 - m % 2, m * group), owner(m, segments)) for m in range(samples)]
    came_project = send(w_project, to_last)
    snapshots = jnp.transpose(grid_state, (0, 2, 1))
    lists = send_rows.shape[0]

    def rows_of(value):
        return jnp.pad(value, ((0, 0), (0, 128 - value.shape[1])))

    packed = jnp.concatenate(
        [
            rows_of(neighbors.T),
            rows_of(send_rows),
            rows_of(grid_mesh.reshape(1, grid_rows)),
            rows_of(halo_count.reshape(1, lists)),
        ],
        axis=0,
    )
    payloads = call(
        functools.partial(encode_kernel, group, mesh_rows, fanout, lists),
        "encode",
        [jax.ShapeDtypeStruct((mesh_rows + 2 * fanout, width), bf16)] * samples,
        [where, snapshots, w_embed, packed],
        "wvvv",
        [pltpu.VMEM((samples * grid_rows, width), bf16)],
    )
    held = call(
        hold_kernel,
        "hold",
        [jax.ShapeDtypeStruct((width, width), bf16)] * 4,
        weights,
        "hhh",
        [pltpu.VMEM((width, width), bf16)] * 2 + [pltpu.SemaphoreType.DMA((5,))],
    )
    own_payload, *held = lax.optimization_barrier((payloads[0], *held))
    longest_first = sorted(range(1, samples), key=lambda turn: (turn < samples // 2, turn))
    arrived = [to_chip(payloads[turn], turn) for turn in longest_first] + [own_payload]
    (joined,) = call(
        functools.partial(join_kernel, longest_first + [0]),
        "join",
        [jax.ShapeDtypeStruct((samples * (mesh_rows + 2 * fanout), width), bf16)],
        arrived,
        "v" * samples,
    )
    lanes = [joined] + [change_lane(joined, -steps) for steps in range(1, group)]
    share = group * mesh_rows
    whole, short, tall = [
        jax.ShapeDtypeStruct((rows, width), bf16) for rows in (nodes, share, share + 2 * fanout)
    ]
    columns_shape = jax.ShapeDtypeStruct((nodes, 128), bf16)
    columns, codes, state = call(
        functools.partial(index_kernel, parts, mesh_rows),
        "index",
        [columns_shape, jax.ShapeDtypeStruct((2 * fanout, width), bf16), whole],
        [where] + lanes,
        "w" + "v" * group,
        [pltpu.VMEM((fanout, nodes), jnp.int32)],
    )
    columns, came_project, *held = lax.optimization_barrier((columns, came_project, *held))
    (pair,) = call(
        functools.partial(pack_kernel, group, last),
        "pack",
        [jax.ShapeDtypeStruct((2, width, width), bf16)],
        [where] + held[2:],
        "wvv",
    )
    came = [came_project, send(pair, to_last)]
    pieces, senders, places, early = [state], [], (0,), []
    for layer in range(last + 1):
        late = layer == last
        pairs = [(owner(m, layer), owner(m, segments if layer + 1 == last else layer + 1)) for m in range(samples)]
        if layer == 0:
            order, sent = list(range(samples)), []
        else:
            first = places[1]
            order = [first] + [(first + step) % samples for step in range(1, samples)]
            (piece,) = call(
                functools.partial(early_kernel, group, layer, late, fanout, places[:-1], first),
                "early",
                [short if late else tall],
                [where, columns] + senders + [pieces[1], pieces[0]] + held + came * late,
                "w" + "v" * (3 + len(senders + held + came * late)),
                [pltpu.VMEM((nodes, width), bf16)],
            )
            if late:
                pieces[-1], piece = lax.optimization_barrier((pieces[-1], piece))
                break
            sent = [send(piece, pairs)]
            pieces[-1], columns = lax.optimization_barrier((pieces[-1], columns))
        start = order[len(sent)] * share
        extra = [codes] * (layer == 0)
        sender, joined_state, piece = call(
            functools.partial(open_kernel, group, layer, fanout, places, start),
            "open",
            [whole, whole, tall if layer == 0 else short],
            [where, columns] + pieces + senders + extra + held,
            "w" + "v" * (1 + len(pieces + senders + extra + held)),
        )
        sent.append(send(piece, pairs))
        for place_sent in order[len(sent) :]:
            (piece,) = call(
                functools.partial(next_kernel, group, layer, fanout, place_sent * share),
                "next",
                [short],
                [where, columns, sender, joined_state] + held,
                "w" + "v" * (3 + len(held)),
            )
            sent.append(send(piece, pairs))
        pieces, senders, places = sent, [], tuple(order)
        if layer == 0:
            ready, table = call(
                prepare_kernel,
                "prepare",
                [
                    jax.ShapeDtypeStruct((grid_rows, width), jnp.float32),
                    jax.ShapeDtypeStruct((mesh_rows, grid_rows), bf16),
                ],
                [where, snapshots, w_embed, w_decode, mesh_grid.reshape(1, grid_rows)],
                "wvvvv",
            )
            pieces[0], ready, table = lax.optimization_barrier((pieces[0], ready, table))
        for number, part in enumerate(pieces[:-1]):
            if senders:
                part, senders[-1] = lax.optimization_barrier((part, senders[-1]))
                pieces[number] = part
            late = layer + 1 == last
            sender, *found = call(
                functools.partial(late_sender_kernel if late else sender_kernel, group, layer + 1, fanout, share),
                "sender",
                [short] + [columns_shape] * (not senders),
                [where, part, held[1]] + came[:1] * late,
                "wvv" + "v" * late,
            )
            columns = found[0] if found else columns
            senders.append(sender)
    (state,) = call(
        functools.partial(layer_kernel, group, last, fanout, places, order[0]),
        "layer",
        [whole],
        [where, columns] + pieces + senders + [piece] + held + came,
        "w" + "v" * (2 + len(pieces + senders + held + came)),
        [pltpu.VMEM((nodes, width), bf16)] * 2,
    )
    sender, *far = call(
        functools.partial(end_kernel, group, last, samples, True, 0, True, fanout),
        "far_half",
        [whole] + [short] * (samples // 2),
        [where, columns, state] + held + came,
        "w" + "v" * 8,
    )
    near = call(
        functools.partial(end_kernel, group, last, samples, False, 0, False, fanout),
        "near_half",
        [short] * (samples // 2),
        [where, columns, state, sender] + held + came,
        "w" + "v" * 9,
    )
    state = far + list(near)
    each = samples // 2
    arrived = []
    for far, blocks in ((1, state[:each]), (0, state[each:])):
        for turn, block in enumerate(blocks):
            pairs = [
                (owner(m, segments), device(m, ((m // each ^ far) * each + turn) * group)) for m in range(samples)
            ]
            arrived.append(send(block, [pair for pair in pairs if pair[0] != pair[1]]))
    crossed = []
    for number, block in enumerate(arrived[:each]):
        crossed = call(
            functools.partial(far_kernel, group, samples, last, number),
            "far",
            [short],
            [where, block] + list(crossed),
            "wv" + "v" * len(crossed),
        )
    parts_of_block = call(
        functools.partial(near_kernel, group, samples, last),
        "near",
        [jax.ShapeDtypeStruct((mesh_rows, width), bf16)] * group,
        [where, crossed[0]] + arrived[each:] + state[each:],
        "w" + "v" * (1 + 2 * each),
    )
    handed = [parts_of_block[0]]
    for steps in range(1, group):
        handed.append(change_lane(parts_of_block[steps], steps))
    (prediction,) = call(
        decode_kernel,
        "decode",
        [jax.ShapeDtypeStruct((channels, grid_rows), bf16)],
        [where, ready, table, w_decode, w_output.T] + handed,
        "wvvvv" + "v" * group,
        [pltpu.VMEM((mesh_rows, width), bf16)],
    )
    return prediction.T.reshape(1, grid_rows, channels)


def chosen_plan(mesh, *arrays):
    segments, parts = mesh.shape["segment"], mesh.shape["dom"]
    samples, width = arrays[0].shape[0], arrays[1].shape[1]
    nodes = parts * arrays[9].shape[0]
    fits = samples == segments == 4 and parts % samples == 0 and parts > samples and nodes == width
    return (resident if fits else streamed)(*arrays)


def solution(mesh):
    return jax.shard_map(
        functools.partial(chosen_plan, mesh),
        mesh=mesh,
        in_specs=(
            P(None, "dom", None),
            P(),
            P("segment", None, None),
            P("segment", None, None),
            P("segment", None, None),
            P(),
            P(),
            P("dom"),
            P("dom"),
            P("dom", None),
            P(None, "dom"),
            P(None, "dom"),
        ),
        out_specs=P("segment", "dom", None),
        check_vma=False,
    )
```

```python
import functools

import jax
import jax.numpy as jnp
from jax import lax
from jax.experimental import pallas as pl
from jax.experimental.pallas import tpu as pltpu
from jax.sharding import PartitionSpec as P

epsilon = 1e-05
DIGIT = 256
VMEM = pl.BlockSpec(memory_space=pltpu.VMEM)
SMEM = pl.BlockSpec(memory_space=pltpu.SMEM)
HBM = pl.BlockSpec(memory_space=pltpu.HBM)


def from_behind(value, axis, steps):
    count = lax.axis_size(axis)
    pairs = [(source, (source + steps) % count) for source in range(count)]
    return lax.ppermute(value, axis, pairs)


def from_behind_2(block, axis, distance):
    devices = range(lax.axis_size(axis))
    route = [(i - distance, i) for i in devices if i - distance in devices]
    return lax.ppermute(block, axis, route)


def from_root(value, axis, source):
    kept = jnp.where(lax.axis_index(axis) == source, value, 0).astype(value.dtype)
    return lax.psum(kept, axis)


def rms_scale(values):
    return values * lax.rsqrt(jnp.mean(values * values, axis=-1, keepdims=True) + epsilon)


def streamed(
    grid_state,
    w_embed,
    w_project,
    w_message,
    w_update,
    w_decode,
    w_output,
    grid_mesh,
    mesh_grid,
    neighbors,
    send_rows,
    halo_count,
):
    segment_index = lax.axis_index("segment")
    segment_count = lax.axis_size("segment")
    final_segment = segment_count - 1
    samples, grid_rows, channels = grid_state.shape
    width = w_embed.shape[1]
    mesh_rows = neighbors.shape[0]
    fanout = neighbors.shape[1]
    halo_rows = send_rows.shape[1]
    share = samples // segment_count
    pool_table = (grid_mesh[None, :] == jnp.arange(mesh_rows, dtype=jnp.int32)[:, None]).astype(
        jnp.bfloat16
    )
    read_table = (mesh_grid[:, None] == jnp.arange(mesh_rows, dtype=jnp.int32)[None, :]).astype(
        jnp.bfloat16
    )
    valid_rows = jnp.arange(halo_rows, dtype=jnp.int32)[None, :] < halo_count[:, 0][:, None]
    source_rows = neighbors.reshape(mesh_rows * fanout)

    def embed_grid(snapshot):
        return jax.nn.silu(jnp.dot(snapshot, w_embed, preferred_element_type=jnp.float32)).astype(
            jnp.bfloat16
        )

    def encode(snapshot):
        latent = embed_grid(snapshot)
        pooled = jnp.dot(pool_table, latent, preferred_element_type=jnp.float32)
        return (rms_scale(pooled).astype(jnp.bfloat16), latent)

    def project(state, weights):
        projected = jnp.dot(state, weights[0], preferred_element_type=jnp.float32)
        return (projected[:, :width], projected[:, width:].astype(jnp.bfloat16))

    def renew(state, receiver, extended, weights):
        fetched = extended[source_rows].reshape(mesh_rows, fanout, width)
        edges = jax.nn.silu(receiver[:, None, :] + fetched.astype(jnp.float32)).astype(jnp.bfloat16)
        messages = jnp.dot(
            edges.reshape(mesh_rows * fanout, width), weights[1], preferred_element_type=jnp.float32
        )
        aggregate = (jnp.sum(messages.reshape(mesh_rows, fanout, width), axis=1) / fanout).astype(
            jnp.bfloat16
        )
        update = jax.nn.silu(
            jnp.dot(state, weights[2][:width], preferred_element_type=jnp.float32)
            + jnp.dot(aggregate, weights[2][width:], preferred_element_type=jnp.float32)
        )
        return (state.astype(jnp.float32) + rms_scale(update)).astype(jnp.bfloat16)

    def decode(state, latent):
        readout = jnp.dot(read_table, state, preferred_element_type=jnp.float32).astype(
            jnp.bfloat16
        )
        hidden = jax.nn.silu(
            jnp.dot(latent, w_decode[:width], preferred_element_type=jnp.float32)
            + jnp.dot(readout, w_decode[width:], preferred_element_type=jnp.float32)
        ).astype(jnp.bfloat16)
        return jnp.dot(hidden, w_output, preferred_element_type=jnp.float32).astype(jnp.bfloat16)

    own_weights = (w_project[0], w_message[0], w_update[0])
    empty_mesh = jnp.zeros((mesh_rows, width), jnp.bfloat16)
    empty_receiver = jnp.zeros((mesh_rows, width), jnp.float32)
    empty_grid = jnp.zeros((grid_rows, width), jnp.bfloat16)
    empty_output = jnp.zeros((grid_rows, channels), jnp.bfloat16)
    received = empty_mesh
    carried = {}
    results = [empty_output for sample in range(samples)]
    for moment in range(samples + final_segment):
        current = received
        if moment < samples:
            snapshot = grid_state[moment]
            started, latent = lax.cond(
                segment_index == 0, lambda: encode(snapshot), lambda: (empty_mesh, empty_grid)
            )
            current = jnp.where(segment_index == 0, started, received)
            carried[moment] = from_behind_2(latent, "segment", final_segment)
        active = (moment - segment_index >= 0) & (moment - segment_index < samples)
        receiver, outgoing = lax.cond(
            active, lambda: project(current, own_weights), lambda: (empty_receiver, empty_mesh)
        )
        picked = jnp.where(valid_rows[:, :, None], outgoing[send_rows], jnp.zeros((), jnp.bfloat16))
        arrived = [outgoing]
        for list_index, offset in enumerate((1, -1, 2, -2)):
            arrived.append(from_behind(picked[list_index], "dom", offset))
        extended = jnp.concatenate(arrived, axis=0)
        renewed = lax.cond(
            active, lambda: renew(current, receiver, extended, own_weights), lambda: empty_mesh
        )
        if moment >= final_segment:
            finished = moment - final_segment
            skipped = carried[finished]
            results[finished] = lax.cond(
                segment_index == final_segment,
                lambda: decode(renewed, skipped),
                lambda: empty_output,
            )
        if moment < samples + final_segment - 1:
            received = from_behind_2(renewed, "segment", 1)
    everything = from_root(jnp.stack(results), "segment", final_segment)
    return lax.dynamic_slice_in_dim(everything, segment_index * share, share, 0)


def silu_by_tanh(values):
    half = 0.5 * values
    return half + half * jnp.tanh(half)


def matmul(left, right):
    return jnp.dot(left, right, preferred_element_type=jnp.float32)


def matmul_nt(left, right):
    return lax.dot_general(left, right, (((1,), (1,)), ((), ())), preferred_element_type=jnp.float32)


def matmul_tn(left, right):
    return lax.dot_general(left, right, (((0,), (0,)), ((), ())), preferred_element_type=jnp.float32)


def place_of(where, group):
    return lax.div(where[1], group), lax.rem(where[1], group)


def owns(where, group, at_segment):
    return jnp.logical_and(where[0] == at_segment, lax.rem(where[1], group) == 0)


def swapped_roles(where, group, at_segment):
    chip, lane = place_of(where, group)
    for number in range(2):
        here = jnp.logical_and(where[0] == at_segment + number, lane == 0)
        yield jnp.logical_and(here, lax.rem(chip, 2) == number), number


def weights_of(came, held, own):
    if own:
        return [block[...] for block in held]
    w_project, pair = came
    width = pair.shape[1]
    return [w_project[0, :, :width], w_project[0, :, width:], pair[0], pair[1]]


def fetch(sources, targets, semaphores):
    copies = [
        pltpu.make_async_copy(source, target, semaphores.at[place])
        for place, (source, target) in enumerate(zip(sources, targets))
    ]
    for copy in copies:
        copy.start()
    return copies


def encode_kernel(group, mesh_rows, fanout, lists, where, snapshots, w_embed, packed, *refs):
    payloads, latent = refs[:-1], refs[-1]
    chip, _ = place_of(where, group)
    neighbors = packed[:fanout, :mesh_rows]
    grid_rows = snapshots.shape[2]
    grid_mesh = packed[fanout + lists : fanout + lists + 1, :grid_rows]
    counts = packed[fanout + lists + 1 : fanout + lists + 2, :lists]
    width = w_embed.shape[1]
    for place in range(snapshots.shape[0]):
        found = silu_by_tanh(matmul_tn(snapshots[place], w_embed[...])).astype(jnp.bfloat16)
        latent[place * grid_rows : (place + 1) * grid_rows, :] = found
    table = lax.broadcasted_iota(jnp.int32, (mesh_rows, grid_rows), 0) == grid_mesh
    table = jnp.where(table, 1.0, 0.0).astype(jnp.bfloat16)
    block = neighbors // mesh_rows
    row = neighbors - block * mesh_rows
    halo_rows = mesh_rows
    position = lax.broadcasted_iota(jnp.int32, (1, halo_rows), 1)
    rows = []
    for list_index in range(lists):
        kept = position < counts[:, list_index : list_index + 1]
        listed = packed[fanout + list_index : fanout + list_index + 1, :halo_rows]
        rows.append(jnp.where(kept, listed, mesh_rows))
    rows.append(jnp.zeros((fanout - lists, halo_rows), jnp.int32))
    filler = jnp.zeros((fanout, 128 - mesh_rows), jnp.int32)
    pieces = [block, filler, row, filler, jnp.concatenate(rows, axis=0), filler]
    coded = jnp.concatenate(pieces + [jnp.zeros((fanout, width - 384), jnp.int32)], axis=1)
    coded = jnp.concatenate([coded, jnp.zeros_like(coded)], axis=0)
    coded = coded.astype(jnp.float32).astype(jnp.bfloat16)
    for turn, payload in enumerate(payloads):
        start = pl.multiple_of(jnp.bitwise_xor(chip, turn) * grid_rows, grid_rows)
        pooled = matmul(table, latent[pl.ds(start, grid_rows), :])
        payload[:mesh_rows, :] = rms_scale(pooled).astype(jnp.bfloat16)
        payload[mesh_rows:, :] = coded


def join_kernel(places, *refs):
    payloads, joined = refs[:-1], refs[-1]
    rows = payloads[0].shape[0]
    for place, payload in zip(places, payloads):
        joined[place * rows : (place + 1) * rows, :] = payload[...]


def columns_of(names):
    fanout, nodes = names.shape
    tile = min(nodes, DIGIT)
    rows = [names - number * tile for number in range(nodes // tile)]
    rows.append(jnp.zeros((128 - fanout * len(rows), nodes), jnp.float32))
    return jnp.transpose(jnp.concatenate(rows, axis=0)).astype(jnp.bfloat16)


def index_kernel(parts, mesh_rows, where, *refs):
    lanes, (columns_out, codes, state), index_out = refs[:-4], refs[-4:-1], refs[-1]
    nodes = columns_out.shape[0]
    group = len(lanes)
    rows = lanes[0].shape[0] // (parts // group)
    chip, _ = place_of(where, group)

    @pl.when(owns(where, group, 0))
    def _():
        tables = []
        for part in range(parts):
            lane, turn = lanes[part % group], jnp.bitwise_xor(chip, part // group)
            base = pl.multiple_of(turn * rows, 16)
            state[part * mesh_rows : (part + 1) * mesh_rows, :] = lane[pl.ds(base, mesh_rows), :]
            base = pl.multiple_of(turn * rows + mesh_rows, 16)
            coded = lane[pl.ds(base, rows - mesh_rows), :384].astype(jnp.float32).astype(jnp.int32)
            tables.append(coded[: coded.shape[0] // 2])
        fanout = tables[0].shape[0]
        for part in range(parts):
            block = tables[part][:, :128]
            row = tables[part][:, 128:256]
            found = part * mesh_rows + row
            for list_index, offset in enumerate((-1, 1, -2, 2)):
                source = (part + offset) % parts
                lists = tables[source][list_index : list_index + 1, 256:384]
                lists = jnp.broadcast_to(lists, (fanout, 128))
                picked = jnp.take_along_axis(lists, row, axis=1)
                picked = jnp.where(picked == mesh_rows, parts * mesh_rows, source * mesh_rows + picked)
                found = jnp.where(block == list_index + 1, picked, found)
            index_out[:, part * mesh_rows : (part + 1) * mesh_rows] = found[:, :mesh_rows]
        names = index_out[...]
        high_digit = names // DIGIT
        digits = jnp.concatenate([high_digit, names - high_digit * DIGIT], axis=0)
        codes[...] = digits.astype(jnp.float32).astype(jnp.bfloat16)
        columns_out[...] = columns_of(names.astype(jnp.float32))


def pack_kernel(group, at_segment, where, *refs):
    @pl.when(jnp.logical_or(owns(where, group, at_segment), owns(where, group, at_segment + 1)))
    def _():
        for place, block in enumerate(refs[:-1]):
            refs[-1][place] = block[...]


def hold_kernel(w_project, w_message, w_update, receive, send, own, edges, message, update, semaphores):
    width = own.shape[0]
    sources = [
        w_message.at[0],
        w_update.at[0, width:],
        w_project.at[0, :, :width],
        w_project.at[0, :, width:],
        w_update.at[0, :width],
    ]
    copies = fetch(sources, [message, update, receive, send, own], semaphores)
    copies[0].wait()
    copies[1].wait()
    edges[...] = matmul(message[...], update[...]).astype(jnp.bfloat16)
    for copy in copies[2:]:
        copy.wait()


def sum_edges(fanout, columns, sender, own, w_receive):
    chunk, width = own.shape
    nodes = sender.shape[0]
    tile = min(nodes, DIGIT)
    names = lax.broadcasted_iota(jnp.int32, (chunk, tile), 1).astype(jnp.float32).astype(jnp.bfloat16)
    one_half = jnp.full((chunk, tile), 0.5, jnp.bfloat16)
    none = jnp.zeros((chunk, tile), jnp.bfloat16)
    receiver = 0.5 * matmul(own, w_receive)
    total = jnp.zeros((chunk, width), jnp.float32)
    for k in range(fanout):
        hits = []
        for number in range(nodes // tile):
            lane = number * fanout + k
            hits.append(jnp.where(columns[:, lane : lane + 1] == names, one_half, none))
        half = receiver + matmul(jnp.concatenate(hits, axis=1), sender)
        total = total + (half + half * jnp.tanh(half))
    return (total * (1.0 / fanout)).astype(jnp.bfloat16)


def update_nodes(own, gathered, w_own, w_edges):
    update = silu_by_tanh(matmul(own, w_own) + matmul(gathered, w_edges))
    return (own.astype(jnp.float32) + rms_scale(update)).astype(jnp.bfloat16)


def sender_kernel(group, at_segment, fanout, rows, where, state, w_send, sender, *columns):
    @pl.when(owns(where, group, at_segment))
    def _():
        sender[...] = matmul(state[:rows, :], w_send[...]).astype(jnp.bfloat16)
        if columns:
            digits = state[rows:, :].astype(jnp.float32)
            columns[0][...] = columns_of(digits[:fanout] * DIGIT + digits[fanout:])


def late_sender_kernel(group, at_segment, fanout, rows, where, state, w_send, w_project, sender, *columns):
    width = state.shape[1]
    for here, number in swapped_roles(where, group, at_segment):

        @pl.when(here)
        def _(number=number):
            weights = w_project[0, :, width:] if number else w_send[...]
            sender[...] = matmul(state[:rows, :], weights).astype(jnp.bfloat16)
            if columns:
                digits = state[rows:, :].astype(jnp.float32)
                columns[0][...] = columns_of(digits[:fanout] * DIGIT + digits[fanout:])


def roles(where, group, at_segment, late):
    return swapped_roles(where, group, at_segment) if late else [(owns(where, group, at_segment), 0)]


def early_kernel(group, at_segment, late, fanout, places, quarter, where, columns, *refs):
    count = len(places)
    senders, refs = refs[:count], refs[count:]
    (own, coded), held, came, (piece, sender) = refs[:2], refs[2:6], refs[6:-2], refs[-2:]
    rows = senders[0].shape[0]
    for here, number in roles(where, group, at_segment, late):

        @pl.when(here)
        def _(number=number):
            w_receive, _, w_own, w_edges = weights_of(came, held, number == 0)
            sender[...] = jnp.zeros_like(sender)
            for place, part in zip(places, senders):
                sender[place * rows : (place + 1) * rows, :] = part[...]
            state = own[:rows, :]
            span = slice(quarter * rows, (quarter + 1) * rows)
            gathered = sum_edges(fanout, columns[span, :], sender[...], state, w_receive)
            piece[:rows, :] = update_nodes(state, gathered, w_own, w_edges)
            if piece.shape[0] > rows:
                piece[rows:, :] = coded[rows:, :]


def layer_kernel(group, at_segment, fanout, places, quarter, where, columns, *refs):
    parts = len(places)
    state, senders, refs = refs[:parts], refs[parts : 2 * parts - 1], refs[2 * parts - 1 :]
    done, held, came, (renewed, whole, sender) = refs[0], refs[1:5], refs[5:7], refs[7:]
    rows = done.shape[0]
    spans = [slice(place * rows, (place + 1) * rows) for place in places]
    own = slice(quarter * rows, (quarter + 1) * rows)
    rest = [slice(0, own.start), slice(own.stop, renewed.shape[0])]
    for here, number in swapped_roles(where, group, at_segment):

        @pl.when(here)
        def _(number=number):
            w_receive, w_send, w_own, w_edges = weights_of(came, held, number == 0)
            for span, part in zip(spans, state):
                whole[span, :] = part[:rows, :]
            for span, part in zip(spans, senders):
                sender[span, :] = part[...]
            sender[spans[-1], :] = matmul(whole[spans[-1], :], w_send).astype(jnp.bfloat16)
            renewed[own, :] = done[...]
            for span in rest:
                if span.stop > span.start:
                    gathered = sum_edges(fanout, columns[span, :], sender[...], whole[span, :], w_receive)
                    renewed[span, :] = update_nodes(whole[span, :], gathered, w_own, w_edges)


def open_kernel(group, at_segment, fanout, places, start, where, columns, *refs):
    parts = len(places)
    state, senders, refs = refs[:parts], refs[parts : 2 * parts - 1], refs[2 * parts - 1 :]
    codes, (w_receive, w_send, w_own, w_edges), (sender, whole, piece) = refs[:-7], refs[-7:-3], refs[-3:]
    rows = whole.shape[0] // parts
    spans = [slice(place * rows, (place + 1) * rows) for place in places]

    @pl.when(owns(where, group, at_segment))
    def _():
        for span, part in zip(spans, state):
            whole[span, :] = part[:rows, :]
        for span, part in zip(spans, senders):
            sender[span, :] = part[...]
        sender[spans[-1], :] = matmul(whole[spans[-1], :], w_send[...]).astype(jnp.bfloat16)
        count = piece.shape[0] - (codes[0].shape[0] if codes else 0)
        span = slice(start, start + count)
        own = whole[span, :]
        gathered = sum_edges(fanout, columns[span, :], sender[...], own, w_receive[...])
        piece[:count, :] = update_nodes(own, gathered, w_own[...], w_edges[...])
        if codes:
            piece[count:, :] = codes[0][...]


def next_kernel(group, at_segment, fanout, start, where, columns, sender, whole, *refs):
    w_receive, _, w_own, w_edges, piece = refs
    span = slice(start, start + piece.shape[0])

    @pl.when(owns(where, group, at_segment))
    def _():
        own = whole[span, :]
        gathered = sum_edges(fanout, columns[span, :], sender[...], own, w_receive[...])
        piece[...] = update_nodes(own, gathered, w_own[...], w_edges[...])


def end_kernel(group, at_segment, chips, far, begin, first, fanout, where, columns, state, *refs):
    senders, refs = (refs[:0], refs) if first else (refs[:1], refs[1:])
    held, came, outs = refs[:4], refs[4:6], refs[6:]
    half = state.shape[0] // 2
    chip, _ = place_of(where, group)
    for here, number in swapped_roles(where, group, at_segment):

        @pl.when(here)
        def _(number=number):
            w_receive, w_send, w_own, w_edges = weights_of(came, held, number == 1)
            pieces = outs
            if first:
                outs[0][...] = matmul(state[...], w_send).astype(jnp.bfloat16)
                pieces = outs[1:]
            sender = outs[0] if first else senders[0]
            rows = sum(piece.shape[0] for piece in pieces)
            if far:
                start = jnp.where(chip < chips // 2, 2 * half - rows - begin, begin)
            else:
                start = jnp.where(chip >= chips // 2, half, 0) + begin
            start = pl.multiple_of(start, rows)
            own = state[pl.ds(start, rows), :]
            gathered = sum_edges(fanout, columns[pl.ds(start, rows), :], sender[...], own, w_receive)
            write_pieces(pieces, update_nodes(own, gathered, w_own, w_edges))


def write_pieces(pieces, value):
    rows = value.shape[0] // len(pieces)
    for place, piece in enumerate(pieces):
        piece[:rows, :] = value[place * rows : (place + 1) * rows]


def arrival(where, group, chips, last):
    each = chips // 2
    segment = where[0]
    chip, _ = place_of(where, group)
    crosses = lax.div(chip, each) != lax.div(segment, each)
    return crosses, jnp.logical_and(segment >= last, chip == segment), lax.rem(chip, each)


def far_kernel(group, chips, last, number, where, *refs):
    block, out = refs[0], refs[-1]
    crosses, _, spot = arrival(where, group, chips, last)
    chip, _ = place_of(where, group)
    spot = jnp.where(chip < chips // 2, chip, chips - 1 - chip)

    @pl.when(jnp.logical_and(crosses, spot == number))
    def _():
        out[...] = block[...]

    if number:

        @pl.when(jnp.logical_and(crosses, spot < number))
        def _():
            out[...] = refs[1][...]


def near_kernel(group, chips, last, where, crossed, *refs):
    each = chips // 2
    near, kept, outs = refs[:each], refs[each : 2 * each], refs[2 * each :]
    rows = outs[0].shape[0]
    crosses, stays, spot = arrival(where, group, chips, last)
    arrives = jnp.logical_not(jnp.logical_or(crosses, stays))

    def give(block):
        for place, out in enumerate(outs):
            out[...] = block[place * rows : (place + 1) * rows, :]

    @pl.when(crosses)
    def _():
        give(crossed)

    for number in range(each):
        for blocks, chosen in ((near, arrives), (kept, stays)):

            @pl.when(jnp.logical_and(chosen, spot == number))
            def _(block=blocks[number]):
                give(block)


def prepare_kernel(where, snapshots, w_embed, w_decode, mesh_grid, ready, table_out):
    snapshot = snapshots[where[0]]
    latent = silu_by_tanh(matmul_tn(snapshot, w_embed[...])).astype(jnp.bfloat16)
    ready[...] = matmul(latent, w_decode[: latent.shape[1], :])
    mesh_rows, grid_rows = table_out.shape
    table = lax.broadcasted_iota(jnp.int32, (mesh_rows, grid_rows), 0) == mesh_grid[...]
    table_out[...] = jnp.where(table, 1.0, 0.0).astype(jnp.bfloat16)


def decode_kernel(where, ready, table, w_decode, w_output, *refs):
    blocks, out, state = refs[:-2], refs[-2], refs[-1]
    width = ready.shape[1]
    _, lane = place_of(where, len(blocks))
    for number, block in enumerate(blocks):

        @pl.when(lane == number)
        def _(block=block):
            state[...] = block[...]

    readout = matmul_tn(table[...], state[...]).astype(jnp.bfloat16)
    hidden = silu_by_tanh(ready[...] + matmul(readout, w_decode[width:, :])).astype(jnp.bfloat16)
    out[...] = matmul_nt(w_output[...], hidden).astype(jnp.bfloat16)


def call(kernel, name, shapes, inputs, places, scratch=(), room=16, flops=0):
    specs, given = [], []
    for value, place in zip(inputs, places):
        specs += [SMEM] * 2 if place == "w" else [VMEM if place == "v" else HBM]
        given += list(value) if place == "w" else [value]
    moved = sum(value.size * value.dtype.itemsize for value in given + list(shapes))

    def located(segment, place, *refs):
        kernel((segment[0], place[0]), *refs)

    return pl.pallas_call(
        located if places[0] == "w" else kernel,
        out_shape=shapes,
        in_specs=specs,
        out_specs=[VMEM] * len(shapes),
        scratch_shapes=list(scratch),
        name=name,
        compiler_params=pltpu.CompilerParams(vmem_limit_bytes=room * 1024 * 1024),
        cost_estimate=pl.CostEstimate(flops=flops, bytes_accessed=moved, transcendentals=0),
    )(*given)


def every_device(pairs, count, group):
    onward = dict(pairs)
    reached = set(onward.values())
    for first in [source for source in onward if source not in reached]:
        last = first
        while last in onward:
            last = onward[last]
        onward.update({last: last + group - 1, last + group - 1: first + group - 1, first + group - 1: first})
    alone = []
    for at in range(0, count, group):
        rest = [lane for lane in range(at, at + group) if lane not in onward]
        if len(rest) > 1:
            onward.update(zip(rest, rest[1:] + rest[:1]))
        else:
            alone += rest
    if len(alone) == 1:
        before = next(at for at in onward if at % group and onward[at] % group == 0)
        onward.update({before: alone[0], alone[0]: onward[before]})
    else:
        onward.update(zip(alone, alone[1:] + alone[:1]))
    return sorted(onward.items())


def resident(
    grid_state,
    w_embed,
    w_project,
    w_message,
    w_update,
    w_decode,
    w_output,
    grid_mesh,
    mesh_grid,
    neighbors,
    send_rows,
    halo_count,
):
    segment = lax.axis_index("segment")
    place = lax.axis_index("dom")
    segments = lax.axis_size("segment")
    parts = lax.axis_size("dom")
    samples, grid_rows, channels = grid_state.shape
    width = w_embed.shape[1]
    mesh_rows, fanout = neighbors.shape
    nodes = parts * mesh_rows
    group = parts // samples
    bf16 = jnp.bfloat16

    def device(at_segment, at_dom):
        return at_segment * parts + at_dom % parts

    def send(value, pairs):
        return lax.ppermute(value, ("segment", "dom"), every_device(pairs, segments * parts, group))

    def to_chip(value, steps):
        giver = steps - 1
        pairs = []
        for at in range(segments):
            for dom in range(parts):
                chip, lane = divmod(dom, group)
                across = (chip ^ steps) * group + lane
                if at == giver:
                    pairs.append((device(at, dom), device(0, across)))
                elif at == 0:
                    pairs.append((device(at, dom), device(giver, dom)))
                else:
                    pairs.append((device(at, dom), device(at, chip * group + (lane + 1) % group)))
        return lax.ppermute(value, ("segment", "dom"), pairs)

    def change_lane(value, steps):
        pairs = [(at, at - at % group + (at + steps) % group) for at in range(parts)]
        return lax.ppermute(value, "dom", pairs)

    def owner(m, at_segment):
        return device(min(at_segment, last + m % 2), m * group)

    own_segment, own_place, w_project = lax.optimization_barrier(
        (segment.reshape(1), place.reshape(1), w_project)
    )
    where = (own_segment, own_place)
    weights = [w_project, w_message, w_update]
    last = segments - 2
    to_last = [(device(last + 1 - m % 2, m * group), owner(m, segments)) for m in range(samples)]
    came_project = send(w_project, to_last)
    snapshots = jnp.transpose(grid_state, (0, 2, 1))
    lists = send_rows.shape[0]

    def rows_of(value):
        return jnp.pad(value, ((0, 0), (0, 128 - value.shape[1])))

    packed = jnp.concatenate(
        [
            rows_of(neighbors.T),
            rows_of(send_rows),
            rows_of(grid_mesh.reshape(1, grid_rows)),
            rows_of(halo_count.reshape(1, lists)),
        ],
        axis=0,
    )
    payloads = call(
        functools.partial(encode_kernel, group, mesh_rows, fanout, lists),
        "encode",
        [jax.ShapeDtypeStruct((mesh_rows + 2 * fanout, width), bf16)] * samples,
        [where, snapshots, w_embed, packed],
        "wvvv",
        [pltpu.VMEM((samples * grid_rows, width), bf16)],
    )
    held = call(
        hold_kernel,
        "hold",
        [jax.ShapeDtypeStruct((width, width), bf16)] * 4,
        weights,
        "hhh",
        [pltpu.VMEM((width, width), bf16)] * 2 + [pltpu.SemaphoreType.DMA((5,))],
    )
    own_payload, *held = lax.optimization_barrier((payloads[0], *held))
    longest_first = sorted(range(1, samples), key=lambda turn: (turn < samples // 2, turn))
    arrived = [to_chip(payloads[turn], turn) for turn in longest_first] + [own_payload]
    (joined,) = call(
        functools.partial(join_kernel, longest_first + [0]),
        "join",
        [jax.ShapeDtypeStruct((samples * (mesh_rows + 2 * fanout), width), bf16)],
        arrived,
        "v" * samples,
    )
    lanes = [joined] + [change_lane(joined, -steps) for steps in range(1, group)]
    share = group * mesh_rows
    whole, short, tall = [
        jax.ShapeDtypeStruct((rows, width), bf16) for rows in (nodes, share, share + 2 * fanout)
    ]
    columns_shape = jax.ShapeDtypeStruct((nodes, 128), bf16)
    columns, codes, state = call(
        functools.partial(index_kernel, parts, mesh_rows),
        "index",
        [columns_shape, jax.ShapeDtypeStruct((2 * fanout, width), bf16), whole],
        [where] + lanes,
        "w" + "v" * group,
        [pltpu.VMEM((fanout, nodes), jnp.int32)],
    )
    columns, came_project, *held = lax.optimization_barrier((columns, came_project, *held))
    (pair,) = call(
        functools.partial(pack_kernel, group, last),
        "pack",
        [jax.ShapeDtypeStruct((2, width, width), bf16)],
        [where] + held[2:],
        "wvv",
    )
    came = [came_project, send(pair, to_last)]
    pieces, senders, places, early = [state], [], (0,), []
    for layer in range(last + 1):
        late = layer == last
        pairs = [(owner(m, layer), owner(m, segments if layer + 1 == last else layer + 1)) for m in range(samples)]
        if layer == 0:
            order, sent = list(range(samples)), []
        else:
            first = places[1]
            order = [first] + [(first + step) % samples for step in range(1, samples)]
            (piece,) = call(
                functools.partial(early_kernel, group, layer, late, fanout, places[:-1], first),
                "early",
                [short if late else tall],
                [where, columns] + senders + [pieces[1], pieces[0]] + held + came * late,
                "w" + "v" * (3 + len(senders + held + came * late)),
                [pltpu.VMEM((nodes, width), bf16)],
            )
            if late:
                pieces[-1], piece = lax.optimization_barrier((pieces[-1], piece))
                break
            sent = [send(piece, pairs)]
            pieces[-1], columns = lax.optimization_barrier((pieces[-1], columns))
        start = order[len(sent)] * share
        extra = [codes] * (layer == 0)
        sender, joined_state, piece = call(
            functools.partial(open_kernel, group, layer, fanout, places, start),
            "open",
            [whole, whole, tall if layer == 0 else short],
            [where, columns] + pieces + senders + extra + held,
            "w" + "v" * (1 + len(pieces + senders + extra + held)),
        )
        sent.append(send(piece, pairs))
        for place_sent in order[len(sent) :]:
            (piece,) = call(
                functools.partial(next_kernel, group, layer, fanout, place_sent * share),
                "next",
                [short],
                [where, columns, sender, joined_state] + held,
                "w" + "v" * (3 + len(held)),
            )
            sent.append(send(piece, pairs))
        pieces, senders, places = sent, [], tuple(order)
        if layer == 0:
            ready, table = call(
                prepare_kernel,
                "prepare",
                [
                    jax.ShapeDtypeStruct((grid_rows, width), jnp.float32),
                    jax.ShapeDtypeStruct((mesh_rows, grid_rows), bf16),
                ],
                [where, snapshots, w_embed, w_decode, mesh_grid.reshape(1, grid_rows)],
                "wvvvv",
            )
            pieces[0], ready, table = lax.optimization_barrier((pieces[0], ready, table))
        for number, part in enumerate(pieces[:-1]):
            if senders:
                part, senders[-1] = lax.optimization_barrier((part, senders[-1]))
                pieces[number] = part
            late = layer + 1 == last
            sender, *found = call(
                functools.partial(late_sender_kernel if late else sender_kernel, group, layer + 1, fanout, share),
                "sender",
                [short] + [columns_shape] * (not senders),
                [where, part, held[1]] + came[:1] * late,
                "wvv" + "v" * late,
            )
            columns = found[0] if found else columns
            senders.append(sender)
    (state,) = call(
        functools.partial(layer_kernel, group, last, fanout, places, order[0]),
        "layer",
        [whole],
        [where, columns] + pieces + senders + [piece] + held + came,
        "w" + "v" * (2 + len(pieces + senders + held + came)),
        [pltpu.VMEM((nodes, width), bf16)] * 2,
    )
    far = []
    for begin in range(0, nodes // 2, share):
        found = call(
            functools.partial(end_kernel, group, last, samples, True, begin, not far, fanout),
            "far_part",
            [whole] * (not far) + [short],
            [where, columns, state] + ([sender] if far else []) + held + came,
            "w" + "v" * (9 if far else 8),
        )
        sender = found[0] if not far else sender
        far.append(found[-1])
    near = []
    for begin in range(0, nodes // 2, share):
        near += call(
            functools.partial(end_kernel, group, last, samples, False, begin, False, fanout),
            "near_part",
            [short],
            [where, columns, state, sender] + held + came,
            "w" + "v" * 9,
        )
    state = far + list(near)
    each = samples // 2
    arrived = []
    for far, blocks in ((1, state[:each]), (0, state[each:])):
        for turn, block in enumerate(blocks):
            if far:
                chips = [samples - 1 - turn if m < each else turn for m in range(samples)]
            else:
                chips = [m // each * each + turn for m in range(samples)]
            pairs = [(owner(m, segments), device(m, chips[m] * group)) for m in range(samples)]
            arrived.append(send(block, [pair for pair in pairs if pair[0] != pair[1]]))
    crossed = []
    for number, block in enumerate(arrived[:each]):
        crossed = call(
            functools.partial(far_kernel, group, samples, last, number),
            "far",
            [short],
            [where, block] + list(crossed),
            "wv" + "v" * len(crossed),
        )
    parts_of_block = call(
        functools.partial(near_kernel, group, samples, last),
        "near",
        [jax.ShapeDtypeStruct((mesh_rows, width), bf16)] * group,
        [where, crossed[0]] + arrived[each:] + state[each:],
        "w" + "v" * (1 + 2 * each),
    )
    handed = [parts_of_block[0]]
    for steps in range(1, group):
        handed.append(change_lane(parts_of_block[steps], steps))
    (prediction,) = call(
        decode_kernel,
        "decode",
        [jax.ShapeDtypeStruct((channels, grid_rows), bf16)],
        [where, ready, table, w_decode, w_output.T] + handed,
        "wvvvv" + "v" * group,
        [pltpu.VMEM((mesh_rows, width), bf16)],
    )
    return prediction.T.reshape(1, grid_rows, channels)


def chosen_plan(mesh, *arrays):
    segments, parts = mesh.shape["segment"], mesh.shape["dom"]
    samples, width = arrays[0].shape[0], arrays[1].shape[1]
    nodes = parts * arrays[9].shape[0]
    fits = samples == segments == 4 and parts % samples == 0 and parts > samples and nodes == width
    return (resident if fits else streamed)(*arrays)


def solution(mesh):
    return jax.shard_map(
        functools.partial(chosen_plan, mesh),
        mesh=mesh,
        in_specs=(
            P(None, "dom", None),
            P(),
            P("segment", None, None),
            P("segment", None, None),
            P("segment", None, None),
            P(),
            P(),
            P("dom"),
            P("dom"),
            P("dom", None),
            P(None, "dom"),
            P(None, "dom"),
        ),
        out_specs=P("segment", "dom", None),
        check_vma=False,
    )
```

```python
import functools

import jax
import jax.numpy as jnp
from jax import lax
from jax.experimental import pallas as pl
from jax.experimental.pallas import tpu as pltpu
from jax.sharding import PartitionSpec as P

epsilon = 1e-05
DIGIT = 256
VMEM = pl.BlockSpec(memory_space=pltpu.VMEM)
SMEM = pl.BlockSpec(memory_space=pltpu.SMEM)
HBM = pl.BlockSpec(memory_space=pltpu.HBM)


def from_behind(value, axis, steps):
    count = lax.axis_size(axis)
    pairs = [(source, (source + steps) % count) for source in range(count)]
    return lax.ppermute(value, axis, pairs)


def from_behind_2(block, axis, distance):
    devices = range(lax.axis_size(axis))
    route = [(i - distance, i) for i in devices if i - distance in devices]
    return lax.ppermute(block, axis, route)


def from_root(value, axis, source):
    kept = jnp.where(lax.axis_index(axis) == source, value, 0).astype(value.dtype)
    return lax.psum(kept, axis)


def rms_scale(values):
    return values * lax.rsqrt(jnp.mean(values * values, axis=-1, keepdims=True) + epsilon)


def streamed(
    grid_state,
    w_embed,
    w_project,
    w_message,
    w_update,
    w_decode,
    w_output,
    grid_mesh,
    mesh_grid,
    neighbors,
    send_rows,
    halo_count,
):
    segment_index = lax.axis_index("segment")
    segment_count = lax.axis_size("segment")
    final_segment = segment_count - 1
    samples, grid_rows, channels = grid_state.shape
    width = w_embed.shape[1]
    mesh_rows = neighbors.shape[0]
    fanout = neighbors.shape[1]
    halo_rows = send_rows.shape[1]
    share = samples // segment_count
    pool_table = (grid_mesh[None, :] == jnp.arange(mesh_rows, dtype=jnp.int32)[:, None]).astype(
        jnp.bfloat16
    )
    read_table = (mesh_grid[:, None] == jnp.arange(mesh_rows, dtype=jnp.int32)[None, :]).astype(
        jnp.bfloat16
    )
    valid_rows = jnp.arange(halo_rows, dtype=jnp.int32)[None, :] < halo_count[:, 0][:, None]
    source_rows = neighbors.reshape(mesh_rows * fanout)

    def embed_grid(snapshot):
        return jax.nn.silu(jnp.dot(snapshot, w_embed, preferred_element_type=jnp.float32)).astype(
            jnp.bfloat16
        )

    def encode(snapshot):
        latent = embed_grid(snapshot)
        pooled = jnp.dot(pool_table, latent, preferred_element_type=jnp.float32)
        return (rms_scale(pooled).astype(jnp.bfloat16), latent)

    def project(state, weights):
        projected = jnp.dot(state, weights[0], preferred_element_type=jnp.float32)
        return (projected[:, :width], projected[:, width:].astype(jnp.bfloat16))

    def renew(state, receiver, extended, weights):
        fetched = extended[source_rows].reshape(mesh_rows, fanout, width)
        edges = jax.nn.silu(receiver[:, None, :] + fetched.astype(jnp.float32)).astype(jnp.bfloat16)
        messages = jnp.dot(
            edges.reshape(mesh_rows * fanout, width), weights[1], preferred_element_type=jnp.float32
        )
        aggregate = (jnp.sum(messages.reshape(mesh_rows, fanout, width), axis=1) / fanout).astype(
            jnp.bfloat16
        )
        update = jax.nn.silu(
            jnp.dot(state, weights[2][:width], preferred_element_type=jnp.float32)
            + jnp.dot(aggregate, weights[2][width:], preferred_element_type=jnp.float32)
        )
        return (state.astype(jnp.float32) + rms_scale(update)).astype(jnp.bfloat16)

    def decode(state, latent):
        readout = jnp.dot(read_table, state, preferred_element_type=jnp.float32).astype(
            jnp.bfloat16
        )
        hidden = jax.nn.silu(
            jnp.dot(latent, w_decode[:width], preferred_element_type=jnp.float32)
            + jnp.dot(readout, w_decode[width:], preferred_element_type=jnp.float32)
        ).astype(jnp.bfloat16)
        return jnp.dot(hidden, w_output, preferred_element_type=jnp.float32).astype(jnp.bfloat16)

    own_weights = (w_project[0], w_message[0], w_update[0])
    empty_mesh = jnp.zeros((mesh_rows, width), jnp.bfloat16)
    empty_receiver = jnp.zeros((mesh_rows, width), jnp.float32)
    empty_grid = jnp.zeros((grid_rows, width), jnp.bfloat16)
    empty_output = jnp.zeros((grid_rows, channels), jnp.bfloat16)
    received = empty_mesh
    carried = {}
    results = [empty_output for sample in range(samples)]
    for moment in range(samples + final_segment):
        current = received
        if moment < samples:
            snapshot = grid_state[moment]
            started, latent = lax.cond(
                segment_index == 0, lambda: encode(snapshot), lambda: (empty_mesh, empty_grid)
            )
            current = jnp.where(segment_index == 0, started, received)
            carried[moment] = from_behind_2(latent, "segment", final_segment)
        active = (moment - segment_index >= 0) & (moment - segment_index < samples)
        receiver, outgoing = lax.cond(
            active, lambda: project(current, own_weights), lambda: (empty_receiver, empty_mesh)
        )
        picked = jnp.where(valid_rows[:, :, None], outgoing[send_rows], jnp.zeros((), jnp.bfloat16))
        arrived = [outgoing]
        for list_index, offset in enumerate((1, -1, 2, -2)):
            arrived.append(from_behind(picked[list_index], "dom", offset))
        extended = jnp.concatenate(arrived, axis=0)
        renewed = lax.cond(
            active, lambda: renew(current, receiver, extended, own_weights), lambda: empty_mesh
        )
        if moment >= final_segment:
            finished = moment - final_segment
            skipped = carried[finished]
            results[finished] = lax.cond(
                segment_index == final_segment,
                lambda: decode(renewed, skipped),
                lambda: empty_output,
            )
        if moment < samples + final_segment - 1:
            received = from_behind_2(renewed, "segment", 1)
    everything = from_root(jnp.stack(results), "segment", final_segment)
    return lax.dynamic_slice_in_dim(everything, segment_index * share, share, 0)


def silu_by_tanh(values):
    half = 0.5 * values
    return half + half * jnp.tanh(half)


def matmul(left, right):
    return jnp.dot(left, right, preferred_element_type=jnp.float32)


def matmul_nt(left, right):
    return lax.dot_general(left, right, (((1,), (1,)), ((), ())), preferred_element_type=jnp.float32)


def matmul_tn(left, right):
    return lax.dot_general(left, right, (((0,), (0,)), ((), ())), preferred_element_type=jnp.float32)


def place_of(where, group):
    return lax.div(where[1], group), lax.rem(where[1], group)


def owns(where, group, at_segment):
    return jnp.logical_and(where[0] == at_segment, lax.rem(where[1], group) == 0)


def swapped_roles(where, group, at_segment):
    chip, lane = place_of(where, group)
    for number in range(2):
        here = jnp.logical_and(where[0] == at_segment + number, lane == 0)
        yield jnp.logical_and(here, lax.rem(chip, 2) == number), number


def weights_of(came, held, own):
    if own:
        return [block[...] for block in held]
    w_project, pair = came
    width = pair.shape[1]
    return [w_project[0, :, :width], w_project[0, :, width:], pair[0], pair[1]]


def fetch(sources, targets, semaphores):
    copies = [
        pltpu.make_async_copy(source, target, semaphores.at[place])
        for place, (source, target) in enumerate(zip(sources, targets))
    ]
    for copy in copies:
        copy.start()
    return copies


def encode_kernel(group, mesh_rows, fanout, lists, where, snapshots, w_embed, packed, *refs):
    payloads, latent = refs[:-1], refs[-1]
    chip, _ = place_of(where, group)
    neighbors = packed[:fanout, :mesh_rows]
    grid_rows = snapshots.shape[2]
    grid_mesh = packed[fanout + lists : fanout + lists + 1, :grid_rows]
    counts = packed[fanout + lists + 1 : fanout + lists + 2, :lists]
    width = w_embed.shape[1]
    for place in range(snapshots.shape[0]):
        found = silu_by_tanh(matmul_tn(snapshots[place], w_embed[...])).astype(jnp.bfloat16)
        latent[place * grid_rows : (place + 1) * grid_rows, :] = found
    table = lax.broadcasted_iota(jnp.int32, (mesh_rows, grid_rows), 0) == grid_mesh
    table = jnp.where(table, 1.0, 0.0).astype(jnp.bfloat16)
    block = neighbors // mesh_rows
    row = neighbors - block * mesh_rows
    halo_rows = mesh_rows
    position = lax.broadcasted_iota(jnp.int32, (1, halo_rows), 1)
    rows = []
    for list_index in range(lists):
        kept = position < counts[:, list_index : list_index + 1]
        listed = packed[fanout + list_index : fanout + list_index + 1, :halo_rows]
        rows.append(jnp.where(kept, listed, mesh_rows))
    rows.append(jnp.zeros((fanout - lists, halo_rows), jnp.int32))
    filler = jnp.zeros((fanout, 128 - mesh_rows), jnp.int32)
    pieces = [block, filler, row, filler, jnp.concatenate(rows, axis=0), filler]
    coded = jnp.concatenate(pieces + [jnp.zeros((fanout, width - 384), jnp.int32)], axis=1)
    coded = jnp.concatenate([coded, jnp.zeros_like(coded)], axis=0)
    coded = coded.astype(jnp.float32).astype(jnp.bfloat16)
    for turn, payload in enumerate(payloads):
        start = pl.multiple_of(jnp.bitwise_xor(chip, turn) * grid_rows, grid_rows)
        pooled = matmul(table, latent[pl.ds(start, grid_rows), :])
        payload[:mesh_rows, :] = rms_scale(pooled).astype(jnp.bfloat16)
        payload[mesh_rows:, :] = coded


def join_kernel(places, *refs):
    payloads, joined = refs[:-1], refs[-1]
    rows = payloads[0].shape[0]
    for place, payload in zip(places, payloads):
        joined[place * rows : (place + 1) * rows, :] = payload[...]


def columns_of(names):
    fanout, nodes = names.shape
    tile = min(nodes, DIGIT)
    rows = [names - number * tile for number in range(nodes // tile)]
    rows.append(jnp.zeros((128 - fanout * len(rows), nodes), jnp.float32))
    return jnp.transpose(jnp.concatenate(rows, axis=0)).astype(jnp.bfloat16)


def index_kernel(parts, mesh_rows, where, *refs):
    lanes, (columns_out, codes, state), index_out = refs[:-4], refs[-4:-1], refs[-1]
    nodes = columns_out.shape[0]
    group = len(lanes)
    rows = lanes[0].shape[0] // (parts // group)
    chip, _ = place_of(where, group)

    @pl.when(owns(where, group, 0))
    def _():
        tables = []
        for part in range(parts):
            lane, turn = lanes[part % group], jnp.bitwise_xor(chip, part // group)
            base = pl.multiple_of(turn * rows, 16)
            state[part * mesh_rows : (part + 1) * mesh_rows, :] = lane[pl.ds(base, mesh_rows), :]
            base = pl.multiple_of(turn * rows + mesh_rows, 16)
            coded = lane[pl.ds(base, rows - mesh_rows), :384].astype(jnp.float32).astype(jnp.int32)
            tables.append(coded[: coded.shape[0] // 2])
        fanout = tables[0].shape[0]
        for part in range(parts):
            block = tables[part][:, :128]
            row = tables[part][:, 128:256]
            found = part * mesh_rows + row
            for list_index, offset in enumerate((-1, 1, -2, 2)):
                source = (part + offset) % parts
                lists = tables[source][list_index : list_index + 1, 256:384]
                lists = jnp.broadcast_to(lists, (fanout, 128))
                picked = jnp.take_along_axis(lists, row, axis=1)
                picked = jnp.where(picked == mesh_rows, parts * mesh_rows, source * mesh_rows + picked)
                found = jnp.where(block == list_index + 1, picked, found)
            index_out[:, part * mesh_rows : (part + 1) * mesh_rows] = found[:, :mesh_rows]
        names = index_out[...]
        high_digit = names // DIGIT
        digits = jnp.concatenate([high_digit, names - high_digit * DIGIT], axis=0)
        codes[...] = digits.astype(jnp.float32).astype(jnp.bfloat16)
        columns_out[...] = columns_of(names.astype(jnp.float32))


def pack_kernel(group, at_segment, where, *refs):
    @pl.when(jnp.logical_or(owns(where, group, at_segment), owns(where, group, at_segment + 1)))
    def _():
        for place, block in enumerate(refs[:-1]):
            refs[-1][place] = block[...]


def hold_kernel(w_project, w_message, w_update, receive, send, own, edges, message, update, semaphores):
    width = own.shape[0]
    sources = [
        w_message.at[0],
        w_update.at[0, width:],
        w_project.at[0, :, :width],
        w_project.at[0, :, width:],
        w_update.at[0, :width],
    ]
    copies = fetch(sources, [message, update, receive, send, own], semaphores)
    copies[0].wait()
    copies[1].wait()
    edges[...] = matmul(message[...], update[...]).astype(jnp.bfloat16)
    for copy in copies[2:]:
        copy.wait()


def sum_edges(fanout, columns, sender, own, w_receive):
    chunk, width = own.shape
    nodes = sender.shape[0]
    tile = min(nodes, DIGIT)
    names = lax.broadcasted_iota(jnp.int32, (chunk, tile), 1).astype(jnp.float32).astype(jnp.bfloat16)
    one_half = jnp.full((chunk, tile), 0.5, jnp.bfloat16)
    none = jnp.zeros((chunk, tile), jnp.bfloat16)
    receiver = 0.5 * matmul(own, w_receive)
    total = jnp.zeros((chunk, width), jnp.float32)
    for first in range(0, fanout, 2):
        tables = []
        for k in range(first, min(first + 2, fanout)):
            hits = []
            for number in range(nodes // tile):
                lane = number * fanout + k
                hits.append(jnp.where(columns[:, lane : lane + 1] == names, one_half, none))
            tables.append(jnp.concatenate(hits, axis=1))
        fetched = matmul(jnp.concatenate(tables, axis=0), sender)
        for place in range(len(tables)):
            half = receiver + fetched[place * chunk : (place + 1) * chunk]
            total = total + (half + half * jnp.tanh(half))
    return (total * (1.0 / fanout)).astype(jnp.bfloat16)


def update_nodes(own, gathered, w_own, w_edges):
    update = silu_by_tanh(matmul(own, w_own) + matmul(gathered, w_edges))
    return (own.astype(jnp.float32) + rms_scale(update)).astype(jnp.bfloat16)


def sender_kernel(group, at_segment, fanout, rows, where, state, w_send, sender, *columns):
    @pl.when(owns(where, group, at_segment))
    def _():
        sender[...] = matmul(state[:rows, :], w_send[...]).astype(jnp.bfloat16)
        if columns:
            digits = state[rows:, :].astype(jnp.float32)
            columns[0][...] = columns_of(digits[:fanout] * DIGIT + digits[fanout:])


def late_sender_kernel(group, at_segment, fanout, rows, where, state, w_send, w_project, sender, *columns):
    width = state.shape[1]
    for here, number in swapped_roles(where, group, at_segment):

        @pl.when(here)
        def _(number=number):
            weights = w_project[0, :, width:] if number else w_send[...]
            sender[...] = matmul(state[:rows, :], weights).astype(jnp.bfloat16)
            if columns:
                digits = state[rows:, :].astype(jnp.float32)
                columns[0][...] = columns_of(digits[:fanout] * DIGIT + digits[fanout:])


def roles(where, group, at_segment, late):
    return swapped_roles(where, group, at_segment) if late else [(owns(where, group, at_segment), 0)]


def early_kernel(group, at_segment, late, fanout, places, quarter, where, columns, *refs):
    count = len(places)
    senders, refs = refs[:count], refs[count:]
    (own, coded), held, came, (piece, sender) = refs[:2], refs[2:6], refs[6:-2], refs[-2:]
    rows = senders[0].shape[0]
    for here, number in roles(where, group, at_segment, late):

        @pl.when(here)
        def _(number=number):
            w_receive, _, w_own, w_edges = weights_of(came, held, number == 0)
            sender[...] = jnp.zeros_like(sender)
            for place, part in zip(places, senders):
                sender[place * rows : (place + 1) * rows, :] = part[...]
            state = own[:rows, :]
            span = slice(quarter * rows, (quarter + 1) * rows)
            gathered = sum_edges(fanout, columns[span, :], sender[...], state, w_receive)
            piece[:rows, :] = update_nodes(state, gathered, w_own, w_edges)
            if piece.shape[0] > rows:
                piece[rows:, :] = coded[rows:, :]


def layer_kernel(group, at_segment, fanout, places, quarter, where, columns, *refs):
    parts = len(places)
    state, senders, refs = refs[:parts], refs[parts : 2 * parts - 1], refs[2 * parts - 1 :]
    done, held, came, (renewed, whole, sender) = refs[0], refs[1:5], refs[5:7], refs[7:]
    rows = done.shape[0]
    spans = [slice(place * rows, (place + 1) * rows) for place in places]
    own = slice(quarter * rows, (quarter + 1) * rows)
    rest = [slice(0, own.start), slice(own.stop, renewed.shape[0])]
    for here, number in swapped_roles(where, group, at_segment):

        @pl.when(here)
        def _(number=number):
            w_receive, w_send, w_own, w_edges = weights_of(came, held, number == 0)
            for span, part in zip(spans, state):
                whole[span, :] = part[:rows, :]
            for span, part in zip(spans, senders):
                sender[span, :] = part[...]
            sender[spans[-1], :] = matmul(whole[spans[-1], :], w_send).astype(jnp.bfloat16)
            renewed[own, :] = done[...]
            for span in rest:
                if span.stop > span.start:
                    gathered = sum_edges(fanout, columns[span, :], sender[...], whole[span, :], w_receive)
                    renewed[span, :] = update_nodes(whole[span, :], gathered, w_own, w_edges)


def open_kernel(group, at_segment, fanout, places, start, where, columns, *refs):
    parts = len(places)
    state, senders, refs = refs[:parts], refs[parts : 2 * parts - 1], refs[2 * parts - 1 :]
    codes, (w_receive, w_send, w_own, w_edges), (sender, whole, piece) = refs[:-7], refs[-7:-3], refs[-3:]
    rows = whole.shape[0] // parts
    spans = [slice(place * rows, (place + 1) * rows) for place in places]

    @pl.when(owns(where, group, at_segment))
    def _():
        for span, part in zip(spans, state):
            whole[span, :] = part[:rows, :]
        for span, part in zip(spans, senders):
            sender[span, :] = part[...]
        sender[spans[-1], :] = matmul(whole[spans[-1], :], w_send[...]).astype(jnp.bfloat16)
        count = piece.shape[0] - (codes[0].shape[0] if codes else 0)
        span = slice(start, start + count)
        own = whole[span, :]
        gathered = sum_edges(fanout, columns[span, :], sender[...], own, w_receive[...])
        piece[:count, :] = update_nodes(own, gathered, w_own[...], w_edges[...])
        if codes:
            piece[count:, :] = codes[0][...]


def next_kernel(group, at_segment, fanout, start, where, columns, sender, whole, *refs):
    w_receive, _, w_own, w_edges, piece = refs
    span = slice(start, start + piece.shape[0])

    @pl.when(owns(where, group, at_segment))
    def _():
        own = whole[span, :]
        gathered = sum_edges(fanout, columns[span, :], sender[...], own, w_receive[...])
        piece[...] = update_nodes(own, gathered, w_own[...], w_edges[...])


def end_kernel(group, at_segment, chips, far, begin, first, fanout, where, columns, state, *refs):
    senders, refs = (refs[:0], refs) if first else (refs[:1], refs[1:])
    held, came, outs = refs[:4], refs[4:6], refs[6:]
    half = state.shape[0] // 2
    chip, _ = place_of(where, group)
    for here, number in swapped_roles(where, group, at_segment):

        @pl.when(here)
        def _(number=number):
            w_receive, w_send, w_own, w_edges = weights_of(came, held, number == 1)
            pieces = outs
            if first:
                outs[0][...] = matmul(state[...], w_send).astype(jnp.bfloat16)
                pieces = outs[1:]
            sender = outs[0] if first else senders[0]
            rows = sum(piece.shape[0] for piece in pieces)
            upper = (chip < chips // 2) if far else (chip >= chips // 2)
            start = pl.multiple_of(jnp.where(upper, half, 0) + begin, rows)
            own = state[pl.ds(start, rows), :]
            gathered = sum_edges(fanout, columns[pl.ds(start, rows), :], sender[...], own, w_receive)
            write_pieces(pieces, update_nodes(own, gathered, w_own, w_edges))


def write_pieces(pieces, value):
    rows = value.shape[0] // len(pieces)
    for place, piece in enumerate(pieces):
        piece[:rows, :] = value[place * rows : (place + 1) * rows]


def arrival(where, group, chips, last):
    each = chips // 2
    segment = where[0]
    chip, _ = place_of(where, group)
    crosses = lax.div(chip, each) != lax.div(segment, each)
    return crosses, jnp.logical_and(segment >= last, chip == segment), lax.rem(chip, each)


def far_kernel(group, chips, last, number, where, *refs):
    block, out = refs[0], refs[-1]
    crosses, _, spot = arrival(where, group, chips, last)

    @pl.when(jnp.logical_and(crosses, spot == number))
    def _():
        out[...] = block[...]

    if number:

        @pl.when(jnp.logical_and(crosses, spot < number))
        def _():
            out[...] = refs[1][...]


def near_kernel(group, chips, last, where, crossed, *refs):
    each = chips // 2
    near, kept, outs = refs[:each], refs[each : 2 * each], refs[2 * each :]
    rows = outs[0].shape[0]
    crosses, stays, spot = arrival(where, group, chips, last)
    arrives = jnp.logical_not(jnp.logical_or(crosses, stays))

    def give(block):
        for place, out in enumerate(outs):
            out[...] = block[place * rows : (place + 1) * rows, :]

    @pl.when(crosses)
    def _():
        give(crossed)

    for number in range(each):
        for blocks, chosen in ((near, arrives), (kept, stays)):

            @pl.when(jnp.logical_and(chosen, spot == number))
            def _(block=blocks[number]):
                give(block)


def prepare_kernel(where, snapshots, w_embed, w_decode, mesh_grid, ready, table_out):
    snapshot = snapshots[where[0]]
    latent = silu_by_tanh(matmul_tn(snapshot, w_embed[...])).astype(jnp.bfloat16)
    ready[...] = matmul(latent, w_decode[: latent.shape[1], :])
    mesh_rows, grid_rows = table_out.shape
    table = lax.broadcasted_iota(jnp.int32, (mesh_rows, grid_rows), 0) == mesh_grid[...]
    table_out[...] = jnp.where(table, 1.0, 0.0).astype(jnp.bfloat16)


def decode_kernel(where, ready, table, w_decode, w_output, *refs):
    blocks, out, state = refs[:-2], refs[-2], refs[-1]
    width = ready.shape[1]
    _, lane = place_of(where, len(blocks))
    for number, block in enumerate(blocks):

        @pl.when(lane == number)
        def _(block=block):
            state[...] = block[...]

    readout = matmul_tn(table[...], state[...]).astype(jnp.bfloat16)
    hidden = silu_by_tanh(ready[...] + matmul(readout, w_decode[width:, :])).astype(jnp.bfloat16)
    out[...] = matmul_nt(w_output[...], hidden).astype(jnp.bfloat16)


def call(kernel, name, shapes, inputs, places, scratch=(), room=16, flops=0):
    specs, given = [], []
    for value, place in zip(inputs, places):
        specs += [SMEM] * 2 if place == "w" else [VMEM if place == "v" else HBM]
        given += list(value) if place == "w" else [value]
    moved = sum(value.size * value.dtype.itemsize for value in given + list(shapes))

    def located(segment, place, *refs):
        kernel((segment[0], place[0]), *refs)

    return pl.pallas_call(
        located if places[0] == "w" else kernel,
        out_shape=shapes,
        in_specs=specs,
        out_specs=[VMEM] * len(shapes),
        scratch_shapes=list(scratch),
        name=name,
        compiler_params=pltpu.CompilerParams(vmem_limit_bytes=room * 1024 * 1024),
        cost_estimate=pl.CostEstimate(flops=flops, bytes_accessed=moved, transcendentals=0),
    )(*given)


def every_device(pairs, count, group):
    onward = dict(pairs)
    reached = set(onward.values())
    for first in [source for source in onward if source not in reached]:
        last = first
        while last in onward:
            last = onward[last]
        onward.update({last: last + group - 1, last + group - 1: first + group - 1, first + group - 1: first})
    alone = []
    for at in range(0, count, group):
        rest = [lane for lane in range(at, at + group) if lane not in onward]
        if len(rest) > 1:
            onward.update(zip(rest, rest[1:] + rest[:1]))
        else:
            alone += rest
    if len(alone) == 1:
        before = next(at for at in onward if at % group and onward[at] % group == 0)
        onward.update({before: alone[0], alone[0]: onward[before]})
    else:
        onward.update(zip(alone, alone[1:] + alone[:1]))
    return sorted(onward.items())


def resident(
    grid_state,
    w_embed,
    w_project,
    w_message,
    w_update,
    w_decode,
    w_output,
    grid_mesh,
    mesh_grid,
    neighbors,
    send_rows,
    halo_count,
):
    segment = lax.axis_index("segment")
    place = lax.axis_index("dom")
    segments = lax.axis_size("segment")
    parts = lax.axis_size("dom")
    samples, grid_rows, channels = grid_state.shape
    width = w_embed.shape[1]
    mesh_rows, fanout = neighbors.shape
    nodes = parts * mesh_rows
    group = parts // samples
    bf16 = jnp.bfloat16

    def device(at_segment, at_dom):
        return at_segment * parts + at_dom % parts

    def send(value, pairs):
        return lax.ppermute(value, ("segment", "dom"), every_device(pairs, segments * parts, group))

    def to_chip(value, steps):
        giver = steps - 1
        pairs = []
        for at in range(segments):
            for dom in range(parts):
                chip, lane = divmod(dom, group)
                across = (chip ^ steps) * group + lane
                if at == giver:
                    pairs.append((device(at, dom), device(0, across)))
                elif at == 0:
                    pairs.append((device(at, dom), device(giver, dom)))
                else:
                    pairs.append((device(at, dom), device(at, chip * group + (lane + 1) % group)))
        return lax.ppermute(value, ("segment", "dom"), pairs)

    def change_lane(value, steps):
        pairs = [(at, at - at % group + (at + steps) % group) for at in range(parts)]
        return lax.ppermute(value, "dom", pairs)

    def owner(m, at_segment):
        return device(min(at_segment, last + m % 2), m * group)

    own_segment, own_place, w_project = lax.optimization_barrier(
        (segment.reshape(1), place.reshape(1), w_project)
    )
    where = (own_segment, own_place)
    weights = [w_project, w_message, w_update]
    last = segments - 2
    to_last = [(device(last + 1 - m % 2, m * group), owner(m, segments)) for m in range(samples)]
    came_project = send(w_project, to_last)
    snapshots = jnp.transpose(grid_state, (0, 2, 1))
    lists = send_rows.shape[0]

    def rows_of(value):
        return jnp.pad(value, ((0, 0), (0, 128 - value.shape[1])))

    packed = jnp.concatenate(
        [
            rows_of(neighbors.T),
            rows_of(send_rows),
            rows_of(grid_mesh.reshape(1, grid_rows)),
            rows_of(halo_count.reshape(1, lists)),
        ],
        axis=0,
    )
    payloads = call(
        functools.partial(encode_kernel, group, mesh_rows, fanout, lists),
        "encode",
        [jax.ShapeDtypeStruct((mesh_rows + 2 * fanout, width), bf16)] * samples,
        [where, snapshots, w_embed, packed],
        "wvvv",
        [pltpu.VMEM((samples * grid_rows, width), bf16)],
    )
    held = call(
        hold_kernel,
        "hold",
        [jax.ShapeDtypeStruct((width, width), bf16)] * 4,
        weights,
        "hhh",
        [pltpu.VMEM((width, width), bf16)] * 2 + [pltpu.SemaphoreType.DMA((5,))],
    )
    own_payload, *held = lax.optimization_barrier((payloads[0], *held))
    longest_first = sorted(range(1, samples), key=lambda turn: (turn < samples // 2, turn))
    arrived = [to_chip(payloads[turn], turn) for turn in longest_first] + [own_payload]
    (joined,) = call(
        functools.partial(join_kernel, longest_first + [0]),
        "join",
        [jax.ShapeDtypeStruct((samples * (mesh_rows + 2 * fanout), width), bf16)],
        arrived,
        "v" * samples,
    )
    lanes = [joined] + [change_lane(joined, -steps) for steps in range(1, group)]
    share = group * mesh_rows
    whole, short, tall = [
        jax.ShapeDtypeStruct((rows, width), bf16) for rows in (nodes, share, share + 2 * fanout)
    ]
    columns_shape = jax.ShapeDtypeStruct((nodes, 128), bf16)
    columns, codes, state = call(
        functools.partial(index_kernel, parts, mesh_rows),
        "index",
        [columns_shape, jax.ShapeDtypeStruct((2 * fanout, width), bf16), whole],
        [where] + lanes,
        "w" + "v" * group,
        [pltpu.VMEM((fanout, nodes), jnp.int32)],
    )
    columns, came_project, *held = lax.optimization_barrier((columns, came_project, *held))
    (pair,) = call(
        functools.partial(pack_kernel, group, last),
        "pack",
        [jax.ShapeDtypeStruct((2, width, width), bf16)],
        [where] + held[2:],
        "wvv",
    )
    came = [came_project, send(pair, to_last)]
    pieces, senders, places, early = [state], [], (0,), []
    for layer in range(last + 1):
        late = layer == last
        pairs = [(owner(m, layer), owner(m, segments if layer + 1 == last else layer + 1)) for m in range(samples)]
        if layer == 0:
            order, sent = list(range(samples)), []
        else:
            first = places[1]
            order = [first] + [(first + step) % samples for step in range(1, samples)]
            (piece,) = call(
                functools.partial(early_kernel, group, layer, late, fanout, places[:-1], first),
                "early",
                [short if late else tall],
                [where, columns] + senders + [pieces[1], pieces[0]] + held + came * late,
                "w" + "v" * (3 + len(senders + held + came * late)),
                [pltpu.VMEM((nodes, width), bf16)],
            )
            if late:
                pieces[-1], piece = lax.optimization_barrier((pieces[-1], piece))
                break
            sent = [send(piece, pairs)]
            pieces[-1], columns = lax.optimization_barrier((pieces[-1], columns))
        start = order[len(sent)] * share
        extra = [codes] * (layer == 0)
        sender, joined_state, piece = call(
            functools.partial(open_kernel, group, layer, fanout, places, start),
            "open",
            [whole, whole, tall if layer == 0 else short],
            [where, columns] + pieces + senders + extra + held,
            "w" + "v" * (1 + len(pieces + senders + extra + held)),
        )
        sent.append(send(piece, pairs))
        for place_sent in order[len(sent) :]:
            (piece,) = call(
                functools.partial(next_kernel, group, layer, fanout, place_sent * share),
                "next",
                [short],
                [where, columns, sender, joined_state] + held,
                "w" + "v" * (3 + len(held)),
            )
            sent.append(send(piece, pairs))
        pieces, senders, places = sent, [], tuple(order)
        if layer == 0:
            ready, table = call(
                prepare_kernel,
                "prepare",
                [
                    jax.ShapeDtypeStruct((grid_rows, width), jnp.float32),
                    jax.ShapeDtypeStruct((mesh_rows, grid_rows), bf16),
                ],
                [where, snapshots, w_embed, w_decode, mesh_grid.reshape(1, grid_rows)],
                "wvvvv",
            )
            pieces[0], ready, table = lax.optimization_barrier((pieces[0], ready, table))
        for number, part in enumerate(pieces[:-1]):
            if senders:
                part, senders[-1] = lax.optimization_barrier((part, senders[-1]))
                pieces[number] = part
            late = layer + 1 == last
            sender, *found = call(
                functools.partial(late_sender_kernel if late else sender_kernel, group, layer + 1, fanout, share),
                "sender",
                [short] + [columns_shape] * (not senders),
                [where, part, held[1]] + came[:1] * late,
                "wvv" + "v" * late,
            )
            columns = found[0] if found else columns
            senders.append(sender)
    (state,) = call(
        functools.partial(layer_kernel, group, last, fanout, places, order[0]),
        "layer",
        [whole],
        [where, columns] + pieces + senders + [piece] + held + came,
        "w" + "v" * (2 + len(pieces + senders + held + came)),
        [pltpu.VMEM((nodes, width), bf16)] * 2,
    )
    far = []
    for begin in range(0, nodes // 2, share):
        found = call(
            functools.partial(end_kernel, group, last, samples, True, begin, not far, fanout),
            "far_part",
            [whole] * (not far) + [short],
            [where, columns, state] + ([sender] if far else []) + held + came,
            "w" + "v" * (9 if far else 8),
        )
        sender = found[0] if not far else sender
        far.append(found[-1])
    near = []
    for begin in range(0, nodes // 2, share):
        near += call(
            functools.partial(end_kernel, group, last, samples, False, begin, False, fanout),
            "near_part",
            [short],
            [where, columns, state, sender] + held + came,
            "w" + "v" * 9,
        )
    state = far + list(near)
    each = samples // 2
    arrived = []
    for far, blocks in ((1, state[:each]), (0, state[each:])):
        for turn, block in enumerate(blocks):
            pairs = [
                (owner(m, segments), device(m, ((m // each ^ far) * each + turn) * group)) for m in range(samples)
            ]
            arrived.append(send(block, [pair for pair in pairs if pair[0] != pair[1]]))
    crossed = []
    for number, block in enumerate(arrived[:each]):
        crossed = call(
            functools.partial(far_kernel, group, samples, last, number),
            "far",
            [short],
            [where, block] + list(crossed),
            "wv" + "v" * len(crossed),
        )
    parts_of_block = call(
        functools.partial(near_kernel, group, samples, last),
        "near",
        [jax.ShapeDtypeStruct((mesh_rows, width), bf16)] * group,
        [where, crossed[0]] + arrived[each:] + state[each:],
        "w" + "v" * (1 + 2 * each),
    )
    handed = [parts_of_block[0]]
    for steps in range(1, group):
        handed.append(change_lane(parts_of_block[steps], steps))
    (prediction,) = call(
        decode_kernel,
        "decode",
        [jax.ShapeDtypeStruct((channels, grid_rows), bf16)],
        [where, ready, table, w_decode, w_output.T] + handed,
        "wvvvv" + "v" * group,
        [pltpu.VMEM((mesh_rows, width), bf16)],
    )
    return prediction.T.reshape(1, grid_rows, channels)


def chosen_plan(mesh, *arrays):
    segments, parts = mesh.shape["segment"], mesh.shape["dom"]
    samples, width = arrays[0].shape[0], arrays[1].shape[1]
    nodes = parts * arrays[9].shape[0]
    fits = samples == segments == 4 and parts % samples == 0 and parts > samples and nodes == width
    return (resident if fits else streamed)(*arrays)


def solution(mesh):
    return jax.shard_map(
        functools.partial(chosen_plan, mesh),
        mesh=mesh,
        in_specs=(
            P(None, "dom", None),
            P(),
            P("segment", None, None),
            P("segment", None, None),
            P("segment", None, None),
            P(),
            P(),
            P("dom"),
            P("dom"),
            P("dom", None),
            P(None, "dom"),
            P(None, "dom"),
        ),
        out_specs=P("segment", "dom", None),
        check_vma=False,
    )
```
